32 devices in a mesh: rep: 2 (over x), sp: 16 (over z, y, core).
Axes of the slice: x: 2, y: 2, z: 4, core: 2. Of those that a mesh axis runs over, the one named last changes fastest.
Arguments:
- volume: bfloat16 [128, 16, 16, 128], P(('rep', 'sp')), parts along dimension 0, may hold values from -6 to 6
- first_kernel: bfloat16 [3, 3, 3, 128, 128], replicated, may hold values from -0.15625 to 0.15625
- second_kernel: bfloat16 [3, 3, 3, 128, 256], replicated, may hold values from -0.15625 to 0.15625
- deep_kernel: bfloat16 [3, 3, 3, 256, 512], P(None, None, None, None, 'sp'), may hold values from -0.109375 to 0.109375
- deeper_kernel: bfloat16 [3, 3, 3, 512, 512], P(None, None, None, None, 'sp'), may hold values from -0.078125 to 0.078125
- rise_kernel: bfloat16 [2, 2, 2, 512, 256], replicated, may hold values from -0.375 to 0.375
- decode_kernel: bfloat16 [3, 3, 3, 512, 256], P(None, None, None, 'sp'), may hold values from -0.078125 to 0.078125
- final_kernel: bfloat16 [2, 2, 2, 256, 128], replicated, may hold values from -0.5 to 0.5
Outputs:
- segmented: bfloat16 [128, 16, 16, 128], P(('rep', 'sp')), parts along dimension 0
The draws below stay inside these ranges and needn't reach their ends.
There are 2 independent parts, one for each index of `rep`. The reference program is written for one: setup_inputs(seed, part) draws one part's arguments, and reference() takes and returns one part's arrays. A program takes and returns all parts, laid end to end along the dimension named above; an argument that names none is the same for every part. Nothing has to cross between parts.
All inputs are finite; a program needn't handle non-finite values.
Results may differ from the reference program's by a relative error of at most 0.015.
Values may be sent and summed in bfloat16 or wider, within the bound.
No kernel may reach another device: no remote copies, remote signals or barrier semaphores. Data moves between devices by JAX's collectives and lax.ppermute only.
A program may use at most 64 MiB of HBM per device.

```python
import jax
import jax.numpy as jnp
from jax import lax

C1 = 128
C2 = 256
C3 = 512
HT = 16
WD = 16
DEPTH = 64


def draw_volume(key, part):
    fine_key = jax.random.fold_in(key, 11)
    coarse_key = jax.random.fold_in(key, 23)
    coarse_shape = (DEPTH // 4, HT // 4, WD // 4, C1)
    fine = 0.6 * jax.random.normal(fine_key, (DEPTH, HT, WD, C1), jnp.float32)
    coarse = 1.4 * jax.random.normal(coarse_key, coarse_shape, jnp.float32)
    coarse_full = jnp.repeat(jnp.repeat(jnp.repeat(coarse, 4, axis=0), 4, axis=1), 4, axis=2)
    return jnp.clip(fine + coarse_full, -6.0, 6.0).astype(jnp.bfloat16)


def shard_levels(stream_key, extent, pieces, smallest, high):
    factor_of = 1.0
    for dim, shards_of in pieces:
        draws = jax.random.uniform(jax.random.fold_in(jax.random.fold_in(stream_key, 6), dim), (shards_of,), jnp.float32, smallest / len(pieces), high / len(pieces))
        factor_of = factor_of * jnp.repeat(jnp.exp(draws), extent[dim] // shards_of).reshape((-1,) + (1,) * (len(extent) - 1 - dim))
    return factor_of


def noise(rng, shape, deviation, reach, shards=(), held_as=jnp.bfloat16):
    gain = shard_levels(rng, shape, shards, -0.22, 0.18) if shards else 1.0
    values = jax.random.normal(rng, shape, jnp.float32) * deviation * gain
    return jnp.minimum(jnp.maximum(values, -reach), reach).astype(held_as)


def setup_inputs(seed: int = 0, part: int = 0) -> dict:
    seeds = jax.random.split(jax.random.key(seed), 9)
    own_keys = jax.random.split(jax.random.fold_in(seeds[8], part), 9)
    return {
        "volume": draw_volume(jax.random.fold_in(jax.random.fold_in(seeds[8], part), 71), part),
        "first_kernel": noise(seeds[1], (3, 3, 3, C1, C1), (27 * C1 // 2) ** -0.5, 0.15625),
        "second_kernel": noise(seeds[2], (3, 3, 3, C1, C2), (27 * C1 // 2) ** -0.5, 0.15625),
        "deep_kernel": noise(seeds[3], (3, 3, 3, C2, C3), (27 * C2 // 2) ** -0.5, 0.109375, ((4, 16),)),
        "deeper_kernel": noise(seeds[4], (3, 3, 3, C3, C3), (27 * C3 // 2) ** -0.5, 0.078125, ((4, 16),)),
        "rise_kernel": noise(seeds[5], (2, 2, 2, C3, C2), (C3 // 2) ** -0.5, 0.375),
        "decode_kernel": noise(seeds[6], (3, 3, 3, 2 * C2, C2), (27 * C2) ** -0.5, 0.078125, ((3, 16),)),
        "final_kernel": noise(seeds[7], (2, 2, 2, C2, C1), (C2 // 2) ** -0.5, 0.5),
    }


def conv_cube(values, kernel):
    result = lax.conv_general_dilated(values.astype(jnp.float32)[None], kernel.astype(jnp.float32), (1, 1, 1), "SAME", dimension_numbers=("NDHWC", "DHWIO", "NDHWC"), precision=lax.Precision.HIGHEST)
    return result[0]


def pool_mean(values):
    depth, height, width, chans = values.shape
    blocks = values.astype(jnp.float32).reshape(depth // 2, 2, height // 2, 2, width // 2, 2, chans)
    return jnp.mean(blocks, axis=(1, 3, 5)).astype(jnp.bfloat16)


def up_conv(values, kernel):
    depth, height, width, chans = values.shape
    result = jnp.einsum("dhwi,abcio->dahbwco", values.astype(jnp.float32), kernel.astype(jnp.float32), precision=lax.Precision.HIGHEST)
    return result.reshape(2 * depth, 2 * height, 2 * width, kernel.shape[4])


def reference(volume, first_kernel, second_kernel, deep_kernel, deeper_kernel, rise_kernel, decode_kernel, final_kernel):
    first = jax.nn.relu(conv_cube(volume, first_kernel)).astype(jnp.bfloat16)
    pooled_one = pool_mean(first)
    skip = jax.nn.relu(conv_cube(pooled_one, second_kernel)).astype(jnp.bfloat16)
    pooled_two = pool_mean(skip)
    deep = jax.nn.relu(conv_cube(pooled_two, deep_kernel)).astype(jnp.bfloat16)
    deeper = jax.nn.relu(conv_cube(deep, deeper_kernel)).astype(jnp.bfloat16)
    risen = up_conv(deeper, rise_kernel).astype(jnp.bfloat16)
    joined = jnp.concatenate([risen, skip], axis=3)
    decoded = jax.nn.relu(conv_cube(joined, decode_kernel)).astype(jnp.bfloat16)
    return up_conv(decoded, final_kernel).astype(jnp.bfloat16)
```

```python
import jax
import jax.numpy as jnp
from jax import lax
from jax.sharding import PartitionSpec as P

GROUP = 4


def conv_depth(padded, kernel):
    result = lax.conv_general_dilated(
        padded[None],
        kernel,
        (1, 1, 1),
        ((0, 0), (1, 1), (1, 1)),
        dimension_numbers=("NDHWC", "DHWIO", "NDHWC"),
        preferred_element_type=jnp.float32,
    )
    return result[0]


def pad_depth(values):
    return jnp.pad(values, ((1, 1), (0, 0), (0, 0), (0, 0)))


def pool_mean(values):
    depth, height, width, chans = values.shape
    blocks = values.astype(jnp.float32).reshape(depth // 2, 2, height // 2, 2, width // 2, 2, chans)
    return jnp.mean(blocks, axis=(1, 3, 5)).astype(jnp.bfloat16)


def up_conv(values, kernel):
    depth, height, width, chans = values.shape
    result = jnp.einsum("dhwi,abcio->dahbwco", values, kernel, preferred_element_type=jnp.float32)
    return result.reshape(2 * depth, 2 * height, 2 * width, kernel.shape[4])


def exchange(payload):
    return lax.all_to_all(payload, "sp", split_axis=0, concat_axis=0, tiled=True)


def body(
    volume,
    first_kernel,
    second_kernel,
    deep_kernel,
    deeper_kernel,
    rise_kernel,
    decode_kernel,
    final_kernel,
):
    n = lax.axis_size("sp")
    place = lax.axis_index("sp")
    planes = n // GROUP
    plane, rank = place // GROUP, place % GROUP
    chans = deep_kernel.shape[4]
    halves = planes // 2
    columns = [[r + GROUP * j for j in range(planes)] for r in range(GROUP)]
    rows = [[GROUP * p + r for r in range(GROUP)] for p in range(planes)]

    decode_part = lax.all_gather(
        decode_kernel, "sp", axis=3, tiled=True, axis_index_groups=columns
    )

    forward = [(i, i + 1) for i in range(n - 1)]
    backward = [(target, source) for source, target in forward]
    low = lax.ppermute(volume[1:], "sp", forward)
    high = lax.ppermute(volume[:3], "sp", backward)
    padded = jnp.concatenate([low, volume, high], axis=0)
    first = jax.nn.relu(conv_depth(padded, first_kernel)).astype(jnp.bfloat16)
    pooled_one = pool_mean(first)
    inside = jnp.stack([place > 0, True, True, place < n - 1]).reshape(4, 1, 1, 1)
    pooled_one = jnp.where(inside, pooled_one, jnp.zeros((), jnp.bfloat16))
    skip = jax.nn.relu(conv_depth(pooled_one, second_kernel)).astype(jnp.bfloat16)
    pooled_two = pool_mean(skip).reshape(16, 256)

    pooled_whole = exchange(jnp.broadcast_to(pooled_two[None], (n, 16, 256)))
    pooled_whole = pooled_whole.reshape(n, 4, 4, 256)

    sends = skip.reshape(2, 64, halves, GROUP, chans).transpose(3, 1, 0, 2, 4)
    sends = jnp.broadcast_to(sends.reshape(1, GROUP, 64, 128), (planes, GROUP, 64, 128))
    skips = exchange(sends.reshape(n, 64, 128))
    skips = jnp.pad(skips, ((1, 1), (0, 0), (0, 0)))
    skips = lax.dynamic_slice_in_dim(skips, GROUP * plane, GROUP + 2, axis=0)
    skips = skips.reshape(6, 64, 2, 64).transpose(0, 2, 1, 3).reshape(12, 8, 8, 64)[1:11]

    deep = jax.nn.relu(conv_depth(pad_depth(pooled_whole), deep_kernel)).astype(jnp.bfloat16)
    deep = deep.reshape(16 * n, chans).T
    deep_whole = exchange(jnp.broadcast_to(deep[None], (n, chans, 16 * n)))
    deep_whole = deep_whole.reshape(n * chans, 16 * n).T.reshape(n, 4, 4, n * chans)

    deeper = jax.nn.relu(conv_depth(pad_depth(deep_whole), deeper_kernel)).astype(jnp.bfloat16)
    deeper = jnp.pad(deeper.reshape(16 * n, chans).T, ((0, 0), (16, 16)))
    sends = jnp.stack([deeper[:, 64 * p : 64 * p + 96] for p in range(planes)])
    sends = jnp.broadcast_to(sends[:, None], (planes, GROUP, chans, 96))
    deeper_near = exchange(sends.reshape(n, chans, 96))
    deeper_near = deeper_near.reshape(n * chans, 96).T.reshape(6, 4, 4, n * chans)

    rise_part = rise_kernel.reshape(2, 2, 2, n * chans, halves, GROUP, chans)
    rise_part = lax.dynamic_index_in_dim(rise_part, rank, axis=5, keepdims=False)
    rise_part = rise_part.reshape(2, 2, 2, n * chans, 64)
    risen = up_conv(deeper_near, rise_part).astype(jnp.bfloat16)[1:11]

    joined = jnp.concatenate([risen, skips], axis=3)
    partial = conv_depth(joined, decode_part).astype(jnp.bfloat16)
    partial = partial.reshape(GROUP, 128, 256)
    partial = lax.all_to_all(
        partial, "sp", split_axis=0, concat_axis=0, tiled=True, axis_index_groups=rows
    )
    decoded = jax.nn.relu(jnp.sum(partial.astype(jnp.float32), axis=0)).astype(jnp.bfloat16)
    return up_conv(decoded.reshape(2, 8, 8, 256), final_kernel).astype(jnp.bfloat16)


def solution(mesh):
    return jax.shard_map(
        body,
        mesh=mesh,
        in_specs=(
            P(("rep", "sp"), None, None, None),
            P(),
            P(),
            P(None, None, None, None, "sp"),
            P(None, None, None, None, "sp"),
            P(),
            P(None, None, None, "sp", None),
            P(),
        ),
        out_specs=P(("rep", "sp"), None, None, None),
        check_vma=False,
    )
```

```python
import functools

import jax
import jax.numpy as jnp
import numpy as np
from jax import lax
from jax.experimental import pallas as pl
from jax.experimental.pallas import tpu as pltpu
from jax.sharding import PartitionSpec as P

GROUP = 4
MIB = 1024 * 1024


def call(kernel, outs, scratch, args, flops, vmem_mib, scalars=0):
    spaces = [pltpu.SMEM] * scalars + [pltpu.VMEM] * (len(args) - scalars)
    return pl.pallas_call(
        kernel,
        out_shape=outs,
        in_specs=[pl.BlockSpec(memory_space=space) for space in spaces],
        out_specs=jax.tree.map(lambda _: pl.BlockSpec(memory_space=pltpu.VMEM), outs),
        scratch_shapes=scratch,
        compiler_params=pltpu.CompilerParams(vmem_limit_bytes=vmem_mib * MIB),
        cost_estimate=pl.CostEstimate(
            flops=flops,
            bytes_accessed=sum(a.size * a.dtype.itemsize for a in args),
            transcendentals=0,
        ),
    )(*args)


def dot(left, right, dims=((1,), (0,))):
    return lax.dot_general(left, right, (dims, ((), ())), preferred_element_type=jnp.float32)


def round_once(values):
    return values.astype(jnp.bfloat16).astype(jnp.float32)


def fill_patches(framed, patches, slices):
    for b in range(3):
        for c in range(3):
            tap = framed[:, b : b + 8, 7 + c : 15 + c, :].reshape(slices * 64, 128)
            col = (b * 3 + c) * 128
            patches[:, col : col + 128] = tap.astype(jnp.bfloat16)


def stem_kernel(
    ends, low, volume, high, toeplitz, second, order,
    pooled_out, skip_out,
    shifted, halves, framed, patches, quarters,
):
    zero_row = jnp.zeros((16, 384), jnp.bfloat16)
    row = lax.broadcasted_iota(jnp.int32, (256, 128), 0) & 15
    for s in range(10):
        ref, at = (low, s) if s < 3 else (volume, s - 3) if s < 7 else (high, s - 7)
        here = ref[at].reshape(256, 128).astype(jnp.float32)
        before = jnp.where(row == 0, 0.0, pltpu.roll(here, 1, 0))
        after = jnp.where(row == 15, 0.0, pltpu.roll(here, 255, 0))
        shifted[s, 0] = zero_row
        shifted[s, 17] = zero_row
        for c, tap in enumerate((before, here, after)):
            shifted[s, 1:17, :, 128 * c : 128 * c + 128] = tap.astype(jnp.bfloat16).reshape(16, 16, 128)
    framed[...] = jnp.zeros(framed.shape, jnp.float32)
    for m in range(4):
        left = jnp.concatenate(
            [shifted[2 * m + j, b : b + 16].reshape(256, 384) for j in range(4) for b in range(3)],
            axis=1,
        )
        first = round_once(jnp.maximum(dot(left, toeplitz[...]), 0.0))
        pair = (first[:, :128] + first[:, 128:]).reshape(8, 32, 128)
        halves[...] = (pair[:, :16] + pair[:, 16:]).reshape(128, 128)
        pooled = halves[pl.ds(0, 64, stride=2), :] + halves[pl.ds(1, 64, stride=2), :]
        pooled = round_once(pooled * 0.125)
        if m == 0:
            pooled = jnp.where(ends[0] == 0, 0.0, pooled)
        if m == 3:
            pooled = jnp.where(ends[1] == 0, 0.0, pooled)
        framed[m, 1:9, 8:16, :] = pooled.reshape(8, 8, 128)
    fill_patches(framed, patches, 4)
    skip = dot(patches[0:128], second[0])
    skip += dot(patches[64:192], second[1])
    skip += dot(patches[128:256], second[2])
    skip = jnp.maximum(skip, 0.0).astype(jnp.bfloat16)
    wide = skip.astype(jnp.float32)
    pair = (wide[:64] + wide[64:]).reshape(4, 16, 256)
    pair = (pair[:, :8] + pair[:, 8:]).reshape(32, 256)
    for k in range(2):
        quarters[k] = pair[:, 128 * k : 128 * k + 128]
    pooled = jnp.concatenate(
        [
            quarters[k, pl.ds(0, 16, stride=2), :] + quarters[k, pl.ds(1, 16, stride=2), :]
            for k in range(2)
        ],
        axis=1,
    )
    pooled = (pooled * 0.125).astype(jnp.bfloat16)
    for dest in range(pooled_out.shape[0]):
        pooled_out[dest] = pooled
    sorted_skip = dot(skip, order[...])
    for r in range(GROUP):
        near, far = sorted_skip[:64, 64 * r : 64 * r + 64], sorted_skip[64:, 64 * r : 64 * r + 64]
        block = jnp.concatenate([near, far], axis=1).astype(jnp.bfloat16)
        for p in range(skip_out.shape[0] // GROUP):
            skip_out[GROUP * p + r] = block


def spread_taps(weights, values, dims, chans, voxels):
    lane = lax.broadcasted_iota(jnp.int32, (chans, voxels), 1)

    def moved(term, tap, step, place, last):
        if tap == 1:
            return term
        keep = place > 0 if tap == 0 else place < last
        return jnp.where(keep, pltpu.roll(term, ((1 - tap) * step) % voxels, 1), 0.0)

    total = None
    for a in range(3):
        products = dot(weights[a * 9 * chans : (a + 1) * 9 * chans, :], values, dims)
        plane = None
        for b in range(3):
            line = None
            for c in range(3):
                at = (b * 3 + c) * chans
                term = moved(products[at : at + chans], c, 1, lane & 3, 3)
                line = term if line is None else line + term
            line = moved(line, b, 4, (lane >> 2) & 3, 3)
            plane = line if plane is None else plane + line
        plane = moved(plane, a, 16, lane >> 4, voxels // 16 - 1)
        total = plane if total is None else total + plane
    return jnp.maximum(total, 0.0)


def deep_stage(pooled, weights, out):
    n, chans, voxels = out.shape
    deep = spread_taps(weights, pooled[...], ((1,), (1,)), chans, voxels).astype(jnp.bfloat16)
    for dest in range(n):
        out[dest] = deep


def deeper_stage(deep, weights, out):
    n, chans, _ = out.shape
    voxels = deep.shape[1]
    deeper = spread_taps(weights, deep[...], ((1,), (0,)), chans, voxels)
    lane = lax.broadcasted_iota(jnp.int32, (chans, 128), 1)
    planes = n // GROUP
    for p in range(planes):
        part = pltpu.roll(deeper, (16 - 64 * p) % voxels, 1)[:, :128]
        if p == 0:
            part = jnp.where(lane < 16, 0.0, part)
        if p == planes - 1:
            part = jnp.where(lane >= 80, 0.0, part)
        part = part.astype(jnp.bfloat16)
        for r in range(GROUP):
            out[GROUP * p + r] = part


def decode_stage(deeper, rise, skips, weights, out, framed, patches, risen):
    framed[...] = jnp.zeros(framed.shape, jnp.float32)
    spread = round_once(dot(deeper[...].astype(jnp.float32).T.astype(jnp.bfloat16), rise[...]))
    for pair in range(4):
        both = spread[:, 128 * pair : 128 * pair + 128]
        risen[2 * pair] = both
        risen[2 * pair + 1] = pltpu.roll(both, 64, 1)
    upper = lax.broadcasted_iota(jnp.int32, (64, 128), 1) >= 64
    for s in range(10):
        d, a = (s + 1) // 2, (s + 1) % 2
        for h in range(4):
            for b in range(2):
                for c in range(2):
                    framed[s, 1 + 2 * h + b, pl.ds(8 + c, 4, stride=2), :] = risen[
                        4 * a + 2 * b + c, 16 * d + 4 * h : 16 * d + 4 * h + 4, :
                    ]
        skip = skips[d].astype(jnp.float32)
        if a == 0:
            skip = pltpu.roll(skip, 64, 1)
        joined = framed[s, 1:9, 8:16, :].reshape(64, 128)
        framed[s, 1:9, 8:16, :] = jnp.where(upper, skip, joined).reshape(8, 8, 128)
    fill_patches(framed, patches, 10)
    partial = dot(patches[0:512], weights[0])
    partial += dot(patches[64:576], weights[1])
    partial += dot(patches[128:640], weights[2])
    out[...] = partial.astype(jnp.bfloat16)


def final_stage(partials, weights, out, spaced):
    decoded = partials[0].astype(jnp.float32)
    for g in range(1, GROUP):
        decoded += partials[g].astype(jnp.float32)
    decoded = jnp.maximum(decoded, 0.0).astype(jnp.bfloat16)
    for a in range(2):
        for b in range(2):
            for c in range(2):
                values = dot(decoded, weights[4 * a + 2 * b + c])
                for d in range(2):
                    for h in range(8):
                        at = ((2 * d + a) * 16 + 2 * h + b) * 16 + c
                        spaced[pl.ds(at, 8, stride=2), :] = values[64 * d + 8 * h : 64 * d + 8 * h + 8]
    out[...] = spaced[...].astype(jnp.bfloat16)


def exchange(payload, groups=None):
    return lax.all_to_all(
        payload, "sp", split_axis=0, concat_axis=0, tiled=True, axis_index_groups=groups
    )


def body(
    volume,
    first_kernel,
    second_kernel,
    deep_kernel,
    deeper_kernel,
    rise_kernel,
    decode_kernel,
    final_kernel,
):
    n = lax.axis_size("sp")
    place = lax.axis_index("sp")
    planes = n // GROUP
    plane, rank = place // GROUP, place % GROUP
    chans = deep_kernel.shape[4]
    voxels = 16 * n
    columns = [[r + GROUP * j for j in range(planes)] for r in range(GROUP)]
    rows = [[GROUP * p + r for r in range(GROUP)] for p in range(planes)]
    bf16 = functools.partial(jax.ShapeDtypeStruct, dtype=jnp.bfloat16)

    decode_part = lax.all_gather(
        decode_kernel, "sp", axis=3, tiled=True, axis_index_groups=columns
    ).reshape(3, 1152, 256)

    forward = [(i, i + 1) for i in range(n - 1)]
    backward = [(target, source) for source, target in forward]
    low = lax.ppermute(volume[1:], "sp", forward)
    high = lax.ppermute(volume[:3], "sp", backward)

    lane = np.arange(256)
    source = (lane // 64 + GROUP * (lane % 64 // chans)) * chans + lane % chans
    order = jnp.asarray(np.arange(256)[:, None] == source[None, :], jnp.bfloat16)
    taps = first_kernel.reshape(3, 1152, 128)
    none = jnp.zeros((1, 1152, 128), jnp.bfloat16)
    toeplitz = jnp.concatenate(
        [jnp.concatenate([taps, none], axis=0), jnp.concatenate([none, taps], axis=0)], axis=2
    ).reshape(4608, 256)
    ends = jnp.stack([place, n - 1 - place]).astype(jnp.int32)
    pooled_two, sends = call(
        stem_kernel,
        (bf16((n, 16, 256)), bf16((n, 64, 128))),
        [
            pltpu.VMEM((10, 18, 16, 384), jnp.bfloat16),
            pltpu.VMEM((128, 128), jnp.float32),
            pltpu.VMEM((4, 10, 24, 128), jnp.float32),
            pltpu.VMEM((256, 1152), jnp.bfloat16),
            pltpu.VMEM((2, 32, 128), jnp.float32),
        ],
        (ends, low, volume, high, toeplitz, second_kernel.reshape(3, 1152, 256), order),
        2 * 1024 * 4608 * 256,
        24,
        scalars=1,
    )
    pooled_whole = exchange(pooled_two)
    skips = exchange(sends)

    deep = call(
        deep_stage,
        bf16((n, chans, voxels)),
        [],
        (
            pooled_whole.reshape(voxels, 256),
            deep_kernel.transpose(0, 1, 2, 4, 3).reshape(27 * chans, 256),
        ),
        2 * 27 * chans * 256 * voxels,
        16,
    )
    deep_whole = exchange(deep).reshape(n * chans, voxels)

    deeper = call(
        deeper_stage,
        bf16((n, chans, 128)),
        [],
        (deep_whole, deeper_kernel.transpose(0, 1, 2, 4, 3).reshape(27 * chans, n * chans)),
        2 * 27 * chans * n * chans * voxels,
        16,
    )
    deeper_near = exchange(deeper).reshape(n * chans, 128)

    mine = lax.dynamic_slice_in_dim(order, 64 * rank, 64, axis=1)
    rise_part = jnp.einsum("pio,os->ips", rise_kernel.reshape(8, n * chans, 256), mine)
    rise_part = rise_part.reshape(n * chans, 512)
    skips = jnp.pad(skips, ((1, 1), (0, 0), (0, 0)))
    skips = lax.dynamic_slice_in_dim(skips, GROUP * plane, GROUP + 2, axis=0)
    partial = call(
        decode_stage,
        bf16((512, 256)),
        [
            pltpu.VMEM((10, 10, 24, 128), jnp.float32),
            pltpu.VMEM((640, 1152), jnp.bfloat16),
            pltpu.VMEM((8, 128, 128), jnp.float32),
        ],
        (deeper_near, rise_part, skips, decode_part),
        2 * 512 * 3456 * 256,
        24,
    )
    partials = exchange(partial.reshape(GROUP, 128, 256), rows)
    out = call(
        final_stage,
        bf16((1024, 128)),
        [pltpu.VMEM((1024, 128), jnp.float32)],
        (partials, final_kernel.reshape(8, 256, 128)),
        2 * 128 * 256 * 1024,
        16,
    )
    return out.reshape(4, 16, 16, 128)


def solution(mesh):
    return jax.shard_map(
        body,
        mesh=mesh,
        in_specs=(
            P(("rep", "sp"), None, None, None),
            P(),
            P(),
            P(None, None, None, None, "sp"),
            P(None, None, None, None, "sp"),
            P(),
            P(None, None, None, "sp", None),
            P(),
        ),
        out_specs=P(("rep", "sp"), None, None, None),
        check_vma=False,
    )
```

```python
import functools

import jax
import jax.numpy as jnp
import numpy as np
from jax import lax
from jax.experimental import pallas as pl
from jax.experimental.pallas import tpu as pltpu
from jax.sharding import PartitionSpec as P

GROUP = 4
MIB = 1024 * 1024


def call(kernel, outs, scratch, args, flops, vmem_mib, scalars=0, far=()):
    spaces = [
        pltpu.SMEM if i < scalars else pltpu.HBM if i in far else pltpu.VMEM
        for i in range(len(args))
    ]
    return pl.pallas_call(
        kernel,
        out_shape=outs,
        in_specs=[pl.BlockSpec(memory_space=space) for space in spaces],
        out_specs=jax.tree.map(lambda _: pl.BlockSpec(memory_space=pltpu.VMEM), outs),
        scratch_shapes=scratch,
        compiler_params=pltpu.CompilerParams(vmem_limit_bytes=vmem_mib * MIB),
        cost_estimate=pl.CostEstimate(
            flops=flops,
            bytes_accessed=sum(a.size * a.dtype.itemsize for a in args),
            transcendentals=0,
        ),
    )(*args)


def dot(left, right, dims=((1,), (0,))):
    return lax.dot_general(left, right, (dims, ((), ())), preferred_element_type=jnp.float32)


def round_once(values):
    return values.astype(jnp.bfloat16).astype(jnp.float32)


def fill_patches(framed, patches, slices):
    for b in range(3):
        for c in range(3):
            tap = framed[:, b : b + 8, 7 + c : 15 + c, :].reshape(slices * 64, 128)
            col = (b * 3 + c) * 128
            patches[:, col : col + 128] = tap.astype(jnp.bfloat16)


def shift_slice(shifted, s, values):
    row = lax.broadcasted_iota(jnp.int32, (256, 128), 0) & 15
    here = values.reshape(256, 128).astype(jnp.float32)
    before = jnp.where(row == 0, 0.0, pltpu.roll(here, 1, 0))
    after = jnp.where(row == 15, 0.0, pltpu.roll(here, 255, 0))
    shifted[s, 0] = jnp.zeros((16, 384), jnp.bfloat16)
    shifted[s, 17] = jnp.zeros((16, 384), jnp.bfloat16)
    for c, tap in enumerate((before, here, after)):
        tap = tap.astype(jnp.bfloat16).reshape(16, 16, 128)
        shifted[s, 1:17, :, 128 * c : 128 * c + 128] = tap


def depth_pair(shifted, slices, weights, steps):
    left = jnp.concatenate(
        [shifted[s, b : b + 16].reshape(256, 384) for s in slices for b in range(3)], axis=1
    )
    none = jnp.zeros((1152, 128), jnp.bfloat16)
    right = [
        jnp.concatenate(
            [weights[j] if j < 3 else none, weights[j - 1] if j > 0 else none], axis=1
        )
        for j in steps
    ]
    return dot(left, jnp.concatenate(right, axis=0))


def depth_one(shifted, s, weights):
    left = jnp.concatenate([shifted[s, b : b + 16].reshape(256, 384) for b in range(3)], axis=1)
    return dot(left, weights)


def own_stage(volume, weights, out, shifted):
    for s in range(4):
        shift_slice(shifted, s, volume[s])
    out[0, :, :128] = jnp.zeros((256, 128), jnp.float32)
    out[0, :, 128:] = depth_one(shifted, 0, weights[2])
    out[1] = depth_pair(shifted, (0, 1, 2), weights, (1, 2, 3))
    out[2] = depth_pair(shifted, (1, 2, 3), weights, (0, 1, 2))
    out[3, :, :128] = depth_one(shifted, 3, weights[0])
    out[3, :, 128:] = jnp.zeros((256, 128), jnp.float32)


def stem_stage(
    ends, low, high, own, weights, second, order, out, shifted, halves, framed, patches, quarters
):
    for s in range(3):
        shift_slice(shifted, s, low[s])
        shift_slice(shifted, 3 + s, high[s])
    framed[...] = jnp.zeros(framed.shape, jnp.float32)
    for m in range(4):
        if m == 0:
            first = own[0] + depth_pair(shifted, (0, 1, 2), weights, (0, 1, 2))
        elif m == 3:
            first = own[3] + depth_pair(shifted, (3, 4, 5), weights, (1, 2, 3))
        elif m == 1:
            near = own[1, :, :128] + depth_one(shifted, 2, weights[0])
            first = jnp.concatenate([near, own[1, :, 128:]], axis=1)
        else:
            far = own[2, :, 128:] + depth_one(shifted, 3, weights[2])
            first = jnp.concatenate([own[2, :, :128], far], axis=1)
        first = round_once(jnp.maximum(first, 0.0))
        pair = (first[:, :128] + first[:, 128:]).reshape(8, 32, 128)
        halves[...] = (pair[:, :16] + pair[:, 16:]).reshape(128, 128)
        pooled = halves[pl.ds(0, 64, stride=2), :] + halves[pl.ds(1, 64, stride=2), :]
        pooled = round_once(pooled * 0.125)
        if m == 0:
            pooled = jnp.where(ends[0] == 0, 0.0, pooled)
        if m == 3:
            pooled = jnp.where(ends[1] == 0, 0.0, pooled)
        framed[m, 1:9, 8:16, :] = pooled.reshape(8, 8, 128)
    fill_patches(framed, patches, 4)
    skip = dot(patches[0:128], second[0])
    skip += dot(patches[64:192], second[1])
    skip += dot(patches[128:256], second[2])
    skip = jnp.maximum(skip, 0.0).astype(jnp.bfloat16)
    wide = skip.astype(jnp.float32)
    pair = (wide[:64] + wide[64:]).reshape(4, 16, 256)
    pair = (pair[:, :8] + pair[:, 8:]).reshape(32, 256)
    for k in range(2):
        quarters[k] = pair[:, 128 * k : 128 * k + 128]
    pooled = jnp.concatenate(
        [
            quarters[k, pl.ds(0, 16, stride=2), :] + quarters[k, pl.ds(1, 16, stride=2), :]
            for k in range(2)
        ],
        axis=1,
    )
    pooled = (pooled * 0.125).astype(jnp.bfloat16)
    sorted_skip = dot(skip, order[...])
    for r in range(GROUP):
        near, far = sorted_skip[:64, 64 * r : 64 * r + 64], sorted_skip[64:, 64 * r : 64 * r + 64]
        block = jnp.concatenate([near, far], axis=1)
        block = jnp.concatenate([block[:32], block[32:]], axis=1).astype(jnp.bfloat16)
        out[r, 0:16, :] = pooled
        out[r, 16:48, :] = block


def relay_stage(plane, near, out):
    lower = lax.broadcasted_iota(jnp.int32, (16, 128), 1) < 64

    def edge(block, far):
        sides = []
        for k in range(2):
            half = block[:, 128 * k : 128 * k + 128]
            top, bottom = half[:16], half[16:]
            if far:
                top = pltpu.roll(top, 64, 1)
            else:
                bottom = pltpu.roll(bottom, 64, 1)
            sides.append(jnp.where(lower, top, bottom))
        return jnp.concatenate(sides, axis=1)

    first = edge(near[0, 16:48, :].astype(jnp.float32), False)
    last = edge(near[GROUP - 1, 16:48, :].astype(jnp.float32), True)
    pooled = [near[r, 0:16, :] for r in range(GROUP)]
    for p in range(out.shape[0]):
        for r in range(GROUP):
            out[p, 16 * r : 16 * r + 16, :] = pooled[r]
        out[p, 64:80, :] = jnp.where(plane[0] < p, last, first).astype(jnp.bfloat16)


def spread_taps(weights, values, dims, chans, voxels):
    lane = lax.broadcasted_iota(jnp.int32, (chans, voxels), 1)

    def moved(term, tap, step, place, last):
        if tap == 1:
            return term
        keep = place > 0 if tap == 0 else place < last
        return jnp.where(keep, pltpu.roll(term, ((1 - tap) * step) % voxels, 1), 0.0)

    total = None
    for a in range(3):
        products = dot(weights[a * 9 * chans : (a + 1) * 9 * chans, :], values, dims)
        plane = None
        for b in range(3):
            line = None
            for c in range(3):
                at = (b * 3 + c) * chans
                term = moved(products[at : at + chans], c, 1, lane & 3, 3)
                line = term if line is None else line + term
            line = moved(line, b, 4, (lane >> 2) & 3, 3)
            plane = line if plane is None else plane + line
        plane = moved(plane, a, 16, lane >> 4, voxels // 16 - 1)
        total = plane if total is None else total + plane
    return jnp.maximum(total, 0.0)


def deep_stage(pooled, weights, out):
    n, chans, voxels = out.shape
    values = jnp.concatenate([pooled[p, 0:64, :] for p in range(n // GROUP)], axis=0)
    deep = spread_taps(weights, values, ((1,), (1,)), chans, voxels).astype(jnp.bfloat16)
    for dest in range(n):
        out[dest] = deep


def deeper_stage(deep, weights, out):
    n, chans, _ = out.shape
    voxels = deep.shape[1]
    deeper = spread_taps(weights, deep[...], ((1,), (0,)), chans, voxels)
    lane = lax.broadcasted_iota(jnp.int32, (chans, 128), 1)
    planes = n // GROUP
    for p in range(planes):
        part = pltpu.roll(deeper, (16 - 64 * p) % voxels, 1)[:, :128]
        if p == 0:
            part = jnp.where(lane < 16, 0.0, part)
        if p == planes - 1:
            part = jnp.where(lane >= 80, 0.0, part)
        part = part.astype(jnp.bfloat16)
        for r in range(GROUP):
            out[GROUP * p + r] = part


def decode_stage(
    plane, deeper, rise, near, relayed, decode, out, framed, patches, risen, weights, arrived
):
    copies = [pltpu.make_async_copy(decode.at[a], weights.at[a], arrived.at[a]) for a in range(3)]
    for copy in copies:
        copy.start()
    planes = relayed.shape[0]
    framed[...] = jnp.zeros(framed.shape, jnp.float32)
    spread = round_once(dot(deeper[...].astype(jnp.float32).T.astype(jnp.bfloat16), rise[...]))
    for pair in range(4):
        both = spread[:, 128 * pair : 128 * pair + 128]
        risen[2 * pair] = both
        risen[2 * pair + 1] = pltpu.roll(both, 64, 1)
    upper = lax.broadcasted_iota(jnp.int32, (64, 128), 1) >= 64
    for s in range(10):
        d, a = (s + 1) // 2, (s + 1) % 2
        for h in range(4):
            for b in range(2):
                for c in range(2):
                    framed[s, 1 + 2 * h + b, pl.ds(8 + c, 4, stride=2), :] = risen[
                        4 * a + 2 * b + c, 16 * d + 4 * h : 16 * d + 4 * h + 4, :
                    ]
        if s == 0 or s == 9:
            other = jnp.maximum(plane[0] - 1, 0) if s == 0 else jnp.minimum(plane[0] + 1, planes - 1)
            edge = relayed[other, 64:80, :].astype(jnp.float32)
            edge = jnp.where(other == plane[0], 0.0, edge)
            parts = []
            for k in range(2):
                half = edge[:, 128 * k : 128 * k + 128]
                parts += [pltpu.roll(half, 64, 1), half]
            skip = jnp.concatenate(parts, axis=0)
        else:
            both = near[(s - 1) // 2, 16:48, :].astype(jnp.float32)
            skip = jnp.concatenate([both[:, :128], both[:, 128:]], axis=0)
            if (s - 1) % 2 == 0:
                skip = pltpu.roll(skip, 64, 1)
        joined = framed[s, 1:9, 8:16, :].reshape(64, 128)
        framed[s, 1:9, 8:16, :] = jnp.where(upper, skip, joined).reshape(8, 8, 128)
    fill_patches(framed, patches, 10)
    partial = None
    for a in range(3):
        copies[a].wait()
        term = dot(patches[64 * a : 64 * a + 512], weights[a])
        partial = term if partial is None else partial + term
    out[...] = partial.astype(jnp.bfloat16)


def final_stage(partials, weights, out, spaced):
    decoded = partials[0].astype(jnp.float32)
    for g in range(1, GROUP):
        decoded += partials[g].astype(jnp.float32)
    decoded = jnp.maximum(decoded, 0.0).astype(jnp.bfloat16)
    for a in range(2):
        for b in range(2):
            for c in range(2):
                values = dot(decoded, weights[4 * a + 2 * b + c])
                for d in range(2):
                    for h in range(8):
                        at = ((2 * d + a) * 16 + 2 * h + b) * 16 + c
                        spaced[pl.ds(at, 8, stride=2), :] = values[64 * d + 8 * h : 64 * d + 8 * h + 8]
    out[...] = spaced[...].astype(jnp.bfloat16)


def exchange(payload, groups=None):
    return lax.all_to_all(
        payload, "sp", split_axis=0, concat_axis=0, tiled=True, axis_index_groups=groups
    )


def body(
    volume,
    first_kernel,
    second_kernel,
    deep_kernel,
    deeper_kernel,
    rise_kernel,
    decode_kernel,
    final_kernel,
):
    n = lax.axis_size("sp")
    place = lax.axis_index("sp")
    planes = n // GROUP
    plane, rank = place // GROUP, place % GROUP
    chans = deep_kernel.shape[4]
    voxels = 16 * n
    columns = [[r + GROUP * j for j in range(planes)] for r in range(GROUP)]
    rows = [[GROUP * p + r for r in range(GROUP)] for p in range(planes)]
    bf16 = functools.partial(jax.ShapeDtypeStruct, dtype=jnp.bfloat16)

    decode_part = lax.all_gather(
        decode_kernel, "sp", axis=3, tiled=True, axis_index_groups=columns
    ).reshape(3, 1152, 256)

    forward = [(i, i + 1) for i in range(n - 1)]
    backward = [(target, source) for source, target in forward]
    low = lax.ppermute(volume[1:], "sp", forward)
    high = lax.ppermute(volume[:3], "sp", backward)

    taps = first_kernel.reshape(3, 1152, 128)
    own = call(
        own_stage,
        jax.ShapeDtypeStruct((4, 256, 256), jnp.float32),
        [pltpu.VMEM((4, 18, 16, 384), jnp.bfloat16)],
        (volume, taps),
        2 * 1024 * 2304 * 256,
        24,
    )
    lane = np.arange(256)
    source = (lane // 64 + GROUP * (lane % 64 // chans)) * chans + lane % chans
    order = jnp.asarray(np.arange(256)[:, None] == source[None, :], jnp.bfloat16)
    ends = jnp.stack([place, n - 1 - place]).astype(jnp.int32)
    sends = call(
        stem_stage,
        bf16((GROUP, 48, 256)),
        [
            pltpu.VMEM((6, 18, 16, 384), jnp.bfloat16),
            pltpu.VMEM((128, 128), jnp.float32),
            pltpu.VMEM((4, 10, 24, 128), jnp.float32),
            pltpu.VMEM((256, 1152), jnp.bfloat16),
            pltpu.VMEM((2, 32, 128), jnp.float32),
        ],
        (ends, low, high, own, taps, second_kernel.reshape(3, 1152, 256), order),
        2 * 1024 * 2304 * 256,
        24,
        scalars=1,
    )
    near = exchange(sends, rows)
    plane_ref = plane.astype(jnp.int32).reshape(1)
    relays = call(
        relay_stage, bf16((planes, 80, 256)), [], (plane_ref, near), 0, 16, scalars=1
    )
    relayed = exchange(relays, columns)

    deep = call(
        deep_stage,
        bf16((n, chans, voxels)),
        [],
        (relayed, deep_kernel.transpose(0, 1, 2, 4, 3).reshape(27 * chans, 256)),
        2 * 27 * chans * 256 * voxels,
        16,
    )
    deep_whole = exchange(deep).reshape(n * chans, voxels)

    deeper = call(
        deeper_stage,
        bf16((n, chans, 128)),
        [],
        (deep_whole, deeper_kernel.transpose(0, 1, 2, 4, 3).reshape(27 * chans, n * chans)),
        2 * 27 * chans * n * chans * voxels,
        16,
    )
    deeper_near = exchange(deeper).reshape(n * chans, 128)

    mine = lax.dynamic_slice_in_dim(order, 64 * rank, 64, axis=1)
    rise_part = jnp.einsum("pio,os->ips", rise_kernel.reshape(8, n * chans, 256), mine)
    rise_part = rise_part.reshape(n * chans, 512)
    partial = call(
        decode_stage,
        bf16((512, 256)),
        [
            pltpu.VMEM((10, 10, 24, 128), jnp.float32),
            pltpu.VMEM((640, 1152), jnp.bfloat16),
            pltpu.VMEM((8, 128, 128), jnp.float32),
            pltpu.VMEM((3, 1152, 256), jnp.bfloat16),
            pltpu.SemaphoreType.DMA((3,)),
        ],
        (plane_ref, deeper_near, rise_part, near, relayed, decode_part),
        2 * 512 * 3456 * 256,
        24,
        scalars=1,
        far=(5,),
    )
    partials = exchange(partial.reshape(GROUP, 128, 256), rows)
    out = call(
        final_stage,
        bf16((1024, 128)),
        [pltpu.VMEM((1024, 128), jnp.float32)],
        (partials, final_kernel.reshape(8, 256, 128)),
        2 * 128 * 256 * 1024,
        16,
    )
    return out.reshape(4, 16, 16, 128)


def solution(mesh):
    return jax.shard_map(
        body,
        mesh=mesh,
        in_specs=(
            P(("rep", "sp"), None, None, None),
            P(),
            P(),
            P(None, None, None, None, "sp"),
            P(None, None, None, None, "sp"),
            P(),
            P(None, None, None, "sp", None),
            P(),
        ),
        out_specs=P(("rep", "sp"), None, None, None),
        check_vma=False,
    )
```

```python
import functools

import jax
import jax.numpy as jnp
import numpy as np
from jax import lax
from jax.experimental import pallas as pl
from jax.experimental.pallas import tpu as pltpu
from jax.sharding import PartitionSpec as P

GROUP = 4
MIB = 1024 * 1024


def call(kernel, outs, scratch, args, flops, vmem_mib, scalars=0, far=()):
    spaces = [
        pltpu.SMEM if i < scalars else pltpu.HBM if i in far else pltpu.VMEM
        for i in range(len(args))
    ]
    return pl.pallas_call(
        kernel,
        out_shape=outs,
        in_specs=[pl.BlockSpec(memory_space=space) for space in spaces],
        out_specs=jax.tree.map(lambda _: pl.BlockSpec(memory_space=pltpu.VMEM), outs),
        scratch_shapes=scratch,
        compiler_params=pltpu.CompilerParams(vmem_limit_bytes=vmem_mib * MIB),
        cost_estimate=pl.CostEstimate(
            flops=flops,
            bytes_accessed=sum(a.size * a.dtype.itemsize for a in args),
            transcendentals=0,
        ),
    )(*args)


def dot(left, right, dims=((1,), (0,))):
    return lax.dot_general(left, right, (dims, ((), ())), preferred_element_type=jnp.float32)


def round_once(values):
    return values.astype(jnp.bfloat16).astype(jnp.float32)


def fill_patches(framed, patches, slices):
    for b in range(3):
        for c in range(3):
            tap = framed[:, b : b + 8, 7 + c : 15 + c, :].reshape(slices * 64, 128)
            col = (b * 3 + c) * 128
            patches[:, col : col + 128] = tap.astype(jnp.bfloat16)


def shift_slice(shifted, s, values):
    row = lax.broadcasted_iota(jnp.int32, (256, 128), 0) & 15
    here = values.reshape(256, 128).astype(jnp.float32)
    before = jnp.where(row == 0, 0.0, pltpu.roll(here, 1, 0))
    after = jnp.where(row == 15, 0.0, pltpu.roll(here, 255, 0))
    shifted[s, 0] = jnp.zeros((16, 384), jnp.bfloat16)
    shifted[s, 17] = jnp.zeros((16, 384), jnp.bfloat16)
    for c, tap in enumerate((before, here, after)):
        tap = tap.astype(jnp.bfloat16).reshape(16, 16, 128)
        shifted[s, 1:17, :, 128 * c : 128 * c + 128] = tap


def depth_pair(shifted, slices, weights, steps):
    left = jnp.concatenate(
        [shifted[s, b : b + 16].reshape(256, 384) for s in slices for b in range(3)], axis=1
    )
    none = jnp.zeros((1152, 128), jnp.bfloat16)
    right = [
        jnp.concatenate(
            [weights[j] if j < 3 else none, weights[j - 1] if j > 0 else none], axis=1
        )
        for j in steps
    ]
    return dot(left, jnp.concatenate(right, axis=0))


def depth_one(shifted, s, weights):
    left = jnp.concatenate([shifted[s, b : b + 16].reshape(256, 384) for b in range(3)], axis=1)
    return dot(left, weights)


def own_stage(volume, weights, out, shifted):
    for s in range(4):
        shift_slice(shifted, s, volume[s])
    out[0, :, :128] = jnp.zeros((256, 128), jnp.float32)
    out[0, :, 128:] = depth_one(shifted, 0, weights[2])
    out[1] = depth_pair(shifted, (0, 1, 2), weights, (1, 2, 3))
    out[2] = depth_pair(shifted, (1, 2, 3), weights, (0, 1, 2))
    out[3, :, :128] = depth_one(shifted, 3, weights[0])
    out[3, :, 128:] = jnp.zeros((256, 128), jnp.float32)


def stem_stage(
    ends, low, high, own, weights, second, order, out, shifted, halves, framed, patches, quarters
):
    for s in range(3):
        shift_slice(shifted, s, low[s])
        shift_slice(shifted, 3 + s, high[s])
    framed[...] = jnp.zeros(framed.shape, jnp.float32)
    for m in range(4):
        if m == 0:
            first = own[0] + depth_pair(shifted, (0, 1, 2), weights, (0, 1, 2))
        elif m == 3:
            first = own[3] + depth_pair(shifted, (3, 4, 5), weights, (1, 2, 3))
        elif m == 1:
            near = own[1, :, :128] + depth_one(shifted, 2, weights[0])
            first = jnp.concatenate([near, own[1, :, 128:]], axis=1)
        else:
            far = own[2, :, 128:] + depth_one(shifted, 3, weights[2])
            first = jnp.concatenate([own[2, :, :128], far], axis=1)
        first = round_once(jnp.maximum(first, 0.0))
        pair = (first[:, :128] + first[:, 128:]).reshape(8, 32, 128)
        halves[...] = (pair[:, :16] + pair[:, 16:]).reshape(128, 128)
        pooled = halves[pl.ds(0, 64, stride=2), :] + halves[pl.ds(1, 64, stride=2), :]
        pooled = round_once(pooled * 0.125)
        if m == 0:
            pooled = jnp.where(ends[0] == 0, 0.0, pooled)
        if m == 3:
            pooled = jnp.where(ends[1] == 0, 0.0, pooled)
        framed[m, 1:9, 8:16, :] = pooled.reshape(8, 8, 128)
    fill_patches(framed, patches, 4)
    skip = dot(patches[0:128], second[0])
    skip += dot(patches[64:192], second[1])
    skip += dot(patches[128:256], second[2])
    skip = jnp.maximum(skip, 0.0).astype(jnp.bfloat16)
    wide = skip.astype(jnp.float32)
    pair = (wide[:64] + wide[64:]).reshape(4, 16, 256)
    pair = (pair[:, :8] + pair[:, 8:]).reshape(32, 256)
    for k in range(2):
        quarters[k] = pair[:, 128 * k : 128 * k + 128]
    pooled = jnp.concatenate(
        [
            quarters[k, pl.ds(0, 16, stride=2), :] + quarters[k, pl.ds(1, 16, stride=2), :]
            for k in range(2)
        ],
        axis=1,
    )
    pooled = (pooled * 0.125).astype(jnp.bfloat16)
    sorted_skip = dot(skip, order[...])
    for r in range(GROUP):
        near, far = sorted_skip[:64, 64 * r : 64 * r + 64], sorted_skip[64:, 64 * r : 64 * r + 64]
        block = jnp.concatenate([near, far], axis=1)
        block = jnp.concatenate([block[:32], block[32:]], axis=1).astype(jnp.bfloat16)
        out[r, 0:16, :] = pooled
        out[r, 16:48, :] = block


def relay_stage(plane, near, out):
    lower = lax.broadcasted_iota(jnp.int32, (16, 128), 1) < 64

    def edge(block, far):
        sides = []
        for k in range(2):
            half = block[:, 128 * k : 128 * k + 128]
            top, bottom = half[:16], half[16:]
            if far:
                top = pltpu.roll(top, 64, 1)
            else:
                bottom = pltpu.roll(bottom, 64, 1)
            sides.append(jnp.where(lower, top, bottom))
        return jnp.concatenate(sides, axis=1)

    first = edge(near[0, 16:48, :].astype(jnp.float32), False)
    last = edge(near[GROUP - 1, 16:48, :].astype(jnp.float32), True)
    pooled = [near[r, 0:16, :] for r in range(GROUP)]
    for p in range(out.shape[0]):
        for r in range(GROUP):
            out[p, 16 * r : 16 * r + 16, :] = pooled[r]
        out[p, 64:80, :] = jnp.where(plane[0] < p, last, first).astype(jnp.bfloat16)


def spread_taps(weights, values, dims, chans, voxels):
    lane = lax.broadcasted_iota(jnp.int32, (chans, voxels), 1)

    def moved(term, tap, step, place, last):
        if tap == 1:
            return term
        keep = place > 0 if tap == 0 else place < last
        return jnp.where(keep, pltpu.roll(term, ((1 - tap) * step) % voxels, 1), 0.0)

    total = None
    for a in range(3):
        products = dot(weights[a * 9 * chans : (a + 1) * 9 * chans, :], values, dims)
        plane = None
        for b in range(3):
            line = None
            for c in range(3):
                at = (b * 3 + c) * chans
                term = moved(products[at : at + chans], c, 1, lane & 3, 3)
                line = term if line is None else line + term
            line = moved(line, b, 4, (lane >> 2) & 3, 3)
            plane = line if plane is None else plane + line
        plane = moved(plane, a, 16, lane >> 4, voxels // 16 - 1)
        total = plane if total is None else total + plane
    return jnp.maximum(total, 0.0)


def deep_stage(pooled, weights, out):
    n, chans, voxels = out.shape
    values = jnp.concatenate([pooled[p, 0:64, :] for p in range(n // GROUP)], axis=0)
    deep = spread_taps(weights, values, ((1,), (1,)), chans, voxels).astype(jnp.bfloat16)
    for dest in range(n):
        out[dest] = deep


def deeper_stage(deep, weights, out):
    n, chans, _ = out.shape
    voxels = deep.shape[1]
    deeper = spread_taps(weights, deep[...], ((1,), (0,)), chans, voxels)
    lane = lax.broadcasted_iota(jnp.int32, (chans, 128), 1)
    planes = n // GROUP
    for p in range(planes):
        part = pltpu.roll(deeper, (16 - 64 * p) % voxels, 1)[:, :128]
        if p == 0:
            part = jnp.where(lane < 16, 0.0, part)
        if p == planes - 1:
            part = jnp.where(lane >= 80, 0.0, part)
        part = part.astype(jnp.bfloat16)
        for r in range(GROUP):
            out[GROUP * p + r] = part


def decode_stage(
    plane, deeper, rise, near, relayed, decode, out, framed, patches, risen, weights, arrived
):
    copies = [
        pltpu.make_async_copy(
            decode.at[9 * a : 9 * a + 9], weights.at[9 * a : 9 * a + 9], arrived.at[a]
        )
        for a in range(3)
    ]
    for copy in copies:
        copy.start()
    planes = relayed.shape[0]
    framed[...] = jnp.zeros(framed.shape, jnp.float32)
    spread = round_once(dot(deeper[...].astype(jnp.float32).T.astype(jnp.bfloat16), rise[...]))
    for pair in range(4):
        both = spread[:, 128 * pair : 128 * pair + 128]
        risen[2 * pair] = both
        risen[2 * pair + 1] = pltpu.roll(both, 64, 1)
    upper = lax.broadcasted_iota(jnp.int32, (64, 128), 1) >= 64
    for s in range(10):
        d, a = (s + 1) // 2, (s + 1) % 2
        for h in range(4):
            for b in range(2):
                for c in range(2):
                    framed[s, 1 + 2 * h + b, pl.ds(8 + c, 4, stride=2), :] = risen[
                        4 * a + 2 * b + c, 16 * d + 4 * h : 16 * d + 4 * h + 4, :
                    ]
        if s == 0 or s == 9:
            other = jnp.maximum(plane[0] - 1, 0) if s == 0 else jnp.minimum(plane[0] + 1, planes - 1)
            edge = relayed[other, 64:80, :].astype(jnp.float32)
            edge = jnp.where(other == plane[0], 0.0, edge)
            parts = []
            for k in range(2):
                half = edge[:, 128 * k : 128 * k + 128]
                parts += [pltpu.roll(half, 64, 1), half]
            skip = jnp.concatenate(parts, axis=0)
        else:
            both = near[(s - 1) // 2, 16:48, :].astype(jnp.float32)
            skip = jnp.concatenate([both[:, :128], both[:, 128:]], axis=0)
            if (s - 1) % 2 == 0:
                skip = pltpu.roll(skip, 64, 1)
        joined = framed[s, 1:9, 8:16, :].reshape(64, 128)
        framed[s, 1:9, 8:16, :] = jnp.where(upper, skip, joined).reshape(8, 8, 128)
    fill_patches(framed, patches, 10)
    partial = None
    for a in range(3):
        copies[a].wait()
        right = [
            weights[9 * a : 9 * a + 9, at : at + 128, :].reshape(1152, weights.shape[2])
            for at in range(0, weights.shape[1], 128)
        ]
        term = dot(patches[64 * a : 64 * a + 512], jnp.concatenate(right, axis=1))
        partial = term if partial is None else partial + term
    out[...] = partial.astype(jnp.bfloat16)


def final_stage(partials, weights, out, spaced):
    decoded = partials[0].astype(jnp.float32)
    for g in range(1, GROUP):
        decoded += partials[g].astype(jnp.float32)
    decoded = jnp.maximum(decoded, 0.0).astype(jnp.bfloat16)
    for a in range(2):
        for b in range(2):
            for c in range(2):
                values = dot(decoded, weights[4 * a + 2 * b + c])
                for d in range(2):
                    for h in range(8):
                        at = ((2 * d + a) * 16 + 2 * h + b) * 16 + c
                        spaced[pl.ds(at, 8, stride=2), :] = values[64 * d + 8 * h : 64 * d + 8 * h + 8]
    out[...] = spaced[...].astype(jnp.bfloat16)


ALL = ("z", "r")


def exchange(payload, axis):
    return lax.all_to_all(payload, axis, split_axis=0, concat_axis=0, tiled=True)


def body(
    volume,
    first_kernel,
    second_kernel,
    deep_kernel,
    deeper_kernel,
    rise_kernel,
    decode_kernel,
    final_kernel,
):
    n = lax.axis_size(ALL)
    place = lax.axis_index(ALL)
    planes = n // GROUP
    plane, rank = lax.axis_index("z"), lax.axis_index("r")
    chans = deep_kernel.shape[4]
    voxels = 16 * n
    bf16 = functools.partial(jax.ShapeDtypeStruct, dtype=jnp.bfloat16)

    decode_part = decode_kernel.reshape(27, chans, 256)
    if lax.axis_size("rep") == 2:
        decode_part = lax.dynamic_slice_in_dim(
            decode_part, 128 * lax.axis_index("rep"), 128, axis=2
        )
        decode_part = lax.all_gather(decode_part, ("rep", "z"), axis=1, tiled=True)
    else:
        decode_part = lax.all_gather(decode_part, "z", axis=1, tiled=True)

    forward = [(i, i + 1) for i in range(n - 1)]
    backward = [(target, source) for source, target in forward]
    low = lax.ppermute(volume[1:], ALL, forward)
    high = lax.ppermute(volume[:3], ALL, backward)

    taps = first_kernel.reshape(3, 1152, 128)
    own = call(
        own_stage,
        jax.ShapeDtypeStruct((4, 256, 256), jnp.float32),
        [pltpu.VMEM((4, 18, 16, 384), jnp.bfloat16)],
        (volume, taps),
        2 * 1024 * 2304 * 256,
        60,
    )
    lane = np.arange(256)
    source = (lane // 64 + GROUP * (lane % 64 // chans)) * chans + lane % chans
    order = jnp.asarray(np.arange(256)[:, None] == source[None, :], jnp.bfloat16)
    ends = jnp.stack([place, n - 1 - place]).astype(jnp.int32)
    sends = call(
        stem_stage,
        bf16((GROUP, 48, 256)),
        [
            pltpu.VMEM((6, 18, 16, 384), jnp.bfloat16),
            pltpu.VMEM((128, 128), jnp.float32),
            pltpu.VMEM((4, 10, 24, 128), jnp.float32),
            pltpu.VMEM((256, 1152), jnp.bfloat16),
            pltpu.VMEM((2, 32, 128), jnp.float32),
        ],
        (ends, low, high, own, taps, second_kernel.reshape(3, 1152, 256), order),
        2 * 1024 * 2304 * 256,
        24,
        scalars=1,
    )
    near = exchange(sends, "r")
    plane_ref = plane.astype(jnp.int32).reshape(1)
    relays = call(
        relay_stage, bf16((planes, 80, 256)), [], (plane_ref, near), 0, 16, scalars=1
    )
    relayed = exchange(relays, "z")

    deep = call(
        deep_stage,
        bf16((n, chans, voxels)),
        [],
        (relayed, deep_kernel.transpose(0, 1, 2, 4, 3).reshape(27 * chans, 256)),
        2 * 27 * chans * 256 * voxels,
        16,
    )
    deep_whole = exchange(deep, ALL).reshape(n * chans, voxels)

    deeper = call(
        deeper_stage,
        bf16((n, chans, 128)),
        [],
        (deep_whole, deeper_kernel.transpose(0, 1, 2, 4, 3).reshape(27 * chans, n * chans)),
        2 * 27 * chans * n * chans * voxels,
        16,
    )
    deeper_near = exchange(deeper, ALL).reshape(n * chans, 128)

    mine = lax.dynamic_slice_in_dim(order, 64 * rank, 64, axis=1)
    rise_part = jnp.einsum("pio,os->ips", rise_kernel.reshape(8, n * chans, 256), mine)
    rise_part = rise_part.reshape(n * chans, 512)
    partial = call(
        decode_stage,
        bf16((512, 256)),
        [
            pltpu.VMEM((10, 10, 24, 128), jnp.float32),
            pltpu.VMEM((640, 1152), jnp.bfloat16),
            pltpu.VMEM((8, 128, 128), jnp.float32),
            pltpu.VMEM(decode_part.shape, jnp.bfloat16),
            pltpu.SemaphoreType.DMA((3,)),
        ],
        (plane_ref, deeper_near, rise_part, near, relayed, decode_part),
        2 * 512 * 3456 * 256,
        60,
        scalars=1,
        far=(5,),
    )
    partials = exchange(partial.reshape(GROUP, 128, 256), "r")
    out = call(
        final_stage,
        bf16((1024, 128)),
        [pltpu.VMEM((1024, 128), jnp.float32)],
        (partials, final_kernel.reshape(8, 256, 128)),
        2 * 128 * 256 * 1024,
        16,
    )
    return out.reshape(4, 16, 16, 128)


def solution(mesh):
    reps, n = mesh.devices.shape
    grid = jax.sharding.Mesh(mesh.devices.reshape(reps, n // GROUP, GROUP), ("rep",) + ALL)
    return jax.shard_map(
        body,
        mesh=grid,
        in_specs=(
            P(("rep",) + ALL, None, None, None),
            P(),
            P(),
            P(None, None, None, None, ALL),
            P(None, None, None, None, ALL),
            P(),
            P(None, None, None, ALL, None),
            P(),
        ),
        out_specs=P(("rep",) + ALL, None, None, None),
        check_vma=False,
    )
```

```python
import functools

import jax
import jax.numpy as jnp
import numpy as np
from jax import lax
from jax.experimental import pallas as pl
from jax.experimental.pallas import tpu as pltpu
from jax.sharding import PartitionSpec as P

GROUP = 4
MIB = 1024 * 1024


def call(kernel, outs, scratch, args, flops, vmem_mib, scalars=0):
    spaces = [
        pltpu.SMEM if i < scalars else pltpu.VMEM
        for i in range(len(args))
    ]
    return pl.pallas_call(
        kernel,
        out_shape=outs,
        in_specs=[pl.BlockSpec(memory_space=space) for space in spaces],
        out_specs=jax.tree.map(lambda _: pl.BlockSpec(memory_space=pltpu.VMEM), outs),
        scratch_shapes=scratch,
        compiler_params=pltpu.CompilerParams(vmem_limit_bytes=vmem_mib * MIB),
        cost_estimate=pl.CostEstimate(
            flops=flops,
            bytes_accessed=sum(a.size * a.dtype.itemsize for a in args),
            transcendentals=0,
        ),
    )(*args)


def dot(left, right, dims=((1,), (0,))):
    return lax.dot_general(left, right, (dims, ((), ())), preferred_element_type=jnp.float32)


def round_once(values):
    return values.astype(jnp.bfloat16).astype(jnp.float32)


def fill_patches(framed, patches, slices):
    for b in range(3):
        for c in range(3):
            tap = framed[:, b : b + 8, 7 + c : 15 + c, :].reshape(slices * 64, 128)
            col = (b * 3 + c) * 128
            patches[:, col : col + 128] = tap.astype(jnp.bfloat16)


def shift_slice(shifted, s, values):
    row = lax.broadcasted_iota(jnp.int32, (256, 128), 0) & 15
    here = values.reshape(256, 128).astype(jnp.float32)
    before = jnp.where(row == 0, 0.0, pltpu.roll(here, 1, 0))
    after = jnp.where(row == 15, 0.0, pltpu.roll(here, 255, 0))
    shifted[s, 0] = jnp.zeros((16, 384), jnp.bfloat16)
    shifted[s, 17] = jnp.zeros((16, 384), jnp.bfloat16)
    for c, tap in enumerate((before, here, after)):
        tap = tap.astype(jnp.bfloat16).reshape(16, 16, 128)
        shifted[s, 1:17, :, 128 * c : 128 * c + 128] = tap


def depth_pair(shifted, slices, weights, steps):
    left = jnp.concatenate(
        [shifted[s, b : b + 16].reshape(256, 384) for s in slices for b in range(3)], axis=1
    )
    none = jnp.zeros((1152, 128), jnp.bfloat16)
    right = [
        jnp.concatenate(
            [weights[j] if j < 3 else none, weights[j - 1] if j > 0 else none], axis=1
        )
        for j in steps
    ]
    return dot(left, jnp.concatenate(right, axis=0))


def depth_one(shifted, s, weights):
    left = jnp.concatenate([shifted[s, b : b + 16].reshape(256, 384) for b in range(3)], axis=1)
    return dot(left, weights)


def own_stage(volume, weights, out, shifted):
    for s in range(4):
        shift_slice(shifted, s, volume[s])
    out[0, :, :128] = jnp.zeros((256, 128), jnp.float32)
    out[0, :, 128:] = depth_one(shifted, 0, weights[2])
    out[1] = depth_pair(shifted, (0, 1, 2), weights, (1, 2, 3))
    out[2] = depth_pair(shifted, (1, 2, 3), weights, (0, 1, 2))
    out[3, :, :128] = depth_one(shifted, 3, weights[0])
    out[3, :, 128:] = jnp.zeros((256, 128), jnp.float32)


def stem_stage(
    ends, low, high, own, weights, second, order, out, shifted, halves, framed, patches, quarters
):
    for s in range(3):
        shift_slice(shifted, s, low[s])
        shift_slice(shifted, 3 + s, high[s])
    framed[...] = jnp.zeros(framed.shape, jnp.float32)
    for m in range(4):
        if m == 0:
            first = own[0] + depth_pair(shifted, (0, 1, 2), weights, (0, 1, 2))
        elif m == 3:
            first = own[3] + depth_pair(shifted, (3, 4, 5), weights, (1, 2, 3))
        elif m == 1:
            near = own[1, :, :128] + depth_one(shifted, 2, weights[0])
            first = jnp.concatenate([near, own[1, :, 128:]], axis=1)
        else:
            far = own[2, :, 128:] + depth_one(shifted, 3, weights[2])
            first = jnp.concatenate([own[2, :, :128], far], axis=1)
        first = round_once(jnp.maximum(first, 0.0))
        pair = (first[:, :128] + first[:, 128:]).reshape(8, 32, 128)
        halves[...] = (pair[:, :16] + pair[:, 16:]).reshape(128, 128)
        pooled = halves[pl.ds(0, 64, stride=2), :] + halves[pl.ds(1, 64, stride=2), :]
        pooled = round_once(pooled * 0.125)
        if m == 0:
            pooled = jnp.where(ends[0] == 0, 0.0, pooled)
        if m == 3:
            pooled = jnp.where(ends[1] == 0, 0.0, pooled)
        framed[m, 1:9, 8:16, :] = pooled.reshape(8, 8, 128)
    fill_patches(framed, patches, 4)
    skip = dot(patches[0:128], second[0])
    skip += dot(patches[64:192], second[1])
    skip += dot(patches[128:256], second[2])
    skip = jnp.maximum(skip, 0.0).astype(jnp.bfloat16)
    wide = skip.astype(jnp.float32)
    pair = (wide[:64] + wide[64:]).reshape(4, 16, 256)
    pair = (pair[:, :8] + pair[:, 8:]).reshape(32, 256)
    for k in range(2):
        quarters[k] = pair[:, 128 * k : 128 * k + 128]
    pooled = jnp.concatenate(
        [
            quarters[k, pl.ds(0, 16, stride=2), :] + quarters[k, pl.ds(1, 16, stride=2), :]
            for k in range(2)
        ],
        axis=1,
    )
    pooled = (pooled * 0.125).astype(jnp.bfloat16)
    sorted_skip = dot(skip, order[...])
    for r in range(GROUP):
        near, far = sorted_skip[:64, 64 * r : 64 * r + 64], sorted_skip[64:, 64 * r : 64 * r + 64]
        block = jnp.concatenate([near, far], axis=1)
        block = jnp.concatenate([block[:32], block[32:]], axis=1).astype(jnp.bfloat16)
        out[r, 0:16, :] = pooled
        out[r, 16:48, :] = block


def relay_stage(plane, near, out):
    lower = lax.broadcasted_iota(jnp.int32, (16, 128), 1) < 64

    def edge(block, far):
        sides = []
        for k in range(2):
            half = block[:, 128 * k : 128 * k + 128]
            top, bottom = half[:16], half[16:]
            if far:
                top = pltpu.roll(top, 64, 1)
            else:
                bottom = pltpu.roll(bottom, 64, 1)
            sides.append(jnp.where(lower, top, bottom))
        return jnp.concatenate(sides, axis=1)

    first = edge(near[0, 16:48, :].astype(jnp.float32), False)
    last = edge(near[GROUP - 1, 16:48, :].astype(jnp.float32), True)
    pooled = [near[r, 0:16, :] for r in range(GROUP)]
    for p in range(out.shape[0]):
        for r in range(GROUP):
            out[p, 16 * r : 16 * r + 16, :] = pooled[r]
        out[p, 64:80, :] = jnp.where(plane[0] < p, last, first).astype(jnp.bfloat16)


def spread_taps(weights, values, dims, chans, voxels):
    lane = lax.broadcasted_iota(jnp.int32, (chans, voxels), 1)

    def moved(term, tap, step, place, last):
        if tap == 1:
            return term
        keep = place > 0 if tap == 0 else place < last
        return jnp.where(keep, pltpu.roll(term, ((1 - tap) * step) % voxels, 1), 0.0)

    total = None
    for a in range(3):
        products = dot(weights[a * 9 * chans : (a + 1) * 9 * chans, :], values, dims)
        plane = None
        for b in range(3):
            line = None
            for c in range(3):
                at = (b * 3 + c) * chans
                term = moved(products[at : at + chans], c, 1, lane & 3, 3)
                line = term if line is None else line + term
            line = moved(line, b, 4, (lane >> 2) & 3, 3)
            plane = line if plane is None else plane + line
        plane = moved(plane, a, 16, lane >> 4, voxels // 16 - 1)
        total = plane if total is None else total + plane
    return jnp.maximum(total, 0.0)


def deep_stage(pooled, weights, out):
    n, chans, voxels = out.shape
    values = jnp.concatenate([pooled[p, 0:64, :] for p in range(n // GROUP)], axis=0)
    deep = spread_taps(weights, values, ((1,), (1,)), chans, voxels).astype(jnp.bfloat16)
    for dest in range(n):
        out[dest] = deep


def deeper_stage(deep, weights, out):
    n, chans, _ = out.shape
    voxels = deep.shape[1]
    deeper = spread_taps(weights, deep[...], ((1,), (0,)), chans, voxels)
    lane = lax.broadcasted_iota(jnp.int32, (chans, 128), 1)
    planes = n // GROUP
    for p in range(planes):
        part = pltpu.roll(deeper, (16 - 64 * p) % voxels, 1)[:, :128]
        if p == 0:
            part = jnp.where(lane < 16, 0.0, part)
        if p == planes - 1:
            part = jnp.where(lane >= 80, 0.0, part)
        part = part.astype(jnp.bfloat16)
        for r in range(GROUP):
            out[GROUP * p + r] = part


def decode_stage(
    plane, deeper, rise, near, relayed, decode, out, framed, patches, risen
):
    planes = relayed.shape[0]
    framed[...] = jnp.zeros(framed.shape, jnp.float32)
    spread = round_once(dot(deeper[...].astype(jnp.float32).T.astype(jnp.bfloat16), rise[...]))
    for pair in range(4):
        both = spread[:, 128 * pair : 128 * pair + 128]
        risen[2 * pair] = both
        risen[2 * pair + 1] = pltpu.roll(both, 64, 1)
    upper = lax.broadcasted_iota(jnp.int32, (64, 128), 1) >= 64
    for s in range(10):
        d, a = (s + 1) // 2, (s + 1) % 2
        for h in range(4):
            for b in range(2):
                for c in range(2):
                    framed[s, 1 + 2 * h + b, pl.ds(8 + c, 4, stride=2), :] = risen[
                        4 * a + 2 * b + c, 16 * d + 4 * h : 16 * d + 4 * h + 4, :
                    ]
        if s == 0 or s == 9:
            other = jnp.maximum(plane[0] - 1, 0) if s == 0 else jnp.minimum(plane[0] + 1, planes - 1)
            edge = relayed[other, 64:80, :].astype(jnp.float32)
            edge = jnp.where(other == plane[0], 0.0, edge)
            parts = []
            for k in range(2):
                half = edge[:, 128 * k : 128 * k + 128]
                parts += [pltpu.roll(half, 64, 1), half]
            skip = jnp.concatenate(parts, axis=0)
        else:
            both = near[(s - 1) // 2, 16:48, :].astype(jnp.float32)
            skip = jnp.concatenate([both[:, :128], both[:, 128:]], axis=0)
            if (s - 1) % 2 == 0:
                skip = pltpu.roll(skip, 64, 1)
        joined = framed[s, 1:9, 8:16, :].reshape(64, 128)
        framed[s, 1:9, 8:16, :] = jnp.where(upper, skip, joined).reshape(8, 8, 128)
    fill_patches(framed, patches, 10)
    blocks = decode.shape[0]
    step = 128 // blocks
    partial = None
    for a in range(3):
        right = [
            decode[z, tap * step : (tap + 1) * step, :]
            for tap in range(9 * a, 9 * a + 9)
            for z in range(blocks)
        ]
        term = dot(patches[64 * a : 64 * a + 512], jnp.concatenate(right, axis=0))
        partial = term if partial is None else partial + term
    out[...] = partial.astype(jnp.bfloat16)


def final_stage(partials, weights, out, spaced):
    decoded = partials[0].astype(jnp.float32)
    for g in range(1, GROUP):
        decoded += partials[g].astype(jnp.float32)
    decoded = jnp.maximum(decoded, 0.0).astype(jnp.bfloat16)
    for a in range(2):
        for b in range(2):
            for c in range(2):
                values = dot(decoded, weights[4 * a + 2 * b + c])
                for d in range(2):
                    for h in range(8):
                        at = ((2 * d + a) * 16 + 2 * h + b) * 16 + c
                        spaced[pl.ds(at, 8, stride=2), :] = values[64 * d + 8 * h : 64 * d + 8 * h + 8]
    out[...] = spaced[...].astype(jnp.bfloat16)


ALL = ("z", "r")


def exchange(payload, axis):
    return lax.all_to_all(payload, axis, split_axis=0, concat_axis=0, tiled=True)


def body(
    volume,
    first_kernel,
    second_kernel,
    deep_kernel,
    deeper_kernel,
    rise_kernel,
    decode_kernel,
    final_kernel,
):
    n = lax.axis_size(ALL)
    place = lax.axis_index(ALL)
    planes = n // GROUP
    plane, rank = lax.axis_index("z"), lax.axis_index("r")
    chans = deep_kernel.shape[4]
    voxels = 16 * n
    bf16 = functools.partial(jax.ShapeDtypeStruct, dtype=jnp.bfloat16)

    decode_part = lax.all_gather(decode_kernel.reshape(27 * chans, 256), "z", axis=0)
    if chans % 16:
        decode_part = decode_part.reshape(planes, 27, chans, 256).transpose(1, 0, 2, 3)
        decode_part = decode_part.reshape(1, 27 * 128, 256)

    forward = [(i, i + 1) for i in range(n - 1)]
    backward = [(target, source) for source, target in forward]
    low = lax.ppermute(volume[1:], ALL, forward)
    high = lax.ppermute(volume[:3], ALL, backward)

    taps = first_kernel.reshape(3, 1152, 128)
    own = call(
        own_stage,
        jax.ShapeDtypeStruct((4, 256, 256), jnp.float32),
        [pltpu.VMEM((4, 18, 16, 384), jnp.bfloat16)],
        (volume, taps),
        2 * 1024 * 2304 * 256,
        24,
    )
    lane = np.arange(256)
    source = (lane // 64 + GROUP * (lane % 64 // chans)) * chans + lane % chans
    order = jnp.asarray(np.arange(256)[:, None] == source[None, :], jnp.bfloat16)
    ends = jnp.stack([place, n - 1 - place]).astype(jnp.int32)
    sends = call(
        stem_stage,
        bf16((GROUP, 48, 256)),
        [
            pltpu.VMEM((6, 18, 16, 384), jnp.bfloat16),
            pltpu.VMEM((128, 128), jnp.float32),
            pltpu.VMEM((4, 10, 24, 128), jnp.float32),
            pltpu.VMEM((256, 1152), jnp.bfloat16),
            pltpu.VMEM((2, 32, 128), jnp.float32),
        ],
        (ends, low, high, own, taps, second_kernel.reshape(3, 1152, 256), order),
        2 * 1024 * 2304 * 256,
        24,
        scalars=1,
    )
    near = exchange(sends, "r")
    plane_ref = plane.astype(jnp.int32).reshape(1)
    relays = call(
        relay_stage, bf16((planes, 80, 256)), [], (plane_ref, near), 0, 16, scalars=1
    )
    relayed = exchange(relays, "z")

    deep = call(
        deep_stage,
        bf16((n, chans, voxels)),
        [],
        (relayed, deep_kernel.transpose(0, 1, 2, 4, 3).reshape(27 * chans, 256)),
        2 * 27 * chans * 256 * voxels,
        16,
    )
    deep_whole = exchange(deep, ALL).reshape(n * chans, voxels)

    deeper = call(
        deeper_stage,
        bf16((n, chans, 128)),
        [],
        (deep_whole, deeper_kernel.transpose(0, 1, 2, 4, 3).reshape(27 * chans, n * chans)),
        2 * 27 * chans * n * chans * voxels,
        16,
    )
    deeper_near = exchange(deeper, ALL).reshape(n * chans, 128)

    mine = lax.dynamic_slice_in_dim(order, 64 * rank, 64, axis=1)
    rise_part = jnp.einsum("pio,os->ips", rise_kernel.reshape(8, n * chans, 256), mine)
    rise_part = rise_part.reshape(n * chans, 512)
    partial = call(
        decode_stage,
        bf16((512, 256)),
        [
            pltpu.VMEM((10, 10, 24, 128), jnp.float32),
            pltpu.VMEM((640, 1152), jnp.bfloat16),
            pltpu.VMEM((8, 128, 128), jnp.float32),
        ],
        (plane_ref, deeper_near, rise_part, near, relayed, decode_part),
        2 * 512 * 3456 * 256,
        24,
        scalars=1,
    )
    partials = exchange(partial.reshape(GROUP, 128, 256), "r")
    out = call(
        final_stage,
        bf16((1024, 128)),
        [pltpu.VMEM((1024, 128), jnp.float32)],
        (partials, final_kernel.reshape(8, 256, 128)),
        2 * 128 * 256 * 1024,
        16,
    )
    return out.reshape(4, 16, 16, 128)


def solution(mesh):
    reps, n = mesh.devices.shape
    grid = jax.sharding.Mesh(mesh.devices.reshape(reps, n // GROUP, GROUP), ("rep",) + ALL)
    return jax.shard_map(
        body,
        mesh=grid,
        in_specs=(
            P(("rep",) + ALL, None, None, None),
            P(),
            P(),
            P(None, None, None, None, ALL),
            P(None, None, None, None, ALL),
            P(),
            P(None, None, None, ALL, None),
            P(),
        ),
        out_specs=P(("rep",) + ALL, None, None, None),
        check_vma=False,
    )
```

```python
import functools

import jax
import jax.numpy as jnp
import numpy as np
from jax import lax
from jax.experimental import pallas as pl
from jax.experimental.pallas import tpu as pltpu
from jax.sharding import PartitionSpec as P

GROUP = 4
MIB = 1024 * 1024


def call(kernel, outs, scratch, args, flops, vmem_mib, scalars=0):
    spaces = [
        pltpu.SMEM if i < scalars else pltpu.VMEM
        for i in range(len(args))
    ]
    return pl.pallas_call(
        kernel,
        out_shape=outs,
        in_specs=[pl.BlockSpec(memory_space=space) for space in spaces],
        out_specs=jax.tree.map(lambda _: pl.BlockSpec(memory_space=pltpu.VMEM), outs),
        scratch_shapes=scratch,
        compiler_params=pltpu.CompilerParams(vmem_limit_bytes=vmem_mib * MIB),
        cost_estimate=pl.CostEstimate(
            flops=flops,
            bytes_accessed=sum(a.size * a.dtype.itemsize for a in args),
            transcendentals=0,
        ),
    )(*args)


def dot(left, right, dims=((1,), (0,))):
    return lax.dot_general(left, right, (dims, ((), ())), preferred_element_type=jnp.float32)


def round_once(values):
    return values.astype(jnp.bfloat16).astype(jnp.float32)


def fill_patches(framed, patches, slices):
    for b in range(3):
        for c in range(3):
            tap = framed[:, b : b + 8, 7 + c : 15 + c, :].reshape(slices * 64, 128)
            col = (b * 3 + c) * 128
            patches[:, col : col + 128] = tap.astype(jnp.bfloat16)


def shift_slice(shifted, s, values):
    row = lax.broadcasted_iota(jnp.int32, (256, 128), 0) & 15
    here = values.reshape(256, 128).astype(jnp.float32)
    before = jnp.where(row == 0, 0.0, pltpu.roll(here, 1, 0))
    after = jnp.where(row == 15, 0.0, pltpu.roll(here, 255, 0))
    shifted[s, 0] = jnp.zeros((16, 384), jnp.bfloat16)
    shifted[s, 17] = jnp.zeros((16, 384), jnp.bfloat16)
    for c, tap in enumerate((before, here, after)):
        tap = tap.astype(jnp.bfloat16).reshape(16, 16, 128)
        shifted[s, 1:17, :, 128 * c : 128 * c + 128] = tap


def depth_pair(shifted, slices, weights, steps):
    left = jnp.concatenate(
        [shifted[s, b : b + 16].reshape(256, 384) for s in slices for b in range(3)], axis=1
    )
    none = jnp.zeros((1152, 128), jnp.bfloat16)
    right = [
        jnp.concatenate(
            [weights[j] if j < 3 else none, weights[j - 1] if j > 0 else none], axis=1
        )
        for j in steps
    ]
    return dot(left, jnp.concatenate(right, axis=0))


def depth_one(shifted, s, weights):
    left = jnp.concatenate([shifted[s, b : b + 16].reshape(256, 384) for b in range(3)], axis=1)
    return dot(left, weights)


def own_stage(volume, weights, out, shifted):
    for s in range(4):
        shift_slice(shifted, s, volume[s])
    out[0, :, :128] = jnp.zeros((256, 128), jnp.float32)
    out[0, :, 128:] = depth_one(shifted, 0, weights[2])
    out[1] = depth_pair(shifted, (0, 1, 2), weights, (1, 2, 3))
    out[2] = depth_pair(shifted, (1, 2, 3), weights, (0, 1, 2))
    out[3, :, :128] = depth_one(shifted, 3, weights[0])
    out[3, :, 128:] = jnp.zeros((256, 128), jnp.float32)


def stem_stage(
    ends, low, high, own, weights, second, order,
    pooled_out, skip_out,
    shifted, halves, framed, patches, quarters,
):
    for s in range(3):
        shift_slice(shifted, s, low[s])
        shift_slice(shifted, 3 + s, high[s])
    framed[...] = jnp.zeros(framed.shape, jnp.float32)
    for m in range(4):
        if m == 0:
            first = own[0] + depth_pair(shifted, (0, 1, 2), weights, (0, 1, 2))
        elif m == 3:
            first = own[3] + depth_pair(shifted, (3, 4, 5), weights, (1, 2, 3))
        elif m == 1:
            near = own[1, :, :128] + depth_one(shifted, 2, weights[0])
            first = jnp.concatenate([near, own[1, :, 128:]], axis=1)
        else:
            far = own[2, :, 128:] + depth_one(shifted, 3, weights[2])
            first = jnp.concatenate([own[2, :, :128], far], axis=1)
        first = round_once(jnp.maximum(first, 0.0))
        pair = (first[:, :128] + first[:, 128:]).reshape(8, 32, 128)
        halves[...] = (pair[:, :16] + pair[:, 16:]).reshape(128, 128)
        pooled = halves[pl.ds(0, 64, stride=2), :] + halves[pl.ds(1, 64, stride=2), :]
        pooled = round_once(pooled * 0.125)
        if m == 0:
            pooled = jnp.where(ends[0] == 0, 0.0, pooled)
        if m == 3:
            pooled = jnp.where(ends[1] == 0, 0.0, pooled)
        framed[m, 1:9, 8:16, :] = pooled.reshape(8, 8, 128)
    fill_patches(framed, patches, 4)
    skip = dot(patches[0:128], second[0])
    skip += dot(patches[64:192], second[1])
    skip += dot(patches[128:256], second[2])
    skip = jnp.maximum(skip, 0.0).astype(jnp.bfloat16)
    wide = skip.astype(jnp.float32)
    pair = (wide[:64] + wide[64:]).reshape(4, 16, 256)
    pair = (pair[:, :8] + pair[:, 8:]).reshape(32, 256)
    for k in range(2):
        quarters[k] = pair[:, 128 * k : 128 * k + 128]
    pooled = jnp.concatenate(
        [
            quarters[k, pl.ds(0, 16, stride=2), :] + quarters[k, pl.ds(1, 16, stride=2), :]
            for k in range(2)
        ],
        axis=1,
    )
    pooled = (pooled * 0.125).astype(jnp.bfloat16)
    for p in range(pooled_out.shape[0]):
        pooled_out[p] = pooled
    sorted_skip = dot(skip, order[...])
    for r in range(GROUP):
        near, far = sorted_skip[:64, 64 * r : 64 * r + 64], sorted_skip[64:, 64 * r : 64 * r + 64]
        block = jnp.concatenate([near, far], axis=1)
        block = jnp.concatenate([block[:32], block[32:]], axis=1).astype(jnp.bfloat16)
        skip_out[r] = block


def relay_stage(pooled, skips, out):
    planes = pooled.shape[0]
    for r in range(GROUP):
        for p in range(planes):
            out[r, 16 * p : 16 * p + 16, :] = pooled[p]
        out[r, 16 * planes :, :] = skips[r]


def edge_slice(block, far):
    lower = lax.broadcasted_iota(jnp.int32, (16, 128), 1) < 64
    sides = []
    for k in range(2):
        half = block[:, 128 * k : 128 * k + 128].astype(jnp.float32)
        top, bottom = half[:16], half[16:]
        if far:
            top = pltpu.roll(top, 64, 1)
        else:
            bottom = pltpu.roll(bottom, 64, 1)
        sides.append(jnp.where(lower, top, bottom))
    return jnp.concatenate(sides, axis=1).astype(jnp.bfloat16)


def spread_taps(weights, values, dims, chans, voxels):
    lane = lax.broadcasted_iota(jnp.int32, (chans, voxels), 1)

    def moved(term, tap, step, place, last):
        if tap == 1:
            return term
        keep = place > 0 if tap == 0 else place < last
        return jnp.where(keep, pltpu.roll(term, ((1 - tap) * step) % voxels, 1), 0.0)

    total = None
    for a in range(3):
        products = dot(weights[a * 9 * chans : (a + 1) * 9 * chans, :], values, dims)
        plane = None
        for b in range(3):
            line = None
            for c in range(3):
                at = (b * 3 + c) * chans
                term = moved(products[at : at + chans], c, 1, lane & 3, 3)
                line = term if line is None else line + term
            line = moved(line, b, 4, (lane >> 2) & 3, 3)
            plane = line if plane is None else plane + line
        plane = moved(plane, a, 16, lane >> 4, voxels // 16 - 1)
        total = plane if total is None else total + plane
    return jnp.maximum(total, 0.0)


def deep_stage(near, weights, out, first, last):
    n, chans, voxels = out.shape
    values = [near[r, 16 * p : 16 * p + 16, :] for p in range(n // GROUP) for r in range(GROUP)]
    values = jnp.concatenate(values, axis=0)
    deep = spread_taps(weights, values, ((1,), (1,)), chans, voxels).astype(jnp.bfloat16)
    for dest in range(n):
        out[dest] = deep
    first[...] = edge_slice(near[0, voxels // GROUP :, :], False)
    last[...] = edge_slice(near[GROUP - 1, voxels // GROUP :, :], True)


def deeper_stage(deep, weights, out):
    n, chans, _ = out.shape
    voxels = deep.shape[1]
    deeper = spread_taps(weights, deep[...], ((1,), (0,)), chans, voxels)
    lane = lax.broadcasted_iota(jnp.int32, (chans, 128), 1)
    planes = n // GROUP
    for p in range(planes):
        part = pltpu.roll(deeper, (16 - 64 * p) % voxels, 1)[:, :128]
        if p == 0:
            part = jnp.where(lane < 16, 0.0, part)
        if p == planes - 1:
            part = jnp.where(lane >= 80, 0.0, part)
        part = part.astype(jnp.bfloat16)
        for r in range(GROUP):
            out[GROUP * p + r] = part


def decode_stage(
    deeper, rise, near, low, high, decode, out, framed, patches, risen
):
    framed[...] = jnp.zeros(framed.shape, jnp.float32)
    spread = round_once(dot(deeper[...].astype(jnp.float32).T.astype(jnp.bfloat16), rise[...]))
    for pair in range(4):
        both = spread[:, 128 * pair : 128 * pair + 128]
        risen[2 * pair] = both
        risen[2 * pair + 1] = pltpu.roll(both, 64, 1)
    upper = lax.broadcasted_iota(jnp.int32, (64, 128), 1) >= 64
    for s in range(10):
        d, a = (s + 1) // 2, (s + 1) % 2
        for h in range(4):
            for b in range(2):
                for c in range(2):
                    framed[s, 1 + 2 * h + b, pl.ds(8 + c, 4, stride=2), :] = risen[
                        4 * a + 2 * b + c, 16 * d + 4 * h : 16 * d + 4 * h + 4, :
                    ]
        if s == 0 or s == 9:
            edge = (low if s == 0 else high)[...].astype(jnp.float32)
            parts = []
            for k in range(2):
                half = edge[:, 128 * k : 128 * k + 128]
                parts += [pltpu.roll(half, 64, 1), half]
            skip = jnp.concatenate(parts, axis=0)
        else:
            both = near[(s - 1) // 2, near.shape[1] - 32 :, :].astype(jnp.float32)
            skip = jnp.concatenate([both[:, :128], both[:, 128:]], axis=0)
            if (s - 1) % 2 == 0:
                skip = pltpu.roll(skip, 64, 1)
        joined = framed[s, 1:9, 8:16, :].reshape(64, 128)
        framed[s, 1:9, 8:16, :] = jnp.where(upper, skip, joined).reshape(8, 8, 128)
    fill_patches(framed, patches, 10)
    blocks = decode.shape[0]
    step = 128 // blocks
    partial = None
    for a in range(3):
        right = [
            decode[z, tap * step : (tap + 1) * step, :]
            for tap in range(9 * a, 9 * a + 9)
            for z in range(blocks)
        ]
        term = dot(patches[64 * a : 64 * a + 512], jnp.concatenate(right, axis=0))
        partial = term if partial is None else partial + term
    out[...] = partial.astype(jnp.bfloat16)


def final_stage(partials, weights, out, spaced):
    decoded = partials[0].astype(jnp.float32)
    for g in range(1, GROUP):
        decoded += partials[g].astype(jnp.float32)
    decoded = jnp.maximum(decoded, 0.0).astype(jnp.bfloat16)
    for a in range(2):
        for b in range(2):
            for c in range(2):
                values = dot(decoded, weights[4 * a + 2 * b + c])
                for d in range(2):
                    for h in range(8):
                        at = ((2 * d + a) * 16 + 2 * h + b) * 16 + c
                        spaced[pl.ds(at, 8, stride=2), :] = values[64 * d + 8 * h : 64 * d + 8 * h + 8]
    out[...] = spaced[...].astype(jnp.bfloat16)


ALL = ("z", "r")


def exchange(payload, axis):
    return lax.all_to_all(payload, axis, split_axis=0, concat_axis=0, tiled=True)


def body(
    volume,
    first_kernel,
    second_kernel,
    deep_kernel,
    deeper_kernel,
    rise_kernel,
    decode_kernel,
    final_kernel,
):
    n = lax.axis_size(ALL)
    place = lax.axis_index(ALL)
    planes = n // GROUP
    rank = lax.axis_index("r")
    chans = deep_kernel.shape[4]
    voxels = 16 * n
    bf16 = functools.partial(jax.ShapeDtypeStruct, dtype=jnp.bfloat16)

    decode_part = lax.all_gather(decode_kernel.reshape(27 * chans, 256), "z", axis=0)
    if chans % 16:
        decode_part = decode_part.reshape(planes, 27, chans, 256).transpose(1, 0, 2, 3)
        decode_part = decode_part.reshape(1, 27 * 128, 256)

    forward = [(i, i + 1) for i in range(n - 1)]
    backward = [(target, source) for source, target in forward]
    low = lax.ppermute(volume[1:], ALL, forward)
    high = lax.ppermute(volume[:3], ALL, backward)

    taps = first_kernel.reshape(3, 1152, 128)
    own = call(
        own_stage,
        jax.ShapeDtypeStruct((4, 256, 256), jnp.float32),
        [pltpu.VMEM((4, 18, 16, 384), jnp.bfloat16)],
        (volume, taps),
        2 * 1024 * 2304 * 256,
        24,
    )
    lane = np.arange(256)
    source = (lane // 64 + GROUP * (lane % 64 // chans)) * chans + lane % chans
    order = jnp.asarray(np.arange(256)[:, None] == source[None, :], jnp.bfloat16)
    ends = jnp.stack([place, n - 1 - place]).astype(jnp.int32)
    pooled_two, skips = call(
        stem_stage,
        (bf16((planes, 16, 256)), bf16((GROUP, 32, 256))),
        [
            pltpu.VMEM((6, 18, 16, 384), jnp.bfloat16),
            pltpu.VMEM((128, 128), jnp.float32),
            pltpu.VMEM((4, 10, 24, 128), jnp.float32),
            pltpu.VMEM((256, 1152), jnp.bfloat16),
            pltpu.VMEM((2, 32, 128), jnp.float32),
        ],
        (ends, low, high, own, taps, second_kernel.reshape(3, 1152, 256), order),
        2 * 1024 * 2304 * 256,
        24,
        scalars=1,
    )
    pooled_line = exchange(pooled_two, "z")
    relays = call(
        relay_stage, bf16((GROUP, 16 * planes + 32, 256)), [], (pooled_line, skips), 0, 16
    )
    near = exchange(relays, "r")

    deep, first, last = call(
        deep_stage,
        (bf16((n, chans, voxels)), bf16((16, 256)), bf16((16, 256))),
        [],
        (near, deep_kernel.transpose(0, 1, 2, 4, 3).reshape(27 * chans, 256)),
        2 * 27 * chans * 256 * voxels,
        16,
    )
    skip_low = lax.ppermute(last, "z", [(p, p + 1) for p in range(planes - 1)])
    skip_high = lax.ppermute(first, "z", [(p + 1, p) for p in range(planes - 1)])
    deep_whole = exchange(deep, ALL).reshape(n * chans, voxels)

    deeper = call(
        deeper_stage,
        bf16((n, chans, 128)),
        [],
        (deep_whole, deeper_kernel.transpose(0, 1, 2, 4, 3).reshape(27 * chans, n * chans)),
        2 * 27 * chans * n * chans * voxels,
        16,
    )
    deeper_near = exchange(deeper, ALL).reshape(n * chans, 128)

    mine = lax.dynamic_slice_in_dim(order, 64 * rank, 64, axis=1)
    rise_part = jnp.einsum("pio,os->ips", rise_kernel.reshape(8, n * chans, 256), mine)
    rise_part = rise_part.reshape(n * chans, 512)
    partial = call(
        decode_stage,
        bf16((512, 256)),
        [
            pltpu.VMEM((10, 10, 24, 128), jnp.float32),
            pltpu.VMEM((640, 1152), jnp.bfloat16),
            pltpu.VMEM((8, 128, 128), jnp.float32),
        ],
        (deeper_near, rise_part, near, skip_low, skip_high, decode_part),
        2 * 512 * 3456 * 256,
        24,
    )
    partials = exchange(partial.reshape(GROUP, 128, 256), "r")
    out = call(
        final_stage,
        bf16((1024, 128)),
        [pltpu.VMEM((1024, 128), jnp.float32)],
        (partials, final_kernel.reshape(8, 256, 128)),
        2 * 128 * 256 * 1024,
        16,
    )
    return out.reshape(4, 16, 16, 128)


def solution(mesh):
    reps, n = mesh.devices.shape
    grid = jax.sharding.Mesh(mesh.devices.reshape(reps, n // GROUP, GROUP), ("rep",) + ALL)
    return jax.shard_map(
        body,
        mesh=grid,
        in_specs=(
            P(("rep",) + ALL, None, None, None),
            P(),
            P(),
            P(None, None, None, None, ALL),
            P(None, None, None, None, ALL),
            P(),
            P(None, None, None, ALL, None),
            P(),
        ),
        out_specs=P(("rep",) + ALL, None, None, None),
        check_vma=False,
    )
```

```python
import functools

import jax
import jax.numpy as jnp
import numpy as np
from jax import lax
from jax.experimental import pallas as pl
from jax.experimental.pallas import tpu as pltpu
from jax.sharding import PartitionSpec as P

GROUP = 4
MIB = 1024 * 1024


def call(kernel, outs, scratch, args, flops, vmem_mib, scalars=0, unread=0):
    spaces = [pltpu.SMEM] * scalars + [pltpu.VMEM] * (len(args) - scalars - unread)
    spaces += [pl.ANY] * unread
    return pl.pallas_call(
        kernel,
        out_shape=outs,
        in_specs=[pl.BlockSpec(memory_space=space) for space in spaces],
        out_specs=jax.tree.map(lambda _: pl.BlockSpec(memory_space=pltpu.VMEM), outs),
        scratch_shapes=scratch,
        compiler_params=pltpu.CompilerParams(vmem_limit_bytes=vmem_mib * MIB),
        cost_estimate=pl.CostEstimate(
            flops=flops,
            bytes_accessed=sum(a.size * a.dtype.itemsize for a in args[: len(args) - unread]),
            transcendentals=0,
        ),
    )(*args)


def dot(left, right, dims=((1,), (0,))):
    return lax.dot_general(left, right, (dims, ((), ())), preferred_element_type=jnp.float32)


def round_once(values):
    return values.astype(jnp.bfloat16).astype(jnp.float32)


def fill_patches(framed, patches, slices):
    for b in range(3):
        for c in range(3):
            tap = framed[:, b : b + 8, 7 + c : 15 + c, :].reshape(slices * 64, 128)
            col = (b * 3 + c) * 128
            patches[:, col : col + 128] = tap.astype(jnp.bfloat16)


def shift_slice(shifted, s, values):
    row = lax.broadcasted_iota(jnp.int32, (256, 128), 0) & 15
    here = values.reshape(256, 128).astype(jnp.float32)
    before = jnp.where(row == 0, 0.0, pltpu.roll(here, 1, 0))
    after = jnp.where(row == 15, 0.0, pltpu.roll(here, 255, 0))
    shifted[s, 0] = jnp.zeros((16, 384), jnp.bfloat16)
    shifted[s, 17] = jnp.zeros((16, 384), jnp.bfloat16)
    for c, tap in enumerate((before, here, after)):
        tap = tap.astype(jnp.bfloat16).reshape(16, 16, 128)
        shifted[s, 1:17, :, 128 * c : 128 * c + 128] = tap


def depth_pair(shifted, slices, weights, steps):
    left = jnp.concatenate(
        [shifted[s, b : b + 16].reshape(256, 384) for s in slices for b in range(3)], axis=1
    )
    none = jnp.zeros((1152, 128), jnp.bfloat16)
    right = [
        jnp.concatenate(
            [weights[j] if j < 3 else none, weights[j - 1] if j > 0 else none], axis=1
        )
        for j in steps
    ]
    return dot(left, jnp.concatenate(right, axis=0))


def depth_one(shifted, s, weights):
    left = jnp.concatenate([shifted[s, b : b + 16].reshape(256, 384) for b in range(3)], axis=1)
    return dot(left, weights)


def front_stage(volume, tail, head, whole):
    tail[...] = volume[1:]
    head[...] = volume[:3]
    whole[...] = volume[...]


def own_stage(volume, weights, out, shifted):
    for s in range(4):
        shift_slice(shifted, s, volume[s])
    out[0, :, :128] = jnp.zeros((256, 128), jnp.float32)
    out[0, :, 128:] = depth_one(shifted, 0, weights[2])
    out[1] = depth_pair(shifted, (0, 1, 2), weights, (1, 2, 3))
    out[2] = depth_pair(shifted, (1, 2, 3), weights, (0, 1, 2))
    out[3, :, :128] = depth_one(shifted, 3, weights[0])
    out[3, :, 128:] = jnp.zeros((256, 128), jnp.float32)


def stem_stage(
    ends, low, high, own, weights, second, order,
    pooled_out, skip_out,
    shifted, halves, framed, patches, quarters,
):
    for s in range(3):
        shift_slice(shifted, s, low[s])
        shift_slice(shifted, 3 + s, high[s])
    framed[...] = jnp.zeros(framed.shape, jnp.float32)
    for m in range(4):
        if m == 0:
            first = own[0] + depth_pair(shifted, (0, 1, 2), weights, (0, 1, 2))
        elif m == 3:
            first = own[3] + depth_pair(shifted, (3, 4, 5), weights, (1, 2, 3))
        elif m == 1:
            near = own[1, :, :128] + depth_one(shifted, 2, weights[0])
            first = jnp.concatenate([near, own[1, :, 128:]], axis=1)
        else:
            far = own[2, :, 128:] + depth_one(shifted, 3, weights[2])
            first = jnp.concatenate([own[2, :, :128], far], axis=1)
        first = round_once(jnp.maximum(first, 0.0))
        pair = (first[:, :128] + first[:, 128:]).reshape(8, 32, 128)
        halves[...] = (pair[:, :16] + pair[:, 16:]).reshape(128, 128)
        pooled = halves[pl.ds(0, 64, stride=2), :] + halves[pl.ds(1, 64, stride=2), :]
        pooled = round_once(pooled * 0.125)
        if m == 0:
            pooled = jnp.where(ends[0] == 0, 0.0, pooled)
        if m == 3:
            pooled = jnp.where(ends[1] == 0, 0.0, pooled)
        framed[m, 1:9, 8:16, :] = pooled.reshape(8, 8, 128)
    fill_patches(framed, patches, 4)
    skip = dot(patches[0:128], second[0])
    skip += dot(patches[64:192], second[1])
    skip += dot(patches[128:256], second[2])
    skip = jnp.maximum(skip, 0.0).astype(jnp.bfloat16)
    wide = skip.astype(jnp.float32)
    pair = (wide[:64] + wide[64:]).reshape(4, 16, 256)
    pair = (pair[:, :8] + pair[:, 8:]).reshape(32, 256)
    for k in range(2):
        quarters[k] = pair[:, 128 * k : 128 * k + 128]
    pooled = jnp.concatenate(
        [
            quarters[k, pl.ds(0, 16, stride=2), :] + quarters[k, pl.ds(1, 16, stride=2), :]
            for k in range(2)
        ],
        axis=1,
    )
    pooled = (pooled * 0.125).astype(jnp.bfloat16)
    for p in range(pooled_out.shape[0]):
        pooled_out[p] = pooled
    sorted_skip = dot(skip, order[...])
    for r in range(GROUP):
        near, far = sorted_skip[:64, 64 * r : 64 * r + 64], sorted_skip[64:, 64 * r : 64 * r + 64]
        block = jnp.concatenate([near, far], axis=1)
        block = jnp.concatenate([block[:32], block[32:]], axis=1).astype(jnp.bfloat16)
        skip_out[r] = block


def relay_stage(pooled, skips, out):
    planes = pooled.shape[0]
    for r in range(GROUP):
        for p in range(planes):
            out[r, 16 * p : 16 * p + 16, :] = pooled[p]
        out[r, 16 * planes :, :] = skips[r]


def edge_slice(block, far):
    lower = lax.broadcasted_iota(jnp.int32, (16, 128), 1) < 64
    sides = []
    for k in range(2):
        half = block[:, 128 * k : 128 * k + 128].astype(jnp.float32)
        top, bottom = half[:16], half[16:]
        if far:
            top = pltpu.roll(top, 64, 1)
        else:
            bottom = pltpu.roll(bottom, 64, 1)
        sides.append(jnp.where(lower, top, bottom))
    return jnp.concatenate(sides, axis=1).astype(jnp.bfloat16)


def spread_taps(weights, values, dims, chans, voxels):
    lane = lax.broadcasted_iota(jnp.int32, (chans, voxels), 1)

    def moved(term, tap, step, place, last):
        if tap == 1:
            return term
        keep = place > 0 if tap == 0 else place < last
        return jnp.where(keep, pltpu.roll(term, ((1 - tap) * step) % voxels, 1), 0.0)

    total = None
    for a in range(3):
        products = dot(weights[a * 9 * chans : (a + 1) * 9 * chans, :], values, dims)
        plane = None
        for b in range(3):
            line = None
            for c in range(3):
                at = (b * 3 + c) * chans
                term = moved(products[at : at + chans], c, 1, lane & 3, 3)
                line = term if line is None else line + term
            line = moved(line, b, 4, (lane >> 2) & 3, 3)
            plane = line if plane is None else plane + line
        plane = moved(plane, a, 16, lane >> 4, voxels // 16 - 1)
        total = plane if total is None else total + plane
    return jnp.maximum(total, 0.0)


def deep_stage(near, weights, out, first, last):
    n, chans, voxels = out.shape
    values = [near[r, 16 * p : 16 * p + 16, :] for p in range(n // GROUP) for r in range(GROUP)]
    values = jnp.concatenate(values, axis=0)
    deep = spread_taps(weights, values, ((1,), (1,)), chans, voxels).astype(jnp.bfloat16)
    for dest in range(n):
        out[dest] = deep
    first[...] = edge_slice(near[0, voxels // GROUP :, :], False)
    last[...] = edge_slice(near[GROUP - 1, voxels // GROUP :, :], True)


def deeper_stage(deep, weights, out):
    n, chans, _ = out.shape
    voxels = deep.shape[1]
    deeper = spread_taps(weights, deep[...], ((1,), (0,)), chans, voxels)
    lane = lax.broadcasted_iota(jnp.int32, (chans, 128), 1)
    planes = n // GROUP
    for p in range(planes):
        part = pltpu.roll(deeper, (16 - 64 * p) % voxels, 1)[:, :128]
        if p == 0:
            part = jnp.where(lane < 16, 0.0, part)
        if p == planes - 1:
            part = jnp.where(lane >= 80, 0.0, part)
        part = part.astype(jnp.bfloat16)
        for r in range(GROUP):
            out[GROUP * p + r] = part


def rise_stage(rank, chans, rise, _, out):
    lane = lax.broadcasted_iota(jnp.int32, (256, 64), 1)
    row = lax.broadcasted_iota(jnp.int32, (256, 64), 0)
    source = (rank[0] + GROUP * (lane // chans)) * chans + lane % chans
    mine = jnp.where(row == source, 1.0, 0.0).astype(jnp.bfloat16)
    for pair in range(4):
        both = [dot(rise[2 * pair + k], mine) for k in range(2)]
        both = jnp.concatenate(both, axis=1).astype(jnp.bfloat16)
        out[:, 128 * pair : 128 * pair + 128] = both


def decode_stage(
    deeper, rise, near, low, high, decode, out, framed, patches, risen
):
    framed[...] = jnp.zeros(framed.shape, jnp.float32)
    spread = round_once(dot(deeper[...].astype(jnp.float32).T.astype(jnp.bfloat16), rise[...]))
    for pair in range(4):
        both = spread[:, 128 * pair : 128 * pair + 128]
        risen[2 * pair] = both
        risen[2 * pair + 1] = pltpu.roll(both, 64, 1)
    upper = lax.broadcasted_iota(jnp.int32, (64, 128), 1) >= 64
    for s in range(10):
        d, a = (s + 1) // 2, (s + 1) % 2
        for h in range(4):
            for b in range(2):
                for c in range(2):
                    framed[s, 1 + 2 * h + b, pl.ds(8 + c, 4, stride=2), :] = risen[
                        4 * a + 2 * b + c, 16 * d + 4 * h : 16 * d + 4 * h + 4, :
                    ]
        if s == 0 or s == 9:
            edge = (low if s == 0 else high)[...].astype(jnp.float32)
            parts = []
            for k in range(2):
                half = edge[:, 128 * k : 128 * k + 128]
                parts += [pltpu.roll(half, 64, 1), half]
            skip = jnp.concatenate(parts, axis=0)
        else:
            both = near[(s - 1) // 2, near.shape[1] - 32 :, :].astype(jnp.float32)
            skip = jnp.concatenate([both[:, :128], both[:, 128:]], axis=0)
            if (s - 1) % 2 == 0:
                skip = pltpu.roll(skip, 64, 1)
        joined = framed[s, 1:9, 8:16, :].reshape(64, 128)
        framed[s, 1:9, 8:16, :] = jnp.where(upper, skip, joined).reshape(8, 8, 128)
    fill_patches(framed, patches, 10)
    blocks = decode.shape[0]
    step = 128 // blocks
    partial = None
    for a in range(3):
        right = [
            decode[z, tap * step : (tap + 1) * step, :]
            for tap in range(9 * a, 9 * a + 9)
            for z in range(blocks)
        ]
        term = dot(patches[64 * a : 64 * a + 512], jnp.concatenate(right, axis=0))
        partial = term if partial is None else partial + term
    out[...] = partial.astype(jnp.bfloat16)


def final_stage(partials, weights, out, spaced):
    decoded = partials[0].astype(jnp.float32)
    for g in range(1, GROUP):
        decoded += partials[g].astype(jnp.float32)
    decoded = jnp.maximum(decoded, 0.0).astype(jnp.bfloat16)
    for a in range(2):
        for b in range(2):
            for c in range(2):
                values = dot(decoded, weights[4 * a + 2 * b + c])
                for d in range(2):
                    for h in range(8):
                        at = ((2 * d + a) * 16 + 2 * h + b) * 16 + c
                        spaced[pl.ds(at, 8, stride=2), :] = values[64 * d + 8 * h : 64 * d + 8 * h + 8]
    out[...] = spaced[...].astype(jnp.bfloat16)


ALL = ("z", "r")


def exchange(payload, axis):
    return lax.all_to_all(payload, axis, split_axis=0, concat_axis=0, tiled=True)


def body(
    volume,
    first_kernel,
    second_kernel,
    deep_kernel,
    deeper_kernel,
    rise_kernel,
    decode_kernel,
    final_kernel,
):
    n = lax.axis_size(ALL)
    place = lax.axis_index(ALL)
    planes = n // GROUP
    rank = lax.axis_index("r")
    chans = deep_kernel.shape[4]
    voxels = 16 * n
    bf16 = functools.partial(jax.ShapeDtypeStruct, dtype=jnp.bfloat16)

    decode_part = lax.all_gather(decode_kernel.reshape(27 * chans, 256), "z", axis=0)
    if chans % 16:
        decode_part = decode_part.reshape(planes, 27, chans, 256).transpose(1, 0, 2, 3)
        decode_part = decode_part.reshape(1, 27 * 128, 256)

    forward = [(i, i + 1) for i in range(n - 1)]
    backward = [(target, source) for source, target in forward]
    tail, head, volume = call(
        front_stage,
        (bf16((3, 16, 16, 128)), bf16((3, 16, 16, 128)), bf16((4, 16, 16, 128))),
        [],
        (volume,),
        3 * 10**9,
        16,
    )
    low = lax.ppermute(tail, ALL, forward)
    high = lax.ppermute(head, ALL, backward)

    taps = first_kernel.reshape(3, 1152, 128)
    own = call(
        own_stage,
        jax.ShapeDtypeStruct((4, 256, 256), jnp.float32),
        [pltpu.VMEM((4, 18, 16, 384), jnp.bfloat16)],
        (volume, taps),
        2 * 1024 * 2304 * 256,
        24,
    )
    lane = np.arange(256)
    source = (lane // 64 + GROUP * (lane % 64 // chans)) * chans + lane % chans
    order = jnp.asarray(np.arange(256)[:, None] == source[None, :], jnp.bfloat16)
    ends = jnp.stack([place, n - 1 - place]).astype(jnp.int32)
    pooled_two, skips = call(
        stem_stage,
        (bf16((planes, 16, 256)), bf16((GROUP, 32, 256))),
        [
            pltpu.VMEM((6, 18, 16, 384), jnp.bfloat16),
            pltpu.VMEM((128, 128), jnp.float32),
            pltpu.VMEM((4, 10, 24, 128), jnp.float32),
            pltpu.VMEM((256, 1152), jnp.bfloat16),
            pltpu.VMEM((2, 32, 128), jnp.float32),
        ],
        (ends, low, high, own, taps, second_kernel.reshape(3, 1152, 256), order),
        2 * 1024 * 2304 * 256,
        24,
        scalars=1,
    )
    pooled_line = exchange(pooled_two, "z")
    relays = call(
        relay_stage, bf16((GROUP, 16 * planes + 32, 256)), [], (pooled_line, skips), 0, 16
    )
    near = exchange(relays, "r")

    deep, first, last = call(
        deep_stage,
        (bf16((n, chans, voxels)), bf16((16, 256)), bf16((16, 256))),
        [],
        (near, deep_kernel.transpose(0, 1, 2, 4, 3).reshape(27 * chans, 256)),
        2 * 27 * chans * 256 * voxels,
        16,
    )
    skip_low = lax.ppermute(last, "z", [(p, p + 1) for p in range(planes - 1)])
    skip_high = lax.ppermute(first, "z", [(p + 1, p) for p in range(planes - 1)])
    deep_whole = exchange(deep, ALL).reshape(n * chans, voxels)

    deeper = call(
        deeper_stage,
        bf16((n, chans, 128)),
        [],
        (deep_whole, deeper_kernel.transpose(0, 1, 2, 4, 3).reshape(27 * chans, n * chans)),
        2 * 27 * chans * n * chans * voxels,
        16,
    )
    deeper_near = exchange(deeper, ALL).reshape(n * chans, 128)

    rise_part = call(
        lambda rank_ref, *refs: rise_stage(rank_ref, chans, *refs),
        bf16((n * chans, 512)),
        [],
        (rank.astype(jnp.int32).reshape(1), rise_kernel.reshape(8, n * chans, 256), decode_part[0, :16]),
        2 * 8 * n * chans * 256 * 64,
        16,
        scalars=1,
        unread=1,
    )
    partial = call(
        decode_stage,
        bf16((512, 256)),
        [
            pltpu.VMEM((10, 10, 24, 128), jnp.float32),
            pltpu.VMEM((640, 1152), jnp.bfloat16),
            pltpu.VMEM((8, 128, 128), jnp.float32),
        ],
        (deeper_near, rise_part, near, skip_low, skip_high, decode_part),
        2 * 512 * 3456 * 256,
        24,
    )
    partials = exchange(partial.reshape(GROUP, 128, 256), "r")
    out = call(
        final_stage,
        bf16((1024, 128)),
        [pltpu.VMEM((1024, 128), jnp.float32)],
        (partials, final_kernel.reshape(8, 256, 128)),
        2 * 128 * 256 * 1024,
        16,
    )
    return out.reshape(4, 16, 16, 128)


def solution(mesh):
    reps, n = mesh.devices.shape
    grid = jax.sharding.Mesh(mesh.devices.reshape(reps, n // GROUP, GROUP), ("rep",) + ALL)
    return jax.shard_map(
        body,
        mesh=grid,
        in_specs=(
            P(("rep",) + ALL, None, None, None),
            P(),
            P(),
            P(None, None, None, None, ALL),
            P(None, None, None, None, ALL),
            P(),
            P(None, None, None, ALL, None),
            P(),
        ),
        out_specs=P(("rep",) + ALL, None, None, None),
        check_vma=False,
    )
```

```python
import functools

import jax
import jax.numpy as jnp
import numpy as np
from jax import lax
from jax.experimental import pallas as pl
from jax.experimental.pallas import tpu as pltpu
from jax.sharding import PartitionSpec as P

GROUP = 4
MIB = 1024 * 1024


def call(kernel, outs, scratch, args, flops, vmem_mib, scalars=0, far=0, far_outs=0):
    spaces = [pltpu.SMEM] * scalars + [pltpu.VMEM] * (len(args) - scalars - far)
    spaces += [pl.ANY] * far
    several = isinstance(outs, tuple)
    out_spaces = [pltpu.VMEM] * ((len(outs) if several else 1) - far_outs) + [pl.ANY] * far_outs
    out_specs = [pl.BlockSpec(memory_space=space) for space in out_spaces]
    return pl.pallas_call(
        kernel,
        out_shape=outs,
        in_specs=[pl.BlockSpec(memory_space=space) for space in spaces],
        out_specs=out_specs if several else out_specs[0],
        scratch_shapes=scratch,
        compiler_params=pltpu.CompilerParams(vmem_limit_bytes=vmem_mib * MIB),
        cost_estimate=pl.CostEstimate(
            flops=flops,
            bytes_accessed=sum(a.size * a.dtype.itemsize for a in args[: len(args) - far]),
            transcendentals=0,
        ),
    )(*args)


def dot(left, right, dims=((1,), (0,))):
    return lax.dot_general(left, right, (dims, ((), ())), preferred_element_type=jnp.float32)


def round_once(values):
    return values.astype(jnp.bfloat16).astype(jnp.float32)


def fill_patches(framed, patches, slices):
    for b in range(3):
        for c in range(3):
            tap = framed[:, b : b + 8, 7 + c : 15 + c, :].reshape(slices * 64, 128)
            col = (b * 3 + c) * 128
            patches[:, col : col + 128] = tap.astype(jnp.bfloat16)


def shift_slice(shifted, s, values):
    row = lax.broadcasted_iota(jnp.int32, (256, 128), 0) & 15
    here = values.reshape(256, 128).astype(jnp.float32)
    before = jnp.where(row == 0, 0.0, pltpu.roll(here, 1, 0))
    after = jnp.where(row == 15, 0.0, pltpu.roll(here, 255, 0))
    shifted[s, 0] = jnp.zeros((16, 384), jnp.bfloat16)
    shifted[s, 17] = jnp.zeros((16, 384), jnp.bfloat16)
    for c, tap in enumerate((before, here, after)):
        tap = tap.astype(jnp.bfloat16).reshape(16, 16, 128)
        shifted[s, 1:17, :, 128 * c : 128 * c + 128] = tap


def depth_pair(shifted, slices, weights, steps):
    left = jnp.concatenate(
        [shifted[s, b : b + 16].reshape(256, 384) for s in slices for b in range(3)], axis=1
    )
    none = jnp.zeros((1152, 128), jnp.bfloat16)
    right = [
        jnp.concatenate(
            [weights[j] if j < 3 else none, weights[j - 1] if j > 0 else none], axis=1
        )
        for j in steps
    ]
    return dot(left, jnp.concatenate(right, axis=0))


def depth_one(shifted, s, weights):
    left = jnp.concatenate([shifted[s, b : b + 16].reshape(256, 384) for b in range(3)], axis=1)
    return dot(left, weights)


def front_stage(rep, volume, decode, tail, head, whole, block, done):
    rows = block.shape[0]
    at = pl.multiple_of(jnp.where(rows == decode.shape[0], 0, rep[0] * rows), 16)
    copy = pltpu.make_async_copy(decode.at[pl.ds(at, rows)], block, done)
    copy.start()
    tail[...] = volume[1:]
    head[...] = volume[:3]
    whole[...] = volume[...]
    copy.wait()


def own_stage(volume, weights, out, shifted):
    for s in range(4):
        shift_slice(shifted, s, volume[s])
    out[0, :, :128] = jnp.zeros((256, 128), jnp.float32)
    out[0, :, 128:] = depth_one(shifted, 0, weights[2])
    out[1] = depth_pair(shifted, (0, 1, 2), weights, (1, 2, 3))
    out[2] = depth_pair(shifted, (1, 2, 3), weights, (0, 1, 2))
    out[3, :, :128] = depth_one(shifted, 3, weights[0])
    out[3, :, 128:] = jnp.zeros((256, 128), jnp.float32)


def stem_stage(
    ends, low, high, own, weights, second, order,
    pooled_out, skip_out,
    shifted, halves, framed, patches, quarters,
):
    for s in range(3):
        shift_slice(shifted, s, low[s])
        shift_slice(shifted, 3 + s, high[s])
    framed[...] = jnp.zeros(framed.shape, jnp.float32)
    for m in range(4):
        if m == 0:
            first = own[0] + depth_pair(shifted, (0, 1, 2), weights, (0, 1, 2))
        elif m == 3:
            first = own[3] + depth_pair(shifted, (3, 4, 5), weights, (1, 2, 3))
        elif m == 1:
            near = own[1, :, :128] + depth_one(shifted, 2, weights[0])
            first = jnp.concatenate([near, own[1, :, 128:]], axis=1)
        else:
            far = own[2, :, 128:] + depth_one(shifted, 3, weights[2])
            first = jnp.concatenate([own[2, :, :128], far], axis=1)
        first = round_once(jnp.maximum(first, 0.0))
        pair = (first[:, :128] + first[:, 128:]).reshape(8, 32, 128)
        halves[...] = (pair[:, :16] + pair[:, 16:]).reshape(128, 128)
        pooled = halves[pl.ds(0, 64, stride=2), :] + halves[pl.ds(1, 64, stride=2), :]
        pooled = round_once(pooled * 0.125)
        if m == 0:
            pooled = jnp.where(ends[0] == 0, 0.0, pooled)
        if m == 3:
            pooled = jnp.where(ends[1] == 0, 0.0, pooled)
        framed[m, 1:9, 8:16, :] = pooled.reshape(8, 8, 128)
    fill_patches(framed, patches, 4)
    skip = dot(patches[0:128], second[0])
    skip += dot(patches[64:192], second[1])
    skip += dot(patches[128:256], second[2])
    skip = jnp.maximum(skip, 0.0).astype(jnp.bfloat16)
    wide = skip.astype(jnp.float32)
    pair = (wide[:64] + wide[64:]).reshape(4, 16, 256)
    pair = (pair[:, :8] + pair[:, 8:]).reshape(32, 256)
    for k in range(2):
        quarters[k] = pair[:, 128 * k : 128 * k + 128]
    pooled = jnp.concatenate(
        [
            quarters[k, pl.ds(0, 16, stride=2), :] + quarters[k, pl.ds(1, 16, stride=2), :]
            for k in range(2)
        ],
        axis=1,
    )
    pooled = (pooled * 0.125).astype(jnp.bfloat16)
    for p in range(pooled_out.shape[0]):
        pooled_out[p] = pooled
    sorted_skip = dot(skip, order[...])
    for r in range(GROUP):
        near, far = sorted_skip[:64, 64 * r : 64 * r + 64], sorted_skip[64:, 64 * r : 64 * r + 64]
        block = jnp.concatenate([near, far], axis=1)
        block = jnp.concatenate([block[:32], block[32:]], axis=1).astype(jnp.bfloat16)
        skip_out[r] = block


def relay_stage(pooled, skips, out):
    planes = pooled.shape[0]
    for r in range(GROUP):
        for p in range(planes):
            out[r, 16 * p : 16 * p + 16, :] = pooled[p]
        out[r, 16 * planes :, :] = skips[r]


def edge_slice(block, far):
    lower = lax.broadcasted_iota(jnp.int32, (16, 128), 1) < 64
    sides = []
    for k in range(2):
        half = block[:, 128 * k : 128 * k + 128].astype(jnp.float32)
        top, bottom = half[:16], half[16:]
        if far:
            top = pltpu.roll(top, 64, 1)
        else:
            bottom = pltpu.roll(bottom, 64, 1)
        sides.append(jnp.where(lower, top, bottom))
    return jnp.concatenate(sides, axis=1).astype(jnp.bfloat16)


def spread_taps(weights, values, dims, chans, voxels):
    lane = lax.broadcasted_iota(jnp.int32, (chans, voxels), 1)

    def moved(term, tap, step, place, last):
        if tap == 1:
            return term
        keep = place > 0 if tap == 0 else place < last
        return jnp.where(keep, pltpu.roll(term, ((1 - tap) * step) % voxels, 1), 0.0)

    total = None
    for a in range(3):
        products = dot(weights[a * 9 * chans : (a + 1) * 9 * chans, :], values, dims)
        plane = None
        for b in range(3):
            line = None
            for c in range(3):
                at = (b * 3 + c) * chans
                term = moved(products[at : at + chans], c, 1, lane & 3, 3)
                line = term if line is None else line + term
            line = moved(line, b, 4, (lane >> 2) & 3, 3)
            plane = line if plane is None else plane + line
        plane = moved(plane, a, 16, lane >> 4, voxels // 16 - 1)
        total = plane if total is None else total + plane
    return jnp.maximum(total, 0.0)


def deep_stage(near, weights, out, first, last):
    n, chans, voxels = out.shape
    values = [near[r, 16 * p : 16 * p + 16, :] for p in range(n // GROUP) for r in range(GROUP)]
    values = jnp.concatenate(values, axis=0)
    deep = spread_taps(weights, values, ((1,), (1,)), chans, voxels).astype(jnp.bfloat16)
    for dest in range(n):
        out[dest] = deep
    first[...] = edge_slice(near[0, voxels // GROUP :, :], False)
    last[...] = edge_slice(near[GROUP - 1, voxels // GROUP :, :], True)


def deeper_stage(deep, weights, _, __, out):
    n, chans, _ = out.shape
    voxels = deep.shape[1]
    deeper = spread_taps(weights, deep[...], ((1,), (0,)), chans, voxels)
    lane = lax.broadcasted_iota(jnp.int32, (chans, 128), 1)
    planes = n // GROUP
    for p in range(planes):
        part = pltpu.roll(deeper, (16 - 64 * p) % voxels, 1)[:, :128]
        if p == 0:
            part = jnp.where(lane < 16, 0.0, part)
        if p == planes - 1:
            part = jnp.where(lane >= 80, 0.0, part)
        part = part.astype(jnp.bfloat16)
        for r in range(GROUP):
            out[GROUP * p + r] = part


def rise_stage(rank, chans, rise, decode, out, weights, done):
    copy = pltpu.make_async_copy(decode, weights, done)
    copy.start()
    lane = lax.broadcasted_iota(jnp.int32, (256, 64), 1)
    row = lax.broadcasted_iota(jnp.int32, (256, 64), 0)
    source = (rank[0] + GROUP * (lane // chans)) * chans + lane % chans
    mine = jnp.where(row == source, 1.0, 0.0).astype(jnp.bfloat16)
    for pair in range(4):
        both = [dot(rise[2 * pair + k], mine) for k in range(2)]
        both = jnp.concatenate(both, axis=1).astype(jnp.bfloat16)
        out[:, 128 * pair : 128 * pair + 128] = both
    copy.wait()


def decode_stage(
    deeper, rise, near, low, high, decode, out, framed, patches, risen
):
    framed[...] = jnp.zeros(framed.shape, jnp.float32)
    spread = round_once(dot(deeper[...].astype(jnp.float32).T.astype(jnp.bfloat16), rise[...]))
    for pair in range(4):
        both = spread[:, 128 * pair : 128 * pair + 128]
        risen[2 * pair] = both
        risen[2 * pair + 1] = pltpu.roll(both, 64, 1)
    upper = lax.broadcasted_iota(jnp.int32, (64, 128), 1) >= 64
    for s in range(10):
        d, a = (s + 1) // 2, (s + 1) % 2
        for h in range(4):
            for b in range(2):
                for c in range(2):
                    framed[s, 1 + 2 * h + b, pl.ds(8 + c, 4, stride=2), :] = risen[
                        4 * a + 2 * b + c, 16 * d + 4 * h : 16 * d + 4 * h + 4, :
                    ]
        if s == 0 or s == 9:
            edge = (low if s == 0 else high)[...].astype(jnp.float32)
            parts = []
            for k in range(2):
                half = edge[:, 128 * k : 128 * k + 128]
                parts += [pltpu.roll(half, 64, 1), half]
            skip = jnp.concatenate(parts, axis=0)
        else:
            both = near[(s - 1) // 2, near.shape[1] - 32 :, :].astype(jnp.float32)
            skip = jnp.concatenate([both[:, :128], both[:, 128:]], axis=0)
            if (s - 1) % 2 == 0:
                skip = pltpu.roll(skip, 64, 1)
        joined = framed[s, 1:9, 8:16, :].reshape(64, 128)
        framed[s, 1:9, 8:16, :] = jnp.where(upper, skip, joined).reshape(8, 8, 128)
    fill_patches(framed, patches, 10)
    _, blocks, rows, _ = decode.shape
    step = 128 // blocks
    partial = None
    for a in range(3):
        right = [
            decode[row // rows, z, row % rows : row % rows + 16, :]
            for tap in range(9 * a, 9 * a + 9)
            for z in range(blocks)
            for row in range(tap * step, (tap + 1) * step, 16)
        ]
        term = dot(patches[64 * a : 64 * a + 512], jnp.concatenate(right, axis=0))
        partial = term if partial is None else partial + term
    out[...] = partial.astype(jnp.bfloat16)


def final_stage(partials, weights, out, spaced):
    decoded = partials[0].astype(jnp.float32)
    for g in range(1, GROUP):
        decoded += partials[g].astype(jnp.float32)
    decoded = jnp.maximum(decoded, 0.0).astype(jnp.bfloat16)
    for a in range(2):
        for b in range(2):
            for c in range(2):
                values = dot(decoded, weights[4 * a + 2 * b + c])
                for d in range(2):
                    for h in range(8):
                        at = ((2 * d + a) * 16 + 2 * h + b) * 16 + c
                        spaced[pl.ds(at, 8, stride=2), :] = values[64 * d + 8 * h : 64 * d + 8 * h + 8]
    out[...] = spaced[...].astype(jnp.bfloat16)


ALL = ("z", "r")


def exchange(payload, axis):
    return lax.all_to_all(payload, axis, split_axis=0, concat_axis=0, tiled=True)


def body(
    volume,
    first_kernel,
    second_kernel,
    deep_kernel,
    deeper_kernel,
    rise_kernel,
    decode_kernel,
    final_kernel,
):
    n = lax.axis_size(ALL)
    place = lax.axis_index(ALL)
    planes = n // GROUP
    rank = lax.axis_index("r")
    chans = deep_kernel.shape[4]
    voxels = 16 * n
    bf16 = functools.partial(jax.ShapeDtypeStruct, dtype=jnp.bfloat16)

    shares = 2 if lax.axis_size("rep") == 2 and 27 * chans % 32 == 0 else 1
    rows = 27 * chans // shares
    tail, head, volume, block = call(
        front_stage,
        (
            bf16((3, 16, 16, 128)),
            bf16((3, 16, 16, 128)),
            bf16((4, 16, 16, 128)),
            bf16((rows, 256)),
        ),
        [pltpu.SemaphoreType.DMA],
        (
            lax.axis_index("rep").astype(jnp.int32).reshape(1),
            volume,
            decode_kernel.reshape(27 * chans, 256),
        ),
        3 * 10**9,
        16,
        scalars=1,
        far=1,
        far_outs=1,
    )
    decode_part = lax.all_gather(block, "z", axis=0)
    if shares == 2:
        decode_part = lax.all_gather(decode_part, "rep", axis=0)
    elif chans % 16:
        decode_part = decode_part.reshape(planes, 27, chans, 256).transpose(1, 0, 2, 3)
        decode_part = decode_part.reshape(1, 1, 27 * 128, 256)
    else:
        decode_part = decode_part[None]

    forward = [(i, i + 1) for i in range(n - 1)]
    backward = [(target, source) for source, target in forward]
    low = lax.ppermute(tail, ALL, forward)
    high = lax.ppermute(head, ALL, backward)

    taps = first_kernel.reshape(3, 1152, 128)
    own = call(
        own_stage,
        jax.ShapeDtypeStruct((4, 256, 256), jnp.float32),
        [pltpu.VMEM((4, 18, 16, 384), jnp.bfloat16)],
        (volume, taps),
        2 * 1024 * 2304 * 256,
        24,
    )
    lane = np.arange(256)
    source = (lane // 64 + GROUP * (lane % 64 // chans)) * chans + lane % chans
    order = jnp.asarray(np.arange(256)[:, None] == source[None, :], jnp.bfloat16)
    ends = jnp.stack([place, n - 1 - place]).astype(jnp.int32)
    pooled_two, skips = call(
        stem_stage,
        (bf16((planes, 16, 256)), bf16((GROUP, 32, 256))),
        [
            pltpu.VMEM((6, 18, 16, 384), jnp.bfloat16),
            pltpu.VMEM((128, 128), jnp.float32),
            pltpu.VMEM((4, 10, 24, 128), jnp.float32),
            pltpu.VMEM((256, 1152), jnp.bfloat16),
            pltpu.VMEM((2, 32, 128), jnp.float32),
        ],
        (ends, low, high, own, taps, second_kernel.reshape(3, 1152, 256), order),
        2 * 1024 * 2304 * 256,
        24,
        scalars=1,
    )
    pooled_line = exchange(pooled_two, "z")
    relays = call(
        relay_stage, bf16((GROUP, 16 * planes + 32, 256)), [], (pooled_line, skips), 0, 16
    )
    near = exchange(relays, "r")

    deep, first, last = call(
        deep_stage,
        (bf16((n, chans, voxels)), bf16((16, 256)), bf16((16, 256))),
        [],
        (near, deep_kernel.transpose(0, 1, 2, 4, 3).reshape(27 * chans, 256)),
        2 * 27 * chans * 256 * voxels,
        16,
    )
    skip_low = lax.ppermute(last, "z", [(p, p + 1) for p in range(planes - 1)])
    skip_high = lax.ppermute(first, "z", [(p + 1, p) for p in range(planes - 1)])
    deep_whole = exchange(deep, ALL).reshape(n * chans, voxels)

    deeper = call(
        deeper_stage,
        bf16((n, chans, 128)),
        [],
        (
            deep_whole,
            deeper_kernel.transpose(0, 1, 2, 4, 3).reshape(27 * chans, n * chans),
            skip_low,
            skip_high,
        ),
        2 * 27 * chans * n * chans * voxels,
        16,
        far=2,
    )
    deeper_near = exchange(deeper, ALL).reshape(n * chans, 128)

    rise_part, decode_part = call(
        lambda rank_ref, *refs: rise_stage(rank_ref, chans, *refs),
        (bf16((n * chans, 512)), bf16(decode_part.shape)),
        [pltpu.SemaphoreType.DMA],
        (rank.astype(jnp.int32).reshape(1), rise_kernel.reshape(8, n * chans, 256), decode_part),
        2 * 8 * n * chans * 256 * 64,
        16,
        scalars=1,
        far=1,
    )
    partial = call(
        decode_stage,
        bf16((512, 256)),
        [
            pltpu.VMEM((10, 10, 24, 128), jnp.float32),
            pltpu.VMEM((640, 1152), jnp.bfloat16),
            pltpu.VMEM((8, 128, 128), jnp.float32),
        ],
        (deeper_near, rise_part, near, skip_low, skip_high, decode_part),
        2 * 512 * 3456 * 256,
        24,
    )
    partials = exchange(partial.reshape(GROUP, 128, 256), "r")
    out = call(
        final_stage,
        bf16((1024, 128)),
        [pltpu.VMEM((1024, 128), jnp.float32)],
        (partials, final_kernel.reshape(8, 256, 128)),
        2 * 128 * 256 * 1024,
        16,
    )
    return out.reshape(4, 16, 16, 128)


def solution(mesh):
    reps, n = mesh.devices.shape
    grid = jax.sharding.Mesh(mesh.devices.reshape(reps, n // GROUP, GROUP), ("rep",) + ALL)
    return jax.shard_map(
        body,
        mesh=grid,
        in_specs=(
            P(("rep",) + ALL, None, None, None),
            P(),
            P(),
            P(None, None, None, None, ALL),
            P(None, None, None, None, ALL),
            P(),
            P(None, None, None, ALL, None),
            P(),
        ),
        out_specs=P(("rep",) + ALL, None, None, None),
        check_vma=False,
    )
```

```python
import functools

import jax
import jax.numpy as jnp
import numpy as np
from jax import lax
from jax.experimental import pallas as pl
from jax.experimental.pallas import tpu as pltpu
from jax.sharding import PartitionSpec as P

GROUP = 4
MIB = 1024 * 1024


def call(kernel, outs, scratch, args, flops, vmem_mib, scalars=0, unread=0):
    spaces = [pltpu.SMEM] * scalars + [pltpu.VMEM] * (len(args) - scalars - unread)
    spaces += [pl.ANY] * unread
    return pl.pallas_call(
        kernel,
        out_shape=outs,
        in_specs=[pl.BlockSpec(memory_space=space) for space in spaces],
        out_specs=jax.tree.map(lambda _: pl.BlockSpec(memory_space=pltpu.VMEM), outs),
        scratch_shapes=scratch,
        compiler_params=pltpu.CompilerParams(vmem_limit_bytes=vmem_mib * MIB),
        cost_estimate=pl.CostEstimate(
            flops=flops,
            bytes_accessed=sum(a.size * a.dtype.itemsize for a in args[: len(args) - unread]),
            transcendentals=0,
        ),
    )(*args)


def dot(left, right, dims=((1,), (0,))):
    return lax.dot_general(left, right, (dims, ((), ())), preferred_element_type=jnp.float32)


def round_once(values):
    return values.astype(jnp.bfloat16).astype(jnp.float32)


def fill_patches(framed, patches, slices):
    for b in range(3):
        for c in range(3):
            tap = framed[:, b : b + 8, 7 + c : 15 + c, :].reshape(slices * 64, 128)
            col = (b * 3 + c) * 128
            patches[:, col : col + 128] = tap.astype(jnp.bfloat16)


def shift_slice(shifted, s, values):
    row = lax.broadcasted_iota(jnp.int32, (256, 128), 0) & 15
    here = values.reshape(256, 128).astype(jnp.float32)
    before = jnp.where(row == 0, 0.0, pltpu.roll(here, 1, 0))
    after = jnp.where(row == 15, 0.0, pltpu.roll(here, 255, 0))
    shifted[s, 0] = jnp.zeros((16, 384), jnp.bfloat16)
    shifted[s, 17] = jnp.zeros((16, 384), jnp.bfloat16)
    for c, tap in enumerate((before, here, after)):
        tap = tap.astype(jnp.bfloat16).reshape(16, 16, 128)
        shifted[s, 1:17, :, 128 * c : 128 * c + 128] = tap


def depth_pair(shifted, slices, weights, steps):
    left = jnp.concatenate(
        [shifted[s, b : b + 16].reshape(256, 384) for s in slices for b in range(3)], axis=1
    )
    none = jnp.zeros((1152, 128), jnp.bfloat16)
    right = [
        jnp.concatenate(
            [weights[j] if j < 3 else none, weights[j - 1] if j > 0 else none], axis=1
        )
        for j in steps
    ]
    return dot(left, jnp.concatenate(right, axis=0))


def depth_one(shifted, s, weights):
    left = jnp.concatenate([shifted[s, b : b + 16].reshape(256, 384) for b in range(3)], axis=1)
    return dot(left, weights)


def front_stage(odd, volume, off_chip, on_chip, whole):
    for s in range(3):
        off_chip[s] = jnp.where(odd[0] == 0, volume[s], volume[s + 1])
        on_chip[s] = jnp.where(odd[0] == 0, volume[s + 1], volume[s])
    whole[...] = volume[...]


def own_stage(volume, weights, out, shifted):
    for s in range(4):
        shift_slice(shifted, s, volume[s])
    out[0, :, :128] = jnp.zeros((256, 128), jnp.float32)
    out[0, :, 128:] = depth_one(shifted, 0, weights[2])
    out[1] = depth_pair(shifted, (0, 1, 2), weights, (1, 2, 3))
    out[2] = depth_pair(shifted, (1, 2, 3), weights, (0, 1, 2))
    out[3, :, :128] = depth_one(shifted, 3, weights[0])
    out[3, :, 128:] = jnp.zeros((256, 128), jnp.float32)


def stem_stage(
    ends, off_chip, on_chip, own, weights, second, order,
    pooled_out, skip_out,
    shifted, halves, framed, patches, quarters,
):
    for s in range(3):
        even = ends[2] == 0
        shift_slice(shifted, s, jnp.where(even, off_chip[s], on_chip[s]))
        shift_slice(shifted, 3 + s, jnp.where(even, on_chip[s], off_chip[s]))
    framed[...] = jnp.zeros(framed.shape, jnp.float32)
    for m in range(4):
        if m == 0:
            first = own[0] + depth_pair(shifted, (0, 1, 2), weights, (0, 1, 2))
        elif m == 3:
            first = own[3] + depth_pair(shifted, (3, 4, 5), weights, (1, 2, 3))
        elif m == 1:
            near = own[1, :, :128] + depth_one(shifted, 2, weights[0])
            first = jnp.concatenate([near, own[1, :, 128:]], axis=1)
        else:
            far = own[2, :, 128:] + depth_one(shifted, 3, weights[2])
            first = jnp.concatenate([own[2, :, :128], far], axis=1)
        first = round_once(jnp.maximum(first, 0.0))
        pair = (first[:, :128] + first[:, 128:]).reshape(8, 32, 128)
        halves[...] = (pair[:, :16] + pair[:, 16:]).reshape(128, 128)
        pooled = halves[pl.ds(0, 64, stride=2), :] + halves[pl.ds(1, 64, stride=2), :]
        pooled = round_once(pooled * 0.125)
        if m == 0:
            pooled = jnp.where(ends[0] == 0, 0.0, pooled)
        if m == 3:
            pooled = jnp.where(ends[1] == 0, 0.0, pooled)
        framed[m, 1:9, 8:16, :] = pooled.reshape(8, 8, 128)
    fill_patches(framed, patches, 4)
    skip = dot(patches[0:128], second[0])
    skip += dot(patches[64:192], second[1])
    skip += dot(patches[128:256], second[2])
    skip = jnp.maximum(skip, 0.0).astype(jnp.bfloat16)
    wide = skip.astype(jnp.float32)
    pair = (wide[:64] + wide[64:]).reshape(4, 16, 256)
    pair = (pair[:, :8] + pair[:, 8:]).reshape(32, 256)
    for k in range(2):
        quarters[k] = pair[:, 128 * k : 128 * k + 128]
    pooled = jnp.concatenate(
        [
            quarters[k, pl.ds(0, 16, stride=2), :] + quarters[k, pl.ds(1, 16, stride=2), :]
            for k in range(2)
        ],
        axis=1,
    )
    pooled = (pooled * 0.125).astype(jnp.bfloat16)
    for p in range(pooled_out.shape[0]):
        pooled_out[p] = pooled
    sorted_skip = dot(skip, order[...])
    for r in range(GROUP):
        near, far = sorted_skip[:64, 64 * r : 64 * r + 64], sorted_skip[64:, 64 * r : 64 * r + 64]
        block = jnp.concatenate([near, far], axis=1)
        block = jnp.concatenate([block[:32], block[32:]], axis=1).astype(jnp.bfloat16)
        skip_out[r] = block


def relay_stage(pooled, skips, out):
    planes = pooled.shape[0]
    for r in range(GROUP):
        for p in range(planes):
            out[r, 16 * p : 16 * p + 16, :] = pooled[p]
        out[r, 16 * planes :, :] = skips[r]


def edge_slice(block, far):
    lower = lax.broadcasted_iota(jnp.int32, (16, 128), 1) < 64
    sides = []
    for k in range(2):
        half = block[:, 128 * k : 128 * k + 128].astype(jnp.float32)
        top, bottom = half[:16], half[16:]
        if far:
            top = pltpu.roll(top, 64, 1)
        else:
            bottom = pltpu.roll(bottom, 64, 1)
        sides.append(jnp.where(lower, top, bottom))
    return jnp.concatenate(sides, axis=1).astype(jnp.bfloat16)


def spread_taps(weights, values, dims, chans, voxels):
    lane = lax.broadcasted_iota(jnp.int32, (chans, voxels), 1)

    def moved(term, tap, step, place, last):
        if tap == 1:
            return term
        keep = place > 0 if tap == 0 else place < last
        return jnp.where(keep, pltpu.roll(term, ((1 - tap) * step) % voxels, 1), 0.0)

    total = None
    for a in range(3):
        products = dot(weights[a * 9 * chans : (a + 1) * 9 * chans, :], values, dims)
        plane = None
        for b in range(3):
            line = None
            for c in range(3):
                at = (b * 3 + c) * chans
                term = moved(products[at : at + chans], c, 1, lane & 3, 3)
                line = term if line is None else line + term
            line = moved(line, b, 4, (lane >> 2) & 3, 3)
            plane = line if plane is None else plane + line
        plane = moved(plane, a, 16, lane >> 4, voxels // 16 - 1)
        total = plane if total is None else total + plane
    return jnp.maximum(total, 0.0)


def deep_stage(near, weights, out, first, last):
    chans, voxels = out.shape
    n = voxels // 16
    values = [near[r, 16 * p : 16 * p + 16, :] for p in range(n // GROUP) for r in range(GROUP)]
    values = jnp.concatenate(values, axis=0)
    deep = spread_taps(weights, values, ((1,), (1,)), chans, voxels).astype(jnp.bfloat16)
    out[...] = deep
    first[...] = edge_slice(near[0, voxels // GROUP :, :], False)
    last[...] = edge_slice(near[GROUP - 1, voxels // GROUP :, :], True)


def deeper_stage(deep, weights, _, __, out):
    n, chans, _ = out.shape
    voxels = deep.shape[1]
    deeper = spread_taps(weights, deep[...], ((1,), (0,)), chans, voxels)
    lane = lax.broadcasted_iota(jnp.int32, (chans, 128), 1)
    planes = n // GROUP
    for p in range(planes):
        part = pltpu.roll(deeper, (16 - 64 * p) % voxels, 1)[:, :128]
        if p == 0:
            part = jnp.where(lane < 16, 0.0, part)
        if p == planes - 1:
            part = jnp.where(lane >= 80, 0.0, part)
        part = part.astype(jnp.bfloat16)
        for r in range(GROUP):
            out[GROUP * p + r] = part


def rise_stage(rank, chans, rise, out):
    lane = lax.broadcasted_iota(jnp.int32, (256, 64), 1)
    row = lax.broadcasted_iota(jnp.int32, (256, 64), 0)
    source = (rank[0] + GROUP * (lane // chans)) * chans + lane % chans
    mine = jnp.where(row == source, 1.0, 0.0).astype(jnp.bfloat16)
    for pair in range(4):
        both = [dot(rise[2 * pair + k], mine) for k in range(2)]
        both = jnp.concatenate(both, axis=1).astype(jnp.bfloat16)
        out[:, 128 * pair : 128 * pair + 128] = both


def decode_stage(
    deeper, rise, near, low, high, decode, out, framed, patches, risen
):
    framed[...] = jnp.zeros(framed.shape, jnp.float32)
    spread = round_once(dot(deeper[...].astype(jnp.float32).T.astype(jnp.bfloat16), rise[...]))
    for pair in range(4):
        both = spread[:, 128 * pair : 128 * pair + 128]
        risen[2 * pair] = both
        risen[2 * pair + 1] = pltpu.roll(both, 64, 1)
    upper = lax.broadcasted_iota(jnp.int32, (64, 128), 1) >= 64
    for s in range(10):
        d, a = (s + 1) // 2, (s + 1) % 2
        for h in range(4):
            for b in range(2):
                for c in range(2):
                    framed[s, 1 + 2 * h + b, pl.ds(8 + c, 4, stride=2), :] = risen[
                        4 * a + 2 * b + c, 16 * d + 4 * h : 16 * d + 4 * h + 4, :
                    ]
        if s == 0 or s == 9:
            edge = (low if s == 0 else high)[...].astype(jnp.float32)
            parts = []
            for k in range(2):
                half = edge[:, 128 * k : 128 * k + 128]
                parts += [pltpu.roll(half, 64, 1), half]
            skip = jnp.concatenate(parts, axis=0)
        else:
            both = near[(s - 1) // 2, near.shape[1] - 32 :, :].astype(jnp.float32)
            skip = jnp.concatenate([both[:, :128], both[:, 128:]], axis=0)
            if (s - 1) % 2 == 0:
                skip = pltpu.roll(skip, 64, 1)
        joined = framed[s, 1:9, 8:16, :].reshape(64, 128)
        framed[s, 1:9, 8:16, :] = jnp.where(upper, skip, joined).reshape(8, 8, 128)
    fill_patches(framed, patches, 10)
    blocks = decode.shape[0]
    step = 128 // blocks
    partial = None
    for a in range(3):
        right = [
            decode[z, tap * step : (tap + 1) * step, :]
            for tap in range(9 * a, 9 * a + 9)
            for z in range(blocks)
        ]
        term = dot(patches[64 * a : 64 * a + 512], jnp.concatenate(right, axis=0))
        partial = term if partial is None else partial + term
    out[...] = partial.astype(jnp.bfloat16)


def final_stage(partials, weights, out, spaced):
    decoded = partials[0].astype(jnp.float32)
    for g in range(1, GROUP):
        decoded += partials[g].astype(jnp.float32)
    decoded = jnp.maximum(decoded, 0.0).astype(jnp.bfloat16)
    for a in range(2):
        for b in range(2):
            for c in range(2):
                values = dot(decoded, weights[4 * a + 2 * b + c])
                for d in range(2):
                    for h in range(8):
                        at = ((2 * d + a) * 16 + 2 * h + b) * 16 + c
                        spaced[pl.ds(at, 8, stride=2), :] = values[64 * d + 8 * h : 64 * d + 8 * h + 8]
    out[...] = spaced[...].astype(jnp.bfloat16)


ALL = ("z", "r")


def exchange(payload, axis):
    return lax.all_to_all(payload, axis, split_axis=0, concat_axis=0, tiled=True)


def body(
    volume,
    first_kernel,
    second_kernel,
    deep_kernel,
    deeper_kernel,
    rise_kernel,
    decode_kernel,
    final_kernel,
):
    n = lax.axis_size(ALL)
    place = lax.axis_index(ALL)
    planes = n // GROUP
    rank = lax.axis_index("r")
    chans = deep_kernel.shape[4]
    voxels = 16 * n
    bf16 = functools.partial(jax.ShapeDtypeStruct, dtype=jnp.bfloat16)

    decode_part = lax.all_gather(decode_kernel.reshape(27 * chans, 256), "z", axis=0)
    if chans % 16:
        decode_part = decode_part.reshape(planes, 27, chans, 256).transpose(1, 0, 2, 3)
        decode_part = decode_part.reshape(1, 27 * 128, 256)

    odd = (place % 2).astype(jnp.int32)
    off_chip, on_chip, volume = call(
        front_stage,
        (bf16((3, 16, 16, 128)), bf16((3, 16, 16, 128)), bf16((4, 16, 16, 128))),
        [],
        (odd.reshape(1), volume),
        3 * 10**9,
        16,
        scalars=1,
    )
    pairs = [(i, i + 1) for i in range(1, n - 1, 2)]
    off_chip = lax.ppermute(off_chip, ALL, pairs + [(j, i) for i, j in pairs])
    on_chip = lax.ppermute(on_chip, ALL, [(i, i ^ 1) for i in range(n)])

    taps = first_kernel.reshape(3, 1152, 128)
    own = call(
        own_stage,
        jax.ShapeDtypeStruct((4, 256, 256), jnp.float32),
        [pltpu.VMEM((4, 18, 16, 384), jnp.bfloat16)],
        (volume, taps),
        2 * 1024 * 2304 * 256,
        24,
    )
    lane = np.arange(256)
    source = (lane // 64 + GROUP * (lane % 64 // chans)) * chans + lane % chans
    order = jnp.asarray(np.arange(256)[:, None] == source[None, :], jnp.bfloat16)
    ends = jnp.stack([place, n - 1 - place, odd]).astype(jnp.int32)
    pooled_two, skips = call(
        stem_stage,
        (bf16((planes, 16, 256)), bf16((GROUP, 32, 256))),
        [
            pltpu.VMEM((6, 18, 16, 384), jnp.bfloat16),
            pltpu.VMEM((128, 128), jnp.float32),
            pltpu.VMEM((4, 10, 24, 128), jnp.float32),
            pltpu.VMEM((256, 1152), jnp.bfloat16),
            pltpu.VMEM((2, 32, 128), jnp.float32),
        ],
        (ends, off_chip, on_chip, own, taps, second_kernel.reshape(3, 1152, 256), order),
        2 * 1024 * 2304 * 256,
        24,
        scalars=1,
    )
    pooled_line = exchange(pooled_two, "z")
    relays = call(
        relay_stage, bf16((GROUP, 16 * planes + 32, 256)), [], (pooled_line, skips), 0, 16
    )
    near = exchange(relays, "r")

    deep, first, last = call(
        deep_stage,
        (bf16((chans, voxels)), bf16((16, 256)), bf16((16, 256))),
        [],
        (near, deep_kernel.transpose(0, 1, 2, 4, 3).reshape(27 * chans, 256)),
        2 * 27 * chans * 256 * voxels,
        16,
    )
    skip_low = lax.ppermute(last, "z", [(p, p + 1) for p in range(planes - 1)])
    skip_high = lax.ppermute(first, "z", [(p + 1, p) for p in range(planes - 1)])
    deep_whole = lax.all_gather(deep, ALL, axis=0).reshape(n * chans, voxels)

    deeper = call(
        deeper_stage,
        bf16((n, chans, 128)),
        [],
        (
            deep_whole,
            deeper_kernel.transpose(0, 1, 2, 4, 3).reshape(27 * chans, n * chans),
            skip_low,
            skip_high,
        ),
        2 * 27 * chans * n * chans * voxels,
        16,
        unread=2,
    )
    deeper_near = exchange(deeper, ALL).reshape(n * chans, 128)

    rise_part = call(
        lambda rank_ref, *refs: rise_stage(rank_ref, chans, *refs),
        bf16((n * chans, 512)),
        [],
        (rank.astype(jnp.int32).reshape(1), rise_kernel.reshape(8, n * chans, 256)),
        2 * 8 * n * chans * 256 * 64,
        16,
        scalars=1,
    )
    partial = call(
        decode_stage,
        bf16((512, 256)),
        [
            pltpu.VMEM((10, 10, 24, 128), jnp.float32),
            pltpu.VMEM((640, 1152), jnp.bfloat16),
            pltpu.VMEM((8, 128, 128), jnp.float32),
        ],
        (deeper_near, rise_part, near, skip_low, skip_high, decode_part),
        2 * 512 * 3456 * 256,
        24,
    )
    partials = exchange(partial.reshape(GROUP, 128, 256), "r")
    out = call(
        final_stage,
        bf16((1024, 128)),
        [pltpu.VMEM((1024, 128), jnp.float32)],
        (partials, final_kernel.reshape(8, 256, 128)),
        2 * 128 * 256 * 1024,
        16,
    )
    return out.reshape(4, 16, 16, 128)


def solution(mesh):
    reps, n = mesh.devices.shape
    grid = jax.sharding.Mesh(mesh.devices.reshape(reps, n // GROUP, GROUP), ("rep",) + ALL)
    return jax.shard_map(
        body,
        mesh=grid,
        in_specs=(
            P(("rep",) + ALL, None, None, None),
            P(),
            P(),
            P(None, None, None, None, ALL),
            P(None, None, None, None, ALL),
            P(),
            P(None, None, None, ALL, None),
            P(),
        ),
        out_specs=P(("rep",) + ALL, None, None, None),
        check_vma=False,
    )
```

```python
import functools

import jax
import jax.numpy as jnp
import numpy as np
from jax import lax
from jax.experimental import pallas as pl
from jax.experimental.pallas import tpu as pltpu
from jax.sharding import PartitionSpec as P

GROUP = 4
MIB = 1024 * 1024


def call(kernel, outs, scratch, args, flops, vmem_mib, scalars=0, unread=0):
    spaces = [pltpu.SMEM] * scalars + [pltpu.VMEM] * (len(args) - scalars - unread)
    spaces += [pl.ANY] * unread
    return pl.pallas_call(
        kernel,
        out_shape=outs,
        in_specs=[pl.BlockSpec(memory_space=space) for space in spaces],
        out_specs=jax.tree.map(lambda _: pl.BlockSpec(memory_space=pltpu.VMEM), outs),
        scratch_shapes=scratch,
        compiler_params=pltpu.CompilerParams(vmem_limit_bytes=vmem_mib * MIB),
        cost_estimate=pl.CostEstimate(
            flops=flops,
            bytes_accessed=sum(a.size * a.dtype.itemsize for a in args[: len(args) - unread]),
            transcendentals=0,
        ),
    )(*args)


def dot(left, right, dims=((1,), (0,))):
    return lax.dot_general(left, right, (dims, ((), ())), preferred_element_type=jnp.float32)


def round_once(values):
    return values.astype(jnp.bfloat16).astype(jnp.float32)


def fill_patches(framed, patches, slices):
    for b in range(3):
        for c in range(3):
            tap = framed[:, b : b + 8, 7 + c : 15 + c, :].reshape(slices * 64, 128)
            col = (b * 3 + c) * 128
            patches[:, col : col + 128] = tap.astype(jnp.bfloat16)


def shift_slice(shifted, s, values):
    row = lax.broadcasted_iota(jnp.int32, (256, 128), 0) & 15
    here = values.reshape(256, 128).astype(jnp.float32)
    before = jnp.where(row == 0, 0.0, pltpu.roll(here, 1, 0))
    after = jnp.where(row == 15, 0.0, pltpu.roll(here, 255, 0))
    shifted[s, 0] = jnp.zeros((16, 384), jnp.bfloat16)
    shifted[s, 17] = jnp.zeros((16, 384), jnp.bfloat16)
    for c, tap in enumerate((before, here, after)):
        tap = tap.astype(jnp.bfloat16).reshape(16, 16, 128)
        shifted[s, 1:17, :, 128 * c : 128 * c + 128] = tap


def depth_pair(shifted, slices, weights, steps):
    left = jnp.concatenate(
        [shifted[s, b : b + 16].reshape(256, 384) for s in slices for b in range(3)], axis=1
    )
    none = jnp.zeros((1152, 128), jnp.bfloat16)
    right = [
        jnp.concatenate(
            [weights[j] if j < 3 else none, weights[j - 1] if j > 0 else none], axis=1
        )
        for j in steps
    ]
    return dot(left, jnp.concatenate(right, axis=0))


def depth_one(shifted, s, weights):
    left = jnp.concatenate([shifted[s, b : b + 16].reshape(256, 384) for b in range(3)], axis=1)
    return dot(left, weights)


def front_stage(odd, volume, off_chip, on_chip, whole):
    for s in range(3):
        off_chip[s] = jnp.where(odd[0] == 0, volume[s], volume[s + 1])
        on_chip[s] = jnp.where(odd[0] == 0, volume[s + 1], volume[s])
    whole[...] = volume[...]


def own_stage(volume, weights, out, shifted):
    for s in range(4):
        shift_slice(shifted, s, volume[s])
    out[0, :, :128] = jnp.zeros((256, 128), jnp.float32)
    out[0, :, 128:] = depth_one(shifted, 0, weights[2])
    out[1] = depth_pair(shifted, (0, 1, 2), weights, (1, 2, 3))
    out[2] = depth_pair(shifted, (1, 2, 3), weights, (0, 1, 2))
    out[3, :, :128] = depth_one(shifted, 3, weights[0])
    out[3, :, 128:] = jnp.zeros((256, 128), jnp.float32)


def stem_stage(ends, off_chip, on_chip, own, weights, second, order, *refs):
    pooled_out, skip_outs = refs[0], refs[1 : 1 + GROUP]
    shifted, halves, framed, patches, quarters, blocks = refs[1 + GROUP :]
    for s in range(3):
        even = ends[2] == 0
        shift_slice(shifted, s, jnp.where(even, off_chip[s], on_chip[s]))
        shift_slice(shifted, 3 + s, jnp.where(even, on_chip[s], off_chip[s]))
    framed[...] = jnp.zeros(framed.shape, jnp.float32)
    for m in range(4):
        if m == 0:
            first = own[0] + depth_pair(shifted, (0, 1, 2), weights, (0, 1, 2))
        elif m == 3:
            first = own[3] + depth_pair(shifted, (3, 4, 5), weights, (1, 2, 3))
        elif m == 1:
            near = own[1, :, :128] + depth_one(shifted, 2, weights[0])
            first = jnp.concatenate([near, own[1, :, 128:]], axis=1)
        else:
            far = own[2, :, 128:] + depth_one(shifted, 3, weights[2])
            first = jnp.concatenate([own[2, :, :128], far], axis=1)
        first = round_once(jnp.maximum(first, 0.0))
        pair = (first[:, :128] + first[:, 128:]).reshape(8, 32, 128)
        halves[...] = (pair[:, :16] + pair[:, 16:]).reshape(128, 128)
        pooled = halves[pl.ds(0, 64, stride=2), :] + halves[pl.ds(1, 64, stride=2), :]
        pooled = round_once(pooled * 0.125)
        if m == 0:
            pooled = jnp.where(ends[0] == 0, 0.0, pooled)
        if m == 3:
            pooled = jnp.where(ends[1] == 0, 0.0, pooled)
        framed[m, 1:9, 8:16, :] = pooled.reshape(8, 8, 128)
    fill_patches(framed, patches, 4)
    skip = dot(patches[0:128], second[0])
    skip += dot(patches[64:192], second[1])
    skip += dot(patches[128:256], second[2])
    skip = jnp.maximum(skip, 0.0).astype(jnp.bfloat16)
    wide = skip.astype(jnp.float32)
    pair = (wide[:64] + wide[64:]).reshape(4, 16, 256)
    pair = (pair[:, :8] + pair[:, 8:]).reshape(32, 256)
    for k in range(2):
        quarters[k] = pair[:, 128 * k : 128 * k + 128]
    pooled = jnp.concatenate(
        [
            quarters[k, pl.ds(0, 16, stride=2), :] + quarters[k, pl.ds(1, 16, stride=2), :]
            for k in range(2)
        ],
        axis=1,
    )
    pooled = (pooled * 0.125).astype(jnp.bfloat16)
    for p in range(pooled_out.shape[0]):
        pooled_out[p] = pooled
    sorted_skip = dot(skip, order[...])
    for r in range(GROUP):
        near, far = sorted_skip[:64, 64 * r : 64 * r + 64], sorted_skip[64:, 64 * r : 64 * r + 64]
        block = jnp.concatenate([near, far], axis=1)
        block = jnp.concatenate([block[:32], block[32:]], axis=1).astype(jnp.bfloat16)
        blocks[r] = block
    for k in range(GROUP):
        skip_outs[k][...] = blocks[ends[3] ^ k]


def edge_slice(block, far):
    lower = lax.broadcasted_iota(jnp.int32, (16, 128), 1) < 64
    sides = []
    for k in range(2):
        half = block[:, 128 * k : 128 * k + 128].astype(jnp.float32)
        top, bottom = half[:16], half[16:]
        if far:
            top = pltpu.roll(top, 64, 1)
        else:
            bottom = pltpu.roll(bottom, 64, 1)
        sides.append(jnp.where(lower, top, bottom))
    return jnp.concatenate(sides, axis=1).astype(jnp.bfloat16)


def spread_taps(weights, values, dims, chans, voxels):
    lane = lax.broadcasted_iota(jnp.int32, (chans, voxels), 1)

    def moved(term, tap, step, place, last):
        if tap == 1:
            return term
        keep = place > 0 if tap == 0 else place < last
        return jnp.where(keep, pltpu.roll(term, ((1 - tap) * step) % voxels, 1), 0.0)

    total = None
    for a in range(3):
        products = dot(weights[a * 9 * chans : (a + 1) * 9 * chans, :], values, dims)
        plane = None
        for b in range(3):
            line = None
            for c in range(3):
                at = (b * 3 + c) * chans
                term = moved(products[at : at + chans], c, 1, lane & 3, 3)
                line = term if line is None else line + term
            line = moved(line, b, 4, (lane >> 2) & 3, 3)
            plane = line if plane is None else plane + line
        plane = moved(plane, a, 16, lane >> 4, voxels // 16 - 1)
        total = plane if total is None else total + plane
    return jnp.maximum(total, 0.0)


def by_rank(rank, near, blocks):
    for k in range(GROUP):
        blocks[rank[0] ^ k] = near[k][...]


def edge_stage(rank, *refs):
    near, (first, last, blocks) = refs[:GROUP], refs[GROUP:]
    by_rank(rank, near, blocks)
    first[...] = edge_slice(blocks[0], False)
    last[...] = edge_slice(blocks[GROUP - 1], True)


def deep_stage(pooled, weights, out):
    n, chans, voxels = out.shape
    deep = spread_taps(weights, pooled[...], ((1,), (1,)), chans, voxels).astype(jnp.bfloat16)
    for dest in range(n):
        out[dest] = deep


def deeper_stage(deep, weights, *refs):
    out = refs[-1]
    n, chans, _ = out.shape
    voxels = deep.shape[1]
    deeper = spread_taps(weights, deep[...], ((1,), (0,)), chans, voxels)
    lane = lax.broadcasted_iota(jnp.int32, (chans, 128), 1)
    planes = n // GROUP
    for p in range(planes):
        part = pltpu.roll(deeper, (16 - 64 * p) % voxels, 1)[:, :128]
        if p == 0:
            part = jnp.where(lane < 16, 0.0, part)
        if p == planes - 1:
            part = jnp.where(lane >= 80, 0.0, part)
        part = part.astype(jnp.bfloat16)
        for r in range(GROUP):
            out[GROUP * p + r] = part


def rise_stage(rank, chans, rise, out):
    lane = lax.broadcasted_iota(jnp.int32, (256, 64), 1)
    row = lax.broadcasted_iota(jnp.int32, (256, 64), 0)
    source = (rank[0] + GROUP * (lane // chans)) * chans + lane % chans
    mine = jnp.where(row == source, 1.0, 0.0).astype(jnp.bfloat16)
    for pair in range(4):
        both = [dot(rise[2 * pair + k], mine) for k in range(2)]
        both = jnp.concatenate(both, axis=1).astype(jnp.bfloat16)
        out[:, 128 * pair : 128 * pair + 128] = both


def decode_stage(rank, deeper, rise, low, high, decode, *refs):
    near, (out, framed, patches, risen, blocks) = refs[:GROUP], refs[GROUP:]
    by_rank(rank, near, blocks)
    framed[...] = jnp.zeros(framed.shape, jnp.float32)
    spread = round_once(dot(deeper[...].astype(jnp.float32).T.astype(jnp.bfloat16), rise[...]))
    for pair in range(4):
        both = spread[:, 128 * pair : 128 * pair + 128]
        risen[2 * pair] = both
        risen[2 * pair + 1] = pltpu.roll(both, 64, 1)
    upper = lax.broadcasted_iota(jnp.int32, (64, 128), 1) >= 64
    for s in range(10):
        d, a = (s + 1) // 2, (s + 1) % 2
        for h in range(4):
            for b in range(2):
                for c in range(2):
                    framed[s, 1 + 2 * h + b, pl.ds(8 + c, 4, stride=2), :] = risen[
                        4 * a + 2 * b + c, 16 * d + 4 * h : 16 * d + 4 * h + 4, :
                    ]
        if s == 0 or s == 9:
            edge = (low if s == 0 else high)[...].astype(jnp.float32)
            parts = []
            for k in range(2):
                half = edge[:, 128 * k : 128 * k + 128]
                parts += [pltpu.roll(half, 64, 1), half]
            skip = jnp.concatenate(parts, axis=0)
        else:
            both = blocks[(s - 1) // 2].astype(jnp.float32)
            skip = jnp.concatenate([both[:, :128], both[:, 128:]], axis=0)
            if (s - 1) % 2 == 0:
                skip = pltpu.roll(skip, 64, 1)
        joined = framed[s, 1:9, 8:16, :].reshape(64, 128)
        framed[s, 1:9, 8:16, :] = jnp.where(upper, skip, joined).reshape(8, 8, 128)
    fill_patches(framed, patches, 10)
    blocks = decode.shape[0]
    step = 128 // blocks
    partial = None
    for a in range(3):
        right = [
            decode[z, tap * step : (tap + 1) * step, :]
            for tap in range(9 * a, 9 * a + 9)
            for z in range(blocks)
        ]
        term = dot(patches[64 * a : 64 * a + 512], jnp.concatenate(right, axis=0))
        partial = term if partial is None else partial + term
    out[...] = partial.astype(jnp.bfloat16)


def final_stage(partials, weights, out, spaced):
    decoded = partials[0].astype(jnp.float32)
    for g in range(1, GROUP):
        decoded += partials[g].astype(jnp.float32)
    decoded = jnp.maximum(decoded, 0.0).astype(jnp.bfloat16)
    for a in range(2):
        for b in range(2):
            for c in range(2):
                values = dot(decoded, weights[4 * a + 2 * b + c])
                for d in range(2):
                    for h in range(8):
                        at = ((2 * d + a) * 16 + 2 * h + b) * 16 + c
                        spaced[pl.ds(at, 8, stride=2), :] = values[64 * d + 8 * h : 64 * d + 8 * h + 8]
    out[...] = spaced[...].astype(jnp.bfloat16)


ALL = ("z", "r")


def exchange(payload, axis):
    return lax.all_to_all(payload, axis, split_axis=0, concat_axis=0, tiled=True)


def body(
    volume,
    first_kernel,
    second_kernel,
    deep_kernel,
    deeper_kernel,
    rise_kernel,
    decode_kernel,
    final_kernel,
):
    n = lax.axis_size(ALL)
    place = lax.axis_index(ALL)
    planes = n // GROUP
    rank = lax.axis_index("r")
    chans = deep_kernel.shape[4]
    voxels = 16 * n
    bf16 = functools.partial(jax.ShapeDtypeStruct, dtype=jnp.bfloat16)

    decode_part = lax.all_gather(decode_kernel.reshape(27 * chans, 256), "z", axis=0)
    if chans % 16:
        decode_part = decode_part.reshape(planes, 27, chans, 256).transpose(1, 0, 2, 3)
        decode_part = decode_part.reshape(1, 27 * 128, 256)

    odd = (place % 2).astype(jnp.int32)
    off_chip, on_chip, volume = call(
        front_stage,
        (bf16((3, 16, 16, 128)), bf16((3, 16, 16, 128)), bf16((4, 16, 16, 128))),
        [],
        (odd.reshape(1), volume),
        3 * 10**9,
        16,
        scalars=1,
    )
    pairs = [(i, i + 1) for i in range(1, n - 1, 2)]
    off_chip = lax.ppermute(off_chip, ALL, pairs + [(j, i) for i, j in pairs])
    on_chip = lax.ppermute(on_chip, ALL, [(i, i ^ 1) for i in range(n)])

    taps = first_kernel.reshape(3, 1152, 128)
    own = call(
        own_stage,
        jax.ShapeDtypeStruct((4, 256, 256), jnp.float32),
        [pltpu.VMEM((4, 18, 16, 384), jnp.bfloat16)],
        (volume, taps),
        2 * 1024 * 2304 * 256,
        24,
    )
    lane = np.arange(256)
    source = (lane // 64 + GROUP * (lane % 64 // chans)) * chans + lane % chans
    order = jnp.asarray(np.arange(256)[:, None] == source[None, :], jnp.bfloat16)
    ends = jnp.stack([place, n - 1 - place, odd, rank]).astype(jnp.int32)
    pooled_two, *skips = call(
        stem_stage,
        (bf16((n, 16, 256)),) + (bf16((32, 256)),) * GROUP,
        [
            pltpu.VMEM((6, 18, 16, 384), jnp.bfloat16),
            pltpu.VMEM((128, 128), jnp.float32),
            pltpu.VMEM((4, 10, 24, 128), jnp.float32),
            pltpu.VMEM((256, 1152), jnp.bfloat16),
            pltpu.VMEM((2, 32, 128), jnp.float32),
            pltpu.VMEM((GROUP, 32, 256), jnp.bfloat16),
        ],
        (ends, off_chip, on_chip, own, taps, second_kernel.reshape(3, 1152, 256), order),
        2 * 1024 * 2304 * 256,
        24,
        scalars=1,
    )
    pooled_whole = exchange(pooled_two, ALL)
    near = [skips[0]] + [
        lax.ppermute(skips[k], "r", [(r, r ^ k) for r in range(GROUP)]) for k in range(1, GROUP)
    ]
    rank_ref = rank.astype(jnp.int32).reshape(1)
    blocks = pltpu.VMEM((GROUP, 32, 256), jnp.bfloat16)

    deep = call(
        deep_stage,
        bf16((n, chans, voxels)),
        [],
        (
            pooled_whole.reshape(voxels, 256),
            deep_kernel.transpose(0, 1, 2, 4, 3).reshape(27 * chans, 256),
        ),
        2 * 27 * chans * 256 * voxels,
        16,
    )
    first, last = call(
        edge_stage,
        (bf16((16, 256)), bf16((16, 256))),
        [blocks],
        (rank_ref, *near),
        0,
        16,
        scalars=1,
    )
    skip_low = lax.ppermute(last, "z", [(p, p + 1) for p in range(planes - 1)])
    skip_high = lax.ppermute(first, "z", [(p + 1, p) for p in range(planes - 1)])
    rise_part = call(
        lambda rank_ref, *refs: rise_stage(rank_ref, chans, *refs),
        bf16((n * chans, 512)),
        [],
        (rank_ref, rise_kernel.reshape(8, n * chans, 256)),
        2 * 8 * n * chans * 256 * 64,
        16,
        scalars=1,
    )
    deep_whole = exchange(deep, ALL).reshape(n * chans, voxels)

    deeper = call(
        deeper_stage,
        bf16((n, chans, 128)),
        [],
        (
            deep_whole,
            deeper_kernel.transpose(0, 1, 2, 4, 3).reshape(27 * chans, n * chans),
            skip_low,
            skip_high,
            rise_part,
        ),
        2 * 27 * chans * n * chans * voxels,
        16,
        unread=3,
    )
    deeper_near = exchange(deeper, ALL).reshape(n * chans, 128)

    partial = call(
        decode_stage,
        bf16((512, 256)),
        [
            pltpu.VMEM((10, 10, 24, 128), jnp.float32),
            pltpu.VMEM((640, 1152), jnp.bfloat16),
            pltpu.VMEM((8, 128, 128), jnp.float32),
            blocks,
        ],
        (rank_ref, deeper_near, rise_part, skip_low, skip_high, decode_part, *near),
        2 * 512 * 3456 * 256,
        24,
        scalars=1,
    )
    partials = exchange(partial.reshape(GROUP, 128, 256), "r")
    out = call(
        final_stage,
        bf16((1024, 128)),
        [pltpu.VMEM((1024, 128), jnp.float32)],
        (partials, final_kernel.reshape(8, 256, 128)),
        2 * 128 * 256 * 1024,
        16,
    )
    return out.reshape(4, 16, 16, 128)


def solution(mesh):
    reps, n = mesh.devices.shape
    grid = jax.sharding.Mesh(mesh.devices.reshape(reps, n // GROUP, GROUP), ("rep",) + ALL)
    return jax.shard_map(
        body,
        mesh=grid,
        in_specs=(
            P(("rep",) + ALL, None, None, None),
            P(),
            P(),
            P(None, None, None, None, ALL),
            P(None, None, None, None, ALL),
            P(),
            P(None, None, None, ALL, None),
            P(),
        ),
        out_specs=P(("rep",) + ALL, None, None, None),
        check_vma=False,
    )
```

```python
import functools

import jax
import jax.numpy as jnp
import numpy as np
from jax import lax
from jax.experimental import pallas as pl
from jax.experimental.pallas import tpu as pltpu
from jax.sharding import PartitionSpec as P

GROUP = 4
MIB = 1024 * 1024


def call(kernel, outs, scratch, args, flops, vmem_mib, scalars=0, unread=0):
    spaces = [pltpu.SMEM] * scalars + [pltpu.VMEM] * (len(args) - scalars - unread)
    spaces += [pl.ANY] * unread
    return pl.pallas_call(
        kernel,
        out_shape=outs,
        in_specs=[pl.BlockSpec(memory_space=space) for space in spaces],
        out_specs=jax.tree.map(lambda _: pl.BlockSpec(memory_space=pltpu.VMEM), outs),
        scratch_shapes=scratch,
        compiler_params=pltpu.CompilerParams(vmem_limit_bytes=vmem_mib * MIB),
        cost_estimate=pl.CostEstimate(
            flops=flops,
            bytes_accessed=sum(a.size * a.dtype.itemsize for a in args[: len(args) - unread]),
            transcendentals=0,
        ),
    )(*args)


def dot(left, right, dims=((1,), (0,))):
    return lax.dot_general(left, right, (dims, ((), ())), preferred_element_type=jnp.float32)


def round_once(values):
    return values.astype(jnp.bfloat16).astype(jnp.float32)


def fill_patches(framed, patches, slices):
    for b in range(3):
        for c in range(3):
            tap = framed[:, b : b + 8, 7 + c : 15 + c, :].reshape(slices * 64, 128)
            col = (b * 3 + c) * 128
            patches[:, col : col + 128] = tap.astype(jnp.bfloat16)


def shift_slice(shifted, s, values):
    row = lax.broadcasted_iota(jnp.int32, (256, 128), 0) & 15
    here = values.reshape(256, 128).astype(jnp.float32)
    before = jnp.where(row == 0, 0.0, pltpu.roll(here, 1, 0))
    after = jnp.where(row == 15, 0.0, pltpu.roll(here, 255, 0))
    shifted[s, 0] = jnp.zeros((16, 384), jnp.bfloat16)
    shifted[s, 17] = jnp.zeros((16, 384), jnp.bfloat16)
    for c, tap in enumerate((before, here, after)):
        tap = tap.astype(jnp.bfloat16).reshape(16, 16, 128)
        shifted[s, 1:17, :, 128 * c : 128 * c + 128] = tap


def depth_pair(shifted, slices, weights, steps):
    left = jnp.concatenate(
        [shifted[s, b : b + 16].reshape(256, 384) for s in slices for b in range(3)], axis=1
    )
    none = jnp.zeros((1152, 128), jnp.bfloat16)
    right = [
        jnp.concatenate(
            [weights[j] if j < 3 else none, weights[j - 1] if j > 0 else none], axis=1
        )
        for j in steps
    ]
    return dot(left, jnp.concatenate(right, axis=0))


def depth_one(shifted, s, weights):
    left = jnp.concatenate([shifted[s, b : b + 16].reshape(256, 384) for b in range(3)], axis=1)
    return dot(left, weights)


def front_stage(odd, volume, off_chip, on_chip, whole):
    for s in range(3):
        off_chip[s] = jnp.where(odd[0] == 0, volume[s], volume[s + 1])
        on_chip[s] = jnp.where(odd[0] == 0, volume[s + 1], volume[s])
    whole[...] = volume[...]


def own_stage(volume, weights, out, shifted):
    for s in range(4):
        shift_slice(shifted, s, volume[s])
    out[0, :, :128] = jnp.zeros((256, 128), jnp.float32)
    out[0, :, 128:] = depth_one(shifted, 0, weights[2])
    out[1] = depth_pair(shifted, (0, 1, 2), weights, (1, 2, 3))
    out[2] = depth_pair(shifted, (1, 2, 3), weights, (0, 1, 2))
    out[3, :, :128] = depth_one(shifted, 3, weights[0])
    out[3, :, 128:] = jnp.zeros((256, 128), jnp.float32)


def stem_stage(ends, off_chip, on_chip, own, weights, second, order, *refs):
    pooled_out, skip_outs = refs[0], refs[1 : 1 + GROUP]
    shifted, halves, framed, patches, quarters, blocks = refs[1 + GROUP :]
    for s in range(3):
        even = ends[2] == 0
        shift_slice(shifted, s, jnp.where(even, off_chip[s], on_chip[s]))
        shift_slice(shifted, 3 + s, jnp.where(even, on_chip[s], off_chip[s]))
    framed[...] = jnp.zeros(framed.shape, jnp.float32)
    for m in range(4):
        if m == 0:
            first = own[0] + depth_pair(shifted, (0, 1, 2), weights, (0, 1, 2))
        elif m == 3:
            first = own[3] + depth_pair(shifted, (3, 4, 5), weights, (1, 2, 3))
        elif m == 1:
            near = own[1, :, :128] + depth_one(shifted, 2, weights[0])
            first = jnp.concatenate([near, own[1, :, 128:]], axis=1)
        else:
            far = own[2, :, 128:] + depth_one(shifted, 3, weights[2])
            first = jnp.concatenate([own[2, :, :128], far], axis=1)
        first = round_once(jnp.maximum(first, 0.0))
        pair = (first[:, :128] + first[:, 128:]).reshape(8, 32, 128)
        halves[...] = (pair[:, :16] + pair[:, 16:]).reshape(128, 128)
        pooled = halves[pl.ds(0, 64, stride=2), :] + halves[pl.ds(1, 64, stride=2), :]
        pooled = round_once(pooled * 0.125)
        if m == 0:
            pooled = jnp.where(ends[0] == 0, 0.0, pooled)
        if m == 3:
            pooled = jnp.where(ends[1] == 0, 0.0, pooled)
        framed[m, 1:9, 8:16, :] = pooled.reshape(8, 8, 128)
    fill_patches(framed, patches, 4)
    skip = dot(patches[0:128], second[0])
    skip += dot(patches[64:192], second[1])
    skip += dot(patches[128:256], second[2])
    skip = jnp.maximum(skip, 0.0).astype(jnp.bfloat16)
    wide = skip.astype(jnp.float32)
    pair = (wide[:64] + wide[64:]).reshape(4, 16, 256)
    pair = (pair[:, :8] + pair[:, 8:]).reshape(32, 256)
    for k in range(2):
        quarters[k] = pair[:, 128 * k : 128 * k + 128]
    pooled = jnp.concatenate(
        [
            quarters[k, pl.ds(0, 16, stride=2), :] + quarters[k, pl.ds(1, 16, stride=2), :]
            for k in range(2)
        ],
        axis=1,
    )
    pooled = (pooled * 0.125).astype(jnp.bfloat16)
    for p in range(pooled_out.shape[0]):
        pooled_out[p] = pooled
    sorted_skip = dot(skip, order[...])
    for r in range(GROUP):
        near, far = sorted_skip[:64, 64 * r : 64 * r + 64], sorted_skip[64:, 64 * r : 64 * r + 64]
        block = jnp.concatenate([near, far], axis=1)
        block = jnp.concatenate([block[:32], block[32:]], axis=1).astype(jnp.bfloat16)
        blocks[r] = block
    for k in range(GROUP):
        skip_outs[k][...] = blocks[ends[3] ^ k]


def edge_slice(block, far):
    lower = lax.broadcasted_iota(jnp.int32, (16, 128), 1) < 64
    sides = []
    for k in range(2):
        half = block[:, 128 * k : 128 * k + 128].astype(jnp.float32)
        top, bottom = half[:16], half[16:]
        if far:
            top = pltpu.roll(top, 64, 1)
        else:
            bottom = pltpu.roll(bottom, 64, 1)
        sides.append(jnp.where(lower, top, bottom))
    return jnp.concatenate(sides, axis=1).astype(jnp.bfloat16)


def spread_taps(weights, values, dims, chans, voxels):
    lane = lax.broadcasted_iota(jnp.int32, (chans, voxels), 1)

    def moved(term, tap, step, place, last):
        if tap == 1:
            return term
        keep = place > 0 if tap == 0 else place < last
        return jnp.where(keep, pltpu.roll(term, ((1 - tap) * step) % voxels, 1), 0.0)

    total = None
    for a in range(3):
        products = dot(weights[a * 9 * chans : (a + 1) * 9 * chans, :], values, dims)
        plane = None
        for b in range(3):
            line = None
            for c in range(3):
                at = (b * 3 + c) * chans
                term = moved(products[at : at + chans], c, 1, lane & 3, 3)
                line = term if line is None else line + term
            line = moved(line, b, 4, (lane >> 2) & 3, 3)
            plane = line if plane is None else plane + line
        plane = moved(plane, a, 16, lane >> 4, voxels // 16 - 1)
        total = plane if total is None else total + plane
    return jnp.maximum(total, 0.0)


def by_rank(rank, near, blocks):
    for k in range(GROUP):
        blocks[rank[0] ^ k] = near[k][...]


def edge_stage(rank, *refs):
    near, (first, last, blocks) = refs[:GROUP], refs[GROUP:]
    by_rank(rank, near, blocks)
    first[...] = edge_slice(blocks[0], False)
    last[...] = edge_slice(blocks[GROUP - 1], True)


def deep_stage(pooled, weights, *refs):
    out = refs[-1]
    n, chans, voxels = out.shape
    deep = spread_taps(weights, pooled[...], ((1,), (1,)), chans, voxels).astype(jnp.bfloat16)
    for dest in range(n):
        out[dest] = deep


def deeper_stage(deep, weights, *refs):
    out = refs[-1]
    n, chans, _ = out.shape
    voxels = deep.shape[1]
    deeper = spread_taps(weights, deep[...], ((1,), (0,)), chans, voxels)
    lane = lax.broadcasted_iota(jnp.int32, (chans, 128), 1)
    planes = n // GROUP
    for p in range(planes):
        part = pltpu.roll(deeper, (16 - 64 * p) % voxels, 1)[:, :128]
        if p == 0:
            part = jnp.where(lane < 16, 0.0, part)
        if p == planes - 1:
            part = jnp.where(lane >= 80, 0.0, part)
        part = part.astype(jnp.bfloat16)
        for r in range(GROUP):
            out[GROUP * p + r] = part


def rise_stage(rank, chans, rise, out):
    lane = lax.broadcasted_iota(jnp.int32, (256, 64), 1)
    row = lax.broadcasted_iota(jnp.int32, (256, 64), 0)
    source = (rank[0] + GROUP * (lane // chans)) * chans + lane % chans
    mine = jnp.where(row == source, 1.0, 0.0).astype(jnp.bfloat16)
    for pair in range(4):
        both = [dot(rise[2 * pair + k], mine) for k in range(2)]
        both = jnp.concatenate(both, axis=1).astype(jnp.bfloat16)
        out[:, 128 * pair : 128 * pair + 128] = both


def decode_stage(rank, deeper, rise, low, high, decode, *refs):
    near, (out, framed, patches, risen, blocks) = refs[:GROUP], refs[GROUP:]
    by_rank(rank, near, blocks)
    framed[...] = jnp.zeros(framed.shape, jnp.float32)
    spread = round_once(dot(deeper[...].astype(jnp.float32).T.astype(jnp.bfloat16), rise[...]))
    for pair in range(4):
        both = spread[:, 128 * pair : 128 * pair + 128]
        risen[2 * pair] = both
        risen[2 * pair + 1] = pltpu.roll(both, 64, 1)
    upper = lax.broadcasted_iota(jnp.int32, (64, 128), 1) >= 64
    for s in range(10):
        d, a = (s + 1) // 2, (s + 1) % 2
        for h in range(4):
            for b in range(2):
                for c in range(2):
                    framed[s, 1 + 2 * h + b, pl.ds(8 + c, 4, stride=2), :] = risen[
                        4 * a + 2 * b + c, 16 * d + 4 * h : 16 * d + 4 * h + 4, :
                    ]
        if s == 0 or s == 9:
            edge = (low if s == 0 else high)[...].astype(jnp.float32)
            parts = []
            for k in range(2):
                half = edge[:, 128 * k : 128 * k + 128]
                parts += [pltpu.roll(half, 64, 1), half]
            skip = jnp.concatenate(parts, axis=0)
        else:
            both = blocks[(s - 1) // 2].astype(jnp.float32)
            skip = jnp.concatenate([both[:, :128], both[:, 128:]], axis=0)
            if (s - 1) % 2 == 0:
                skip = pltpu.roll(skip, 64, 1)
        joined = framed[s, 1:9, 8:16, :].reshape(64, 128)
        framed[s, 1:9, 8:16, :] = jnp.where(upper, skip, joined).reshape(8, 8, 128)
    fill_patches(framed, patches, 10)
    blocks = decode.shape[0]
    step = 128 // blocks
    partial = None
    for a in range(3):
        right = [
            decode[z, tap * step : (tap + 1) * step, :]
            for tap in range(9 * a, 9 * a + 9)
            for z in range(blocks)
        ]
        term = dot(patches[64 * a : 64 * a + 512], jnp.concatenate(right, axis=0))
        partial = term if partial is None else partial + term
    out[...] = partial.astype(jnp.bfloat16)


def final_stage(partials, weights, out, spaced):
    decoded = partials[0].astype(jnp.float32)
    for g in range(1, GROUP):
        decoded += partials[g].astype(jnp.float32)
    decoded = jnp.maximum(decoded, 0.0).astype(jnp.bfloat16)
    for a in range(2):
        for b in range(2):
            for c in range(2):
                values = dot(decoded, weights[4 * a + 2 * b + c])
                for d in range(2):
                    for h in range(8):
                        at = ((2 * d + a) * 16 + 2 * h + b) * 16 + c
                        spaced[pl.ds(at, 8, stride=2), :] = values[64 * d + 8 * h : 64 * d + 8 * h + 8]
    out[...] = spaced[...].astype(jnp.bfloat16)


ALL = ("z", "r")


def exchange(payload, axis):
    return lax.all_to_all(payload, axis, split_axis=0, concat_axis=0, tiled=True)


def body(
    volume,
    first_kernel,
    second_kernel,
    deep_kernel,
    deeper_kernel,
    rise_kernel,
    decode_kernel,
    final_kernel,
):
    n = lax.axis_size(ALL)
    place = lax.axis_index(ALL)
    planes = n // GROUP
    rank = lax.axis_index("r")
    chans = deep_kernel.shape[4]
    voxels = 16 * n
    bf16 = functools.partial(jax.ShapeDtypeStruct, dtype=jnp.bfloat16)

    decode_part = lax.all_gather(decode_kernel.reshape(27 * chans, 256), "z", axis=0)
    if chans % 16:
        decode_part = decode_part.reshape(planes, 27, chans, 256).transpose(1, 0, 2, 3)
        decode_part = decode_part.reshape(1, 27 * 128, 256)

    odd = (place % 2).astype(jnp.int32)
    off_chip, on_chip, volume = call(
        front_stage,
        (bf16((3, 16, 16, 128)), bf16((3, 16, 16, 128)), bf16((4, 16, 16, 128))),
        [],
        (odd.reshape(1), volume),
        3 * 10**9,
        16,
        scalars=1,
    )
    pairs = [(i, i + 1) for i in range(1, n - 1, 2)]
    off_chip = lax.ppermute(off_chip, ALL, pairs + [(j, i) for i, j in pairs])
    on_chip = lax.ppermute(on_chip, ALL, [(i, i ^ 1) for i in range(n)])

    taps = first_kernel.reshape(3, 1152, 128)
    own = call(
        own_stage,
        jax.ShapeDtypeStruct((4, 256, 256), jnp.float32),
        [pltpu.VMEM((4, 18, 16, 384), jnp.bfloat16)],
        (volume, taps),
        2 * 1024 * 2304 * 256,
        24,
    )
    lane = np.arange(256)
    source = (lane // 64 + GROUP * (lane % 64 // chans)) * chans + lane % chans
    order = jnp.asarray(np.arange(256)[:, None] == source[None, :], jnp.bfloat16)
    ends = jnp.stack([place, n - 1 - place, odd, rank]).astype(jnp.int32)
    pooled_two, *skips = call(
        stem_stage,
        (bf16((n, 16, 256)),) + (bf16((32, 256)),) * GROUP,
        [
            pltpu.VMEM((6, 18, 16, 384), jnp.bfloat16),
            pltpu.VMEM((128, 128), jnp.float32),
            pltpu.VMEM((4, 10, 24, 128), jnp.float32),
            pltpu.VMEM((256, 1152), jnp.bfloat16),
            pltpu.VMEM((2, 32, 128), jnp.float32),
            pltpu.VMEM((GROUP, 32, 256), jnp.bfloat16),
        ],
        (ends, off_chip, on_chip, own, taps, second_kernel.reshape(3, 1152, 256), order),
        2 * 1024 * 2304 * 256,
        24,
        scalars=1,
    )
    pooled_whole = exchange(pooled_two, ALL)
    near = [skips[0]] + [
        lax.ppermute(skips[k], "r", [(r, r ^ k) for r in range(GROUP)]) for k in range(1, GROUP)
    ]
    rank_ref = rank.astype(jnp.int32).reshape(1)
    blocks = pltpu.VMEM((GROUP, 32, 256), jnp.bfloat16)

    deep = call(
        deep_stage,
        bf16((n, chans, voxels)),
        [],
        (
            pooled_whole.reshape(voxels, 256),
            deep_kernel.transpose(0, 1, 2, 4, 3).reshape(27 * chans, 256),
            *near[1:],
        ),
        2 * 27 * chans * 256 * voxels,
        16,
        unread=GROUP - 1,
    )
    first, last = call(
        edge_stage,
        (bf16((16, 256)), bf16((16, 256))),
        [blocks],
        (rank_ref, *near),
        0,
        16,
        scalars=1,
    )
    skip_low = lax.ppermute(last, "z", [(p, p + 1) for p in range(planes - 1)])
    skip_high = lax.ppermute(first, "z", [(p + 1, p) for p in range(planes - 1)])
    rise_part = call(
        lambda rank_ref, *refs: rise_stage(rank_ref, chans, *refs),
        bf16((n * chans, 512)),
        [],
        (rank_ref, rise_kernel.reshape(8, n * chans, 256)),
        2 * 8 * n * chans * 256 * 64,
        16,
        scalars=1,
    )
    deep_whole = exchange(deep, ALL).reshape(n * chans, voxels)

    deeper = call(
        deeper_stage,
        bf16((n, chans, 128)),
        [],
        (
            deep_whole,
            deeper_kernel.transpose(0, 1, 2, 4, 3).reshape(27 * chans, n * chans),
            skip_low,
            skip_high,
            rise_part,
        ),
        2 * 27 * chans * n * chans * voxels,
        16,
        unread=3,
    )
    deeper_near = exchange(deeper, ALL).reshape(n * chans, 128)

    partial = call(
        decode_stage,
        bf16((512, 256)),
        [
            pltpu.VMEM((10, 10, 24, 128), jnp.float32),
            pltpu.VMEM((640, 1152), jnp.bfloat16),
            pltpu.VMEM((8, 128, 128), jnp.float32),
            blocks,
        ],
        (rank_ref, deeper_near, rise_part, skip_low, skip_high, decode_part, *near),
        2 * 512 * 3456 * 256,
        24,
        scalars=1,
    )
    partials = exchange(partial.reshape(GROUP, 128, 256), "r")
    out = call(
        final_stage,
        bf16((1024, 128)),
        [pltpu.VMEM((1024, 128), jnp.float32)],
        (partials, final_kernel.reshape(8, 256, 128)),
        2 * 128 * 256 * 1024,
        16,
    )
    return out.reshape(4, 16, 16, 128)


def solution(mesh):
    reps, n = mesh.devices.shape
    grid = jax.sharding.Mesh(mesh.devices.reshape(reps, n // GROUP, GROUP), ("rep",) + ALL)
    return jax.shard_map(
        body,
        mesh=grid,
        in_specs=(
            P(("rep",) + ALL, None, None, None),
            P(),
            P(),
            P(None, None, None, None, ALL),
            P(None, None, None, None, ALL),
            P(),
            P(None, None, None, ALL, None),
            P(),
        ),
        out_specs=P(("rep",) + ALL, None, None, None),
        check_vma=False,
    )
```

```python
import functools

import jax
import jax.numpy as jnp
import numpy as np
from jax import lax
from jax.experimental import pallas as pl
from jax.experimental.pallas import tpu as pltpu
from jax.sharding import PartitionSpec as P

GROUP = 4
MIB = 1024 * 1024


def call(kernel, outs, scratch, args, flops, vmem_mib, scalars=0, unread=0, far_outs=0):
    spaces = [pltpu.SMEM] * scalars + [pltpu.VMEM] * (len(args) - scalars - unread)
    spaces += [pl.ANY] * unread
    return pl.pallas_call(
        kernel,
        out_shape=outs,
        in_specs=[pl.BlockSpec(memory_space=space) for space in spaces],
        out_specs=jax.tree.map(
            lambda _: pl.BlockSpec(memory_space=pl.ANY if far_outs else pltpu.VMEM), outs
        ),
        scratch_shapes=scratch,
        compiler_params=pltpu.CompilerParams(vmem_limit_bytes=vmem_mib * MIB),
        cost_estimate=pl.CostEstimate(
            flops=flops,
            bytes_accessed=sum(a.size * a.dtype.itemsize for a in args[: len(args) - unread]),
            transcendentals=0,
        ),
    )(*args)


def dot(left, right, dims=((1,), (0,))):
    return lax.dot_general(left, right, (dims, ((), ())), preferred_element_type=jnp.float32)


def round_once(values):
    return values.astype(jnp.bfloat16).astype(jnp.float32)


def fill_patches(framed, patches, slices):
    for b in range(3):
        for c in range(3):
            tap = framed[:, b : b + 8, 7 + c : 15 + c, :].reshape(slices * 64, 128)
            col = (b * 3 + c) * 128
            patches[:, col : col + 128] = tap.astype(jnp.bfloat16)


def shift_slice(shifted, s, values):
    row = lax.broadcasted_iota(jnp.int32, (256, 128), 0) & 15
    here = values.reshape(256, 128).astype(jnp.float32)
    before = jnp.where(row == 0, 0.0, pltpu.roll(here, 1, 0))
    after = jnp.where(row == 15, 0.0, pltpu.roll(here, 255, 0))
    shifted[s, 0] = jnp.zeros((16, 384), jnp.bfloat16)
    shifted[s, 17] = jnp.zeros((16, 384), jnp.bfloat16)
    for c, tap in enumerate((before, here, after)):
        tap = tap.astype(jnp.bfloat16).reshape(16, 16, 128)
        shifted[s, 1:17, :, 128 * c : 128 * c + 128] = tap


def depth_pair(shifted, slices, weights, steps):
    left = jnp.concatenate(
        [shifted[s, b : b + 16].reshape(256, 384) for s in slices for b in range(3)], axis=1
    )
    none = jnp.zeros((1152, 128), jnp.bfloat16)
    right = [
        jnp.concatenate(
            [weights[j] if j < 3 else none, weights[j - 1] if j > 0 else none], axis=1
        )
        for j in steps
    ]
    return dot(left, jnp.concatenate(right, axis=0))


def depth_one(shifted, s, weights):
    left = jnp.concatenate([shifted[s, b : b + 16].reshape(256, 384) for b in range(3)], axis=1)
    return dot(left, weights)


def front_stage(odd, volume, off_chip, on_chip, whole):
    for s in range(3):
        off_chip[s] = jnp.where(odd[0] == 0, volume[s], volume[s + 1])
        on_chip[s] = jnp.where(odd[0] == 0, volume[s + 1], volume[s])
    whole[...] = volume[...]


def share_stage(place, decode, _, out, done):
    step, rows = decode.shape[0] - out.shape[0], out.shape[0]
    at = pl.multiple_of(place[1] * step, 16)
    copy = pltpu.make_async_copy(decode.at[pl.ds(at, rows)], out, done)
    copy.start()
    copy.wait()


def pick_stage(place, line, _, out, done):
    rows = out.shape[1]
    at = pl.multiple_of(place[1] * (line.shape[1] - rows), 16)
    copy = pltpu.make_async_copy(line.at[:, pl.ds(at, rows)], out, done)
    copy.start()
    copy.wait()


def own_stage(volume, weights, out, shifted):
    for s in range(4):
        shift_slice(shifted, s, volume[s])
    out[0, :, :128] = jnp.zeros((256, 128), jnp.float32)
    out[0, :, 128:] = depth_one(shifted, 0, weights[2])
    out[1] = depth_pair(shifted, (0, 1, 2), weights, (1, 2, 3))
    out[2] = depth_pair(shifted, (1, 2, 3), weights, (0, 1, 2))
    out[3, :, :128] = depth_one(shifted, 3, weights[0])
    out[3, :, 128:] = jnp.zeros((256, 128), jnp.float32)


def stem_stage(ends, off_chip, on_chip, own, weights, second, order, *refs):
    pooled_out, skip_outs = refs[0], refs[1 : 1 + GROUP]
    shifted, halves, framed, patches, quarters, blocks = refs[1 + GROUP :]
    for s in range(3):
        even = ends[2] == 0
        shift_slice(shifted, s, jnp.where(even, off_chip[s], on_chip[s]))
        shift_slice(shifted, 3 + s, jnp.where(even, on_chip[s], off_chip[s]))
    framed[...] = jnp.zeros(framed.shape, jnp.float32)
    for m in range(4):
        if m == 0:
            first = own[0] + depth_pair(shifted, (0, 1, 2), weights, (0, 1, 2))
        elif m == 3:
            first = own[3] + depth_pair(shifted, (3, 4, 5), weights, (1, 2, 3))
        elif m == 1:
            near = own[1, :, :128] + depth_one(shifted, 2, weights[0])
            first = jnp.concatenate([near, own[1, :, 128:]], axis=1)
        else:
            far = own[2, :, 128:] + depth_one(shifted, 3, weights[2])
            first = jnp.concatenate([own[2, :, :128], far], axis=1)
        first = round_once(jnp.maximum(first, 0.0))
        pair = (first[:, :128] + first[:, 128:]).reshape(8, 32, 128)
        halves[...] = (pair[:, :16] + pair[:, 16:]).reshape(128, 128)
        pooled = halves[pl.ds(0, 64, stride=2), :] + halves[pl.ds(1, 64, stride=2), :]
        pooled = round_once(pooled * 0.125)
        if m == 0:
            pooled = jnp.where(ends[0] == 0, 0.0, pooled)
        if m == 3:
            pooled = jnp.where(ends[1] == 0, 0.0, pooled)
        framed[m, 1:9, 8:16, :] = pooled.reshape(8, 8, 128)
    fill_patches(framed, patches, 4)
    skip = dot(patches[0:128], second[0])
    skip += dot(patches[64:192], second[1])
    skip += dot(patches[128:256], second[2])
    skip = jnp.maximum(skip, 0.0).astype(jnp.bfloat16)
    wide = skip.astype(jnp.float32)
    pair = (wide[:64] + wide[64:]).reshape(4, 16, 256)
    pair = (pair[:, :8] + pair[:, 8:]).reshape(32, 256)
    for k in range(2):
        quarters[k] = pair[:, 128 * k : 128 * k + 128]
    pooled = jnp.concatenate(
        [
            quarters[k, pl.ds(0, 16, stride=2), :] + quarters[k, pl.ds(1, 16, stride=2), :]
            for k in range(2)
        ],
        axis=1,
    )
    pooled = (pooled * 0.125).astype(jnp.bfloat16)
    for p in range(pooled_out.shape[0]):
        pooled_out[p] = pooled
    sorted_skip = dot(skip, order[...])
    for r in range(GROUP):
        near, far = sorted_skip[:64, 64 * r : 64 * r + 64], sorted_skip[64:, 64 * r : 64 * r + 64]
        block = jnp.concatenate([near, far], axis=1)
        block = jnp.concatenate([block[:32], block[32:]], axis=1).astype(jnp.bfloat16)
        blocks[r] = block
    for k in range(GROUP):
        skip_outs[k][...] = blocks[ends[3] ^ k]


def edge_slice(block, far):
    lower = lax.broadcasted_iota(jnp.int32, (16, 128), 1) < 64
    sides = []
    for k in range(2):
        half = block[:, 128 * k : 128 * k + 128].astype(jnp.float32)
        top, bottom = half[:16], half[16:]
        if far:
            top = pltpu.roll(top, 64, 1)
        else:
            bottom = pltpu.roll(bottom, 64, 1)
        sides.append(jnp.where(lower, top, bottom))
    return jnp.concatenate(sides, axis=1)


def spread_taps(weights, values, dims, chans, voxels):
    lane = lax.broadcasted_iota(jnp.int32, (chans, voxels), 1)

    def moved(term, tap, step, place, last):
        if tap == 1:
            return term
        keep = place > 0 if tap == 0 else place < last
        return jnp.where(keep, pltpu.roll(term, ((1 - tap) * step) % voxels, 1), 0.0)

    total = None
    for a in range(3):
        products = dot(weights[a * 9 * chans : (a + 1) * 9 * chans, :], values, dims)
        plane = None
        for b in range(3):
            line = None
            for c in range(3):
                at = (b * 3 + c) * chans
                term = moved(products[at : at + chans], c, 1, lane & 3, 3)
                line = term if line is None else line + term
            line = moved(line, b, 4, (lane >> 2) & 3, 3)
            plane = line if plane is None else plane + line
        plane = moved(plane, a, 16, lane >> 4, voxels // 16 - 1)
        total = plane if total is None else total + plane
    return jnp.maximum(total, 0.0)


def by_rank(rank, near, blocks):
    for k in range(GROUP):
        blocks[rank[0] ^ k] = near[k][...]


def edge_stage(place, *refs):
    near, (near_swap, far_swap, blocks) = refs[:GROUP], refs[GROUP:]
    by_rank(place, near, blocks)
    first = edge_slice(blocks[0], False)
    last = edge_slice(blocks[GROUP - 1], True)
    even = place[2] == 0
    near_swap[...] = jnp.where(even, last, first).astype(jnp.bfloat16)
    far_swap[...] = jnp.where(even, first, last).astype(jnp.bfloat16)


def deep_stage(pooled, weights, *refs):
    out = refs[-1]
    n, chans, voxels = out.shape
    deep = spread_taps(weights, pooled[...], ((1,), (1,)), chans, voxels).astype(jnp.bfloat16)
    for dest in range(n):
        out[dest] = deep


def deeper_stage(deep, weights, *refs):
    out = refs[-1]
    n, chans, _ = out.shape
    voxels = deep.shape[1]
    deeper = spread_taps(weights, deep[...], ((1,), (0,)), chans, voxels)
    lane = lax.broadcasted_iota(jnp.int32, (chans, 128), 1)
    planes = n // GROUP
    for p in range(planes):
        part = pltpu.roll(deeper, (16 - 64 * p) % voxels, 1)[:, :128]
        if p == 0:
            part = jnp.where(lane < 16, 0.0, part)
        if p == planes - 1:
            part = jnp.where(lane >= 80, 0.0, part)
        part = part.astype(jnp.bfloat16)
        for r in range(GROUP):
            out[GROUP * p + r] = part


def rise_stage(rank, chans, rise, out):
    lane = lax.broadcasted_iota(jnp.int32, (256, 64), 1)
    row = lax.broadcasted_iota(jnp.int32, (256, 64), 0)
    source = (rank[0] + GROUP * (lane // chans)) * chans + lane % chans
    mine = jnp.where(row == source, 1.0, 0.0).astype(jnp.bfloat16)
    for pair in range(4):
        both = [dot(rise[2 * pair + k], mine) for k in range(2)]
        both = jnp.concatenate(both, axis=1).astype(jnp.bfloat16)
        out[:, 128 * pair : 128 * pair + 128] = both


def decode_stage(place, deeper, rise, near_swap, far_swap, *refs):
    near, (*decode, out, framed, patches, risen, blocks) = refs[:GROUP], refs[GROUP:]
    by_rank(place, near, blocks)
    even = place[2] == 0
    framed[...] = jnp.zeros(framed.shape, jnp.float32)
    spread = round_once(dot(deeper[...].astype(jnp.float32).T.astype(jnp.bfloat16), rise[...]))
    for pair in range(4):
        both = spread[:, 128 * pair : 128 * pair + 128]
        risen[2 * pair] = both
        risen[2 * pair + 1] = pltpu.roll(both, 64, 1)
    upper = lax.broadcasted_iota(jnp.int32, (64, 128), 1) >= 64
    for s in range(10):
        d, a = (s + 1) // 2, (s + 1) % 2
        for h in range(4):
            for b in range(2):
                for c in range(2):
                    framed[s, 1 + 2 * h + b, pl.ds(8 + c, 4, stride=2), :] = risen[
                        4 * a + 2 * b + c, 16 * d + 4 * h : 16 * d + 4 * h + 4, :
                    ]
        if s == 0 or s == 9:
            sides = near_swap[...].astype(jnp.float32), far_swap[...].astype(jnp.float32)
            edge = jnp.where(even, sides[s == 0], sides[s == 9])
            parts = []
            for k in range(2):
                half = edge[:, 128 * k : 128 * k + 128]
                parts += [pltpu.roll(half, 64, 1), half]
            skip = jnp.concatenate(parts, axis=0)
        else:
            both = blocks[(s - 1) // 2].astype(jnp.float32)
            skip = jnp.concatenate([both[:, :128], both[:, 128:]], axis=0)
            if (s - 1) % 2 == 0:
                skip = pltpu.roll(skip, 64, 1)
        joined = framed[s, 1:9, 8:16, :].reshape(64, 128)
        framed[s, 1:9, 8:16, :] = jnp.where(upper, skip, joined).reshape(8, 8, 128)
    fill_patches(framed, patches, 10)
    def multiply(rep):
        if rep == 0:
            parts = decode
        else:
            parts = decode[::-1]
        split = parts[0].shape[1]
        count = decode[0].shape[0]
        step = 128 // count
        partial = None
        for a in range(3):
            right = [
                parts[0][z, row : row + 16, :] if row < split else parts[1][z, row - split : row - split + 16, :]
                for tap in range(9 * a, 9 * a + 9)
                for z in range(count)
                for row in range(tap * step, (tap + 1) * step, 16)
            ]
            term = dot(patches[64 * a : 64 * a + 512], jnp.concatenate(right, axis=0))
            partial = term if partial is None else partial + term
        out[...] = partial.astype(jnp.bfloat16)

    if len(decode) == 1:
        multiply(0)
    else:
        pl.when(place[1] == 0)(lambda: multiply(0))
        pl.when(place[1] == 1)(lambda: multiply(1))


def final_stage(partials, weights, out, spaced):
    decoded = partials[0].astype(jnp.float32)
    for g in range(1, GROUP):
        decoded += partials[g].astype(jnp.float32)
    decoded = jnp.maximum(decoded, 0.0).astype(jnp.bfloat16)
    for a in range(2):
        for b in range(2):
            for c in range(2):
                values = dot(decoded, weights[4 * a + 2 * b + c])
                for d in range(2):
                    for h in range(8):
                        at = ((2 * d + a) * 16 + 2 * h + b) * 16 + c
                        spaced[pl.ds(at, 8, stride=2), :] = values[64 * d + 8 * h : 64 * d + 8 * h + 8]
    out[...] = spaced[...].astype(jnp.bfloat16)


ALL = ("z", "r")


def exchange(payload, axis):
    return lax.all_to_all(payload, axis, split_axis=0, concat_axis=0, tiled=True)


def body(
    volume,
    first_kernel,
    second_kernel,
    deep_kernel,
    deeper_kernel,
    rise_kernel,
    decode_kernel,
    final_kernel,
):
    n = lax.axis_size(ALL)
    place = lax.axis_index(ALL)
    planes = n // GROUP
    rank = lax.axis_index("r")
    chans = deep_kernel.shape[4]
    voxels = 16 * n
    bf16 = functools.partial(jax.ShapeDtypeStruct, dtype=jnp.bfloat16)

    rep = lax.axis_index("rep")
    marks = jnp.stack([rank, rep, lax.axis_index("z") % 2]).astype(jnp.int32)
    odd = (place % 2).astype(jnp.int32)
    off_chip, on_chip, volume = call(
        front_stage,
        (bf16((3, 16, 16, 128)), bf16((3, 16, 16, 128)), bf16((4, 16, 16, 128))),
        [],
        (odd.reshape(1), volume),
        3 * 10**9,
        16,
        scalars=1,
    )
    decode_block = decode_kernel.reshape(27 * chans, 256)
    shared = lax.axis_size("rep") == 2 and chans == 32
    if shared:
        decode_block = call(
            share_stage,
            bf16((528, 256)),
            [pltpu.SemaphoreType.DMA],
            (marks, decode_block, volume),
            0,
            16,
            scalars=1,
            unread=2,
            far_outs=1,
        )
    line = lax.all_gather(decode_block, "z", axis=0)

    pairs = [(i, i + 1) for i in range(1, n - 1, 2)]
    off_chip = lax.ppermute(off_chip, ALL, pairs + [(j, i) for i, j in pairs])
    on_chip = lax.ppermute(on_chip, ALL, [(i, i ^ 1) for i in range(n)])

    taps = first_kernel.reshape(3, 1152, 128)
    own = call(
        own_stage,
        jax.ShapeDtypeStruct((4, 256, 256), jnp.float32),
        [pltpu.VMEM((4, 18, 16, 384), jnp.bfloat16)],
        (volume, taps),
        2 * 1024 * 2304 * 256,
        24,
    )
    lane = np.arange(256)
    source = (lane // 64 + GROUP * (lane % 64 // chans)) * chans + lane % chans
    order = jnp.asarray(np.arange(256)[:, None] == source[None, :], jnp.bfloat16)
    ends = jnp.stack([place, n - 1 - place, odd, rank]).astype(jnp.int32)
    pooled_two, *skips = call(
        stem_stage,
        (bf16((n, 16, 256)),) + (bf16((32, 256)),) * GROUP,
        [
            pltpu.VMEM((6, 18, 16, 384), jnp.bfloat16),
            pltpu.VMEM((128, 128), jnp.float32),
            pltpu.VMEM((4, 10, 24, 128), jnp.float32),
            pltpu.VMEM((256, 1152), jnp.bfloat16),
            pltpu.VMEM((2, 32, 128), jnp.float32),
            pltpu.VMEM((GROUP, 32, 256), jnp.bfloat16),
        ],
        (ends, off_chip, on_chip, own, taps, second_kernel.reshape(3, 1152, 256), order),
        2 * 1024 * 2304 * 256,
        24,
        scalars=1,
    )
    pooled_whole = exchange(pooled_two, ALL)
    near = [skips[0]] + [
        lax.ppermute(skips[k], "r", [(r, r ^ k) for r in range(GROUP)]) for k in range(1, GROUP)
    ]
    blocks = pltpu.VMEM((GROUP, 32, 256), jnp.bfloat16)

    deep = call(
        deep_stage,
        bf16((n, chans, voxels)),
        [],
        (
            pooled_whole.reshape(voxels, 256),
            deep_kernel.transpose(0, 1, 2, 4, 3).reshape(27 * chans, 256),
            *near[1:],
        ),
        2 * 27 * chans * 256 * voxels,
        16,
        unread=GROUP - 1,
    )
    if shared:
        piece = call(
            pick_stage,
            bf16((planes, 336, 256)),
            [pltpu.SemaphoreType.DMA],
            (marks, line, deep),
            0,
            16,
            scalars=1,
            unread=2,
            far_outs=1,
        )
        weights = (line, lax.ppermute(piece, "rep", [(0, 1), (1, 0)]))
    elif chans % 16:
        weights = line.reshape(planes, 27, chans, 256).transpose(1, 0, 2, 3)
        weights = (weights.reshape(1, 27 * 128, 256),)
    else:
        weights = (line,)
    swaps = call(
        edge_stage,
        (bf16((16, 256)), bf16((16, 256))),
        [blocks],
        (marks, *near),
        0,
        16,
        scalars=1,
    )
    near_pairs = [(p, p + 1) for p in range(0, planes - 1, 2)]
    far_pairs = [(p, p + 1) for p in range(1, planes - 1, 2)]
    near_swap = lax.ppermute(swaps[0], "z", near_pairs + [(j, i) for i, j in near_pairs])
    far_swap = lax.ppermute(swaps[1], "z", far_pairs + [(j, i) for i, j in far_pairs])
    rise_part = call(
        lambda rank_ref, *refs: rise_stage(rank_ref, chans, *refs),
        bf16((n * chans, 512)),
        [],
        (marks, rise_kernel.reshape(8, n * chans, 256)),
        2 * 8 * n * chans * 256 * 64,
        16,
        scalars=1,
    )
    deep_whole = exchange(deep, ALL).reshape(n * chans, voxels)

    deeper = call(
        deeper_stage,
        bf16((n, chans, 128)),
        [],
        (
            deep_whole,
            deeper_kernel.transpose(0, 1, 2, 4, 3).reshape(27 * chans, n * chans),
            near_swap,
            far_swap,
            rise_part,
        ),
        2 * 27 * chans * n * chans * voxels,
        16,
        unread=3,
    )
    deeper_near = exchange(deeper, ALL).reshape(n * chans, 128)

    partial = call(
        decode_stage,
        bf16((512, 256)),
        [
            pltpu.VMEM((10, 10, 24, 128), jnp.float32),
            pltpu.VMEM((640, 1152), jnp.bfloat16),
            pltpu.VMEM((8, 128, 128), jnp.float32),
            blocks,
        ],
        (marks, deeper_near, rise_part, near_swap, far_swap, *near, *weights),
        2 * 512 * 3456 * 256,
        24,
        scalars=1,
    )
    partials = exchange(partial.reshape(GROUP, 128, 256), "r")
    out = call(
        final_stage,
        bf16((1024, 128)),
        [pltpu.VMEM((1024, 128), jnp.float32)],
        (partials, final_kernel.reshape(8, 256, 128)),
        2 * 128 * 256 * 1024,
        16,
    )
    return out.reshape(4, 16, 16, 128)


def solution(mesh):
    reps, n = mesh.devices.shape
    grid = jax.sharding.Mesh(mesh.devices.reshape(reps, n // GROUP, GROUP), ("rep",) + ALL)
    return jax.shard_map(
        body,
        mesh=grid,
        in_specs=(
            P(("rep",) + ALL, None, None, None),
            P(),
            P(),
            P(None, None, None, None, ALL),
            P(None, None, None, None, ALL),
            P(),
            P(None, None, None, ALL, None),
            P(),
        ),
        out_specs=P(("rep",) + ALL, None, None, None),
        check_vma=False,
    )
```

```python
import functools

import jax
import jax.numpy as jnp
import numpy as np
from jax import lax
from jax.experimental import pallas as pl
from jax.experimental.pallas import tpu as pltpu
from jax.sharding import PartitionSpec as P

GROUP = 4
MIB = 1024 * 1024


def call(kernel, outs, scratch, args, flops, vmem_mib, scalars=0, unread=0):
    spaces = [pltpu.SMEM] * scalars + [pltpu.VMEM] * (len(args) - scalars - unread)
    spaces += [pl.ANY] * unread
    return pl.pallas_call(
        kernel,
        out_shape=outs,
        in_specs=[pl.BlockSpec(memory_space=space) for space in spaces],
        out_specs=jax.tree.map(lambda _: pl.BlockSpec(memory_space=pltpu.VMEM), outs),
        scratch_shapes=scratch,
        compiler_params=pltpu.CompilerParams(vmem_limit_bytes=vmem_mib * MIB),
        cost_estimate=pl.CostEstimate(
            flops=flops,
            bytes_accessed=sum(a.size * a.dtype.itemsize for a in args[: len(args) - unread]),
            transcendentals=0,
        ),
    )(*args)


def dot(left, right, dims=((1,), (0,))):
    return lax.dot_general(left, right, (dims, ((), ())), preferred_element_type=jnp.float32)


def round_once(values):
    return values.astype(jnp.bfloat16).astype(jnp.float32)


def fill_patches(framed, patches, slices):
    for b in range(3):
        for c in range(3):
            tap = framed[:, b : b + 8, 7 + c : 15 + c, :].reshape(slices * 64, 128)
            col = (b * 3 + c) * 128
            patches[:, col : col + 128] = tap.astype(jnp.bfloat16)


def shift_slice(shifted, s, values):
    row = lax.broadcasted_iota(jnp.int32, (256, 128), 0) & 15
    here = values.reshape(256, 128).astype(jnp.float32)
    before = jnp.where(row == 0, 0.0, pltpu.roll(here, 1, 0))
    after = jnp.where(row == 15, 0.0, pltpu.roll(here, 255, 0))
    shifted[s, 0] = jnp.zeros((16, 384), jnp.bfloat16)
    shifted[s, 17] = jnp.zeros((16, 384), jnp.bfloat16)
    for c, tap in enumerate((before, here, after)):
        tap = tap.astype(jnp.bfloat16).reshape(16, 16, 128)
        shifted[s, 1:17, :, 128 * c : 128 * c + 128] = tap


def depth_pair(shifted, slices, weights, steps):
    left = jnp.concatenate(
        [shifted[s, b : b + 16].reshape(256, 384) for s in slices for b in range(3)], axis=1
    )
    none = jnp.zeros((1152, 128), jnp.bfloat16)
    right = [
        jnp.concatenate(
            [weights[j] if j < 3 else none, weights[j - 1] if j > 0 else none], axis=1
        )
        for j in steps
    ]
    return dot(left, jnp.concatenate(right, axis=0))


def depth_one(shifted, s, weights):
    left = jnp.concatenate([shifted[s, b : b + 16].reshape(256, 384) for b in range(3)], axis=1)
    return dot(left, weights)


def front_stage(odd, volume, off_chip, on_chip, whole):
    for s in range(3):
        off_chip[s] = jnp.where(odd[0] == 0, volume[s], volume[s + 1])
        on_chip[s] = jnp.where(odd[0] == 0, volume[s + 1], volume[s])
    whole[...] = volume[...]


def own_stage(volume, weights, out, shifted):
    for s in range(4):
        shift_slice(shifted, s, volume[s])
    out[0, :, :128] = jnp.zeros((256, 128), jnp.float32)
    out[0, :, 128:] = depth_one(shifted, 0, weights[2])
    out[1] = depth_pair(shifted, (0, 1, 2), weights, (1, 2, 3))
    out[2] = depth_pair(shifted, (1, 2, 3), weights, (0, 1, 2))
    out[3, :, :128] = depth_one(shifted, 3, weights[0])
    out[3, :, 128:] = jnp.zeros((256, 128), jnp.float32)


def stem_stage(ends, off_chip, on_chip, own, weights, second, order, _, *refs):
    pooled_out, skip_outs = refs[0], refs[1 : 1 + GROUP]
    shifted, halves, framed, patches, quarters, blocks = refs[1 + GROUP :]
    for s in range(3):
        even = ends[2] == 0
        shift_slice(shifted, s, jnp.where(even, off_chip[s], on_chip[s]))
        shift_slice(shifted, 3 + s, jnp.where(even, on_chip[s], off_chip[s]))
    framed[...] = jnp.zeros(framed.shape, jnp.float32)
    for m in range(4):
        if m == 0:
            first = own[0] + depth_pair(shifted, (0, 1, 2), weights, (0, 1, 2))
        elif m == 3:
            first = own[3] + depth_pair(shifted, (3, 4, 5), weights, (1, 2, 3))
        elif m == 1:
            near = own[1, :, :128] + depth_one(shifted, 2, weights[0])
            first = jnp.concatenate([near, own[1, :, 128:]], axis=1)
        else:
            far = own[2, :, 128:] + depth_one(shifted, 3, weights[2])
            first = jnp.concatenate([own[2, :, :128], far], axis=1)
        first = round_once(jnp.maximum(first, 0.0))
        pair = (first[:, :128] + first[:, 128:]).reshape(8, 32, 128)
        halves[...] = (pair[:, :16] + pair[:, 16:]).reshape(128, 128)
        pooled = halves[pl.ds(0, 64, stride=2), :] + halves[pl.ds(1, 64, stride=2), :]
        pooled = round_once(pooled * 0.125)
        if m == 0:
            pooled = jnp.where(ends[0] == 0, 0.0, pooled)
        if m == 3:
            pooled = jnp.where(ends[1] == 0, 0.0, pooled)
        framed[m, 1:9, 8:16, :] = pooled.reshape(8, 8, 128)
    fill_patches(framed, patches, 4)
    skip = dot(patches[0:128], second[0])
    skip += dot(patches[64:192], second[1])
    skip += dot(patches[128:256], second[2])
    skip = jnp.maximum(skip, 0.0).astype(jnp.bfloat16)
    wide = skip.astype(jnp.float32)
    pair = (wide[:64] + wide[64:]).reshape(4, 16, 256)
    pair = (pair[:, :8] + pair[:, 8:]).reshape(32, 256)
    for k in range(2):
        quarters[k] = pair[:, 128 * k : 128 * k + 128]
    pooled = jnp.concatenate(
        [
            quarters[k, pl.ds(0, 16, stride=2), :] + quarters[k, pl.ds(1, 16, stride=2), :]
            for k in range(2)
        ],
        axis=1,
    )
    pooled = (pooled * 0.125).astype(jnp.bfloat16)
    for p in range(pooled_out.shape[0]):
        pooled_out[p] = pooled
    sorted_skip = dot(skip, order[...])
    for r in range(GROUP):
        near, far = sorted_skip[:64, 64 * r : 64 * r + 64], sorted_skip[64:, 64 * r : 64 * r + 64]
        block = jnp.concatenate([near, far], axis=1)
        block = jnp.concatenate([block[:32], block[32:]], axis=1).astype(jnp.bfloat16)
        blocks[r] = block
    for k in range(GROUP):
        skip_outs[k][...] = blocks[ends[3] ^ k]


def edge_slice(block, far):
    lower = lax.broadcasted_iota(jnp.int32, (16, 128), 1) < 64
    sides = []
    for k in range(2):
        half = block[:, 128 * k : 128 * k + 128].astype(jnp.float32)
        top, bottom = half[:16], half[16:]
        if far:
            top = pltpu.roll(top, 64, 1)
        else:
            bottom = pltpu.roll(bottom, 64, 1)
        sides.append(jnp.where(lower, top, bottom))
    return jnp.concatenate(sides, axis=1)


def spread_taps(weights, values, dims, chans, voxels):
    lane = lax.broadcasted_iota(jnp.int32, (chans, voxels), 1)

    def moved(term, tap, step, place, last):
        if tap == 1:
            return term
        keep = place > 0 if tap == 0 else place < last
        return jnp.where(keep, pltpu.roll(term, ((1 - tap) * step) % voxels, 1), 0.0)

    total = None
    for a in range(3):
        products = dot(weights[a * 9 * chans : (a + 1) * 9 * chans, :], values, dims)
        plane = None
        for b in range(3):
            line = None
            for c in range(3):
                at = (b * 3 + c) * chans
                term = moved(products[at : at + chans], c, 1, lane & 3, 3)
                line = term if line is None else line + term
            line = moved(line, b, 4, (lane >> 2) & 3, 3)
            plane = line if plane is None else plane + line
        plane = moved(plane, a, 16, lane >> 4, voxels // 16 - 1)
        total = plane if total is None else total + plane
    return jnp.maximum(total, 0.0)


def by_rank(rank, near, blocks):
    for k in range(GROUP):
        blocks[rank[0] ^ k] = near[k][...]


def edge_stage(place, *refs):
    near, (near_swap, far_swap, blocks) = refs[:GROUP], refs[GROUP:]
    by_rank(place, near, blocks)
    first = edge_slice(blocks[0], False)
    last = edge_slice(blocks[GROUP - 1], True)
    even = place[2] == 0
    near_swap[...] = jnp.where(even, last, first).astype(jnp.bfloat16)
    far_swap[...] = jnp.where(even, first, last).astype(jnp.bfloat16)


def deep_stage(pooled, weights, *refs):
    out = refs[-1]
    n, chans, voxels = out.shape
    deep = spread_taps(weights, pooled[...], ((1,), (1,)), chans, voxels).astype(jnp.bfloat16)
    for dest in range(n):
        out[dest] = deep


def deeper_stage(deep, weights, *refs):
    out = refs[-1]
    n, chans, _ = out.shape
    voxels = deep.shape[1]
    deeper = spread_taps(weights, deep[...], ((1,), (0,)), chans, voxels)
    lane = lax.broadcasted_iota(jnp.int32, (chans, 128), 1)
    planes = n // GROUP
    for p in range(planes):
        part = pltpu.roll(deeper, (16 - 64 * p) % voxels, 1)[:, :128]
        if p == 0:
            part = jnp.where(lane < 16, 0.0, part)
        if p == planes - 1:
            part = jnp.where(lane >= 80, 0.0, part)
        part = part.astype(jnp.bfloat16)
        for r in range(GROUP):
            out[GROUP * p + r] = part


def rise_stage(rank, chans, rise, out):
    lane = lax.broadcasted_iota(jnp.int32, (256, 64), 1)
    row = lax.broadcasted_iota(jnp.int32, (256, 64), 0)
    source = (rank[0] + GROUP * (lane // chans)) * chans + lane % chans
    mine = jnp.where(row == source, 1.0, 0.0).astype(jnp.bfloat16)
    for pair in range(4):
        both = [dot(rise[2 * pair + k], mine) for k in range(2)]
        both = jnp.concatenate(both, axis=1).astype(jnp.bfloat16)
        out[:, 128 * pair : 128 * pair + 128] = both


def decode_stage(place, deeper, rise, near_swap, far_swap, *refs):
    near, (*decode, out, framed, patches, risen, blocks) = refs[:GROUP], refs[GROUP:]
    by_rank(place, near, blocks)
    even = place[2] == 0
    framed[...] = jnp.zeros(framed.shape, jnp.float32)
    spread = round_once(dot(deeper[...].astype(jnp.float32).T.astype(jnp.bfloat16), rise[...]))
    for pair in range(4):
        both = spread[:, 128 * pair : 128 * pair + 128]
        risen[2 * pair] = both
        risen[2 * pair + 1] = pltpu.roll(both, 64, 1)
    upper = lax.broadcasted_iota(jnp.int32, (64, 128), 1) >= 64
    for s in range(10):
        d, a = (s + 1) // 2, (s + 1) % 2
        for h in range(4):
            for b in range(2):
                for c in range(2):
                    framed[s, 1 + 2 * h + b, pl.ds(8 + c, 4, stride=2), :] = risen[
                        4 * a + 2 * b + c, 16 * d + 4 * h : 16 * d + 4 * h + 4, :
                    ]
        if s == 0 or s == 9:
            sides = near_swap[...].astype(jnp.float32), far_swap[...].astype(jnp.float32)
            edge = jnp.where(even, sides[s == 0], sides[s == 9])
            parts = []
            for k in range(2):
                half = edge[:, 128 * k : 128 * k + 128]
                parts += [pltpu.roll(half, 64, 1), half]
            skip = jnp.concatenate(parts, axis=0)
        else:
            both = blocks[(s - 1) // 2].astype(jnp.float32)
            skip = jnp.concatenate([both[:, :128], both[:, 128:]], axis=0)
            if (s - 1) % 2 == 0:
                skip = pltpu.roll(skip, 64, 1)
        joined = framed[s, 1:9, 8:16, :].reshape(64, 128)
        framed[s, 1:9, 8:16, :] = jnp.where(upper, skip, joined).reshape(8, 8, 128)
    fill_patches(framed, patches, 10)
    def rows_at(rep, z, row):
        if rep == 0 and row >= 528:
            return decode[1][z, row - 528 : row - 512, :]
        if rep == 1 and row < 336:
            return decode[1][z, row : row + 16, :]
        if rep == 1 and row >= 528:
            row -= 528
        return decode[0][z, row : row + 16, :]

    def multiply(rep):
        count = decode[0].shape[0]
        step = 128 // count
        partial = None
        for a in range(3):
            right = [
                rows_at(rep, z, row)
                for tap in range(9 * a, 9 * a + 9)
                for z in range(count)
                for row in range(tap * step, (tap + 1) * step, 16)
            ]
            term = dot(patches[64 * a : 64 * a + 512], jnp.concatenate(right, axis=0))
            partial = term if partial is None else partial + term
        out[...] = partial.astype(jnp.bfloat16)

    if len(decode) == 1:
        multiply(None)
    else:
        pl.when(place[1] == 0)(lambda: multiply(0))
        pl.when(place[1] == 1)(lambda: multiply(1))


def final_stage(partials, weights, out, spaced):
    decoded = partials[0].astype(jnp.float32)
    for g in range(1, GROUP):
        decoded += partials[g].astype(jnp.float32)
    decoded = jnp.maximum(decoded, 0.0).astype(jnp.bfloat16)
    for a in range(2):
        for b in range(2):
            for c in range(2):
                values = dot(decoded, weights[4 * a + 2 * b + c])
                for d in range(2):
                    for h in range(8):
                        at = ((2 * d + a) * 16 + 2 * h + b) * 16 + c
                        spaced[pl.ds(at, 8, stride=2), :] = values[64 * d + 8 * h : 64 * d + 8 * h + 8]
    out[...] = spaced[...].astype(jnp.bfloat16)


ALL = ("z", "r")


def exchange(payload, axis):
    return lax.all_to_all(payload, axis, split_axis=0, concat_axis=0, tiled=True)


def body(
    volume,
    first_kernel,
    second_kernel,
    deep_kernel,
    deeper_kernel,
    rise_kernel,
    decode_kernel,
    final_kernel,
):
    n = lax.axis_size(ALL)
    place = lax.axis_index(ALL)
    planes = n // GROUP
    rank = lax.axis_index("r")
    chans = deep_kernel.shape[4]
    voxels = 16 * n
    bf16 = functools.partial(jax.ShapeDtypeStruct, dtype=jnp.bfloat16)

    rep = lax.axis_index("rep")
    marks = jnp.stack([rank, rep, lax.axis_index("z") % 2]).astype(jnp.int32)
    odd = (place % 2).astype(jnp.int32)
    off_chip, on_chip, volume = call(
        front_stage,
        (bf16((3, 16, 16, 128)), bf16((3, 16, 16, 128)), bf16((4, 16, 16, 128))),
        [],
        (odd.reshape(1), volume),
        3 * 10**9,
        16,
        scalars=1,
    )
    decode_block = decode_kernel.reshape(27 * chans, 256)
    shared = lax.axis_size("rep") == 2 and chans == 32
    if shared:
        own_rows = lax.dynamic_slice_in_dim(decode_block, 528 * rep, 336, axis=0)
        decode_block = jnp.concatenate([own_rows, decode_block[336:528]], axis=0)
    line = lax.all_gather(decode_block, "z", axis=0)

    pairs = [(i, i + 1) for i in range(1, n - 1, 2)]
    off_chip = lax.ppermute(off_chip, ALL, pairs + [(j, i) for i, j in pairs])
    on_chip = lax.ppermute(on_chip, ALL, [(i, i ^ 1) for i in range(n)])

    taps = first_kernel.reshape(3, 1152, 128)
    own = call(
        own_stage,
        jax.ShapeDtypeStruct((4, 256, 256), jnp.float32),
        [pltpu.VMEM((4, 18, 16, 384), jnp.bfloat16)],
        (volume, taps),
        2 * 1024 * 2304 * 256,
        24,
    )
    lane = np.arange(256)
    source = (lane // 64 + GROUP * (lane % 64 // chans)) * chans + lane % chans
    order = jnp.asarray(np.arange(256)[:, None] == source[None, :], jnp.bfloat16)
    ends = jnp.stack([place, n - 1 - place, odd, rank]).astype(jnp.int32)
    rise_part = call(
        lambda rank_ref, *refs: rise_stage(rank_ref, chans, *refs),
        bf16((n * chans, 512)),
        [],
        (marks, rise_kernel.reshape(8, n * chans, 256)),
        2 * 8 * n * chans * 256 * 64,
        16,
        scalars=1,
    )
    pooled_two, *skips = call(
        stem_stage,
        (bf16((n, 16, 256)),) + (bf16((32, 256)),) * GROUP,
        [
            pltpu.VMEM((6, 18, 16, 384), jnp.bfloat16),
            pltpu.VMEM((128, 128), jnp.float32),
            pltpu.VMEM((4, 10, 24, 128), jnp.float32),
            pltpu.VMEM((256, 1152), jnp.bfloat16),
            pltpu.VMEM((2, 32, 128), jnp.float32),
            pltpu.VMEM((GROUP, 32, 256), jnp.bfloat16),
        ],
        (ends, off_chip, on_chip, own, taps, second_kernel.reshape(3, 1152, 256), order, rise_part),
        2 * 1024 * 2304 * 256,
        24,
        scalars=1,
        unread=1,
    )
    pooled_whole = exchange(pooled_two, ALL)
    near = [skips[0]] + [
        lax.ppermute(skips[k], "r", [(r, r ^ k) for r in range(GROUP)]) for k in range(1, GROUP)
    ]
    blocks = pltpu.VMEM((GROUP, 32, 256), jnp.bfloat16)

    deep = call(
        deep_stage,
        bf16((n, chans, voxels)),
        [],
        (
            pooled_whole.reshape(voxels, 256),
            deep_kernel.transpose(0, 1, 2, 4, 3).reshape(27 * chans, 256),
            *near[1:],
        ),
        2 * 27 * chans * 256 * voxels,
        16,
        unread=GROUP - 1,
    )
    if shared:
        weights = (line, lax.ppermute(line[:, :336], "rep", [(0, 1), (1, 0)]))
    elif chans % 16:
        weights = line.reshape(planes, 27, chans, 256).transpose(1, 0, 2, 3)
        weights = (weights.reshape(1, 27 * 128, 256),)
    else:
        weights = (line,)
    swaps = call(
        edge_stage,
        (bf16((16, 256)), bf16((16, 256))),
        [blocks],
        (marks, *near),
        0,
        16,
        scalars=1,
    )
    near_pairs = [(p, p + 1) for p in range(0, planes - 1, 2)]
    far_pairs = [(p, p + 1) for p in range(1, planes - 1, 2)]
    near_swap = lax.ppermute(swaps[0], "z", near_pairs + [(j, i) for i, j in near_pairs])
    far_swap = lax.ppermute(swaps[1], "z", far_pairs + [(j, i) for i, j in far_pairs])
    deep_whole = exchange(deep, ALL).reshape(n * chans, voxels)

    deeper = call(
        deeper_stage,
        bf16((n, chans, 128)),
        [],
        (
            deep_whole,
            deeper_kernel.transpose(0, 1, 2, 4, 3).reshape(27 * chans, n * chans),
            near_swap,
            far_swap,
        ),
        2 * 27 * chans * n * chans * voxels,
        16,
        unread=2,
    )
    deeper_near = exchange(deeper, ALL).reshape(n * chans, 128)

    partial = call(
        decode_stage,
        bf16((512, 256)),
        [
            pltpu.VMEM((10, 10, 24, 128), jnp.float32),
            pltpu.VMEM((640, 1152), jnp.bfloat16),
            pltpu.VMEM((8, 128, 128), jnp.float32),
            blocks,
        ],
        (marks, deeper_near, rise_part, near_swap, far_swap, *near, *weights),
        2 * 512 * 3456 * 256,
        24,
        scalars=1,
    )
    partials = exchange(partial.reshape(GROUP, 128, 256), "r")
    out = call(
        final_stage,
        bf16((1024, 128)),
        [pltpu.VMEM((1024, 128), jnp.float32)],
        (partials, final_kernel.reshape(8, 256, 128)),
        2 * 128 * 256 * 1024,
        16,
    )
    return out.reshape(4, 16, 16, 128)


def solution(mesh):
    reps, n = mesh.devices.shape
    grid = jax.sharding.Mesh(mesh.devices.reshape(reps, n // GROUP, GROUP), ("rep",) + ALL)
    return jax.shard_map(
        body,
        mesh=grid,
        in_specs=(
            P(("rep",) + ALL, None, None, None),
            P(),
            P(),
            P(None, None, None, None, ALL),
            P(None, None, None, None, ALL),
            P(),
            P(None, None, None, ALL, None),
            P(),
        ),
        out_specs=P(("rep",) + ALL, None, None, None),
        check_vma=False,
    )
```

```python
import functools

import jax
import jax.numpy as jnp
import numpy as np
from jax import lax
from jax.experimental import pallas as pl
from jax.experimental.pallas import tpu as pltpu
from jax.sharding import PartitionSpec as P

GROUP = 4
MIB = 1024 * 1024


def call(kernel, outs, scratch, args, flops, vmem_mib, scalars=0, unread=0):
    spaces = [pltpu.SMEM] * scalars + [pltpu.VMEM] * (len(args) - scalars - unread)
    spaces += [pl.ANY] * unread
    return pl.pallas_call(
        kernel,
        out_shape=outs,
        in_specs=[pl.BlockSpec(memory_space=space) for space in spaces],
        out_specs=jax.tree.map(lambda _: pl.BlockSpec(memory_space=pltpu.VMEM), outs),
        scratch_shapes=scratch,
        compiler_params=pltpu.CompilerParams(vmem_limit_bytes=vmem_mib * MIB),
        cost_estimate=pl.CostEstimate(
            flops=flops,
            bytes_accessed=sum(a.size * a.dtype.itemsize for a in args[: len(args) - unread]),
            transcendentals=0,
        ),
    )(*args)


def dot(left, right, dims=((1,), (0,))):
    return lax.dot_general(left, right, (dims, ((), ())), preferred_element_type=jnp.float32)


def round_once(values):
    return values.astype(jnp.bfloat16).astype(jnp.float32)


def fill_patches(framed, patches, slices):
    for b in range(3):
        for c in range(3):
            tap = framed[:, b : b + 8, 7 + c : 15 + c, :].reshape(slices * 64, 128)
            col = (b * 3 + c) * 128
            patches[:, col : col + 128] = tap.astype(jnp.bfloat16)


def shift_slice(shifted, s, values):
    row = lax.broadcasted_iota(jnp.int32, (256, 128), 0) & 15
    here = values.reshape(256, 128).astype(jnp.float32)
    before = jnp.where(row == 0, 0.0, pltpu.roll(here, 1, 0))
    after = jnp.where(row == 15, 0.0, pltpu.roll(here, 255, 0))
    shifted[s, 0] = jnp.zeros((16, 384), jnp.bfloat16)
    shifted[s, 17] = jnp.zeros((16, 384), jnp.bfloat16)
    for c, tap in enumerate((before, here, after)):
        tap = tap.astype(jnp.bfloat16).reshape(16, 16, 128)
        shifted[s, 1:17, :, 128 * c : 128 * c + 128] = tap


def depth_pair(shifted, slices, weights, steps):
    left = jnp.concatenate(
        [shifted[s, b : b + 16].reshape(256, 384) for s in slices for b in range(3)], axis=1
    )
    none = jnp.zeros((1152, 128), jnp.bfloat16)
    right = [
        jnp.concatenate(
            [weights[j] if j < 3 else none, weights[j - 1] if j > 0 else none], axis=1
        )
        for j in steps
    ]
    return dot(left, jnp.concatenate(right, axis=0))


def depth_one(shifted, s, weights):
    left = jnp.concatenate([shifted[s, b : b + 16].reshape(256, 384) for b in range(3)], axis=1)
    return dot(left, weights)


def front_stage(marks, volume, decode, off_chip, on_chip, *refs):
    block, done = refs if len(refs) == 2 else (None, refs[0])
    odd, rep = marks[4], marks[1]
    pairs = [
        (volume.at[pl.ds(odd, 3)], off_chip),
        (volume.at[pl.ds(1 - odd, 3)], on_chip),
    ]
    if block is not None:
        pairs += [
            (decode.at[pl.ds(pl.multiple_of(528 * rep, 16), 336)], block.at[pl.ds(0, 336)]),
            (decode.at[pl.ds(336, 192)], block.at[pl.ds(336, 192)]),
        ]
    copies = [
        pltpu.make_async_copy(source, target, done.at[i]) for i, (source, target) in enumerate(pairs)
    ]
    for copy in copies:
        copy.start()
    for copy in copies:
        copy.wait()


def own_stage(volume, weights, out, shifted):
    for s in range(4):
        shift_slice(shifted, s, volume[s])
    out[0, :, :128] = jnp.zeros((256, 128), jnp.float32)
    out[0, :, 128:] = depth_one(shifted, 0, weights[2])
    out[1] = depth_pair(shifted, (0, 1, 2), weights, (1, 2, 3))
    out[2] = depth_pair(shifted, (1, 2, 3), weights, (0, 1, 2))
    out[3, :, :128] = depth_one(shifted, 3, weights[0])
    out[3, :, 128:] = jnp.zeros((256, 128), jnp.float32)


def stem_stage(marks, off_chip, on_chip, own, weights, second, order, _, *refs):
    pooled_out, skip_outs = refs[0], refs[1 : 1 + GROUP]
    shifted, halves, framed, patches, quarters, blocks = refs[1 + GROUP :]
    for s in range(3):
        even = marks[4] == 0
        shift_slice(shifted, s, jnp.where(even, off_chip[s], on_chip[s]))
        shift_slice(shifted, 3 + s, jnp.where(even, on_chip[s], off_chip[s]))
    framed[...] = jnp.zeros(framed.shape, jnp.float32)
    for m in range(4):
        if m == 0:
            first = own[0] + depth_pair(shifted, (0, 1, 2), weights, (0, 1, 2))
        elif m == 3:
            first = own[3] + depth_pair(shifted, (3, 4, 5), weights, (1, 2, 3))
        elif m == 1:
            near = own[1, :, :128] + depth_one(shifted, 2, weights[0])
            first = jnp.concatenate([near, own[1, :, 128:]], axis=1)
        else:
            far = own[2, :, 128:] + depth_one(shifted, 3, weights[2])
            first = jnp.concatenate([own[2, :, :128], far], axis=1)
        first = round_once(jnp.maximum(first, 0.0))
        pair = (first[:, :128] + first[:, 128:]).reshape(8, 32, 128)
        halves[...] = (pair[:, :16] + pair[:, 16:]).reshape(128, 128)
        pooled = halves[pl.ds(0, 64, stride=2), :] + halves[pl.ds(1, 64, stride=2), :]
        pooled = round_once(pooled * 0.125)
        if m == 0:
            pooled = jnp.where(marks[5] == 0, 0.0, pooled)
        if m == 3:
            pooled = jnp.where(marks[6] == 0, 0.0, pooled)
        framed[m, 1:9, 8:16, :] = pooled.reshape(8, 8, 128)
    fill_patches(framed, patches, 4)
    skip = dot(patches[0:128], second[0])
    skip += dot(patches[64:192], second[1])
    skip += dot(patches[128:256], second[2])
    skip = jnp.maximum(skip, 0.0).astype(jnp.bfloat16)
    wide = skip.astype(jnp.float32)
    pair = (wide[:64] + wide[64:]).reshape(4, 16, 256)
    pair = (pair[:, :8] + pair[:, 8:]).reshape(32, 256)
    for k in range(2):
        quarters[k] = pair[:, 128 * k : 128 * k + 128]
    pooled = jnp.concatenate(
        [
            quarters[k, pl.ds(0, 16, stride=2), :] + quarters[k, pl.ds(1, 16, stride=2), :]
            for k in range(2)
        ],
        axis=1,
    )
    pooled = (pooled * 0.125).astype(jnp.bfloat16)
    for p in range(pooled_out.shape[0]):
        pooled_out[p] = pooled
    sorted_skip = dot(skip, order[...])
    for r in range(GROUP):
        near, far = sorted_skip[:64, 64 * r : 64 * r + 64], sorted_skip[64:, 64 * r : 64 * r + 64]
        block = jnp.concatenate([near, far], axis=1)
        block = jnp.concatenate([block[:32], block[32:]], axis=1).astype(jnp.bfloat16)
        blocks[r, 0:32, :] = block
        first, last = sorted_skip[16 * r : 16 * r + 16], sorted_skip[64 + 16 * r : 80 + 16 * r]
        blocks[r, 32:48, :] = jnp.where(marks[0] == 0, first, last).astype(jnp.bfloat16)
    for k in range(GROUP):
        skip_outs[k][...] = blocks[marks[0] ^ k]


def edge_slice(block, far):
    lower = lax.broadcasted_iota(jnp.int32, (16, 128), 1) < 64
    sides = []
    for k in range(2):
        half = block[:, 128 * k : 128 * k + 128].astype(jnp.float32)
        top, bottom = half[:16], half[16:]
        if far:
            top = pltpu.roll(top, 64, 1)
        else:
            bottom = pltpu.roll(bottom, 64, 1)
        sides.append(jnp.where(lower, top, bottom))
    return jnp.concatenate(sides, axis=1)


def spread_taps(weights, values, dims, chans, voxels):
    lane = lax.broadcasted_iota(jnp.int32, (chans, voxels), 1)

    def moved(term, tap, step, place, last):
        if tap == 1:
            return term
        keep = place > 0 if tap == 0 else place < last
        return jnp.where(keep, pltpu.roll(term, ((1 - tap) * step) % voxels, 1), 0.0)

    total = None
    for a in range(3):
        products = dot(weights[a * 9 * chans : (a + 1) * 9 * chans, :], values, dims)
        plane = None
        for b in range(3):
            line = None
            for c in range(3):
                at = (b * 3 + c) * chans
                term = moved(products[at : at + chans], c, 1, lane & 3, 3)
                line = term if line is None else line + term
            line = moved(line, b, 4, (lane >> 2) & 3, 3)
            plane = line if plane is None else plane + line
        plane = moved(plane, a, 16, lane >> 4, voxels // 16 - 1)
        total = plane if total is None else total + plane
    return jnp.maximum(total, 0.0)


def by_rank(marks, near, blocks):
    for k in range(GROUP):
        blocks[marks[0] ^ k] = near[k][...]


def edge_stage(marks, *refs):
    near, (near_swap, far_swap, blocks) = refs[:GROUP], refs[GROUP:]
    by_rank(marks, near, blocks)
    first = edge_slice(blocks[0, 0:32, :], False)
    last = edge_slice(blocks[GROUP - 1, 0:32, :], True)
    even = marks[2] == 0
    near_swap[...] = jnp.where(even, last, first).astype(jnp.bfloat16)
    far_swap[...] = jnp.where(even, first, last).astype(jnp.bfloat16)


def deep_stage(pooled, weights, *refs):
    out = refs[-1]
    n, chans, voxels = out.shape
    deep = spread_taps(weights, pooled[...], ((1,), (1,)), chans, voxels).astype(jnp.bfloat16)
    for dest in range(n):
        out[dest] = deep


def deeper_stage(marks, deep, weights, *refs):
    near, out, blocks = refs[:-2], refs[-2], refs[-1]
    n, chans, _ = out.shape
    voxels = deep.shape[1]
    deeper = spread_taps(weights, deep[...], ((1,), (0,)), chans, voxels)
    lane = lax.broadcasted_iota(jnp.int32, (chans, 128), 1)
    planes = n // GROUP
    ride = len(near) == GROUP
    if ride:
        by_rank(marks, near, blocks)
        edges = [blocks[r, 32:48, :].astype(jnp.float32) for r in (0, GROUP - 1)]
        riders = [
            [
                jnp.concatenate(
                    [
                        pltpu.roll(edge[:, at // 128 * 128 : at // 128 * 128 + 128], (96 - at) % 128, 1)
                        for at in (64 * r, 64 * r + 32)
                    ],
                    axis=0,
                )
                for r in range(GROUP)
            ]
            for edge in edges
        ]
    for p in range(planes):
        part = pltpu.roll(deeper, (16 - 64 * p) % voxels, 1)[:, :128]
        if p == 0:
            part = jnp.where(lane < 16, 0.0, part)
        if p == planes - 1:
            part = jnp.where(lane >= 80, 0.0, part)
        for r in range(GROUP):
            whole = part
            if ride:
                rider = jnp.where(marks[3] < p, riders[1][r], riders[0][r])
                whole = jnp.where(lane < 96, part, rider)
            out[GROUP * p + r] = whole.astype(jnp.bfloat16)


def rise_stage(marks, chans, rise, out):
    lane = lax.broadcasted_iota(jnp.int32, (256, 64), 1)
    row = lax.broadcasted_iota(jnp.int32, (256, 64), 0)
    source = (marks[0] + GROUP * (lane // chans)) * chans + lane % chans
    mine = jnp.where(row == source, 1.0, 0.0).astype(jnp.bfloat16)
    for pair in range(4):
        both = [dot(rise[2 * pair + k], mine) for k in range(2)]
        both = jnp.concatenate(both, axis=1).astype(jnp.bfloat16)
        out[:, 128 * pair : 128 * pair + 128] = both


def decode_stage(ride, marks, deeper, rise, *refs):
    swaps = () if ride else refs[:2]
    near, refs = refs[len(swaps) : len(swaps) + GROUP], refs[len(swaps) + GROUP :]
    *decode, out, framed, patches, risen, blocks = refs
    by_rank(marks, near, blocks)
    n, chans, _ = deeper.shape
    plane, planes = marks[3], n // GROUP
    upper = lax.broadcasted_iota(jnp.int32, (64, 128), 1) >= 64

    def edge(low):
        if not ride:
            even = marks[2] == 0
            sides = [swap[...].astype(jnp.float32) for swap in swaps]
            side = jnp.where(even, sides[low], sides[not low])
            parts = []
            for k in range(2):
                half = side[:, 128 * k : 128 * k + 128]
                parts += [pltpu.roll(half, 64, 1), half]
            return jnp.concatenate(parts, axis=0)
        other = jnp.maximum(plane - 1, 0) if low else jnp.minimum(plane + 1, planes - 1)
        lane = lax.broadcasted_iota(jnp.int32, (16, 128), 1)
        parts = []
        for r in range(GROUP):
            block = deeper[GROUP * other + r].astype(jnp.float32)
            parts.append(jnp.where(lane < 96, pltpu.roll(block[:16], 96, 1), block[16:]))
        return jnp.where(other == plane, 0.0, jnp.concatenate(parts, axis=0))

    framed[...] = jnp.zeros(framed.shape, jnp.float32)
    spread = round_once(dot(deeper[...].reshape(n * chans, 128).astype(jnp.float32).T.astype(jnp.bfloat16), rise[...]))
    for pair in range(4):
        both = spread[:, 128 * pair : 128 * pair + 128]
        risen[2 * pair] = both
        risen[2 * pair + 1] = pltpu.roll(both, 64, 1)
    for s in range(10):
        d, a = (s + 1) // 2, (s + 1) % 2
        for h in range(4):
            for b in range(2):
                for c in range(2):
                    framed[s, 1 + 2 * h + b, pl.ds(8 + c, 4, stride=2), :] = risen[
                        4 * a + 2 * b + c, 16 * d + 4 * h : 16 * d + 4 * h + 4, :
                    ]
        if s == 0 or s == 9:
            skip = edge(s == 0)
        else:
            both = blocks[(s - 1) // 2, 0:32, :].astype(jnp.float32)
            skip = jnp.concatenate([both[:, :128], both[:, 128:]], axis=0)
            if (s - 1) % 2 == 0:
                skip = pltpu.roll(skip, 64, 1)
        joined = framed[s, 1:9, 8:16, :].reshape(64, 128)
        framed[s, 1:9, 8:16, :] = jnp.where(upper, skip, joined).reshape(8, 8, 128)
    fill_patches(framed, patches, 10)
    def rows_at(rep, z, row):
        if rep == 0 and row >= 528:
            return decode[1][z, row - 528 : row - 512, :]
        if rep == 1 and row < 336:
            return decode[1][z, row : row + 16, :]
        if rep == 1 and row >= 528:
            row -= 528
        return decode[0][z, row : row + 16, :]

    def multiply(rep):
        count = decode[0].shape[0]
        step = 128 // count
        partial = None
        for a in range(3):
            right = [
                rows_at(rep, z, row)
                for tap in range(9 * a, 9 * a + 9)
                for z in range(count)
                for row in range(tap * step, (tap + 1) * step, 16)
            ]
            term = dot(patches[64 * a : 64 * a + 512], jnp.concatenate(right, axis=0))
            partial = term if partial is None else partial + term
        out[...] = partial.astype(jnp.bfloat16)

    if len(decode) == 1:
        multiply(None)
    else:
        pl.when(marks[1] == 0)(lambda: multiply(0))
        pl.when(marks[1] == 1)(lambda: multiply(1))


def final_stage(partials, weights, out, spaced):
    decoded = partials[0].astype(jnp.float32)
    for g in range(1, GROUP):
        decoded += partials[g].astype(jnp.float32)
    decoded = jnp.maximum(decoded, 0.0).astype(jnp.bfloat16)
    for a in range(2):
        for b in range(2):
            for c in range(2):
                values = dot(decoded, weights[4 * a + 2 * b + c])
                for d in range(2):
                    for h in range(8):
                        at = ((2 * d + a) * 16 + 2 * h + b) * 16 + c
                        spaced[pl.ds(at, 8, stride=2), :] = values[64 * d + 8 * h : 64 * d + 8 * h + 8]
    out[...] = spaced[...].astype(jnp.bfloat16)


ALL = ("z", "r")


def exchange(payload, axis):
    return lax.all_to_all(payload, axis, split_axis=0, concat_axis=0, tiled=True)


def body(
    volume,
    first_kernel,
    second_kernel,
    deep_kernel,
    deeper_kernel,
    rise_kernel,
    decode_kernel,
    final_kernel,
):
    n = lax.axis_size(ALL)
    place = lax.axis_index(ALL)
    planes = n // GROUP
    rank = lax.axis_index("r")
    chans = deep_kernel.shape[4]
    voxels = 16 * n
    bf16 = functools.partial(jax.ShapeDtypeStruct, dtype=jnp.bfloat16)

    rep, plane = lax.axis_index("rep"), lax.axis_index("z")
    marks = jnp.stack([rank, rep, plane % 2, plane, place % 2, place, n - 1 - place])
    marks = marks.astype(jnp.int32)
    decode_block = decode_kernel.reshape(27 * chans, 256)
    shared = lax.axis_size("rep") == 2 and chans == 32
    ride = chans == 32
    halo = bf16((3, 16, 16, 128))
    off_chip, on_chip, *share = pl.pallas_call(
        front_stage,
        out_shape=(halo, halo) + ((bf16((528, 256)),) if shared else ()),
        in_specs=[pl.BlockSpec(memory_space=pltpu.SMEM)] + [pl.BlockSpec(memory_space=pl.ANY)] * 2,
        out_specs=(pl.BlockSpec(memory_space=pl.ANY),) * (3 if shared else 2),
        scratch_shapes=[pltpu.SemaphoreType.DMA((4,))],
        compiler_params=pltpu.CompilerParams(vmem_limit_bytes=60 * MIB),
    )(marks, volume, decode_block)
    pairs = [(i, i + 1) for i in range(1, n - 1, 2)]
    off_chip = lax.ppermute(off_chip, ALL, pairs + [(j, i) for i, j in pairs])
    on_chip = lax.ppermute(on_chip, ALL, [(i, i ^ 1) for i in range(n)])
    if shared:
        decode_block = share[0]
    line = lax.all_gather(decode_block, "z", axis=0)

    pairs = [(i, i + 1) for i in range(1, n - 1, 2)]
    taps = first_kernel.reshape(3, 1152, 128)
    own = call(
        own_stage,
        jax.ShapeDtypeStruct((4, 256, 256), jnp.float32),
        [pltpu.VMEM((4, 18, 16, 384), jnp.bfloat16)],
        (volume, taps),
        2 * 1024 * 2304 * 256,
        24,
    )
    lane = np.arange(256)
    source = (lane // 64 + GROUP * (lane % 64 // chans)) * chans + lane % chans
    order = jnp.asarray(np.arange(256)[:, None] == source[None, :], jnp.bfloat16)
    rise_part = call(
        lambda marks_ref, *refs: rise_stage(marks_ref, chans, *refs),
        bf16((n * chans, 512)),
        [],
        (marks, rise_kernel.reshape(8, n * chans, 256)),
        2 * 8 * n * chans * 256 * 64,
        16,
        scalars=1,
    )
    pooled_two, *skips = call(
        stem_stage,
        (bf16((n, 16, 256)),) + (bf16((48, 256)),) * GROUP,
        [
            pltpu.VMEM((6, 18, 16, 384), jnp.bfloat16),
            pltpu.VMEM((128, 128), jnp.float32),
            pltpu.VMEM((4, 10, 24, 128), jnp.float32),
            pltpu.VMEM((256, 1152), jnp.bfloat16),
            pltpu.VMEM((2, 32, 128), jnp.float32),
            pltpu.VMEM((GROUP, 48, 256), jnp.bfloat16),
        ],
        (marks, off_chip, on_chip, own, taps, second_kernel.reshape(3, 1152, 256), order, rise_part),
        2 * 1024 * 2304 * 256,
        24,
        scalars=1,
        unread=1,
    )
    pooled_whole = exchange(pooled_two, ALL)
    near = [skips[0]] + [
        lax.ppermute(skips[k], "r", [(r, r ^ k) for r in range(GROUP)]) for k in range(1, GROUP)
    ]
    blocks = pltpu.VMEM((GROUP, 48, 256), jnp.bfloat16)

    deep = call(
        deep_stage,
        bf16((n, chans, voxels)),
        [],
        (
            pooled_whole.reshape(voxels, 256),
            deep_kernel.transpose(0, 1, 2, 4, 3).reshape(27 * chans, 256),
            *near[1:],
        ),
        2 * 27 * chans * 256 * voxels,
        16,
        unread=GROUP - 1,
    )
    if shared:
        weights = (line, lax.ppermute(line[:, :336], "rep", [(0, 1), (1, 0)]))
    elif chans % 16:
        weights = line.reshape(planes, 27, chans, 256).transpose(1, 0, 2, 3)
        weights = (weights.reshape(1, 27 * 128, 256),)
    else:
        weights = (line,)
    swaps = ()
    if not ride:
        swaps = call(
            edge_stage,
            (bf16((16, 256)), bf16((16, 256))),
            [blocks],
            (marks, *near),
            0,
            16,
            scalars=1,
        )
        near_pairs = [(p, p + 1) for p in range(0, planes - 1, 2)]
        far_pairs = [(p, p + 1) for p in range(1, planes - 1, 2)]
        near_swap = lax.ppermute(swaps[0], "z", near_pairs + [(j, i) for i, j in near_pairs])
        far_swap = lax.ppermute(swaps[1], "z", far_pairs + [(j, i) for i, j in far_pairs])
        swaps = (near_swap, far_swap)
    deep_whole = exchange(deep, ALL).reshape(n * chans, voxels)

    deeper = call(
        deeper_stage,
        bf16((n, chans, 128)),
        [blocks],
        (
            marks,
            deep_whole,
            deeper_kernel.transpose(0, 1, 2, 4, 3).reshape(27 * chans, n * chans),
            *(near if ride else ()),
        ),
        2 * 27 * chans * n * chans * voxels,
        16,
        scalars=1,
    )
    deeper_near = exchange(deeper, ALL)

    partial = call(
        functools.partial(decode_stage, ride),
        bf16((512, 256)),
        [
            pltpu.VMEM((10, 10, 24, 128), jnp.float32),
            pltpu.VMEM((640, 1152), jnp.bfloat16),
            pltpu.VMEM((8, 128, 128), jnp.float32),
            blocks,
        ],
        (marks, deeper_near, rise_part, *swaps, *near, *weights),
        2 * 512 * 3456 * 256,
        24,
        scalars=1,
    )
    partials = exchange(partial.reshape(GROUP, 128, 256), "r")
    out = call(
        final_stage,
        bf16((1024, 128)),
        [pltpu.VMEM((1024, 128), jnp.float32)],
        (partials, final_kernel.reshape(8, 256, 128)),
        2 * 128 * 256 * 1024,
        16,
    )
    return out.reshape(4, 16, 16, 128)


def solution(mesh):
    reps, n = mesh.devices.shape
    grid = jax.sharding.Mesh(mesh.devices.reshape(reps, n // GROUP, GROUP), ("rep",) + ALL)
    return jax.shard_map(
        body,
        mesh=grid,
        in_specs=(
            P(("rep",) + ALL, None, None, None),
            P(),
            P(),
            P(None, None, None, None, ALL),
            P(None, None, None, None, ALL),
            P(),
            P(None, None, None, ALL, None),
            P(),
        ),
        out_specs=P(("rep",) + ALL, None, None, None),
        check_vma=False,
    )
```

```python
import functools

import jax
import jax.numpy as jnp
import numpy as np
from jax import lax
from jax.experimental import pallas as pl
from jax.experimental.pallas import tpu as pltpu
from jax.sharding import PartitionSpec as P

GROUP = 4
MIB = 1024 * 1024


def call(kernel, outs, scratch, args, flops, vmem_mib, scalars=0, unread=0):
    spaces = [pltpu.SMEM] * scalars + [pltpu.VMEM] * (len(args) - scalars - unread)
    spaces += [pl.ANY] * unread
    return pl.pallas_call(
        kernel,
        out_shape=outs,
        in_specs=[pl.BlockSpec(memory_space=space) for space in spaces],
        out_specs=jax.tree.map(lambda _: pl.BlockSpec(memory_space=pltpu.VMEM), outs),
        scratch_shapes=scratch,
        compiler_params=pltpu.CompilerParams(vmem_limit_bytes=vmem_mib * MIB),
        cost_estimate=pl.CostEstimate(
            flops=flops,
            bytes_accessed=sum(a.size * a.dtype.itemsize for a in args[: len(args) - unread]),
            transcendentals=0,
        ),
    )(*args)


def dot(left, right, dims=((1,), (0,))):
    return lax.dot_general(left, right, (dims, ((), ())), preferred_element_type=jnp.float32)


def round_once(values):
    return values.astype(jnp.bfloat16).astype(jnp.float32)


def fill_patches(framed, patches, slices):
    for b in range(3):
        for c in range(3):
            tap = framed[:, b : b + 8, 7 + c : 15 + c, :].reshape(slices * 64, 128)
            col = (b * 3 + c) * 128
            patches[:, col : col + 128] = tap.astype(jnp.bfloat16)


def shift_slice(shifted, s, values):
    row = lax.broadcasted_iota(jnp.int32, (256, 128), 0) & 15
    here = values.reshape(256, 128).astype(jnp.float32)
    before = jnp.where(row == 0, 0.0, pltpu.roll(here, 1, 0))
    after = jnp.where(row == 15, 0.0, pltpu.roll(here, 255, 0))
    shifted[s, 0] = jnp.zeros((16, 384), jnp.bfloat16)
    shifted[s, 17] = jnp.zeros((16, 384), jnp.bfloat16)
    for c, tap in enumerate((before, here, after)):
        tap = tap.astype(jnp.bfloat16).reshape(16, 16, 128)
        shifted[s, 1:17, :, 128 * c : 128 * c + 128] = tap


def depth_pair(shifted, slices, weights, steps):
    left = jnp.concatenate(
        [shifted[s, b : b + 16].reshape(256, 384) for s in slices for b in range(3)], axis=1
    )
    none = jnp.zeros((1152, 128), jnp.bfloat16)
    right = [
        jnp.concatenate(
            [weights[j] if j < 3 else none, weights[j - 1] if j > 0 else none], axis=1
        )
        for j in steps
    ]
    return dot(left, jnp.concatenate(right, axis=0))


def depth_one(shifted, s, weights):
    left = jnp.concatenate([shifted[s, b : b + 16].reshape(256, 384) for b in range(3)], axis=1)
    return dot(left, weights)


def front_stage(odd, rep, volume, decode, off_chip, on_chip, whole, *refs):
    copies = []
    if len(refs) == 2:
        block, done = refs
        at = pl.multiple_of(528 * rep[0], 16)
        copies = [
            pltpu.make_async_copy(decode.at[pl.ds(at, 336)], block.at[pl.ds(0, 336)], done.at[0]),
            pltpu.make_async_copy(
                decode.at[pl.ds(336, 192)], block.at[pl.ds(336, 192)], done.at[1]
            ),
        ]
    for copy in copies:
        copy.start()
    for s in range(3):
        off_chip[s] = jnp.where(odd[0] == 0, volume[s], volume[s + 1])
        on_chip[s] = jnp.where(odd[0] == 0, volume[s + 1], volume[s])
    whole[...] = volume[...]
    for copy in copies:
        copy.wait()


def own_stage(volume, weights, out, shifted):
    for s in range(4):
        shift_slice(shifted, s, volume[s])
    out[0, :, :128] = jnp.zeros((256, 128), jnp.float32)
    out[0, :, 128:] = depth_one(shifted, 0, weights[2])
    out[1] = depth_pair(shifted, (0, 1, 2), weights, (1, 2, 3))
    out[2] = depth_pair(shifted, (1, 2, 3), weights, (0, 1, 2))
    out[3, :, :128] = depth_one(shifted, 3, weights[0])
    out[3, :, 128:] = jnp.zeros((256, 128), jnp.float32)


def stem_stage(marks, off_chip, on_chip, own, weights, second, order, _, *refs):
    pooled_out, skip_outs = refs[0], refs[1 : 1 + GROUP]
    shifted, halves, framed, patches, quarters, blocks = refs[1 + GROUP :]
    for s in range(3):
        even = marks[4] == 0
        shift_slice(shifted, s, jnp.where(even, off_chip[s], on_chip[s]))
        shift_slice(shifted, 3 + s, jnp.where(even, on_chip[s], off_chip[s]))
    framed[...] = jnp.zeros(framed.shape, jnp.float32)
    for m in range(4):
        if m == 0:
            first = own[0] + depth_pair(shifted, (0, 1, 2), weights, (0, 1, 2))
        elif m == 3:
            first = own[3] + depth_pair(shifted, (3, 4, 5), weights, (1, 2, 3))
        elif m == 1:
            near = own[1, :, :128] + depth_one(shifted, 2, weights[0])
            first = jnp.concatenate([near, own[1, :, 128:]], axis=1)
        else:
            far = own[2, :, 128:] + depth_one(shifted, 3, weights[2])
            first = jnp.concatenate([own[2, :, :128], far], axis=1)
        first = round_once(jnp.maximum(first, 0.0))
        pair = (first[:, :128] + first[:, 128:]).reshape(8, 32, 128)
        halves[...] = (pair[:, :16] + pair[:, 16:]).reshape(128, 128)
        pooled = halves[pl.ds(0, 64, stride=2), :] + halves[pl.ds(1, 64, stride=2), :]
        pooled = round_once(pooled * 0.125)
        if m == 0:
            pooled = jnp.where(marks[5] == 0, 0.0, pooled)
        if m == 3:
            pooled = jnp.where(marks[6] == 0, 0.0, pooled)
        framed[m, 1:9, 8:16, :] = pooled.reshape(8, 8, 128)
    fill_patches(framed, patches, 4)
    skip = dot(patches[0:128], second[0])
    skip += dot(patches[64:192], second[1])
    skip += dot(patches[128:256], second[2])
    skip = jnp.maximum(skip, 0.0).astype(jnp.bfloat16)
    wide = skip.astype(jnp.float32)
    pair = (wide[:64] + wide[64:]).reshape(4, 16, 256)
    pair = (pair[:, :8] + pair[:, 8:]).reshape(32, 256)
    for k in range(2):
        quarters[k] = pair[:, 128 * k : 128 * k + 128]
    pooled = jnp.concatenate(
        [
            quarters[k, pl.ds(0, 16, stride=2), :] + quarters[k, pl.ds(1, 16, stride=2), :]
            for k in range(2)
        ],
        axis=1,
    )
    pooled = (pooled * 0.125).astype(jnp.bfloat16)
    for p in range(pooled_out.shape[0]):
        pooled_out[p] = pooled
    sorted_skip = dot(skip, order[...])
    for r in range(GROUP):
        near, far = sorted_skip[:64, 64 * r : 64 * r + 64], sorted_skip[64:, 64 * r : 64 * r + 64]
        block = jnp.concatenate([near, far], axis=1)
        block = jnp.concatenate([block[:32], block[32:]], axis=1).astype(jnp.bfloat16)
        blocks[r, 0:32, :] = block
        first, last = sorted_skip[16 * r : 16 * r + 16], sorted_skip[64 + 16 * r : 80 + 16 * r]
        blocks[r, 32:48, :] = jnp.where(marks[0] == 0, first, last).astype(jnp.bfloat16)
    for k in range(GROUP):
        skip_outs[k][...] = blocks[marks[0] ^ k]


def edge_slice(block, far):
    lower = lax.broadcasted_iota(jnp.int32, (16, 128), 1) < 64
    sides = []
    for k in range(2):
        half = block[:, 128 * k : 128 * k + 128].astype(jnp.float32)
        top, bottom = half[:16], half[16:]
        if far:
            top = pltpu.roll(top, 64, 1)
        else:
            bottom = pltpu.roll(bottom, 64, 1)
        sides.append(jnp.where(lower, top, bottom))
    return jnp.concatenate(sides, axis=1)


def spread_taps(weights, values, dims, chans, voxels):
    lane = lax.broadcasted_iota(jnp.int32, (chans, voxels), 1)

    def moved(term, tap, step, place, last):
        if tap == 1:
            return term
        keep = place > 0 if tap == 0 else place < last
        return jnp.where(keep, pltpu.roll(term, ((1 - tap) * step) % voxels, 1), 0.0)

    total = None
    for a in range(3):
        products = dot(weights[a * 9 * chans : (a + 1) * 9 * chans, :], values, dims)
        plane = None
        for b in range(3):
            line = None
            for c in range(3):
                at = (b * 3 + c) * chans
                term = moved(products[at : at + chans], c, 1, lane & 3, 3)
                line = term if line is None else line + term
            line = moved(line, b, 4, (lane >> 2) & 3, 3)
            plane = line if plane is None else plane + line
        plane = moved(plane, a, 16, lane >> 4, voxels // 16 - 1)
        total = plane if total is None else total + plane
    return jnp.maximum(total, 0.0)


def by_rank(marks, near, blocks):
    for k in range(GROUP):
        blocks[marks[0] ^ k] = near[k][...]


def edge_stage(marks, *refs):
    near, (near_swap, far_swap, blocks) = refs[:GROUP], refs[GROUP:]
    by_rank(marks, near, blocks)
    first = edge_slice(blocks[0, 0:32, :], False)
    last = edge_slice(blocks[GROUP - 1, 0:32, :], True)
    even = marks[2] == 0
    near_swap[...] = jnp.where(even, last, first).astype(jnp.bfloat16)
    far_swap[...] = jnp.where(even, first, last).astype(jnp.bfloat16)


def deep_stage(pooled, weights, *refs):
    out = refs[-1]
    n, chans, voxels = out.shape
    deep = spread_taps(weights, pooled[...], ((1,), (1,)), chans, voxels).astype(jnp.bfloat16)
    for dest in range(n):
        out[dest] = deep


def deeper_stage(marks, deep, weights, *refs):
    near, out, blocks = refs[:-2], refs[-2], refs[-1]
    n, chans, _ = out.shape
    voxels = deep.shape[1]
    deeper = spread_taps(weights, deep[...], ((1,), (0,)), chans, voxels)
    lane = lax.broadcasted_iota(jnp.int32, (chans, 128), 1)
    planes = n // GROUP
    ride = len(near) == GROUP
    if ride:
        by_rank(marks, near, blocks)
        edges = [blocks[r, 32:48, :].astype(jnp.float32) for r in (0, GROUP - 1)]
        riders = [
            [
                jnp.concatenate(
                    [
                        pltpu.roll(edge[:, at // 128 * 128 : at // 128 * 128 + 128], (96 - at) % 128, 1)
                        for at in (64 * r, 64 * r + 32)
                    ],
                    axis=0,
                )
                for r in range(GROUP)
            ]
            for edge in edges
        ]
    for p in range(planes):
        part = pltpu.roll(deeper, (16 - 64 * p) % voxels, 1)[:, :128]
        if p == 0:
            part = jnp.where(lane < 16, 0.0, part)
        if p == planes - 1:
            part = jnp.where(lane >= 80, 0.0, part)
        for r in range(GROUP):
            whole = part
            if ride:
                rider = jnp.where(marks[3] < p, riders[1][r], riders[0][r])
                whole = jnp.where(lane < 96, part, rider)
            out[GROUP * p + r] = whole.astype(jnp.bfloat16)


def rise_stage(marks, chans, rise, out):
    lane = lax.broadcasted_iota(jnp.int32, (256, 64), 1)
    row = lax.broadcasted_iota(jnp.int32, (256, 64), 0)
    source = (marks[0] + GROUP * (lane // chans)) * chans + lane % chans
    mine = jnp.where(row == source, 1.0, 0.0).astype(jnp.bfloat16)
    for pair in range(4):
        both = [dot(rise[2 * pair + k], mine) for k in range(2)]
        both = jnp.concatenate(both, axis=1).astype(jnp.bfloat16)
        out[:, 128 * pair : 128 * pair + 128] = both


def decode_stage(ride, marks, deeper, rise, *refs):
    swaps = () if ride else refs[:2]
    near, refs = refs[len(swaps) : len(swaps) + GROUP], refs[len(swaps) + GROUP :]
    *decode, out, framed, patches, risen, blocks = refs
    by_rank(marks, near, blocks)
    n, chans, _ = deeper.shape
    plane, planes = marks[3], n // GROUP
    upper = lax.broadcasted_iota(jnp.int32, (64, 128), 1) >= 64

    def edge(low):
        if not ride:
            even = marks[2] == 0
            sides = [swap[...].astype(jnp.float32) for swap in swaps]
            side = jnp.where(even, sides[low], sides[not low])
            parts = []
            for k in range(2):
                half = side[:, 128 * k : 128 * k + 128]
                parts += [pltpu.roll(half, 64, 1), half]
            return jnp.concatenate(parts, axis=0)
        other = jnp.maximum(plane - 1, 0) if low else jnp.minimum(plane + 1, planes - 1)
        lane = lax.broadcasted_iota(jnp.int32, (16, 128), 1)
        parts = []
        for r in range(GROUP):
            block = deeper[GROUP * other + r].astype(jnp.float32)
            parts.append(jnp.where(lane < 96, pltpu.roll(block[:16], 96, 1), block[16:]))
        return jnp.where(other == plane, 0.0, jnp.concatenate(parts, axis=0))

    framed[...] = jnp.zeros(framed.shape, jnp.float32)
    spread = round_once(dot(deeper[...].reshape(n * chans, 128).astype(jnp.float32).T.astype(jnp.bfloat16), rise[...]))
    for pair in range(4):
        both = spread[:, 128 * pair : 128 * pair + 128]
        risen[2 * pair] = both
        risen[2 * pair + 1] = pltpu.roll(both, 64, 1)
    for s in range(10):
        d, a = (s + 1) // 2, (s + 1) % 2
        for h in range(4):
            for b in range(2):
                for c in range(2):
                    framed[s, 1 + 2 * h + b, pl.ds(8 + c, 4, stride=2), :] = risen[
                        4 * a + 2 * b + c, 16 * d + 4 * h : 16 * d + 4 * h + 4, :
                    ]
        if s == 0 or s == 9:
            skip = edge(s == 0)
        else:
            both = blocks[(s - 1) // 2, 0:32, :].astype(jnp.float32)
            skip = jnp.concatenate([both[:, :128], both[:, 128:]], axis=0)
            if (s - 1) % 2 == 0:
                skip = pltpu.roll(skip, 64, 1)
        joined = framed[s, 1:9, 8:16, :].reshape(64, 128)
        framed[s, 1:9, 8:16, :] = jnp.where(upper, skip, joined).reshape(8, 8, 128)
    fill_patches(framed, patches, 10)
    def rows_at(rep, z, row):
        if rep == 0 and row >= 528:
            return decode[1][z, row - 528 : row - 512, :]
        if rep == 1 and row < 336:
            return decode[1][z, row : row + 16, :]
        if rep == 1 and row >= 528:
            row -= 528
        return decode[0][z, row : row + 16, :]

    def multiply(rep):
        count = decode[0].shape[0]
        step = 128 // count
        partial = None
        for a in range(3):
            right = [
                rows_at(rep, z, row)
                for tap in range(9 * a, 9 * a + 9)
                for z in range(count)
                for row in range(tap * step, (tap + 1) * step, 16)
            ]
            term = dot(patches[64 * a : 64 * a + 512], jnp.concatenate(right, axis=0))
            partial = term if partial is None else partial + term
        out[...] = partial.astype(jnp.bfloat16)

    if len(decode) == 1:
        multiply(None)
    else:
        pl.when(marks[1] == 0)(lambda: multiply(0))
        pl.when(marks[1] == 1)(lambda: multiply(1))


def final_stage(partials, weights, out, spaced):
    decoded = partials[0].astype(jnp.float32)
    for g in range(1, GROUP):
        decoded += partials[g].astype(jnp.float32)
    decoded = jnp.maximum(decoded, 0.0).astype(jnp.bfloat16)
    for a in range(2):
        for b in range(2):
            for c in range(2):
                values = dot(decoded, weights[4 * a + 2 * b + c])
                for d in range(2):
                    for h in range(8):
                        at = ((2 * d + a) * 16 + 2 * h + b) * 16 + c
                        spaced[pl.ds(at, 8, stride=2), :] = values[64 * d + 8 * h : 64 * d + 8 * h + 8]
    out[...] = spaced[...].astype(jnp.bfloat16)


ALL = ("z", "r")


def exchange(payload, axis):
    return lax.all_to_all(payload, axis, split_axis=0, concat_axis=0, tiled=True)


def body(
    volume,
    first_kernel,
    second_kernel,
    deep_kernel,
    deeper_kernel,
    rise_kernel,
    decode_kernel,
    final_kernel,
):
    n = lax.axis_size(ALL)
    place = lax.axis_index(ALL)
    planes = n // GROUP
    rank = lax.axis_index("r")
    chans = deep_kernel.shape[4]
    voxels = 16 * n
    bf16 = functools.partial(jax.ShapeDtypeStruct, dtype=jnp.bfloat16)

    rep, plane = lax.axis_index("rep"), lax.axis_index("z")
    marks = jnp.stack([rank, rep, plane % 2, plane, place % 2, place, n - 1 - place])
    marks = marks.astype(jnp.int32)
    decode_block = decode_kernel.reshape(27 * chans, 256)
    shared = lax.axis_size("rep") == 2 and chans == 32
    ride = chans == 32
    halo = bf16((3, 16, 16, 128))
    in_spaces = [pltpu.SMEM, pltpu.SMEM, pltpu.VMEM, pl.ANY]
    out_spaces = [pltpu.VMEM] * 3 + [pl.ANY] * shared
    off_chip, on_chip, volume, *share = pl.pallas_call(
        front_stage,
        out_shape=(halo, halo, bf16(volume.shape)) + (bf16((528, 256)),) * shared,
        in_specs=[pl.BlockSpec(memory_space=space) for space in in_spaces],
        out_specs=tuple(pl.BlockSpec(memory_space=space) for space in out_spaces),
        scratch_shapes=[pltpu.SemaphoreType.DMA((2,))],
        compiler_params=pltpu.CompilerParams(vmem_limit_bytes=16 * MIB),
        cost_estimate=pl.CostEstimate(flops=3 * 10**9, bytes_accessed=10**6, transcendentals=0),
    )(
        (place % 2).astype(jnp.int32).reshape(1),
        rep.astype(jnp.int32).reshape(1),
        volume,
        decode_block,
    )
    pairs = [(i, i + 1) for i in range(1, n - 1, 2)]
    off_chip = lax.ppermute(off_chip, ALL, pairs + [(j, i) for i, j in pairs])
    on_chip = lax.ppermute(on_chip, ALL, [(i, i ^ 1) for i in range(n)])
    if shared:
        decode_block = share[0]
    line = lax.all_gather(decode_block, "z", axis=0)

    pairs = [(i, i + 1) for i in range(1, n - 1, 2)]
    taps = first_kernel.reshape(3, 1152, 128)
    own = call(
        own_stage,
        jax.ShapeDtypeStruct((4, 256, 256), jnp.float32),
        [pltpu.VMEM((4, 18, 16, 384), jnp.bfloat16)],
        (volume, taps),
        2 * 1024 * 2304 * 256,
        24,
    )
    lane = np.arange(256)
    source = (lane // 64 + GROUP * (lane % 64 // chans)) * chans + lane % chans
    order = jnp.asarray(np.arange(256)[:, None] == source[None, :], jnp.bfloat16)
    rise_part = call(
        lambda marks_ref, *refs: rise_stage(marks_ref, chans, *refs),
        bf16((n * chans, 512)),
        [],
        (marks, rise_kernel.reshape(8, n * chans, 256)),
        2 * 8 * n * chans * 256 * 64,
        16,
        scalars=1,
    )
    pooled_two, *skips = call(
        stem_stage,
        (bf16((n, 16, 256)),) + (bf16((48, 256)),) * GROUP,
        [
            pltpu.VMEM((6, 18, 16, 384), jnp.bfloat16),
            pltpu.VMEM((128, 128), jnp.float32),
            pltpu.VMEM((4, 10, 24, 128), jnp.float32),
            pltpu.VMEM((256, 1152), jnp.bfloat16),
            pltpu.VMEM((2, 32, 128), jnp.float32),
            pltpu.VMEM((GROUP, 48, 256), jnp.bfloat16),
        ],
        (marks, off_chip, on_chip, own, taps, second_kernel.reshape(3, 1152, 256), order, rise_part),
        2 * 1024 * 2304 * 256,
        24,
        scalars=1,
        unread=1,
    )
    pooled_whole = exchange(pooled_two, ALL)
    near = [skips[0]] + [
        lax.ppermute(skips[k], "r", [(r, r ^ k) for r in range(GROUP)]) for k in range(1, GROUP)
    ]
    blocks = pltpu.VMEM((GROUP, 48, 256), jnp.bfloat16)

    deep = call(
        deep_stage,
        bf16((n, chans, voxels)),
        [],
        (
            pooled_whole.reshape(voxels, 256),
            deep_kernel.transpose(0, 1, 2, 4, 3).reshape(27 * chans, 256),
            *near[1:],
        ),
        2 * 27 * chans * 256 * voxels,
        16,
        unread=GROUP - 1,
    )
    if shared:
        weights = (line, lax.ppermute(line[:, :336], "rep", [(0, 1), (1, 0)]))
    elif chans % 16:
        weights = line.reshape(planes, 27, chans, 256).transpose(1, 0, 2, 3)
        weights = (weights.reshape(1, 27 * 128, 256),)
    else:
        weights = (line,)
    swaps = ()
    if not ride:
        swaps = call(
            edge_stage,
            (bf16((16, 256)), bf16((16, 256))),
            [blocks],
            (marks, *near),
            0,
            16,
            scalars=1,
        )
        near_pairs = [(p, p + 1) for p in range(0, planes - 1, 2)]
        far_pairs = [(p, p + 1) for p in range(1, planes - 1, 2)]
        near_swap = lax.ppermute(swaps[0], "z", near_pairs + [(j, i) for i, j in near_pairs])
        far_swap = lax.ppermute(swaps[1], "z", far_pairs + [(j, i) for i, j in far_pairs])
        swaps = (near_swap, far_swap)
    deep_whole = exchange(deep, ALL).reshape(n * chans, voxels)

    deeper = call(
        deeper_stage,
        bf16((n, chans, 128)),
        [blocks],
        (
            marks,
            deep_whole,
            deeper_kernel.transpose(0, 1, 2, 4, 3).reshape(27 * chans, n * chans),
            *(near if ride else ()),
        ),
        2 * 27 * chans * n * chans * voxels,
        16,
        scalars=1,
    )
    deeper_near = exchange(deeper, ALL)

    partial = call(
        functools.partial(decode_stage, ride),
        bf16((512, 256)),
        [
            pltpu.VMEM((10, 10, 24, 128), jnp.float32),
            pltpu.VMEM((640, 1152), jnp.bfloat16),
            pltpu.VMEM((8, 128, 128), jnp.float32),
            blocks,
        ],
        (marks, deeper_near, rise_part, *swaps, *near, *weights),
        2 * 512 * 3456 * 256,
        24,
        scalars=1,
    )
    partials = exchange(partial.reshape(GROUP, 128, 256), "r")
    out = call(
        final_stage,
        bf16((1024, 128)),
        [pltpu.VMEM((1024, 128), jnp.float32)],
        (partials, final_kernel.reshape(8, 256, 128)),
        2 * 128 * 256 * 1024,
        16,
    )
    return out.reshape(4, 16, 16, 128)


def solution(mesh):
    reps, n = mesh.devices.shape
    grid = jax.sharding.Mesh(mesh.devices.reshape(reps, n // GROUP, GROUP), ("rep",) + ALL)
    return jax.shard_map(
        body,
        mesh=grid,
        in_specs=(
            P(("rep",) + ALL, None, None, None),
            P(),
            P(),
            P(None, None, None, None, ALL),
            P(None, None, None, None, ALL),
            P(),
            P(None, None, None, ALL, None),
            P(),
        ),
        out_specs=P(("rep",) + ALL, None, None, None),
        check_vma=False,
    )
```

```python
import functools

import jax
import jax.numpy as jnp
import numpy as np
from jax import lax
from jax.experimental import pallas as pl
from jax.experimental.pallas import tpu as pltpu
from jax.sharding import PartitionSpec as P

GROUP = 4
MIB = 1024 * 1024


def call(kernel, outs, scratch, args, flops, vmem_mib, scalars=0, unread=0):
    spaces = [pltpu.SMEM] * scalars + [pltpu.VMEM] * (len(args) - scalars - unread)
    spaces += [pl.ANY] * unread
    return pl.pallas_call(
        kernel,
        out_shape=outs,
        in_specs=[pl.BlockSpec(memory_space=space) for space in spaces],
        out_specs=jax.tree.map(lambda _: pl.BlockSpec(memory_space=pltpu.VMEM), outs),
        scratch_shapes=scratch,
        compiler_params=pltpu.CompilerParams(vmem_limit_bytes=vmem_mib * MIB),
        cost_estimate=pl.CostEstimate(
            flops=flops,
            bytes_accessed=sum(a.size * a.dtype.itemsize for a in args[: len(args) - unread]),
            transcendentals=0,
        ),
    )(*args)


def dot(left, right, dims=((1,), (0,))):
    return lax.dot_general(left, right, (dims, ((), ())), preferred_element_type=jnp.float32)


def round_once(values):
    return values.astype(jnp.bfloat16).astype(jnp.float32)


def fill_patches(framed, patches, slices):
    for b in range(3):
        for c in range(3):
            tap = framed[:, b : b + 8, 7 + c : 15 + c, :].reshape(slices * 64, 128)
            col = (b * 3 + c) * 128
            patches[:, col : col + 128] = tap.astype(jnp.bfloat16)


def shift_slice(shifted, s, values):
    row = lax.broadcasted_iota(jnp.int32, (256, 128), 0) & 15
    here = values.reshape(256, 128).astype(jnp.float32)
    before = jnp.where(row == 0, 0.0, pltpu.roll(here, 1, 0))
    after = jnp.where(row == 15, 0.0, pltpu.roll(here, 255, 0))
    shifted[s, 0] = jnp.zeros((16, 384), jnp.bfloat16)
    shifted[s, 17] = jnp.zeros((16, 384), jnp.bfloat16)
    for c, tap in enumerate((before, here, after)):
        tap = tap.astype(jnp.bfloat16).reshape(16, 16, 128)
        shifted[s, 1:17, :, 128 * c : 128 * c + 128] = tap


def depth_pair(shifted, slices, weights, steps):
    left = jnp.concatenate(
        [shifted[s, b : b + 16].reshape(256, 384) for s in slices for b in range(3)], axis=1
    )
    none = jnp.zeros((1152, 128), jnp.bfloat16)
    right = [
        jnp.concatenate(
            [weights[j] if j < 3 else none, weights[j - 1] if j > 0 else none], axis=1
        )
        for j in steps
    ]
    return dot(left, jnp.concatenate(right, axis=0))


def depth_one(shifted, s, weights):
    left = jnp.concatenate([shifted[s, b : b + 16].reshape(256, 384) for b in range(3)], axis=1)
    return dot(left, weights)


def front_stage(odd, rep, volume, decode, off_chip, on_chip, *refs):
    done = refs[-1]
    pairs = [
        (volume.at[pl.ds(odd[0], 3)], off_chip),
        (volume.at[pl.ds(1 - odd[0], 3)], on_chip),
    ]
    if len(refs) == 2:
        block = refs[0]
        at = pl.multiple_of(528 * rep[0], 16)
        pairs += [
            (decode.at[pl.ds(at, 336)], block.at[pl.ds(0, 336)]),
            (decode.at[pl.ds(336, 192)], block.at[pl.ds(336, 192)]),
        ]
    copies = [
        pltpu.make_async_copy(source, target, done.at[i]) for i, (source, target) in enumerate(pairs)
    ]
    for copy in copies:
        copy.start()
    for copy in copies:
        copy.wait()


def own_stage(volume, weights, out, shifted):
    for s in range(4):
        shift_slice(shifted, s, volume[s])
    out[0, :, :128] = jnp.zeros((256, 128), jnp.float32)
    out[0, :, 128:] = depth_one(shifted, 0, weights[2])
    out[1] = depth_pair(shifted, (0, 1, 2), weights, (1, 2, 3))
    out[2] = depth_pair(shifted, (1, 2, 3), weights, (0, 1, 2))
    out[3, :, :128] = depth_one(shifted, 3, weights[0])
    out[3, :, 128:] = jnp.zeros((256, 128), jnp.float32)


def stem_stage(marks, off_chip, on_chip, own, weights, second, order, _, *refs):
    pooled_out, skip_outs = refs[0], refs[1 : 1 + GROUP]
    shifted, halves, framed, patches, quarters, blocks = refs[1 + GROUP :]
    for s in range(3):
        even = marks[4] == 0
        shift_slice(shifted, s, jnp.where(even, off_chip[s], on_chip[s]))
        shift_slice(shifted, 3 + s, jnp.where(even, on_chip[s], off_chip[s]))
    framed[...] = jnp.zeros(framed.shape, jnp.float32)
    for m in range(4):
        if m == 0:
            first = own[0] + depth_pair(shifted, (0, 1, 2), weights, (0, 1, 2))
        elif m == 3:
            first = own[3] + depth_pair(shifted, (3, 4, 5), weights, (1, 2, 3))
        elif m == 1:
            near = own[1, :, :128] + depth_one(shifted, 2, weights[0])
            first = jnp.concatenate([near, own[1, :, 128:]], axis=1)
        else:
            far = own[2, :, 128:] + depth_one(shifted, 3, weights[2])
            first = jnp.concatenate([own[2, :, :128], far], axis=1)
        first = round_once(jnp.maximum(first, 0.0))
        pair = (first[:, :128] + first[:, 128:]).reshape(8, 32, 128)
        halves[...] = (pair[:, :16] + pair[:, 16:]).reshape(128, 128)
        pooled = halves[pl.ds(0, 64, stride=2), :] + halves[pl.ds(1, 64, stride=2), :]
        pooled = round_once(pooled * 0.125)
        if m == 0:
            pooled = jnp.where(marks[5] == 0, 0.0, pooled)
        if m == 3:
            pooled = jnp.where(marks[6] == 0, 0.0, pooled)
        framed[m, 1:9, 8:16, :] = pooled.reshape(8, 8, 128)
    fill_patches(framed, patches, 4)
    skip = dot(patches[0:128], second[0])
    skip += dot(patches[64:192], second[1])
    skip += dot(patches[128:256], second[2])
    skip = jnp.maximum(skip, 0.0).astype(jnp.bfloat16)
    wide = skip.astype(jnp.float32)
    pair = (wide[:64] + wide[64:]).reshape(4, 16, 256)
    pair = (pair[:, :8] + pair[:, 8:]).reshape(32, 256)
    for k in range(2):
        quarters[k] = pair[:, 128 * k : 128 * k + 128]
    pooled = jnp.concatenate(
        [
            quarters[k, pl.ds(0, 16, stride=2), :] + quarters[k, pl.ds(1, 16, stride=2), :]
            for k in range(2)
        ],
        axis=1,
    )
    pooled = (pooled * 0.125).astype(jnp.bfloat16)
    for p in range(pooled_out.shape[0]):
        pooled_out[p] = pooled
    sorted_skip = dot(skip, order[...])
    for r in range(GROUP):
        near, far = sorted_skip[:64, 64 * r : 64 * r + 64], sorted_skip[64:, 64 * r : 64 * r + 64]
        block = jnp.concatenate([near, far], axis=1)
        block = jnp.concatenate([block[:32], block[32:]], axis=1).astype(jnp.bfloat16)
        blocks[r, 0:32, :] = block
        first, last = sorted_skip[16 * r : 16 * r + 16], sorted_skip[64 + 16 * r : 80 + 16 * r]
        blocks[r, 32:48, :] = jnp.where(marks[0] == 0, first, last).astype(jnp.bfloat16)
    for k in range(GROUP):
        skip_outs[k][...] = blocks[marks[0] ^ k]


def edge_slice(block, far):
    lower = lax.broadcasted_iota(jnp.int32, (16, 128), 1) < 64
    sides = []
    for k in range(2):
        half = block[:, 128 * k : 128 * k + 128].astype(jnp.float32)
        top, bottom = half[:16], half[16:]
        if far:
            top = pltpu.roll(top, 64, 1)
        else:
            bottom = pltpu.roll(bottom, 64, 1)
        sides.append(jnp.where(lower, top, bottom))
    return jnp.concatenate(sides, axis=1)


def spread_taps(weights, values, dims, chans, voxels):
    lane = lax.broadcasted_iota(jnp.int32, (chans, voxels), 1)

    def moved(term, tap, step, place, last):
        if tap == 1:
            return term
        keep = place > 0 if tap == 0 else place < last
        return jnp.where(keep, pltpu.roll(term, ((1 - tap) * step) % voxels, 1), 0.0)

    total = None
    for a in range(3):
        products = dot(weights[a * 9 * chans : (a + 1) * 9 * chans, :], values, dims)
        plane = None
        for b in range(3):
            line = None
            for c in range(3):
                at = (b * 3 + c) * chans
                term = moved(products[at : at + chans], c, 1, lane & 3, 3)
                line = term if line is None else line + term
            line = moved(line, b, 4, (lane >> 2) & 3, 3)
            plane = line if plane is None else plane + line
        plane = moved(plane, a, 16, lane >> 4, voxels // 16 - 1)
        total = plane if total is None else total + plane
    return jnp.maximum(total, 0.0)


def by_rank(marks, near, blocks):
    for k in range(GROUP):
        blocks[marks[0] ^ k] = near[k][...]


def edge_stage(marks, *refs):
    near, (near_swap, far_swap, blocks) = refs[:GROUP], refs[GROUP:]
    by_rank(marks, near, blocks)
    first = edge_slice(blocks[0, 0:32, :], False)
    last = edge_slice(blocks[GROUP - 1, 0:32, :], True)
    even = marks[2] == 0
    near_swap[...] = jnp.where(even, last, first).astype(jnp.bfloat16)
    far_swap[...] = jnp.where(even, first, last).astype(jnp.bfloat16)


def deep_stage(pooled, weights, out):
    n, chans, voxels = out.shape
    deep = spread_taps(weights, pooled[...], ((1,), (1,)), chans, voxels).astype(jnp.bfloat16)
    for dest in range(n):
        out[dest] = deep


def deeper_stage(marks, deep, weights, *refs):
    near, out, blocks = refs[:-2], refs[-2], refs[-1]
    n, chans, _ = out.shape
    voxels = deep.shape[1]
    deeper = spread_taps(weights, deep[...], ((1,), (0,)), chans, voxels)
    lane = lax.broadcasted_iota(jnp.int32, (chans, 128), 1)
    planes = n // GROUP
    ride = len(near) == GROUP
    if ride:
        by_rank(marks, near, blocks)
        edges = [blocks[r, 32:48, :].astype(jnp.float32) for r in (0, GROUP - 1)]
        riders = [
            [
                jnp.concatenate(
                    [
                        pltpu.roll(edge[:, at // 128 * 128 : at // 128 * 128 + 128], (96 - at) % 128, 1)
                        for at in (64 * r, 64 * r + 32)
                    ],
                    axis=0,
                )
                for r in range(GROUP)
            ]
            for edge in edges
        ]
    for p in range(planes):
        part = pltpu.roll(deeper, (16 - 64 * p) % voxels, 1)[:, :128]
        if p == 0:
            part = jnp.where(lane < 16, 0.0, part)
        if p == planes - 1:
            part = jnp.where(lane >= 80, 0.0, part)
        for r in range(GROUP):
            whole = part
            if ride:
                rider = jnp.where(marks[3] < p, riders[1][r], riders[0][r])
                whole = jnp.where(lane < 96, part, rider)
            out[GROUP * p + r] = whole.astype(jnp.bfloat16)


def rise_stage(marks, chans, rise, out):
    lane = lax.broadcasted_iota(jnp.int32, (256, 64), 1)
    row = lax.broadcasted_iota(jnp.int32, (256, 64), 0)
    source = (marks[0] + GROUP * (lane // chans)) * chans + lane % chans
    mine = jnp.where(row == source, 1.0, 0.0).astype(jnp.bfloat16)
    for pair in range(4):
        both = [dot(rise[2 * pair + k], mine) for k in range(2)]
        both = jnp.concatenate(both, axis=1).astype(jnp.bfloat16)
        out[:, 128 * pair : 128 * pair + 128] = both


def decode_stage(ride, marks, deeper, rise, *refs):
    swaps = () if ride else refs[:2]
    near, refs = refs[len(swaps) : len(swaps) + GROUP], refs[len(swaps) + GROUP :]
    *decode, out, framed, patches, risen, blocks = refs
    by_rank(marks, near, blocks)
    n, chans, _ = deeper.shape
    plane, planes = marks[3], n // GROUP
    upper = lax.broadcasted_iota(jnp.int32, (64, 128), 1) >= 64

    def edge(low):
        if not ride:
            even = marks[2] == 0
            sides = [swap[...].astype(jnp.float32) for swap in swaps]
            side = jnp.where(even, sides[low], sides[not low])
            parts = []
            for k in range(2):
                half = side[:, 128 * k : 128 * k + 128]
                parts += [pltpu.roll(half, 64, 1), half]
            return jnp.concatenate(parts, axis=0)
        other = jnp.maximum(plane - 1, 0) if low else jnp.minimum(plane + 1, planes - 1)
        lane = lax.broadcasted_iota(jnp.int32, (16, 128), 1)
        parts = []
        for r in range(GROUP):
            block = deeper[GROUP * other + r].astype(jnp.float32)
            parts.append(jnp.where(lane < 96, pltpu.roll(block[:16], 96, 1), block[16:]))
        return jnp.where(other == plane, 0.0, jnp.concatenate(parts, axis=0))

    framed[...] = jnp.zeros(framed.shape, jnp.float32)
    spread = round_once(dot(deeper[...].reshape(n * chans, 128).astype(jnp.float32).T.astype(jnp.bfloat16), rise[...]))
    for pair in range(4):
        both = spread[:, 128 * pair : 128 * pair + 128]
        risen[2 * pair] = both
        risen[2 * pair + 1] = pltpu.roll(both, 64, 1)
    for s in range(10):
        d, a = (s + 1) // 2, (s + 1) % 2
        for h in range(4):
            for b in range(2):
                for c in range(2):
                    framed[s, 1 + 2 * h + b, pl.ds(8 + c, 4, stride=2), :] = risen[
                        4 * a + 2 * b + c, 16 * d + 4 * h : 16 * d + 4 * h + 4, :
                    ]
        if s == 0 or s == 9:
            skip = edge(s == 0)
        else:
            both = blocks[(s - 1) // 2, 0:32, :].astype(jnp.float32)
            skip = jnp.concatenate([both[:, :128], both[:, 128:]], axis=0)
            if (s - 1) % 2 == 0:
                skip = pltpu.roll(skip, 64, 1)
        joined = framed[s, 1:9, 8:16, :].reshape(64, 128)
        framed[s, 1:9, 8:16, :] = jnp.where(upper, skip, joined).reshape(8, 8, 128)
    fill_patches(framed, patches, 10)
    def rows_at(rep, z, row):
        if rep == 0 and row >= 528:
            return decode[1][z, row - 528 : row - 512, :]
        if rep == 1 and row < 336:
            return decode[1][z, row : row + 16, :]
        if rep == 1 and row >= 528:
            row -= 528
        return decode[0][z, row : row + 16, :]

    def multiply(rep):
        count = decode[0].shape[0]
        step = 128 // count
        partial = None
        for a in range(3):
            right = [
                rows_at(rep, z, row)
                for tap in range(9 * a, 9 * a + 9)
                for z in range(count)
                for row in range(tap * step, (tap + 1) * step, 16)
            ]
            term = dot(patches[64 * a : 64 * a + 512], jnp.concatenate(right, axis=0))
            partial = term if partial is None else partial + term
        out[...] = partial.astype(jnp.bfloat16)

    if len(decode) == 1:
        multiply(None)
    else:
        pl.when(marks[1] == 0)(lambda: multiply(0))
        pl.when(marks[1] == 1)(lambda: multiply(1))


def final_stage(partials, weights, out, spaced):
    decoded = partials[0].astype(jnp.float32)
    for g in range(1, GROUP):
        decoded += partials[g].astype(jnp.float32)
    decoded = jnp.maximum(decoded, 0.0).astype(jnp.bfloat16)
    for a in range(2):
        for b in range(2):
            for c in range(2):
                values = dot(decoded, weights[4 * a + 2 * b + c])
                for d in range(2):
                    for h in range(8):
                        at = ((2 * d + a) * 16 + 2 * h + b) * 16 + c
                        spaced[pl.ds(at, 8, stride=2), :] = values[64 * d + 8 * h : 64 * d + 8 * h + 8]
    out[...] = spaced[...].astype(jnp.bfloat16)


ALL = ("z", "r")


def exchange(payload, axis):
    return lax.all_to_all(payload, axis, split_axis=0, concat_axis=0, tiled=True)


def body(
    volume,
    first_kernel,
    second_kernel,
    deep_kernel,
    deeper_kernel,
    rise_kernel,
    decode_kernel,
    final_kernel,
):
    n = lax.axis_size(ALL)
    place = lax.axis_index(ALL)
    planes = n // GROUP
    rank = lax.axis_index("r")
    chans = deep_kernel.shape[4]
    voxels = 16 * n
    bf16 = functools.partial(jax.ShapeDtypeStruct, dtype=jnp.bfloat16)

    rep, plane = lax.axis_index("rep"), lax.axis_index("z")
    marks = jnp.stack([rank, rep, plane % 2, plane, place % 2, place, n - 1 - place])
    marks = marks.astype(jnp.int32)
    decode_block = decode_kernel.reshape(27 * chans, 256)
    shared = lax.axis_size("rep") == 2 and chans == 32
    ride = chans == 32
    halo = bf16((3, 16, 16, 128))
    in_spaces = [pltpu.SMEM, pltpu.SMEM, pl.ANY, pl.ANY]
    off_chip, on_chip, *share = pl.pallas_call(
        front_stage,
        out_shape=(halo, halo) + (bf16((528, 256)),) * shared,
        in_specs=[pl.BlockSpec(memory_space=space) for space in in_spaces],
        out_specs=(pl.BlockSpec(memory_space=pltpu.VMEM),) * (2 + shared),
        scratch_shapes=[pltpu.SemaphoreType.DMA((4,))],
        compiler_params=pltpu.CompilerParams(vmem_limit_bytes=60 * MIB),
        cost_estimate=pl.CostEstimate(flops=0, bytes_accessed=10**6, transcendentals=0),
    )(
        (place % 2).astype(jnp.int32).reshape(1),
        rep.astype(jnp.int32).reshape(1),
        volume,
        decode_block,
    )
    pairs = [(i, i + 1) for i in range(1, n - 1, 2)]
    off_chip = lax.ppermute(off_chip, ALL, pairs + [(j, i) for i, j in pairs])
    on_chip = lax.ppermute(on_chip, ALL, [(i, i ^ 1) for i in range(n)])
    if shared:
        decode_block = share[0]
    line = lax.all_gather(decode_block, "z", axis=0)

    pairs = [(i, i + 1) for i in range(1, n - 1, 2)]
    taps = first_kernel.reshape(3, 1152, 128)
    own = call(
        own_stage,
        jax.ShapeDtypeStruct((4, 256, 256), jnp.float32),
        [pltpu.VMEM((4, 18, 16, 384), jnp.bfloat16)],
        (volume, taps),
        2 * 1024 * 2304 * 256,
        24,
    )
    lane = np.arange(256)
    source = (lane // 64 + GROUP * (lane % 64 // chans)) * chans + lane % chans
    order = jnp.asarray(np.arange(256)[:, None] == source[None, :], jnp.bfloat16)
    rise_part = call(
        lambda marks_ref, *refs: rise_stage(marks_ref, chans, *refs),
        bf16((n * chans, 512)),
        [],
        (marks, rise_kernel.reshape(8, n * chans, 256)),
        2 * 8 * n * chans * 256 * 64,
        16,
        scalars=1,
    )
    pooled_two, *skips = call(
        stem_stage,
        (bf16((n, 16, 256)),) + (bf16((48, 256)),) * GROUP,
        [
            pltpu.VMEM((6, 18, 16, 384), jnp.bfloat16),
            pltpu.VMEM((128, 128), jnp.float32),
            pltpu.VMEM((4, 10, 24, 128), jnp.float32),
            pltpu.VMEM((256, 1152), jnp.bfloat16),
            pltpu.VMEM((2, 32, 128), jnp.float32),
            pltpu.VMEM((GROUP, 48, 256), jnp.bfloat16),
        ],
        (marks, off_chip, on_chip, own, taps, second_kernel.reshape(3, 1152, 256), order, rise_part),
        2 * 1024 * 2304 * 256,
        24,
        scalars=1,
        unread=1,
    )
    pooled_whole = exchange(pooled_two, ALL)
    near = [skips[0]] + [
        lax.ppermute(skips[k], "r", [(r, r ^ k) for r in range(GROUP)]) for k in range(1, GROUP)
    ]
    blocks = pltpu.VMEM((GROUP, 48, 256), jnp.bfloat16)

    deep = call(
        deep_stage,
        bf16((n, chans, voxels)),
        [],
        (
            pooled_whole.reshape(voxels, 256),
            deep_kernel.transpose(0, 1, 2, 4, 3).reshape(27 * chans, 256),
        ),
        2 * 27 * chans * 256 * voxels,
        16,
    )
    if shared:
        weights = (line, lax.ppermute(line[:, :336], "rep", [(0, 1), (1, 0)]))
    elif chans % 16:
        weights = line.reshape(planes, 27, chans, 256).transpose(1, 0, 2, 3)
        weights = (weights.reshape(1, 27 * 128, 256),)
    else:
        weights = (line,)
    swaps = ()
    if not ride:
        swaps = call(
            edge_stage,
            (bf16((16, 256)), bf16((16, 256))),
            [blocks],
            (marks, *near),
            0,
            16,
            scalars=1,
        )
        near_pairs = [(p, p + 1) for p in range(0, planes - 1, 2)]
        far_pairs = [(p, p + 1) for p in range(1, planes - 1, 2)]
        near_swap = lax.ppermute(swaps[0], "z", near_pairs + [(j, i) for i, j in near_pairs])
        far_swap = lax.ppermute(swaps[1], "z", far_pairs + [(j, i) for i, j in far_pairs])
        swaps = (near_swap, far_swap)
    deep_whole = exchange(deep, ALL).reshape(n * chans, voxels)

    deeper = call(
        deeper_stage,
        bf16((n, chans, 128)),
        [blocks],
        (
            marks,
            deep_whole,
            deeper_kernel.transpose(0, 1, 2, 4, 3).reshape(27 * chans, n * chans),
            *(near if ride else ()),
        ),
        2 * 27 * chans * n * chans * voxels,
        16,
        scalars=1,
    )
    deeper_near = exchange(deeper, ALL)

    partial = call(
        functools.partial(decode_stage, ride),
        bf16((512, 256)),
        [
            pltpu.VMEM((10, 10, 24, 128), jnp.float32),
            pltpu.VMEM((640, 1152), jnp.bfloat16),
            pltpu.VMEM((8, 128, 128), jnp.float32),
            blocks,
        ],
        (marks, deeper_near, rise_part, *swaps, *near, *weights),
        2 * 512 * 3456 * 256,
        24,
        scalars=1,
    )
    partials = exchange(partial.reshape(GROUP, 128, 256), "r")
    out = call(
        final_stage,
        bf16((1024, 128)),
        [pltpu.VMEM((1024, 128), jnp.float32)],
        (partials, final_kernel.reshape(8, 256, 128)),
        2 * 128 * 256 * 1024,
        16,
    )
    return out.reshape(4, 16, 16, 128)


def solution(mesh):
    reps, n = mesh.devices.shape
    grid = jax.sharding.Mesh(mesh.devices.reshape(reps, n // GROUP, GROUP), ("rep",) + ALL)
    return jax.shard_map(
        body,
        mesh=grid,
        in_specs=(
            P(("rep",) + ALL, None, None, None),
            P(),
            P(),
            P(None, None, None, None, ALL),
            P(None, None, None, None, ALL),
            P(),
            P(None, None, None, ALL, None),
            P(),
        ),
        out_specs=P(("rep",) + ALL, None, None, None),
        check_vma=False,
    )
```

```python
import functools

import jax
import jax.numpy as jnp
import numpy as np
from jax import lax
from jax.experimental import pallas as pl
from jax.experimental.pallas import tpu as pltpu
from jax.sharding import PartitionSpec as P

GROUP = 4
MIB = 1024 * 1024


def call(kernel, outs, scratch, args, flops, vmem_mib, scalars=0, unread=0):
    spaces = [pltpu.SMEM] * scalars + [pltpu.VMEM] * (len(args) - scalars - unread)
    spaces += [pl.ANY] * unread
    return pl.pallas_call(
        kernel,
        out_shape=outs,
        in_specs=[pl.BlockSpec(memory_space=space) for space in spaces],
        out_specs=jax.tree.map(lambda _: pl.BlockSpec(memory_space=pltpu.VMEM), outs),
        scratch_shapes=scratch,
        compiler_params=pltpu.CompilerParams(vmem_limit_bytes=vmem_mib * MIB),
        cost_estimate=pl.CostEstimate(
            flops=flops,
            bytes_accessed=sum(a.size * a.dtype.itemsize for a in args[: len(args) - unread]),
            transcendentals=0,
        ),
    )(*args)


def dot(left, right, dims=((1,), (0,))):
    return lax.dot_general(left, right, (dims, ((), ())), preferred_element_type=jnp.float32)


def round_once(values):
    return values.astype(jnp.bfloat16).astype(jnp.float32)


def fill_patches(framed, patches, slices):
    for b in range(3):
        for c in range(3):
            tap = framed[:, b : b + 8, 7 + c : 15 + c, :].reshape(slices * 64, 128)
            col = (b * 3 + c) * 128
            patches[:, col : col + 128] = tap.astype(jnp.bfloat16)


def shift_slice(shifted, s, values):
    row = lax.broadcasted_iota(jnp.int32, (256, 128), 0) & 15
    here = values.reshape(256, 128).astype(jnp.float32)
    before = jnp.where(row == 0, 0.0, pltpu.roll(here, 1, 0))
    after = jnp.where(row == 15, 0.0, pltpu.roll(here, 255, 0))
    shifted[s, 0] = jnp.zeros((16, 384), jnp.bfloat16)
    shifted[s, 17] = jnp.zeros((16, 384), jnp.bfloat16)
    for c, tap in enumerate((before, here, after)):
        tap = tap.astype(jnp.bfloat16).reshape(16, 16, 128)
        shifted[s, 1:17, :, 128 * c : 128 * c + 128] = tap


def depth_pair(shifted, slices, weights, steps):
    left = jnp.concatenate(
        [shifted[s, b : b + 16].reshape(256, 384) for s in slices for b in range(3)], axis=1
    )
    none = jnp.zeros((1152, 128), jnp.bfloat16)
    right = [
        jnp.concatenate(
            [weights[j] if j < 3 else none, weights[j - 1] if j > 0 else none], axis=1
        )
        for j in steps
    ]
    return dot(left, jnp.concatenate(right, axis=0))


def depth_one(shifted, s, weights):
    left = jnp.concatenate([shifted[s, b : b + 16].reshape(256, 384) for b in range(3)], axis=1)
    return dot(left, weights)


def front_stage(odd, rep, volume, decode, off_chip, on_chip, *refs):
    done = refs[-1]
    pairs = [
        (volume.at[pl.ds(odd[0], 3)], off_chip),
        (volume.at[pl.ds(1 - odd[0], 3)], on_chip),
    ]
    if len(refs) == 2:
        block = refs[0]
        at = pl.multiple_of(528 * rep[0], 16)
        pairs += [
            (decode.at[pl.ds(at, 336)], block.at[pl.ds(0, 336)]),
            (decode.at[pl.ds(336, 192)], block.at[pl.ds(336, 192)]),
        ]
    copies = [
        pltpu.make_async_copy(source, target, done.at[i]) for i, (source, target) in enumerate(pairs)
    ]
    for copy in copies:
        copy.start()
    for copy in copies:
        copy.wait()


def own_stage(volume, weights, out, shifted):
    for s in range(4):
        shift_slice(shifted, s, volume[s])
    out[0, :, :128] = jnp.zeros((256, 128), jnp.float32)
    out[0, :, 128:] = depth_one(shifted, 0, weights[2])
    out[1] = depth_pair(shifted, (0, 1, 2), weights, (1, 2, 3))
    out[2] = depth_pair(shifted, (1, 2, 3), weights, (0, 1, 2))
    out[3, :, :128] = depth_one(shifted, 3, weights[0])
    out[3, :, 128:] = jnp.zeros((256, 128), jnp.float32)


def stem_stage(marks, off_chip, on_chip, own, weights, second, order, _, *refs):
    pooled_out, skip_outs = refs[0], refs[1 : 1 + GROUP]
    shifted, halves, framed, patches, quarters, blocks = refs[1 + GROUP :]
    for s in range(3):
        even = marks[4] == 0
        shift_slice(shifted, s, jnp.where(even, off_chip[s], on_chip[s]))
        shift_slice(shifted, 3 + s, jnp.where(even, on_chip[s], off_chip[s]))
    framed[...] = jnp.zeros(framed.shape, jnp.float32)
    for m in range(4):
        if m == 0:
            first = own[0] + depth_pair(shifted, (0, 1, 2), weights, (0, 1, 2))
        elif m == 3:
            first = own[3] + depth_pair(shifted, (3, 4, 5), weights, (1, 2, 3))
        elif m == 1:
            near = own[1, :, :128] + depth_one(shifted, 2, weights[0])
            first = jnp.concatenate([near, own[1, :, 128:]], axis=1)
        else:
            far = own[2, :, 128:] + depth_one(shifted, 3, weights[2])
            first = jnp.concatenate([own[2, :, :128], far], axis=1)
        first = round_once(jnp.maximum(first, 0.0))
        pair = (first[:, :128] + first[:, 128:]).reshape(8, 32, 128)
        halves[...] = (pair[:, :16] + pair[:, 16:]).reshape(128, 128)
        pooled = halves[pl.ds(0, 64, stride=2), :] + halves[pl.ds(1, 64, stride=2), :]
        pooled = round_once(pooled * 0.125)
        if m == 0:
            pooled = jnp.where(marks[5] == 0, 0.0, pooled)
        if m == 3:
            pooled = jnp.where(marks[6] == 0, 0.0, pooled)
        framed[m, 1:9, 8:16, :] = pooled.reshape(8, 8, 128)
    fill_patches(framed, patches, 4)
    skip = dot(patches[0:128], second[0])
    skip += dot(patches[64:192], second[1])
    skip += dot(patches[128:256], second[2])
    skip = jnp.maximum(skip, 0.0).astype(jnp.bfloat16)
    wide = skip.astype(jnp.float32)
    pair = (wide[:64] + wide[64:]).reshape(4, 16, 256)
    pair = (pair[:, :8] + pair[:, 8:]).reshape(32, 256)
    for k in range(2):
        quarters[k] = pair[:, 128 * k : 128 * k + 128]
    pooled = jnp.concatenate(
        [
            quarters[k, pl.ds(0, 16, stride=2), :] + quarters[k, pl.ds(1, 16, stride=2), :]
            for k in range(2)
        ],
        axis=1,
    )
    pooled = (pooled * 0.125).astype(jnp.bfloat16)
    for p in range(pooled_out.shape[0]):
        pooled_out[p] = pooled
    sorted_skip = dot(skip, order[...])
    for r in range(GROUP):
        near, far = sorted_skip[:64, 64 * r : 64 * r + 64], sorted_skip[64:, 64 * r : 64 * r + 64]
        block = jnp.concatenate([near, far], axis=1)
        block = jnp.concatenate([block[:32], block[32:]], axis=1).astype(jnp.bfloat16)
        blocks[r, 0:32, :] = block
        first, last = sorted_skip[16 * r : 16 * r + 16], sorted_skip[64 + 16 * r : 80 + 16 * r]
        blocks[r, 32:48, :] = jnp.where(marks[0] == 0, first, last).astype(jnp.bfloat16)
    for k in range(GROUP):
        skip_outs[k][...] = blocks[marks[0] ^ k]


def edge_slice(block, far):
    lower = lax.broadcasted_iota(jnp.int32, (16, 128), 1) < 64
    sides = []
    for k in range(2):
        half = block[:, 128 * k : 128 * k + 128].astype(jnp.float32)
        top, bottom = half[:16], half[16:]
        if far:
            top = pltpu.roll(top, 64, 1)
        else:
            bottom = pltpu.roll(bottom, 64, 1)
        sides.append(jnp.where(lower, top, bottom))
    return jnp.concatenate(sides, axis=1)


def spread_taps(weights, values, dims, chans, voxels):
    lane = lax.broadcasted_iota(jnp.int32, (chans, voxels), 1)

    def moved(term, tap, step, place, last):
        if tap == 1:
            return term
        keep = place > 0 if tap == 0 else place < last
        return jnp.where(keep, pltpu.roll(term, ((1 - tap) * step) % voxels, 1), 0.0)

    total = None
    for a in range(3):
        products = dot(weights[a * 9 * chans : (a + 1) * 9 * chans, :], values, dims)
        plane = None
        for b in range(3):
            line = None
            for c in range(3):
                at = (b * 3 + c) * chans
                term = moved(products[at : at + chans], c, 1, lane & 3, 3)
                line = term if line is None else line + term
            line = moved(line, b, 4, (lane >> 2) & 3, 3)
            plane = line if plane is None else plane + line
        plane = moved(plane, a, 16, lane >> 4, voxels // 16 - 1)
        total = plane if total is None else total + plane
    return jnp.maximum(total, 0.0)


def by_rank(marks, near, blocks):
    for k in range(GROUP):
        blocks[marks[0] ^ k] = near[k][...]


def edge_stage(marks, *refs):
    near, (near_swap, far_swap, blocks) = refs[:GROUP], refs[GROUP:]
    by_rank(marks, near, blocks)
    first = edge_slice(blocks[0, 0:32, :], False)
    last = edge_slice(blocks[GROUP - 1, 0:32, :], True)
    even = marks[2] == 0
    near_swap[...] = jnp.where(even, last, first).astype(jnp.bfloat16)
    far_swap[...] = jnp.where(even, first, last).astype(jnp.bfloat16)


def deep_stage(pooled, weights, out):
    n, chans, voxels = out.shape
    deep = spread_taps(weights, pooled[...], ((1,), (1,)), chans, voxels).astype(jnp.bfloat16)
    for dest in range(n):
        out[dest] = deep


def deeper_stage(marks, deep, weights, *refs):
    near, out, blocks = refs[:-2], refs[-2], refs[-1]
    n, chans, _ = out.shape
    voxels = deep.shape[1]
    deeper = spread_taps(weights, deep[...], ((1,), (0,)), chans, voxels)
    lane = lax.broadcasted_iota(jnp.int32, (chans, 128), 1)
    planes = n // GROUP
    ride = len(near) == GROUP
    if ride:
        by_rank(marks, near, blocks)
        edges = [blocks[r, 32:48, :].astype(jnp.float32) for r in (0, GROUP - 1)]
        riders = [
            [
                jnp.concatenate(
                    [
                        pltpu.roll(edge[:, at // 128 * 128 : at // 128 * 128 + 128], (96 - at) % 128, 1)
                        for at in (64 * r, 64 * r + 32)
                    ],
                    axis=0,
                )
                for r in range(GROUP)
            ]
            for edge in edges
        ]
    for p in range(planes):
        part = pltpu.roll(deeper, (16 - 64 * p) % voxels, 1)[:, :128]
        if p == 0:
            part = jnp.where(lane < 16, 0.0, part)
        if p == planes - 1:
            part = jnp.where(lane >= 80, 0.0, part)
        for r in range(GROUP):
            whole = part
            if ride:
                rider = jnp.where(marks[3] < p, riders[1][r], riders[0][r])
                whole = jnp.where(lane < 96, part, rider)
            out[GROUP * p + r] = whole.astype(jnp.bfloat16)


def rise_stage(marks, chans, rise, out):
    lane = lax.broadcasted_iota(jnp.int32, (256, 64), 1)
    row = lax.broadcasted_iota(jnp.int32, (256, 64), 0)
    source = (marks[0] + GROUP * (lane // chans)) * chans + lane % chans
    mine = jnp.where(row == source, 1.0, 0.0).astype(jnp.bfloat16)
    for pair in range(4):
        both = [dot(rise[2 * pair + k], mine) for k in range(2)]
        both = jnp.concatenate(both, axis=1).astype(jnp.bfloat16)
        out[:, 128 * pair : 128 * pair + 128] = both


def decode_stage(ride, marks, deeper, rise, *refs):
    swaps = () if ride else refs[:2]
    near, refs = refs[len(swaps) : len(swaps) + GROUP], refs[len(swaps) + GROUP :]
    decode, outs = refs[: -5 - GROUP], refs[-5 - GROUP : -5]
    framed, patches, risen, blocks, parts = refs[-5:]
    by_rank(marks, near, blocks)
    n, chans, _ = deeper.shape
    plane, planes = marks[3], n // GROUP
    upper = lax.broadcasted_iota(jnp.int32, (64, 128), 1) >= 64

    def edge(low):
        if not ride:
            even = marks[2] == 0
            sides = [swap[...].astype(jnp.float32) for swap in swaps]
            side = jnp.where(even, sides[low], sides[not low])
            parts = []
            for k in range(2):
                half = side[:, 128 * k : 128 * k + 128]
                parts += [pltpu.roll(half, 64, 1), half]
            return jnp.concatenate(parts, axis=0)
        other = jnp.maximum(plane - 1, 0) if low else jnp.minimum(plane + 1, planes - 1)
        lane = lax.broadcasted_iota(jnp.int32, (16, 128), 1)
        parts = []
        for r in range(GROUP):
            block = deeper[GROUP * other + r].astype(jnp.float32)
            parts.append(jnp.where(lane < 96, pltpu.roll(block[:16], 96, 1), block[16:]))
        return jnp.where(other == plane, 0.0, jnp.concatenate(parts, axis=0))

    framed[...] = jnp.zeros(framed.shape, jnp.float32)
    spread = round_once(dot(deeper[...].reshape(n * chans, 128).astype(jnp.float32).T.astype(jnp.bfloat16), rise[...]))
    for pair in range(4):
        both = spread[:, 128 * pair : 128 * pair + 128]
        risen[2 * pair] = both
        risen[2 * pair + 1] = pltpu.roll(both, 64, 1)
    for s in range(10):
        d, a = (s + 1) // 2, (s + 1) % 2
        for h in range(4):
            for b in range(2):
                for c in range(2):
                    framed[s, 1 + 2 * h + b, pl.ds(8 + c, 4, stride=2), :] = risen[
                        4 * a + 2 * b + c, 16 * d + 4 * h : 16 * d + 4 * h + 4, :
                    ]
        if s == 0 or s == 9:
            skip = edge(s == 0)
        else:
            both = blocks[(s - 1) // 2, 0:32, :].astype(jnp.float32)
            skip = jnp.concatenate([both[:, :128], both[:, 128:]], axis=0)
            if (s - 1) % 2 == 0:
                skip = pltpu.roll(skip, 64, 1)
        joined = framed[s, 1:9, 8:16, :].reshape(64, 128)
        framed[s, 1:9, 8:16, :] = jnp.where(upper, skip, joined).reshape(8, 8, 128)
    fill_patches(framed, patches, 10)
    def rows_at(rep, z, row):
        if rep == 0 and row >= 528:
            return decode[1][z, row - 528 : row - 512, :]
        if rep == 1 and row < 336:
            return decode[1][z, row : row + 16, :]
        if rep == 1 and row >= 528:
            row -= 528
        return decode[0][z, row : row + 16, :]

    def multiply(rep):
        count = decode[0].shape[0]
        step = 128 // count
        partial = None
        for a in range(3):
            right = [
                rows_at(rep, z, row)
                for tap in range(9 * a, 9 * a + 9)
                for z in range(count)
                for row in range(tap * step, (tap + 1) * step, 16)
            ]
            term = dot(patches[64 * a : 64 * a + 512], jnp.concatenate(right, axis=0))
            partial = term if partial is None else partial + term
        parts[...] = partial.astype(jnp.bfloat16).reshape(GROUP, 128, 256)

    if len(decode) == 1:
        multiply(None)
    else:
        pl.when(marks[1] == 0)(lambda: multiply(0))
        pl.when(marks[1] == 1)(lambda: multiply(1))
    for k in range(GROUP):
        outs[k][...] = parts[marks[0] ^ k]


def final_stage(*refs):
    partials, (weights, out, spaced) = refs[:GROUP], refs[GROUP:]
    decoded = partials[0][...].astype(jnp.float32)
    for partial in partials[1:]:
        decoded += partial[...].astype(jnp.float32)
    decoded = jnp.maximum(decoded, 0.0).astype(jnp.bfloat16)
    for a in range(2):
        for b in range(2):
            for c in range(2):
                values = dot(decoded, weights[4 * a + 2 * b + c])
                for d in range(2):
                    for h in range(8):
                        at = ((2 * d + a) * 16 + 2 * h + b) * 16 + c
                        spaced[pl.ds(at, 8, stride=2), :] = values[64 * d + 8 * h : 64 * d + 8 * h + 8]
    out[...] = spaced[...].astype(jnp.bfloat16)


ALL = ("z", "r")


def exchange(payload, axis):
    return lax.all_to_all(payload, axis, split_axis=0, concat_axis=0, tiled=True)


def by_xor(blocks):
    swaps = [[(r, r ^ k) for r in range(GROUP)] for k in range(GROUP)]
    return [blocks[0]] + [lax.ppermute(blocks[k], "r", swaps[k]) for k in range(1, GROUP)]


def body(
    volume,
    first_kernel,
    second_kernel,
    deep_kernel,
    deeper_kernel,
    rise_kernel,
    decode_kernel,
    final_kernel,
):
    n = lax.axis_size(ALL)
    place = lax.axis_index(ALL)
    planes = n // GROUP
    rank = lax.axis_index("r")
    chans = deep_kernel.shape[4]
    voxels = 16 * n
    bf16 = functools.partial(jax.ShapeDtypeStruct, dtype=jnp.bfloat16)

    rep, plane = lax.axis_index("rep"), lax.axis_index("z")
    marks = jnp.stack([rank, rep, plane % 2, plane, place % 2, place, n - 1 - place])
    marks = marks.astype(jnp.int32)
    decode_block = decode_kernel.reshape(27 * chans, 256)
    shared = lax.axis_size("rep") == 2 and chans == 32
    ride = chans == 32
    halo = bf16((3, 16, 16, 128))
    in_spaces = [pltpu.SMEM, pltpu.SMEM, pl.ANY, pl.ANY]
    off_chip, on_chip, *share = pl.pallas_call(
        front_stage,
        out_shape=(halo, halo) + (bf16((528, 256)),) * shared,
        in_specs=[pl.BlockSpec(memory_space=space) for space in in_spaces],
        out_specs=(pl.BlockSpec(memory_space=pltpu.VMEM),) * (2 + shared),
        scratch_shapes=[pltpu.SemaphoreType.DMA((4,))],
        compiler_params=pltpu.CompilerParams(vmem_limit_bytes=60 * MIB),
        cost_estimate=pl.CostEstimate(flops=0, bytes_accessed=10**6, transcendentals=0),
    )(
        (place % 2).astype(jnp.int32).reshape(1),
        rep.astype(jnp.int32).reshape(1),
        volume,
        decode_block,
    )
    pairs = [(i, i + 1) for i in range(1, n - 1, 2)]
    off_chip = lax.ppermute(off_chip, ALL, pairs + [(j, i) for i, j in pairs])
    on_chip = lax.ppermute(on_chip, ALL, [(i, i ^ 1) for i in range(n)])
    if shared:
        decode_block = share[0]
    line = lax.all_gather(decode_block, "z", axis=0)

    pairs = [(i, i + 1) for i in range(1, n - 1, 2)]
    taps = first_kernel.reshape(3, 1152, 128)
    own = call(
        own_stage,
        jax.ShapeDtypeStruct((4, 256, 256), jnp.float32),
        [pltpu.VMEM((4, 18, 16, 384), jnp.bfloat16)],
        (volume, taps),
        2 * 1024 * 2304 * 256,
        24,
    )
    lane = np.arange(256)
    source = (lane // 64 + GROUP * (lane % 64 // chans)) * chans + lane % chans
    order = jnp.asarray(np.arange(256)[:, None] == source[None, :], jnp.bfloat16)
    rise_part = call(
        lambda marks_ref, *refs: rise_stage(marks_ref, chans, *refs),
        bf16((n * chans, 512)),
        [],
        (marks, rise_kernel.reshape(8, n * chans, 256)),
        2 * 8 * n * chans * 256 * 64,
        16,
        scalars=1,
    )
    pooled_two, *skips = call(
        stem_stage,
        (bf16((n, 16, 256)),) + (bf16((48, 256)),) * GROUP,
        [
            pltpu.VMEM((6, 18, 16, 384), jnp.bfloat16),
            pltpu.VMEM((128, 128), jnp.float32),
            pltpu.VMEM((4, 10, 24, 128), jnp.float32),
            pltpu.VMEM((256, 1152), jnp.bfloat16),
            pltpu.VMEM((2, 32, 128), jnp.float32),
            pltpu.VMEM((GROUP, 48, 256), jnp.bfloat16),
        ],
        (marks, off_chip, on_chip, own, taps, second_kernel.reshape(3, 1152, 256), order, rise_part),
        2 * 1024 * 2304 * 256,
        24,
        scalars=1,
        unread=1,
    )
    pooled_whole = exchange(pooled_two, ALL)
    near = by_xor(skips)
    blocks = pltpu.VMEM((GROUP, 48, 256), jnp.bfloat16)

    deep = call(
        deep_stage,
        bf16((n, chans, voxels)),
        [],
        (
            pooled_whole.reshape(voxels, 256),
            deep_kernel.transpose(0, 1, 2, 4, 3).reshape(27 * chans, 256),
        ),
        2 * 27 * chans * 256 * voxels,
        16,
    )
    if shared:
        weights = (line, lax.ppermute(line[:, :336], "rep", [(0, 1), (1, 0)]))
    elif chans % 16:
        weights = line.reshape(planes, 27, chans, 256).transpose(1, 0, 2, 3)
        weights = (weights.reshape(1, 27 * 128, 256),)
    else:
        weights = (line,)
    swaps = ()
    if not ride:
        swaps = call(
            edge_stage,
            (bf16((16, 256)), bf16((16, 256))),
            [blocks],
            (marks, *near),
            0,
            16,
            scalars=1,
        )
        near_pairs = [(p, p + 1) for p in range(0, planes - 1, 2)]
        far_pairs = [(p, p + 1) for p in range(1, planes - 1, 2)]
        near_swap = lax.ppermute(swaps[0], "z", near_pairs + [(j, i) for i, j in near_pairs])
        far_swap = lax.ppermute(swaps[1], "z", far_pairs + [(j, i) for i, j in far_pairs])
        swaps = (near_swap, far_swap)
    deep_whole = exchange(deep, ALL).reshape(n * chans, voxels)

    deeper = call(
        deeper_stage,
        bf16((n, chans, 128)),
        [blocks],
        (
            marks,
            deep_whole,
            deeper_kernel.transpose(0, 1, 2, 4, 3).reshape(27 * chans, n * chans),
            *(near if ride else ()),
        ),
        2 * 27 * chans * n * chans * voxels,
        16,
        scalars=1,
    )
    deeper_near = exchange(deeper, ALL)

    partials = call(
        functools.partial(decode_stage, ride),
        (bf16((128, 256)),) * GROUP,
        [
            pltpu.VMEM((10, 10, 24, 128), jnp.float32),
            pltpu.VMEM((640, 1152), jnp.bfloat16),
            pltpu.VMEM((8, 128, 128), jnp.float32),
            blocks,
            pltpu.VMEM((GROUP, 128, 256), jnp.bfloat16),
        ],
        (marks, deeper_near, rise_part, *swaps, *near, *weights),
        2 * 512 * 3456 * 256,
        24,
        scalars=1,
    )
    partials = by_xor(partials)
    out = call(
        final_stage,
        bf16((1024, 128)),
        [pltpu.VMEM((1024, 128), jnp.float32)],
        (*partials, final_kernel.reshape(8, 256, 128)),
        2 * 128 * 256 * 1024,
        16,
    )
    return out.reshape(4, 16, 16, 128)


def solution(mesh):
    reps, n = mesh.devices.shape
    grid = jax.sharding.Mesh(mesh.devices.reshape(reps, n // GROUP, GROUP), ("rep",) + ALL)
    return jax.shard_map(
        body,
        mesh=grid,
        in_specs=(
            P(("rep",) + ALL, None, None, None),
            P(),
            P(),
            P(None, None, None, None, ALL),
            P(None, None, None, None, ALL),
            P(),
            P(None, None, None, ALL, None),
            P(),
        ),
        out_specs=P(("rep",) + ALL, None, None, None),
        check_vma=False,
    )
```

```python
import functools

import jax
import jax.numpy as jnp
import numpy as np
from jax import lax
from jax.experimental import pallas as pl
from jax.experimental.pallas import tpu as pltpu
from jax.sharding import PartitionSpec as P

GROUP = 4
MIB = 1024 * 1024


def call(kernel, outs, scratch, args, flops, vmem_mib, scalars=0, unread=0):
    spaces = [pltpu.SMEM] * scalars + [pltpu.VMEM] * (len(args) - scalars - unread)
    spaces += [pl.ANY] * unread
    return pl.pallas_call(
        kernel,
        out_shape=outs,
        in_specs=[pl.BlockSpec(memory_space=space) for space in spaces],
        out_specs=jax.tree.map(lambda _: pl.BlockSpec(memory_space=pltpu.VMEM), outs),
        scratch_shapes=scratch,
        compiler_params=pltpu.CompilerParams(vmem_limit_bytes=vmem_mib * MIB),
        cost_estimate=pl.CostEstimate(
            flops=flops,
            bytes_accessed=sum(a.size * a.dtype.itemsize for a in args[: len(args) - unread]),
            transcendentals=0,
        ),
    )(*args)


def dot(left, right, dims=((1,), (0,))):
    return lax.dot_general(left, right, (dims, ((), ())), preferred_element_type=jnp.float32)


def round_once(values):
    return values.astype(jnp.bfloat16).astype(jnp.float32)


def fill_patches(framed, patches, slices):
    for b in range(3):
        for c in range(3):
            tap = framed[:, b : b + 8, 7 + c : 15 + c, :].reshape(slices * 64, 128)
            col = (b * 3 + c) * 128
            patches[:, col : col + 128] = tap.astype(jnp.bfloat16)


def shift_slice(shifted, s, values):
    row = lax.broadcasted_iota(jnp.int32, (256, 128), 0) & 15
    here = values.reshape(256, 128).astype(jnp.float32)
    before = jnp.where(row == 0, 0.0, pltpu.roll(here, 1, 0))
    after = jnp.where(row == 15, 0.0, pltpu.roll(here, 255, 0))
    shifted[s, 0] = jnp.zeros((16, 384), jnp.bfloat16)
    shifted[s, 17] = jnp.zeros((16, 384), jnp.bfloat16)
    for c, tap in enumerate((before, here, after)):
        tap = tap.astype(jnp.bfloat16).reshape(16, 16, 128)
        shifted[s, 1:17, :, 128 * c : 128 * c + 128] = tap


def depth_pair(shifted, slices, weights, steps):
    left = jnp.concatenate(
        [shifted[s, b : b + 16].reshape(256, 384) for s in slices for b in range(3)], axis=1
    )
    none = jnp.zeros((1152, 128), jnp.bfloat16)
    right = [
        jnp.concatenate(
            [weights[j] if j < 3 else none, weights[j - 1] if j > 0 else none], axis=1
        )
        for j in steps
    ]
    return dot(left, jnp.concatenate(right, axis=0))


def depth_one(shifted, s, weights):
    left = jnp.concatenate([shifted[s, b : b + 16].reshape(256, 384) for b in range(3)], axis=1)
    return dot(left, weights)


def front_stage(odd, rep, volume, decode, off_chip, on_chip, *refs):
    done = refs[-1]
    pairs = [
        (volume.at[pl.ds(odd[0], 3)], off_chip),
        (volume.at[pl.ds(1 - odd[0], 3)], on_chip),
    ]
    if len(refs) == 2:
        block = refs[0]
        at = pl.multiple_of(528 * rep[0], 16)
        pairs += [
            (decode.at[pl.ds(at, 336)], block.at[pl.ds(0, 336)]),
            (decode.at[pl.ds(336, 192)], block.at[pl.ds(336, 192)]),
        ]
    copies = [
        pltpu.make_async_copy(source, target, done.at[i]) for i, (source, target) in enumerate(pairs)
    ]
    for copy in copies:
        copy.start()
    for copy in copies:
        copy.wait()


def own_stage(volume, weights, out, shifted):
    for s in range(4):
        shift_slice(shifted, s, volume[s])
    out[0, :, :128] = jnp.zeros((256, 128), jnp.float32)
    out[0, :, 128:] = depth_one(shifted, 0, weights[2])
    out[1] = depth_pair(shifted, (0, 1, 2), weights, (1, 2, 3))
    out[2] = depth_pair(shifted, (1, 2, 3), weights, (0, 1, 2))
    out[3, :, :128] = depth_one(shifted, 3, weights[0])
    out[3, :, 128:] = jnp.zeros((256, 128), jnp.float32)


def stem_stage(marks, off_chip, on_chip, own, weights, second, order, _, *refs):
    pooled_out, skip_outs = refs[0], refs[1 : 1 + GROUP]
    shifted, halves, framed, patches, quarters, blocks = refs[1 + GROUP :]
    for s in range(3):
        even = marks[4] == 0
        shift_slice(shifted, s, jnp.where(even, off_chip[s], on_chip[s]))
        shift_slice(shifted, 3 + s, jnp.where(even, on_chip[s], off_chip[s]))
    framed[...] = jnp.zeros(framed.shape, jnp.float32)
    for m in range(4):
        if m == 0:
            first = own[0] + depth_pair(shifted, (0, 1, 2), weights, (0, 1, 2))
        elif m == 3:
            first = own[3] + depth_pair(shifted, (3, 4, 5), weights, (1, 2, 3))
        elif m == 1:
            near = own[1, :, :128] + depth_one(shifted, 2, weights[0])
            first = jnp.concatenate([near, own[1, :, 128:]], axis=1)
        else:
            far = own[2, :, 128:] + depth_one(shifted, 3, weights[2])
            first = jnp.concatenate([own[2, :, :128], far], axis=1)
        first = round_once(jnp.maximum(first, 0.0))
        pair = (first[:, :128] + first[:, 128:]).reshape(8, 32, 128)
        halves[...] = (pair[:, :16] + pair[:, 16:]).reshape(128, 128)
        pooled = halves[pl.ds(0, 64, stride=2), :] + halves[pl.ds(1, 64, stride=2), :]
        pooled = round_once(pooled * 0.125)
        if m == 0:
            pooled = jnp.where(marks[5] == 0, 0.0, pooled)
        if m == 3:
            pooled = jnp.where(marks[6] == 0, 0.0, pooled)
        framed[m, 1:9, 8:16, :] = pooled.reshape(8, 8, 128)
    fill_patches(framed, patches, 4)
    skip = dot(patches[0:128], second[0])
    skip += dot(patches[64:192], second[1])
    skip += dot(patches[128:256], second[2])
    skip = jnp.maximum(skip, 0.0).astype(jnp.bfloat16)
    wide = skip.astype(jnp.float32)
    pair = (wide[:64] + wide[64:]).reshape(4, 16, 256)
    pair = (pair[:, :8] + pair[:, 8:]).reshape(32, 256)
    for k in range(2):
        quarters[k] = pair[:, 128 * k : 128 * k + 128]
    pooled = jnp.concatenate(
        [
            quarters[k, pl.ds(0, 16, stride=2), :] + quarters[k, pl.ds(1, 16, stride=2), :]
            for k in range(2)
        ],
        axis=1,
    )
    pooled = (pooled * 0.125).astype(jnp.bfloat16)
    for p in range(pooled_out.shape[0]):
        pooled_out[p] = pooled
    sorted_skip = dot(skip, order[...])
    for r in range(GROUP):
        near, far = sorted_skip[:64, 64 * r : 64 * r + 64], sorted_skip[64:, 64 * r : 64 * r + 64]
        block = jnp.concatenate([near, far], axis=1)
        block = jnp.concatenate([block[:32], block[32:]], axis=1).astype(jnp.bfloat16)
        blocks[r, 0:32, :] = block
        first, last = sorted_skip[16 * r : 16 * r + 16], sorted_skip[64 + 16 * r : 80 + 16 * r]
        blocks[r, 32:48, :] = jnp.where(marks[0] == 0, first, last).astype(jnp.bfloat16)
    for k in range(GROUP):
        skip_outs[k][...] = blocks[marks[0] ^ k]


def edge_slice(block, far):
    lower = lax.broadcasted_iota(jnp.int32, (16, 128), 1) < 64
    sides = []
    for k in range(2):
        half = block[:, 128 * k : 128 * k + 128].astype(jnp.float32)
        top, bottom = half[:16], half[16:]
        if far:
            top = pltpu.roll(top, 64, 1)
        else:
            bottom = pltpu.roll(bottom, 64, 1)
        sides.append(jnp.where(lower, top, bottom))
    return jnp.concatenate(sides, axis=1)


def spread_taps(weights, values, dims, chans, voxels):
    lane = lax.broadcasted_iota(jnp.int32, (chans, voxels), 1)

    def moved(term, tap, step, place, last):
        if tap == 1:
            return term
        keep = place > 0 if tap == 0 else place < last
        return jnp.where(keep, pltpu.roll(term, ((1 - tap) * step) % voxels, 1), 0.0)

    total = None
    for a in range(3):
        products = dot(weights[a * 9 * chans : (a + 1) * 9 * chans, :], values, dims)
        plane = None
        for b in range(3):
            line = None
            for c in range(3):
                at = (b * 3 + c) * chans
                term = moved(products[at : at + chans], c, 1, lane & 3, 3)
                line = term if line is None else line + term
            line = moved(line, b, 4, (lane >> 2) & 3, 3)
            plane = line if plane is None else plane + line
        plane = moved(plane, a, 16, lane >> 4, voxels // 16 - 1)
        total = plane if total is None else total + plane
    return jnp.maximum(total, 0.0)


def by_rank(marks, near, blocks):
    for k in range(GROUP):
        blocks[marks[0] ^ k] = near[k][near[k].shape[0] - 48 :, :]


def by_depth(marks, near, parts, step):
    for k in range(GROUP):
        parts[marks[0] ^ k] = near[k][0 : parts.shape[1], :]
    return jnp.concatenate(
        [
            parts[r, at : at + step, :]
            for at in range(0, parts.shape[1], step)
            for r in range(GROUP)
        ],
        axis=0,
    )


def relay_stage(marks, *refs):
    line, refs = refs[:GROUP], refs[GROUP:]
    step = line[0].shape[0]
    if len(refs) == 1:
        for k in range(GROUP):
            refs[0][pl.ds(pl.multiple_of((marks[3] ^ k) * step, 16), step), :] = line[k][...]
        return
    skips, outs = refs[:GROUP], refs[GROUP:]
    for j in range(GROUP):
        for k in range(GROUP):
            outs[j][pl.ds(pl.multiple_of((marks[3] ^ k) * step, 16), step), :] = line[k][...]
        outs[j][GROUP * step :, :] = skips[j][...]


def edge_stage(marks, *refs):
    near, (near_swap, far_swap, blocks) = refs[:GROUP], refs[GROUP:]
    by_rank(marks, near, blocks)
    first = edge_slice(blocks[0, 0:32, :], False)
    last = edge_slice(blocks[GROUP - 1, 0:32, :], True)
    even = marks[2] == 0
    near_swap[...] = jnp.where(even, last, first).astype(jnp.bfloat16)
    far_swap[...] = jnp.where(even, first, last).astype(jnp.bfloat16)


def deep_stage(marks, weights, *refs):
    near, out, parts = refs[:-2], refs[-2], refs[-1]
    _, chans, voxels = out.shape
    values = near[0][...] if len(near) == 1 else by_depth(marks, near, parts, 16)
    deep = spread_taps(weights, values, ((1,), (1,)), chans, voxels).astype(jnp.bfloat16)
    for dest in range(out.shape[0]):
        out[dest] = deep


def deeper_stage(near_count, marks, weights, *refs):
    near, deep, (out, blocks, parts) = refs[:near_count], refs[near_count:-3], refs[-3:]
    n, chans, _ = out.shape
    voxels = deep[0].shape[1]
    values = deep[0][...] if len(deep) == 1 else by_depth(marks, deep, parts, chans)
    deeper = spread_taps(weights, values, ((1,), (0,)), chans, voxels)
    lane = lax.broadcasted_iota(jnp.int32, (chans, 128), 1)
    planes = n // GROUP
    ride = len(near) == GROUP
    if ride:
        by_rank(marks, near, blocks)
        edges = [blocks[r, 32:48, :].astype(jnp.float32) for r in (0, GROUP - 1)]
        riders = [
            [
                jnp.concatenate(
                    [
                        pltpu.roll(edge[:, at // 128 * 128 : at // 128 * 128 + 128], (96 - at) % 128, 1)
                        for at in (64 * r, 64 * r + 32)
                    ],
                    axis=0,
                )
                for r in range(GROUP)
            ]
            for edge in edges
        ]
    for p in range(planes):
        part = pltpu.roll(deeper, (16 - 64 * p) % voxels, 1)[:, :128]
        if p == 0:
            part = jnp.where(lane < 16, 0.0, part)
        if p == planes - 1:
            part = jnp.where(lane >= 80, 0.0, part)
        for r in range(GROUP):
            whole = part
            if ride:
                rider = jnp.where(marks[3] < p, riders[1][r], riders[0][r])
                whole = jnp.where(lane < 96, part, rider)
            out[GROUP * p + r] = whole.astype(jnp.bfloat16)


def rise_stage(marks, chans, rise, out):
    lane = lax.broadcasted_iota(jnp.int32, (256, 64), 1)
    row = lax.broadcasted_iota(jnp.int32, (256, 64), 0)
    source = (marks[0] + GROUP * (lane // chans)) * chans + lane % chans
    mine = jnp.where(row == source, 1.0, 0.0).astype(jnp.bfloat16)
    for pair in range(4):
        both = [dot(rise[2 * pair + k], mine) for k in range(2)]
        both = jnp.concatenate(both, axis=1).astype(jnp.bfloat16)
        out[:, 128 * pair : 128 * pair + 128] = both


def decode_stage(ride, marks, deeper, rise, *refs):
    swaps = () if ride else refs[:2]
    near, refs = refs[len(swaps) : len(swaps) + GROUP], refs[len(swaps) + GROUP :]
    decode, outs = refs[: -5 - GROUP], refs[-5 - GROUP : -5]
    framed, patches, risen, blocks, parts = refs[-5:]
    by_rank(marks, near, blocks)
    n, chans, _ = deeper.shape
    plane, planes = marks[3], n // GROUP
    upper = lax.broadcasted_iota(jnp.int32, (64, 128), 1) >= 64

    def edge(low):
        if not ride:
            even = marks[2] == 0
            sides = [swap[...].astype(jnp.float32) for swap in swaps]
            side = jnp.where(even, sides[low], sides[not low])
            parts = []
            for k in range(2):
                half = side[:, 128 * k : 128 * k + 128]
                parts += [pltpu.roll(half, 64, 1), half]
            return jnp.concatenate(parts, axis=0)
        other = jnp.maximum(plane - 1, 0) if low else jnp.minimum(plane + 1, planes - 1)
        lane = lax.broadcasted_iota(jnp.int32, (16, 128), 1)
        parts = []
        for r in range(GROUP):
            block = deeper[GROUP * other + r].astype(jnp.float32)
            parts.append(jnp.where(lane < 96, pltpu.roll(block[:16], 96, 1), block[16:]))
        return jnp.where(other == plane, 0.0, jnp.concatenate(parts, axis=0))

    framed[...] = jnp.zeros(framed.shape, jnp.float32)
    spread = round_once(dot(deeper[...].reshape(n * chans, 128).astype(jnp.float32).T.astype(jnp.bfloat16), rise[...]))
    for pair in range(4):
        both = spread[:, 128 * pair : 128 * pair + 128]
        risen[2 * pair] = both
        risen[2 * pair + 1] = pltpu.roll(both, 64, 1)
    for s in range(10):
        d, a = (s + 1) // 2, (s + 1) % 2
        for h in range(4):
            for b in range(2):
                for c in range(2):
                    framed[s, 1 + 2 * h + b, pl.ds(8 + c, 4, stride=2), :] = risen[
                        4 * a + 2 * b + c, 16 * d + 4 * h : 16 * d + 4 * h + 4, :
                    ]
        if s == 0 or s == 9:
            skip = edge(s == 0)
        else:
            both = blocks[(s - 1) // 2, 0:32, :].astype(jnp.float32)
            skip = jnp.concatenate([both[:, :128], both[:, 128:]], axis=0)
            if (s - 1) % 2 == 0:
                skip = pltpu.roll(skip, 64, 1)
        joined = framed[s, 1:9, 8:16, :].reshape(64, 128)
        framed[s, 1:9, 8:16, :] = jnp.where(upper, skip, joined).reshape(8, 8, 128)
    fill_patches(framed, patches, 10)
    def rows_at(rep, z, row):
        if rep == 0 and row >= 528:
            return decode[1][z, row - 528 : row - 512, :]
        if rep == 1 and row < 336:
            return decode[1][z, row : row + 16, :]
        if rep == 1 and row >= 528:
            row -= 528
        return decode[0][z, row : row + 16, :]

    def multiply(rep):
        count = decode[0].shape[0]
        step = 128 // count
        partial = None
        for a in range(3):
            right = [
                rows_at(rep, z, row)
                for tap in range(9 * a, 9 * a + 9)
                for z in range(count)
                for row in range(tap * step, (tap + 1) * step, 16)
            ]
            term = dot(patches[64 * a : 64 * a + 512], jnp.concatenate(right, axis=0))
            partial = term if partial is None else partial + term
        parts[...] = partial.astype(jnp.bfloat16).reshape(GROUP, 128, 256)

    if len(decode) == 1:
        multiply(None)
    else:
        pl.when(marks[1] == 0)(lambda: multiply(0))
        pl.when(marks[1] == 1)(lambda: multiply(1))
    for k in range(GROUP):
        outs[k][...] = parts[marks[0] ^ k]


def final_stage(*refs):
    partials, (weights, out, spaced) = refs[:GROUP], refs[GROUP:]
    decoded = partials[0][...].astype(jnp.float32)
    for partial in partials[1:]:
        decoded += partial[...].astype(jnp.float32)
    decoded = jnp.maximum(decoded, 0.0).astype(jnp.bfloat16)
    for a in range(2):
        for b in range(2):
            for c in range(2):
                values = dot(decoded, weights[4 * a + 2 * b + c])
                for d in range(2):
                    for h in range(8):
                        at = ((2 * d + a) * 16 + 2 * h + b) * 16 + c
                        spaced[pl.ds(at, 8, stride=2), :] = values[64 * d + 8 * h : 64 * d + 8 * h + 8]
    out[...] = spaced[...].astype(jnp.bfloat16)


ALL = ("z", "r")


def exchange(payload, axis):
    return lax.all_to_all(payload, axis, split_axis=0, concat_axis=0, tiled=True)


def by_xor(blocks, axis):
    swaps = [[(r, r ^ k) for r in range(GROUP)] for k in range(GROUP)]
    return [blocks[0]] + [lax.ppermute(blocks[k], axis, swaps[k]) for k in range(1, GROUP)]


def body(
    volume,
    first_kernel,
    second_kernel,
    deep_kernel,
    deeper_kernel,
    rise_kernel,
    decode_kernel,
    final_kernel,
):
    n = lax.axis_size(ALL)
    place = lax.axis_index(ALL)
    planes = n // GROUP
    rank = lax.axis_index("r")
    chans = deep_kernel.shape[4]
    voxels = 16 * n
    bf16 = functools.partial(jax.ShapeDtypeStruct, dtype=jnp.bfloat16)

    rep, plane = lax.axis_index("rep"), lax.axis_index("z")
    marks = jnp.stack([rank, rep, plane % 2, plane, place % 2, place, n - 1 - place])
    marks = marks.astype(jnp.int32)
    decode_block = decode_kernel.reshape(27 * chans, 256)
    shared = lax.axis_size("rep") == 2 and chans == 32
    ride = chans == 32
    paired = planes == GROUP
    halo = bf16((3, 16, 16, 128))
    in_spaces = [pltpu.SMEM, pltpu.SMEM, pl.ANY, pl.ANY]
    off_chip, on_chip, *share = pl.pallas_call(
        front_stage,
        out_shape=(halo, halo) + (bf16((528, 256)),) * shared,
        in_specs=[pl.BlockSpec(memory_space=space) for space in in_spaces],
        out_specs=(pl.BlockSpec(memory_space=pltpu.VMEM),) * (2 + shared),
        scratch_shapes=[pltpu.SemaphoreType.DMA((4,))],
        compiler_params=pltpu.CompilerParams(vmem_limit_bytes=60 * MIB),
        cost_estimate=pl.CostEstimate(flops=0, bytes_accessed=10**6, transcendentals=0),
    )(
        (place % 2).astype(jnp.int32).reshape(1),
        rep.astype(jnp.int32).reshape(1),
        volume,
        decode_block,
    )
    pairs = [(i, i + 1) for i in range(1, n - 1, 2)]
    off_chip = lax.ppermute(off_chip, ALL, pairs + [(j, i) for i, j in pairs])
    on_chip = lax.ppermute(on_chip, ALL, [(i, i ^ 1) for i in range(n)])
    if shared:
        decode_block = share[0]
    line = lax.all_gather(decode_block, "z", axis=0)

    pairs = [(i, i + 1) for i in range(1, n - 1, 2)]
    taps = first_kernel.reshape(3, 1152, 128)
    own = call(
        own_stage,
        jax.ShapeDtypeStruct((4, 256, 256), jnp.float32),
        [pltpu.VMEM((4, 18, 16, 384), jnp.bfloat16)],
        (volume, taps),
        2 * 1024 * 2304 * 256,
        24,
    )
    lane = np.arange(256)
    source = (lane // 64 + GROUP * (lane % 64 // chans)) * chans + lane % chans
    order = jnp.asarray(np.arange(256)[:, None] == source[None, :], jnp.bfloat16)
    rise_part = call(
        lambda marks_ref, *refs: rise_stage(marks_ref, chans, *refs),
        bf16((n * chans, 512)),
        [],
        (marks, rise_kernel.reshape(8, n * chans, 256)),
        2 * 8 * n * chans * 256 * 64,
        16,
        scalars=1,
    )
    pooled_two, *skips = call(
        stem_stage,
        (bf16((1 if paired else n, 16, 256)),) + (bf16((48, 256)),) * GROUP,
        [
            pltpu.VMEM((6, 18, 16, 384), jnp.bfloat16),
            pltpu.VMEM((128, 128), jnp.float32),
            pltpu.VMEM((4, 10, 24, 128), jnp.float32),
            pltpu.VMEM((256, 1152), jnp.bfloat16),
            pltpu.VMEM((2, 32, 128), jnp.float32),
            pltpu.VMEM((GROUP, 48, 256), jnp.bfloat16),
        ],
        (marks, off_chip, on_chip, own, taps, second_kernel.reshape(3, 1152, 256), order, rise_part),
        2 * 1024 * 2304 * 256,
        24,
        scalars=1,
        unread=1,
    )
    if paired:
        line_blocks = by_xor([pooled_two.reshape(16, 256)] * GROUP, "z")
        relays = call(
            relay_stage,
            (bf16((112, 256)),) * GROUP,
            [],
            (marks, *line_blocks, *skips),
            0,
            16,
            scalars=1,
        )
        near = by_xor(relays, "r")
        pooled_whole = near
    else:
        pooled_whole = (exchange(pooled_two, ALL).reshape(voxels, 256),)
        near = by_xor(skips, "r")
    blocks = pltpu.VMEM((GROUP, 48, 256), jnp.bfloat16)

    deep = call(
        deep_stage,
        bf16((1 if paired else n, chans, voxels)),
        [pltpu.VMEM((GROUP, 64, 256), jnp.bfloat16)],
        (
            marks,
            deep_kernel.transpose(0, 1, 2, 4, 3).reshape(27 * chans, 256),
            *pooled_whole,
        ),
        2 * 27 * chans * 256 * voxels,
        16,
        scalars=1,
    )
    if shared:
        weights = (line, lax.ppermute(line[:, :336], "rep", [(0, 1), (1, 0)]))
    elif chans % 16:
        weights = line.reshape(planes, 27, chans, 256).transpose(1, 0, 2, 3)
        weights = (weights.reshape(1, 27 * 128, 256),)
    else:
        weights = (line,)
    swaps = ()
    if not ride:
        swaps = call(
            edge_stage,
            (bf16((16, 256)), bf16((16, 256))),
            [blocks],
            (marks, *near),
            0,
            16,
            scalars=1,
        )
        near_pairs = [(p, p + 1) for p in range(0, planes - 1, 2)]
        far_pairs = [(p, p + 1) for p in range(1, planes - 1, 2)]
        near_swap = lax.ppermute(swaps[0], "z", near_pairs + [(j, i) for i, j in near_pairs])
        far_swap = lax.ppermute(swaps[1], "z", far_pairs + [(j, i) for i, j in far_pairs])
        swaps = (near_swap, far_swap)
    if paired:
        line_blocks = by_xor([deep.reshape(chans, voxels)] * GROUP, "z")
        relay = call(
            relay_stage,
            bf16((GROUP * chans, voxels)),
            [],
            (marks, *line_blocks),
            0,
            16,
            scalars=1,
        )
        deep_whole = by_xor([relay] * GROUP, "r")
    else:
        deep_whole = (exchange(deep, ALL).reshape(n * chans, voxels),)

    riders = near if ride else ()
    deeper = call(
        functools.partial(deeper_stage, len(riders)),
        bf16((n, chans, 128)),
        [blocks, pltpu.VMEM((GROUP, planes * chans, voxels), jnp.bfloat16)],
        (
            marks,
            deeper_kernel.transpose(0, 1, 2, 4, 3).reshape(27 * chans, n * chans),
            *riders,
            *deep_whole,
        ),
        2 * 27 * chans * n * chans * voxels,
        16,
        scalars=1,
    )
    deeper_near = exchange(deeper, ALL)

    partials = call(
        functools.partial(decode_stage, ride),
        (bf16((128, 256)),) * GROUP,
        [
            pltpu.VMEM((10, 10, 24, 128), jnp.float32),
            pltpu.VMEM((640, 1152), jnp.bfloat16),
            pltpu.VMEM((8, 128, 128), jnp.float32),
            blocks,
            pltpu.VMEM((GROUP, 128, 256), jnp.bfloat16),
        ],
        (marks, deeper_near, rise_part, *swaps, *near, *weights),
        2 * 512 * 3456 * 256,
        24,
        scalars=1,
    )
    partials = by_xor(partials, "r")
    out = call(
        final_stage,
        bf16((1024, 128)),
        [pltpu.VMEM((1024, 128), jnp.float32)],
        (*partials, final_kernel.reshape(8, 256, 128)),
        2 * 128 * 256 * 1024,
        16,
    )
    return out.reshape(4, 16, 16, 128)


def solution(mesh):
    reps, n = mesh.devices.shape
    grid = jax.sharding.Mesh(mesh.devices.reshape(reps, n // GROUP, GROUP), ("rep",) + ALL)
    return jax.shard_map(
        body,
        mesh=grid,
        in_specs=(
            P(("rep",) + ALL, None, None, None),
            P(),
            P(),
            P(None, None, None, None, ALL),
            P(None, None, None, None, ALL),
            P(),
            P(None, None, None, ALL, None),
            P(),
        ),
        out_specs=P(("rep",) + ALL, None, None, None),
        check_vma=False,
    )
```

```python
import functools

import jax
import jax.numpy as jnp
import numpy as np
from jax import lax
from jax.experimental import pallas as pl
from jax.experimental.pallas import tpu as pltpu
from jax.sharding import PartitionSpec as P

GROUP = 4
MIB = 1024 * 1024


def call(kernel, outs, scratch, args, flops, vmem_mib, scalars=0, unread=0):
    spaces = [pltpu.SMEM] * scalars + [pltpu.VMEM] * (len(args) - scalars - unread)
    spaces += [pl.ANY] * unread
    return pl.pallas_call(
        kernel,
        out_shape=outs,
        in_specs=[pl.BlockSpec(memory_space=space) for space in spaces],
        out_specs=jax.tree.map(lambda _: pl.BlockSpec(memory_space=pltpu.VMEM), outs),
        scratch_shapes=scratch,
        compiler_params=pltpu.CompilerParams(vmem_limit_bytes=vmem_mib * MIB),
        cost_estimate=pl.CostEstimate(
            flops=flops,
            bytes_accessed=sum(a.size * a.dtype.itemsize for a in args[: len(args) - unread]),
            transcendentals=0,
        ),
    )(*args)


def dot(left, right, dims=((1,), (0,))):
    return lax.dot_general(left, right, (dims, ((), ())), preferred_element_type=jnp.float32)


def round_once(values):
    return values.astype(jnp.bfloat16).astype(jnp.float32)


def fill_patches(framed, patches, slices):
    for b in range(3):
        for c in range(3):
            tap = framed[:, b : b + 8, 7 + c : 15 + c, :].reshape(slices * 64, 128)
            col = (b * 3 + c) * 128
            patches[:, col : col + 128] = tap.astype(jnp.bfloat16)


def shift_slice(shifted, s, values):
    row = lax.broadcasted_iota(jnp.int32, (256, 128), 0) & 15
    here = values.reshape(256, 128).astype(jnp.float32)
    before = jnp.where(row == 0, 0.0, pltpu.roll(here, 1, 0))
    after = jnp.where(row == 15, 0.0, pltpu.roll(here, 255, 0))
    shifted[s, 0] = jnp.zeros((16, 384), jnp.bfloat16)
    shifted[s, 17] = jnp.zeros((16, 384), jnp.bfloat16)
    for c, tap in enumerate((before, here, after)):
        tap = tap.astype(jnp.bfloat16).reshape(16, 16, 128)
        shifted[s, 1:17, :, 128 * c : 128 * c + 128] = tap


def depth_pair(shifted, slices, weights, steps):
    left = jnp.concatenate(
        [shifted[s, b : b + 16].reshape(256, 384) for s in slices for b in range(3)], axis=1
    )
    none = jnp.zeros((1152, 128), jnp.bfloat16)
    right = [
        jnp.concatenate(
            [weights[j] if j < 3 else none, weights[j - 1] if j > 0 else none], axis=1
        )
        for j in steps
    ]
    return dot(left, jnp.concatenate(right, axis=0))


def depth_one(shifted, s, weights):
    left = jnp.concatenate([shifted[s, b : b + 16].reshape(256, 384) for b in range(3)], axis=1)
    return dot(left, weights)


def front_stage(odd, rep, volume, decode, off_chip, on_chip, *refs):
    done = refs[-1]
    pairs = [
        (volume.at[pl.ds(odd[0], 3)], off_chip),
        (volume.at[pl.ds(1 - odd[0], 3)], on_chip),
    ]
    if len(refs) == 2:
        block = refs[0]
        at = pl.multiple_of(528 * rep[0], 16)
        pairs += [
            (decode.at[pl.ds(at, 336)], block.at[pl.ds(0, 336)]),
            (decode.at[pl.ds(336, 192)], block.at[pl.ds(336, 192)]),
        ]
    copies = [
        pltpu.make_async_copy(source, target, done.at[i]) for i, (source, target) in enumerate(pairs)
    ]
    for copy in copies:
        copy.start()
    for copy in copies:
        copy.wait()


def own_stage(volume, weights, out, shifted):
    for s in range(4):
        shift_slice(shifted, s, volume[s])
    out[0, :, :128] = jnp.zeros((256, 128), jnp.float32)
    out[0, :, 128:] = depth_one(shifted, 0, weights[2])
    out[1] = depth_pair(shifted, (0, 1, 2), weights, (1, 2, 3))
    out[2] = depth_pair(shifted, (1, 2, 3), weights, (0, 1, 2))
    out[3, :, :128] = depth_one(shifted, 3, weights[0])
    out[3, :, 128:] = jnp.zeros((256, 128), jnp.float32)


def stem_stage(marks, off_chip, on_chip, own, weights, second, order, _, *refs):
    pooled_out, skip_outs = refs[0], refs[1 : 1 + GROUP]
    shifted, halves, framed, patches, quarters, blocks = refs[1 + GROUP :]
    for s in range(3):
        even = marks[4] == 0
        shift_slice(shifted, s, jnp.where(even, off_chip[s], on_chip[s]))
        shift_slice(shifted, 3 + s, jnp.where(even, on_chip[s], off_chip[s]))
    framed[...] = jnp.zeros(framed.shape, jnp.float32)
    for m in range(4):
        if m == 0:
            first = own[0] + depth_pair(shifted, (0, 1, 2), weights, (0, 1, 2))
        elif m == 3:
            first = own[3] + depth_pair(shifted, (3, 4, 5), weights, (1, 2, 3))
        elif m == 1:
            near = own[1, :, :128] + depth_one(shifted, 2, weights[0])
            first = jnp.concatenate([near, own[1, :, 128:]], axis=1)
        else:
            far = own[2, :, 128:] + depth_one(shifted, 3, weights[2])
            first = jnp.concatenate([own[2, :, :128], far], axis=1)
        first = round_once(jnp.maximum(first, 0.0))
        pair = (first[:, :128] + first[:, 128:]).reshape(8, 32, 128)
        halves[...] = (pair[:, :16] + pair[:, 16:]).reshape(128, 128)
        pooled = halves[pl.ds(0, 64, stride=2), :] + halves[pl.ds(1, 64, stride=2), :]
        pooled = round_once(pooled * 0.125)
        if m == 0:
            pooled = jnp.where(marks[5] == 0, 0.0, pooled)
        if m == 3:
            pooled = jnp.where(marks[6] == 0, 0.0, pooled)
        framed[m, 1:9, 8:16, :] = pooled.reshape(8, 8, 128)
    fill_patches(framed, patches, 4)
    skip = dot(patches[0:128], second[0])
    skip += dot(patches[64:192], second[1])
    skip += dot(patches[128:256], second[2])
    skip = jnp.maximum(skip, 0.0).astype(jnp.bfloat16)
    wide = skip.astype(jnp.float32)
    pair = (wide[:64] + wide[64:]).reshape(4, 16, 256)
    pair = (pair[:, :8] + pair[:, 8:]).reshape(32, 256)
    for k in range(2):
        quarters[k] = pair[:, 128 * k : 128 * k + 128]
    pooled = jnp.concatenate(
        [
            quarters[k, pl.ds(0, 16, stride=2), :] + quarters[k, pl.ds(1, 16, stride=2), :]
            for k in range(2)
        ],
        axis=1,
    )
    pooled = (pooled * 0.125).astype(jnp.bfloat16)
    for p in range(pooled_out.shape[0]):
        pooled_out[p] = pooled
    sorted_skip = dot(skip, order[...])
    for r in range(GROUP):
        near, far = sorted_skip[:64, 64 * r : 64 * r + 64], sorted_skip[64:, 64 * r : 64 * r + 64]
        block = jnp.concatenate([near, far], axis=1)
        block = jnp.concatenate([block[:32], block[32:]], axis=1).astype(jnp.bfloat16)
        blocks[r, 0:32, :] = block
        first, last = sorted_skip[16 * r : 16 * r + 16], sorted_skip[64 + 16 * r : 80 + 16 * r]
        blocks[r, 32:48, :] = jnp.where(marks[0] == 0, first, last).astype(jnp.bfloat16)
    for k in range(GROUP):
        skip_outs[k][...] = blocks[marks[0] ^ k]


def edge_slice(block, far):
    lower = lax.broadcasted_iota(jnp.int32, (16, 128), 1) < 64
    sides = []
    for k in range(2):
        half = block[:, 128 * k : 128 * k + 128].astype(jnp.float32)
        top, bottom = half[:16], half[16:]
        if far:
            top = pltpu.roll(top, 64, 1)
        else:
            bottom = pltpu.roll(bottom, 64, 1)
        sides.append(jnp.where(lower, top, bottom))
    return jnp.concatenate(sides, axis=1)


def spread_taps(weights, values, dims, chans, voxels):
    lane = lax.broadcasted_iota(jnp.int32, (chans, voxels), 1)

    def moved(term, tap, step, place, last):
        if tap == 1:
            return term
        keep = place > 0 if tap == 0 else place < last
        return jnp.where(keep, pltpu.roll(term, ((1 - tap) * step) % voxels, 1), 0.0)

    total = None
    for a in range(3):
        products = dot(weights[a * 9 * chans : (a + 1) * 9 * chans, :], values, dims)
        plane = None
        for b in range(3):
            line = None
            for c in range(3):
                at = (b * 3 + c) * chans
                term = moved(products[at : at + chans], c, 1, lane & 3, 3)
                line = term if line is None else line + term
            line = moved(line, b, 4, (lane >> 2) & 3, 3)
            plane = line if plane is None else plane + line
        plane = moved(plane, a, 16, lane >> 4, voxels // 16 - 1)
        total = plane if total is None else total + plane
    return jnp.maximum(total, 0.0)


def by_rank(marks, near, blocks):
    for k in range(GROUP):
        blocks[marks[0] ^ k] = near[k][near[k].shape[0] - 48 :, :]


def by_depth(marks, near, parts, step):
    for k in range(GROUP):
        parts[marks[0] ^ k] = near[k][0 : parts.shape[1], :]
    return jnp.concatenate(
        [
            parts[r, at : at + step, :]
            for at in range(0, parts.shape[1], step)
            for r in range(GROUP)
        ],
        axis=0,
    )


def relay_stage(marks, *refs):
    line, refs = refs[:GROUP], refs[GROUP:]
    step = line[0].shape[0]
    skips, outs = refs[:GROUP], refs[GROUP:]
    for j in range(GROUP):
        for k in range(GROUP):
            outs[j][pl.ds(pl.multiple_of((marks[3] ^ k) * step, 16), step), :] = line[k][...]
        outs[j][GROUP * step :, :] = skips[j][...]


def edge_stage(marks, *refs):
    near, (near_swap, far_swap, blocks) = refs[:GROUP], refs[GROUP:]
    by_rank(marks, near, blocks)
    first = edge_slice(blocks[0, 0:32, :], False)
    last = edge_slice(blocks[GROUP - 1, 0:32, :], True)
    even = marks[2] == 0
    near_swap[...] = jnp.where(even, last, first).astype(jnp.bfloat16)
    far_swap[...] = jnp.where(even, first, last).astype(jnp.bfloat16)


def deep_stage(marks, weights, *refs):
    near, out, parts = refs[:-2], refs[-2], refs[-1]
    _, chans, voxels = out.shape
    values = near[0][...] if len(near) == 1 else by_depth(marks, near, parts, 16)
    deep = spread_taps(weights, values, ((1,), (1,)), chans, voxels).astype(jnp.bfloat16)
    for dest in range(out.shape[0]):
        out[dest] = deep


def deeper_stage(near_count, marks, weights, *refs):
    near, (deep, out, blocks) = refs[:near_count], refs[near_count:]
    n, chans, _ = out.shape
    voxels = deep.shape[1]
    deeper = spread_taps(weights, deep[...], ((1,), (0,)), chans, voxels)
    lane = lax.broadcasted_iota(jnp.int32, (chans, 128), 1)
    planes = n // GROUP
    ride = len(near) == GROUP
    if ride:
        by_rank(marks, near, blocks)
        edges = [blocks[r, 32:48, :].astype(jnp.float32) for r in (0, GROUP - 1)]
        riders = [
            [
                jnp.concatenate(
                    [
                        pltpu.roll(edge[:, at // 128 * 128 : at // 128 * 128 + 128], (96 - at) % 128, 1)
                        for at in (64 * r, 64 * r + 32)
                    ],
                    axis=0,
                )
                for r in range(GROUP)
            ]
            for edge in edges
        ]
    for p in range(planes):
        part = pltpu.roll(deeper, (16 - 64 * p) % voxels, 1)[:, :128]
        if p == 0:
            part = jnp.where(lane < 16, 0.0, part)
        if p == planes - 1:
            part = jnp.where(lane >= 80, 0.0, part)
        for r in range(GROUP):
            whole = part
            if ride:
                rider = jnp.where(marks[3] < p, riders[1][r], riders[0][r])
                whole = jnp.where(lane < 96, part, rider)
            out[GROUP * p + r] = whole.astype(jnp.bfloat16)


def rise_stage(marks, chans, rise, out):
    lane = lax.broadcasted_iota(jnp.int32, (256, 64), 1)
    row = lax.broadcasted_iota(jnp.int32, (256, 64), 0)
    source = (marks[0] + GROUP * (lane // chans)) * chans + lane % chans
    mine = jnp.where(row == source, 1.0, 0.0).astype(jnp.bfloat16)
    for pair in range(4):
        both = [dot(rise[2 * pair + k], mine) for k in range(2)]
        both = jnp.concatenate(both, axis=1).astype(jnp.bfloat16)
        out[:, 128 * pair : 128 * pair + 128] = both


def decode_stage(ride, marks, deeper, rise, *refs):
    swaps = () if ride else refs[:2]
    near, refs = refs[len(swaps) : len(swaps) + GROUP], refs[len(swaps) + GROUP :]
    decode, outs = refs[: -5 - GROUP], refs[-5 - GROUP : -5]
    framed, patches, risen, blocks, parts = refs[-5:]
    by_rank(marks, near, blocks)
    n, chans, _ = deeper.shape
    plane, planes = marks[3], n // GROUP
    upper = lax.broadcasted_iota(jnp.int32, (64, 128), 1) >= 64

    def edge(low):
        if not ride:
            even = marks[2] == 0
            sides = [swap[...].astype(jnp.float32) for swap in swaps]
            side = jnp.where(even, sides[low], sides[not low])
            parts = []
            for k in range(2):
                half = side[:, 128 * k : 128 * k + 128]
                parts += [pltpu.roll(half, 64, 1), half]
            return jnp.concatenate(parts, axis=0)
        other = jnp.maximum(plane - 1, 0) if low else jnp.minimum(plane + 1, planes - 1)
        lane = lax.broadcasted_iota(jnp.int32, (16, 128), 1)
        parts = []
        for r in range(GROUP):
            block = deeper[GROUP * other + r].astype(jnp.float32)
            parts.append(jnp.where(lane < 96, pltpu.roll(block[:16], 96, 1), block[16:]))
        return jnp.where(other == plane, 0.0, jnp.concatenate(parts, axis=0))

    framed[...] = jnp.zeros(framed.shape, jnp.float32)
    spread = round_once(dot(deeper[...].reshape(n * chans, 128).astype(jnp.float32).T.astype(jnp.bfloat16), rise[...]))
    for pair in range(4):
        both = spread[:, 128 * pair : 128 * pair + 128]
        risen[2 * pair] = both
        risen[2 * pair + 1] = pltpu.roll(both, 64, 1)
    for s in range(10):
        d, a = (s + 1) // 2, (s + 1) % 2
        for h in range(4):
            for b in range(2):
                for c in range(2):
                    framed[s, 1 + 2 * h + b, pl.ds(8 + c, 4, stride=2), :] = risen[
                        4 * a + 2 * b + c, 16 * d + 4 * h : 16 * d + 4 * h + 4, :
                    ]
        if s == 0 or s == 9:
            skip = edge(s == 0)
        else:
            both = blocks[(s - 1) // 2, 0:32, :].astype(jnp.float32)
            skip = jnp.concatenate([both[:, :128], both[:, 128:]], axis=0)
            if (s - 1) % 2 == 0:
                skip = pltpu.roll(skip, 64, 1)
        joined = framed[s, 1:9, 8:16, :].reshape(64, 128)
        framed[s, 1:9, 8:16, :] = jnp.where(upper, skip, joined).reshape(8, 8, 128)
    fill_patches(framed, patches, 10)
    def rows_at(rep, z, row):
        if rep == 0 and row >= 528:
            return decode[1][z, row - 528 : row - 512, :]
        if rep == 1 and row < 336:
            return decode[1][z, row : row + 16, :]
        if rep == 1 and row >= 528:
            row -= 528
        return decode[0][z, row : row + 16, :]

    def multiply(rep):
        count = decode[0].shape[0]
        step = 128 // count
        partial = None
        for a in range(3):
            right = [
                rows_at(rep, z, row)
                for tap in range(9 * a, 9 * a + 9)
                for z in range(count)
                for row in range(tap * step, (tap + 1) * step, 16)
            ]
            term = dot(patches[64 * a : 64 * a + 512], jnp.concatenate(right, axis=0))
            partial = term if partial is None else partial + term
        parts[...] = partial.astype(jnp.bfloat16).reshape(GROUP, 128, 256)

    if len(decode) == 1:
        multiply(None)
    else:
        pl.when(marks[1] == 0)(lambda: multiply(0))
        pl.when(marks[1] == 1)(lambda: multiply(1))
    for k in range(GROUP):
        outs[k][...] = parts[marks[0] ^ k]


def final_stage(*refs):
    partials, (weights, out, spaced) = refs[:GROUP], refs[GROUP:]
    decoded = partials[0][...].astype(jnp.float32)
    for partial in partials[1:]:
        decoded += partial[...].astype(jnp.float32)
    decoded = jnp.maximum(decoded, 0.0).astype(jnp.bfloat16)
    for a in range(2):
        for b in range(2):
            for c in range(2):
                values = dot(decoded, weights[4 * a + 2 * b + c])
                for d in range(2):
                    for h in range(8):
                        at = ((2 * d + a) * 16 + 2 * h + b) * 16 + c
                        spaced[pl.ds(at, 8, stride=2), :] = values[64 * d + 8 * h : 64 * d + 8 * h + 8]
    out[...] = spaced[...].astype(jnp.bfloat16)


ALL = ("z", "r")


def exchange(payload, axis):
    return lax.all_to_all(payload, axis, split_axis=0, concat_axis=0, tiled=True)


def by_xor(blocks, axis):
    swaps = [[(r, r ^ k) for r in range(GROUP)] for k in range(GROUP)]
    return [blocks[0]] + [lax.ppermute(blocks[k], axis, swaps[k]) for k in range(1, GROUP)]


def body(
    volume,
    first_kernel,
    second_kernel,
    deep_kernel,
    deeper_kernel,
    rise_kernel,
    decode_kernel,
    final_kernel,
):
    n = lax.axis_size(ALL)
    place = lax.axis_index(ALL)
    planes = n // GROUP
    rank = lax.axis_index("r")
    chans = deep_kernel.shape[4]
    voxels = 16 * n
    bf16 = functools.partial(jax.ShapeDtypeStruct, dtype=jnp.bfloat16)

    rep, plane = lax.axis_index("rep"), lax.axis_index("z")
    marks = jnp.stack([rank, rep, plane % 2, plane, place % 2, place, n - 1 - place])
    marks = marks.astype(jnp.int32)
    decode_block = decode_kernel.reshape(27 * chans, 256)
    shared = lax.axis_size("rep") == 2 and chans == 32
    ride = chans == 32
    paired = planes == GROUP
    halo = bf16((3, 16, 16, 128))
    in_spaces = [pltpu.SMEM, pltpu.SMEM, pl.ANY, pl.ANY]
    off_chip, on_chip, *share = pl.pallas_call(
        front_stage,
        out_shape=(halo, halo) + (bf16((528, 256)),) * shared,
        in_specs=[pl.BlockSpec(memory_space=space) for space in in_spaces],
        out_specs=(pl.BlockSpec(memory_space=pltpu.VMEM),) * (2 + shared),
        scratch_shapes=[pltpu.SemaphoreType.DMA((4,))],
        compiler_params=pltpu.CompilerParams(vmem_limit_bytes=60 * MIB),
        cost_estimate=pl.CostEstimate(flops=0, bytes_accessed=10**6, transcendentals=0),
    )(
        (place % 2).astype(jnp.int32).reshape(1),
        rep.astype(jnp.int32).reshape(1),
        volume,
        decode_block,
    )
    pairs = [(i, i + 1) for i in range(1, n - 1, 2)]
    off_chip = lax.ppermute(off_chip, ALL, pairs + [(j, i) for i, j in pairs])
    on_chip = lax.ppermute(on_chip, ALL, [(i, i ^ 1) for i in range(n)])
    if shared:
        decode_block = share[0]
    line = lax.all_gather(decode_block, "z", axis=0)

    pairs = [(i, i + 1) for i in range(1, n - 1, 2)]
    taps = first_kernel.reshape(3, 1152, 128)
    own = call(
        own_stage,
        jax.ShapeDtypeStruct((4, 256, 256), jnp.float32),
        [pltpu.VMEM((4, 18, 16, 384), jnp.bfloat16)],
        (volume, taps),
        2 * 1024 * 2304 * 256,
        24,
    )
    lane = np.arange(256)
    source = (lane // 64 + GROUP * (lane % 64 // chans)) * chans + lane % chans
    order = jnp.asarray(np.arange(256)[:, None] == source[None, :], jnp.bfloat16)
    rise_part = call(
        lambda marks_ref, *refs: rise_stage(marks_ref, chans, *refs),
        bf16((n * chans, 512)),
        [],
        (marks, rise_kernel.reshape(8, n * chans, 256)),
        2 * 8 * n * chans * 256 * 64,
        16,
        scalars=1,
    )
    pooled_two, *skips = call(
        stem_stage,
        (bf16((1 if paired else n, 16, 256)),) + (bf16((48, 256)),) * GROUP,
        [
            pltpu.VMEM((6, 18, 16, 384), jnp.bfloat16),
            pltpu.VMEM((128, 128), jnp.float32),
            pltpu.VMEM((4, 10, 24, 128), jnp.float32),
            pltpu.VMEM((256, 1152), jnp.bfloat16),
            pltpu.VMEM((2, 32, 128), jnp.float32),
            pltpu.VMEM((GROUP, 48, 256), jnp.bfloat16),
        ],
        (marks, off_chip, on_chip, own, taps, second_kernel.reshape(3, 1152, 256), order, rise_part),
        2 * 1024 * 2304 * 256,
        24,
        scalars=1,
        unread=1,
    )
    if paired:
        line_blocks = by_xor([pooled_two.reshape(16, 256)] * GROUP, "z")
        relays = call(
            relay_stage,
            (bf16((112, 256)),) * GROUP,
            [],
            (marks, *line_blocks, *skips),
            0,
            16,
            scalars=1,
        )
        near = by_xor(relays, "r")
        pooled_whole = near
    else:
        pooled_whole = (exchange(pooled_two, ALL).reshape(voxels, 256),)
        near = by_xor(skips, "r")
    blocks = pltpu.VMEM((GROUP, 48, 256), jnp.bfloat16)

    deep = call(
        deep_stage,
        bf16((n, chans, voxels)),
        [pltpu.VMEM((GROUP, 64, 256), jnp.bfloat16)],
        (
            marks,
            deep_kernel.transpose(0, 1, 2, 4, 3).reshape(27 * chans, 256),
            *pooled_whole,
        ),
        2 * 27 * chans * 256 * voxels,
        16,
        scalars=1,
    )
    if shared:
        first_row = (deep[0, 0, 0] < 0).astype(jnp.int32)
        piece = lax.dynamic_slice_in_dim(line, first_row, 336, axis=1)
        weights = (line, lax.ppermute(piece, "rep", [(0, 1), (1, 0)]))
    elif chans % 16:
        weights = line.reshape(planes, 27, chans, 256).transpose(1, 0, 2, 3)
        weights = (weights.reshape(1, 27 * 128, 256),)
    else:
        weights = (line,)
    swaps = ()
    if not ride:
        swaps = call(
            edge_stage,
            (bf16((16, 256)), bf16((16, 256))),
            [blocks],
            (marks, *near),
            0,
            16,
            scalars=1,
        )
        near_pairs = [(p, p + 1) for p in range(0, planes - 1, 2)]
        far_pairs = [(p, p + 1) for p in range(1, planes - 1, 2)]
        near_swap = lax.ppermute(swaps[0], "z", near_pairs + [(j, i) for i, j in near_pairs])
        far_swap = lax.ppermute(swaps[1], "z", far_pairs + [(j, i) for i, j in far_pairs])
        swaps = (near_swap, far_swap)
    deep_whole = (exchange(deep, ALL).reshape(n * chans, voxels),)

    riders = near if ride else ()
    deeper = call(
        functools.partial(deeper_stage, len(riders)),
        bf16((n, chans, 128)),
        [blocks],
        (
            marks,
            deeper_kernel.transpose(0, 1, 2, 4, 3).reshape(27 * chans, n * chans),
            *riders,
            *deep_whole,
        ),
        2 * 27 * chans * n * chans * voxels,
        16,
        scalars=1,
    )
    deeper_near = exchange(deeper, ALL)

    partials = call(
        functools.partial(decode_stage, ride),
        (bf16((128, 256)),) * GROUP,
        [
            pltpu.VMEM((10, 10, 24, 128), jnp.float32),
            pltpu.VMEM((640, 1152), jnp.bfloat16),
            pltpu.VMEM((8, 128, 128), jnp.float32),
            blocks,
            pltpu.VMEM((GROUP, 128, 256), jnp.bfloat16),
        ],
        (marks, deeper_near, rise_part, *swaps, *near, *weights),
        2 * 512 * 3456 * 256,
        24,
        scalars=1,
    )
    partials = by_xor(partials, "r")
    out = call(
        final_stage,
        bf16((1024, 128)),
        [pltpu.VMEM((1024, 128), jnp.float32)],
        (*partials, final_kernel.reshape(8, 256, 128)),
        2 * 128 * 256 * 1024,
        16,
    )
    return out.reshape(4, 16, 16, 128)


def solution(mesh):
    reps, n = mesh.devices.shape
    grid = jax.sharding.Mesh(mesh.devices.reshape(reps, n // GROUP, GROUP), ("rep",) + ALL)
    return jax.shard_map(
        body,
        mesh=grid,
        in_specs=(
            P(("rep",) + ALL, None, None, None),
            P(),
            P(),
            P(None, None, None, None, ALL),
            P(None, None, None, None, ALL),
            P(),
            P(None, None, None, ALL, None),
            P(),
        ),
        out_specs=P(("rep",) + ALL, None, None, None),
        check_vma=False,
    )
```

```python
import functools

import jax
import jax.numpy as jnp
import numpy as np
from jax import lax
from jax.experimental import pallas as pl
from jax.experimental.pallas import tpu as pltpu
from jax.sharding import PartitionSpec as P

GROUP = 4
MIB = 1024 * 1024


def call(kernel, outs, scratch, args, flops, vmem_mib, scalars=0, unread=0):
    spaces = [pltpu.SMEM] * scalars + [pltpu.VMEM] * (len(args) - scalars - unread)
    spaces += [pl.ANY] * unread
    return pl.pallas_call(
        kernel,
        out_shape=outs,
        in_specs=[pl.BlockSpec(memory_space=space) for space in spaces],
        out_specs=jax.tree.map(lambda _: pl.BlockSpec(memory_space=pltpu.VMEM), outs),
        scratch_shapes=scratch,
        compiler_params=pltpu.CompilerParams(vmem_limit_bytes=vmem_mib * MIB),
        cost_estimate=pl.CostEstimate(
            flops=flops,
            bytes_accessed=sum(a.size * a.dtype.itemsize for a in args[: len(args) - unread]),
            transcendentals=0,
        ),
    )(*args)


def dot(left, right, dims=((1,), (0,))):
    return lax.dot_general(left, right, (dims, ((), ())), preferred_element_type=jnp.float32)


def round_once(values):
    return values.astype(jnp.bfloat16).astype(jnp.float32)


def fill_patches(framed, patches, slices):
    for b in range(3):
        for c in range(3):
            tap = framed[:, b : b + 8, 7 + c : 15 + c, :].reshape(slices * 64, 128)
            col = (b * 3 + c) * 128
            patches[:, col : col + 128] = tap.astype(jnp.bfloat16)


def shift_slice(shifted, s, values):
    row = lax.broadcasted_iota(jnp.int32, (256, 128), 0) & 15
    here = values.reshape(256, 128).astype(jnp.float32)
    before = jnp.where(row == 0, 0.0, pltpu.roll(here, 1, 0))
    after = jnp.where(row == 15, 0.0, pltpu.roll(here, 255, 0))
    shifted[s, 0] = jnp.zeros((16, 384), jnp.bfloat16)
    shifted[s, 17] = jnp.zeros((16, 384), jnp.bfloat16)
    for c, tap in enumerate((before, here, after)):
        tap = tap.astype(jnp.bfloat16).reshape(16, 16, 128)
        shifted[s, 1:17, :, 128 * c : 128 * c + 128] = tap


def depth_pair(shifted, slices, weights, steps):
    left = jnp.concatenate(
        [shifted[s, b : b + 16].reshape(256, 384) for s in slices for b in range(3)], axis=1
    )
    none = jnp.zeros((1152, 128), jnp.bfloat16)
    right = [
        jnp.concatenate(
            [weights[j] if j < 3 else none, weights[j - 1] if j > 0 else none], axis=1
        )
        for j in steps
    ]
    return dot(left, jnp.concatenate(right, axis=0))


def depth_one(shifted, s, weights):
    left = jnp.concatenate([shifted[s, b : b + 16].reshape(256, 384) for b in range(3)], axis=1)
    return dot(left, weights)


def front_stage(odd, rep, volume, decode, off_chip, on_chip, *refs):
    done = refs[-1]
    pairs = [
        (volume.at[pl.ds(odd[0], 3)], off_chip),
        (volume.at[pl.ds(1 - odd[0], 3)], on_chip),
    ]
    if len(refs) == 2:
        block = refs[0]
        at = pl.multiple_of(528 * rep[0], 16)
        pairs += [
            (decode.at[pl.ds(at, 336)], block.at[pl.ds(0, 336)]),
            (decode.at[pl.ds(336, 192)], block.at[pl.ds(336, 192)]),
        ]
    copies = [
        pltpu.make_async_copy(source, target, done.at[i]) for i, (source, target) in enumerate(pairs)
    ]
    for copy in copies:
        copy.start()
    for copy in copies:
        copy.wait()


def own_stage(volume, weights, out, shifted):
    for s in range(4):
        shift_slice(shifted, s, volume[s])
    out[0, :, :128] = jnp.zeros((256, 128), jnp.float32)
    out[0, :, 128:] = depth_one(shifted, 0, weights[2])
    out[1] = depth_pair(shifted, (0, 1, 2), weights, (1, 2, 3))
    out[2] = depth_pair(shifted, (1, 2, 3), weights, (0, 1, 2))
    out[3, :, :128] = depth_one(shifted, 3, weights[0])
    out[3, :, 128:] = jnp.zeros((256, 128), jnp.float32)


def stem_stage(marks, off_chip, on_chip, own, weights, second, order, _, *refs):
    pooled_out, skip_outs = refs[0], refs[1 : 1 + GROUP]
    shifted, halves, framed, patches, quarters, blocks = refs[1 + GROUP :]
    for s in range(3):
        even = marks[4] == 0
        shift_slice(shifted, s, jnp.where(even, off_chip[s], on_chip[s]))
        shift_slice(shifted, 3 + s, jnp.where(even, on_chip[s], off_chip[s]))
    framed[...] = jnp.zeros(framed.shape, jnp.float32)
    for m in range(4):
        if m == 0:
            first = own[0] + depth_pair(shifted, (0, 1, 2), weights, (0, 1, 2))
        elif m == 3:
            first = own[3] + depth_pair(shifted, (3, 4, 5), weights, (1, 2, 3))
        elif m == 1:
            near = own[1, :, :128] + depth_one(shifted, 2, weights[0])
            first = jnp.concatenate([near, own[1, :, 128:]], axis=1)
        else:
            far = own[2, :, 128:] + depth_one(shifted, 3, weights[2])
            first = jnp.concatenate([own[2, :, :128], far], axis=1)
        first = round_once(jnp.maximum(first, 0.0))
        pair = (first[:, :128] + first[:, 128:]).reshape(8, 32, 128)
        halves[...] = (pair[:, :16] + pair[:, 16:]).reshape(128, 128)
        pooled = halves[pl.ds(0, 64, stride=2), :] + halves[pl.ds(1, 64, stride=2), :]
        pooled = round_once(pooled * 0.125)
        if m == 0:
            pooled = jnp.where(marks[5] == 0, 0.0, pooled)
        if m == 3:
            pooled = jnp.where(marks[6] == 0, 0.0, pooled)
        framed[m, 1:9, 8:16, :] = pooled.reshape(8, 8, 128)
    fill_patches(framed, patches, 4)
    skip = dot(patches[0:128], second[0])
    skip += dot(patches[64:192], second[1])
    skip += dot(patches[128:256], second[2])
    skip = jnp.maximum(skip, 0.0).astype(jnp.bfloat16)
    wide = skip.astype(jnp.float32)
    pair = (wide[:64] + wide[64:]).reshape(4, 16, 256)
    pair = (pair[:, :8] + pair[:, 8:]).reshape(32, 256)
    for k in range(2):
        quarters[k] = pair[:, 128 * k : 128 * k + 128]
    pooled = jnp.concatenate(
        [
            quarters[k, pl.ds(0, 16, stride=2), :] + quarters[k, pl.ds(1, 16, stride=2), :]
            for k in range(2)
        ],
        axis=1,
    )
    pooled = (pooled * 0.125).astype(jnp.bfloat16)
    for p in range(pooled_out.shape[0]):
        pooled_out[p] = pooled
    sorted_skip = dot(skip, order[...])
    for r in range(GROUP):
        near, far = sorted_skip[:64, 64 * r : 64 * r + 64], sorted_skip[64:, 64 * r : 64 * r + 64]
        block = jnp.concatenate([near, far], axis=1)
        block = jnp.concatenate([block[:32], block[32:]], axis=1).astype(jnp.bfloat16)
        blocks[r, 0:32, :] = block
        first, last = sorted_skip[16 * r : 16 * r + 16], sorted_skip[64 + 16 * r : 80 + 16 * r]
        blocks[r, 32:48, :] = jnp.where(marks[0] == 0, first, last).astype(jnp.bfloat16)
    for k in range(GROUP):
        skip_outs[k][...] = blocks[marks[0] ^ k]


def edge_slice(block, far):
    lower = lax.broadcasted_iota(jnp.int32, (16, 128), 1) < 64
    sides = []
    for k in range(2):
        half = block[:, 128 * k : 128 * k + 128].astype(jnp.float32)
        top, bottom = half[:16], half[16:]
        if far:
            top = pltpu.roll(top, 64, 1)
        else:
            bottom = pltpu.roll(bottom, 64, 1)
        sides.append(jnp.where(lower, top, bottom))
    return jnp.concatenate(sides, axis=1)


def spread_taps(weights, values, dims, chans, voxels):
    lane = lax.broadcasted_iota(jnp.int32, (chans, voxels), 1)

    def moved(term, tap, step, place, last):
        if tap == 1:
            return term
        keep = place > 0 if tap == 0 else place < last
        return jnp.where(keep, pltpu.roll(term, ((1 - tap) * step) % voxels, 1), 0.0)

    total = None
    for a in range(3):
        products = dot(weights[a * 9 * chans : (a + 1) * 9 * chans, :], values, dims)
        plane = None
        for b in range(3):
            line = None
            for c in range(3):
                at = (b * 3 + c) * chans
                term = moved(products[at : at + chans], c, 1, lane & 3, 3)
                line = term if line is None else line + term
            line = moved(line, b, 4, (lane >> 2) & 3, 3)
            plane = line if plane is None else plane + line
        plane = moved(plane, a, 16, lane >> 4, voxels // 16 - 1)
        total = plane if total is None else total + plane
    return jnp.maximum(total, 0.0)


def by_rank(marks, near, blocks):
    for k in range(GROUP):
        blocks[marks[0] ^ k] = near[k][near[k].shape[0] - 48 :, :]


def by_depth(marks, near, parts, step):
    for k in range(GROUP):
        parts[marks[0] ^ k] = near[k][0 : parts.shape[1], :]
    return jnp.concatenate(
        [
            parts[r, at : at + step, :]
            for at in range(0, parts.shape[1], step)
            for r in range(GROUP)
        ],
        axis=0,
    )


def relay_stage(marks, *refs):
    line, refs = refs[:GROUP], refs[GROUP:]
    step = line[0].shape[0]
    skips, outs = refs[:GROUP], refs[GROUP:]
    for j in range(GROUP):
        for k in range(GROUP):
            outs[j][pl.ds(pl.multiple_of((marks[3] ^ k) * step, 16), step), :] = line[k][...]
        outs[j][GROUP * step :, :] = skips[j][...]


def edge_stage(marks, *refs):
    near, (near_swap, far_swap, blocks) = refs[:GROUP], refs[GROUP:]
    by_rank(marks, near, blocks)
    first = edge_slice(blocks[0, 0:32, :], False)
    last = edge_slice(blocks[GROUP - 1, 0:32, :], True)
    even = marks[2] == 0
    near_swap[...] = jnp.where(even, last, first).astype(jnp.bfloat16)
    far_swap[...] = jnp.where(even, first, last).astype(jnp.bfloat16)


def deep_stage(marks, weights, *refs):
    near, (out, after, parts) = refs[:-3], refs[-3:]
    after[0] = 0
    _, chans, voxels = out.shape
    values = near[0][...] if len(near) == 1 else by_depth(marks, near, parts, 16)
    deep = spread_taps(weights, values, ((1,), (1,)), chans, voxels).astype(jnp.bfloat16)
    for dest in range(out.shape[0]):
        out[dest] = deep


def deeper_stage(near_count, marks, weights, *refs):
    near, (deep, out, blocks) = refs[:near_count], refs[near_count:]
    n, chans, _ = out.shape
    voxels = deep.shape[1]
    deeper = spread_taps(weights, deep[...], ((1,), (0,)), chans, voxels)
    lane = lax.broadcasted_iota(jnp.int32, (chans, 128), 1)
    planes = n // GROUP
    ride = len(near) == GROUP
    if ride:
        by_rank(marks, near, blocks)
        edges = [blocks[r, 32:48, :].astype(jnp.float32) for r in (0, GROUP - 1)]
        riders = [
            [
                jnp.concatenate(
                    [
                        pltpu.roll(edge[:, at // 128 * 128 : at // 128 * 128 + 128], (96 - at) % 128, 1)
                        for at in (64 * r, 64 * r + 32)
                    ],
                    axis=0,
                )
                for r in range(GROUP)
            ]
            for edge in edges
        ]
    for p in range(planes):
        part = pltpu.roll(deeper, (16 - 64 * p) % voxels, 1)[:, :128]
        if p == 0:
            part = jnp.where(lane < 16, 0.0, part)
        if p == planes - 1:
            part = jnp.where(lane >= 80, 0.0, part)
        for r in range(GROUP):
            whole = part
            if ride:
                rider = jnp.where(marks[3] < p, riders[1][r], riders[0][r])
                whole = jnp.where(lane < 96, part, rider)
            out[GROUP * p + r] = whole.astype(jnp.bfloat16)


def rise_stage(marks, chans, rise, out):
    lane = lax.broadcasted_iota(jnp.int32, (256, 64), 1)
    row = lax.broadcasted_iota(jnp.int32, (256, 64), 0)
    source = (marks[0] + GROUP * (lane // chans)) * chans + lane % chans
    mine = jnp.where(row == source, 1.0, 0.0).astype(jnp.bfloat16)
    for pair in range(4):
        both = [dot(rise[2 * pair + k], mine) for k in range(2)]
        both = jnp.concatenate(both, axis=1).astype(jnp.bfloat16)
        out[:, 128 * pair : 128 * pair + 128] = both


def decode_stage(ride, marks, deeper, rise, *refs):
    swaps = () if ride else refs[:2]
    near, refs = refs[len(swaps) : len(swaps) + GROUP], refs[len(swaps) + GROUP :]
    decode, outs = refs[: -5 - GROUP], refs[-5 - GROUP : -5]
    framed, patches, risen, blocks, parts = refs[-5:]
    by_rank(marks, near, blocks)
    n, chans, _ = deeper.shape
    plane, planes = marks[3], n // GROUP
    upper = lax.broadcasted_iota(jnp.int32, (64, 128), 1) >= 64

    def edge(low):
        if not ride:
            even = marks[2] == 0
            sides = [swap[...].astype(jnp.float32) for swap in swaps]
            side = jnp.where(even, sides[low], sides[not low])
            parts = []
            for k in range(2):
                half = side[:, 128 * k : 128 * k + 128]
                parts += [pltpu.roll(half, 64, 1), half]
            return jnp.concatenate(parts, axis=0)
        other = jnp.maximum(plane - 1, 0) if low else jnp.minimum(plane + 1, planes - 1)
        lane = lax.broadcasted_iota(jnp.int32, (16, 128), 1)
        parts = []
        for r in range(GROUP):
            block = deeper[GROUP * other + r].astype(jnp.float32)
            parts.append(jnp.where(lane < 96, pltpu.roll(block[:16], 96, 1), block[16:]))
        return jnp.where(other == plane, 0.0, jnp.concatenate(parts, axis=0))

    framed[...] = jnp.zeros(framed.shape, jnp.float32)
    spread = round_once(dot(deeper[...].reshape(n * chans, 128).astype(jnp.float32).T.astype(jnp.bfloat16), rise[...]))
    for pair in range(4):
        both = spread[:, 128 * pair : 128 * pair + 128]
        risen[2 * pair] = both
        risen[2 * pair + 1] = pltpu.roll(both, 64, 1)
    for s in range(10):
        d, a = (s + 1) // 2, (s + 1) % 2
        for h in range(4):
            for b in range(2):
                for c in range(2):
                    framed[s, 1 + 2 * h + b, pl.ds(8 + c, 4, stride=2), :] = risen[
                        4 * a + 2 * b + c, 16 * d + 4 * h : 16 * d + 4 * h + 4, :
                    ]
        if s == 0 or s == 9:
            skip = edge(s == 0)
        else:
            both = blocks[(s - 1) // 2, 0:32, :].astype(jnp.float32)
            skip = jnp.concatenate([both[:, :128], both[:, 128:]], axis=0)
            if (s - 1) % 2 == 0:
                skip = pltpu.roll(skip, 64, 1)
        joined = framed[s, 1:9, 8:16, :].reshape(64, 128)
        framed[s, 1:9, 8:16, :] = jnp.where(upper, skip, joined).reshape(8, 8, 128)
    fill_patches(framed, patches, 10)
    def rows_at(rep, z, row):
        if rep == 0 and row >= 528:
            return decode[1][z, row - 528 : row - 512, :]
        if rep == 1 and row < 336:
            return decode[1][z, row : row + 16, :]
        if rep == 1 and row >= 528:
            row -= 528
        return decode[0][z, row : row + 16, :]

    def multiply(rep):
        count = decode[0].shape[0]
        step = 128 // count
        partial = None
        for a in range(3):
            right = [
                rows_at(rep, z, row)
                for tap in range(9 * a, 9 * a + 9)
                for z in range(count)
                for row in range(tap * step, (tap + 1) * step, 16)
            ]
            term = dot(patches[64 * a : 64 * a + 512], jnp.concatenate(right, axis=0))
            partial = term if partial is None else partial + term
        parts[...] = partial.astype(jnp.bfloat16).reshape(GROUP, 128, 256)

    if len(decode) == 1:
        multiply(None)
    else:
        pl.when(marks[1] == 0)(lambda: multiply(0))
        pl.when(marks[1] == 1)(lambda: multiply(1))
    for k in range(GROUP):
        outs[k][...] = parts[marks[0] ^ k]


def final_stage(*refs):
    partials, (weights, out, spaced) = refs[:GROUP], refs[GROUP:]
    decoded = partials[0][...].astype(jnp.float32)
    for partial in partials[1:]:
        decoded += partial[...].astype(jnp.float32)
    decoded = jnp.maximum(decoded, 0.0).astype(jnp.bfloat16)
    for a in range(2):
        for b in range(2):
            for c in range(2):
                values = dot(decoded, weights[4 * a + 2 * b + c])
                for d in range(2):
                    for h in range(8):
                        at = ((2 * d + a) * 16 + 2 * h + b) * 16 + c
                        spaced[pl.ds(at, 8, stride=2), :] = values[64 * d + 8 * h : 64 * d + 8 * h + 8]
    out[...] = spaced[...].astype(jnp.bfloat16)


ALL = ("z", "r")


def exchange(payload, axis):
    return lax.all_to_all(payload, axis, split_axis=0, concat_axis=0, tiled=True)


def by_xor(blocks, axis):
    swaps = [[(r, r ^ k) for r in range(GROUP)] for k in range(GROUP)]
    return [blocks[0]] + [lax.ppermute(blocks[k], axis, swaps[k]) for k in range(1, GROUP)]


def body(
    volume,
    first_kernel,
    second_kernel,
    deep_kernel,
    deeper_kernel,
    rise_kernel,
    decode_kernel,
    final_kernel,
):
    n = lax.axis_size(ALL)
    place = lax.axis_index(ALL)
    planes = n // GROUP
    rank = lax.axis_index("r")
    chans = deep_kernel.shape[4]
    voxels = 16 * n
    bf16 = functools.partial(jax.ShapeDtypeStruct, dtype=jnp.bfloat16)

    rep, plane = lax.axis_index("rep"), lax.axis_index("z")
    marks = jnp.stack([rank, rep, plane % 2, plane, place % 2, place, n - 1 - place])
    marks = marks.astype(jnp.int32)
    decode_block = decode_kernel.reshape(27 * chans, 256)
    shared = lax.axis_size("rep") == 2 and chans == 32
    ride = chans == 32
    paired = planes == GROUP
    halo = bf16((3, 16, 16, 128))
    in_spaces = [pltpu.SMEM, pltpu.SMEM, pl.ANY, pl.ANY]
    off_chip, on_chip, *share = pl.pallas_call(
        front_stage,
        out_shape=(halo, halo) + (bf16((528, 256)),) * shared,
        in_specs=[pl.BlockSpec(memory_space=space) for space in in_spaces],
        out_specs=(pl.BlockSpec(memory_space=pltpu.VMEM),) * (2 + shared),
        scratch_shapes=[pltpu.SemaphoreType.DMA((4,))],
        compiler_params=pltpu.CompilerParams(vmem_limit_bytes=60 * MIB),
        cost_estimate=pl.CostEstimate(flops=0, bytes_accessed=10**6, transcendentals=0),
    )(
        (place % 2).astype(jnp.int32).reshape(1),
        rep.astype(jnp.int32).reshape(1),
        volume,
        decode_block,
    )
    pairs = [(i, i + 1) for i in range(1, n - 1, 2)]
    off_chip = lax.ppermute(off_chip, ALL, pairs + [(j, i) for i, j in pairs])
    on_chip = lax.ppermute(on_chip, ALL, [(i, i ^ 1) for i in range(n)])
    if shared:
        decode_block = share[0]
    line = lax.all_gather(decode_block, "z", axis=0)

    pairs = [(i, i + 1) for i in range(1, n - 1, 2)]
    taps = first_kernel.reshape(3, 1152, 128)
    own = call(
        own_stage,
        jax.ShapeDtypeStruct((4, 256, 256), jnp.float32),
        [pltpu.VMEM((4, 18, 16, 384), jnp.bfloat16)],
        (volume, taps),
        2 * 1024 * 2304 * 256,
        24,
    )
    lane = np.arange(256)
    source = (lane // 64 + GROUP * (lane % 64 // chans)) * chans + lane % chans
    order = jnp.asarray(np.arange(256)[:, None] == source[None, :], jnp.bfloat16)
    rise_part = call(
        lambda marks_ref, *refs: rise_stage(marks_ref, chans, *refs),
        bf16((n * chans, 512)),
        [],
        (marks, rise_kernel.reshape(8, n * chans, 256)),
        2 * 8 * n * chans * 256 * 64,
        16,
        scalars=1,
    )
    pooled_two, *skips = call(
        stem_stage,
        (bf16((1 if paired else n, 16, 256)),) + (bf16((48, 256)),) * GROUP,
        [
            pltpu.VMEM((6, 18, 16, 384), jnp.bfloat16),
            pltpu.VMEM((128, 128), jnp.float32),
            pltpu.VMEM((4, 10, 24, 128), jnp.float32),
            pltpu.VMEM((256, 1152), jnp.bfloat16),
            pltpu.VMEM((2, 32, 128), jnp.float32),
            pltpu.VMEM((GROUP, 48, 256), jnp.bfloat16),
        ],
        (marks, off_chip, on_chip, own, taps, second_kernel.reshape(3, 1152, 256), order, rise_part),
        2 * 1024 * 2304 * 256,
        24,
        scalars=1,
        unread=1,
    )
    if paired:
        line_blocks = by_xor([pooled_two.reshape(16, 256)] * GROUP, "z")
        relays = call(
            relay_stage,
            (bf16((112, 256)),) * GROUP,
            [],
            (marks, *line_blocks, *skips),
            0,
            16,
            scalars=1,
        )
        near = by_xor(relays, "r")
        pooled_whole = near
    else:
        pooled_whole = (exchange(pooled_two, ALL).reshape(voxels, 256),)
        near = by_xor(skips, "r")
    blocks = pltpu.VMEM((GROUP, 48, 256), jnp.bfloat16)

    deep, after = pl.pallas_call(
        deep_stage,
        out_shape=(bf16((n, chans, voxels)), jax.ShapeDtypeStruct((1,), jnp.int32)),
        in_specs=[pl.BlockSpec(memory_space=pltpu.SMEM)]
        + [pl.BlockSpec(memory_space=pltpu.VMEM)] * (1 + len(pooled_whole)),
        out_specs=(
            pl.BlockSpec(memory_space=pltpu.VMEM),
            pl.BlockSpec(memory_space=pltpu.SMEM),
        ),
        scratch_shapes=[pltpu.VMEM((GROUP, 64, 256), jnp.bfloat16)],
        compiler_params=pltpu.CompilerParams(vmem_limit_bytes=16 * MIB),
        cost_estimate=pl.CostEstimate(
            flops=2 * 27 * chans * 256 * voxels, bytes_accessed=10**6, transcendentals=0
        ),
    )(
        marks,
        deep_kernel.transpose(0, 1, 2, 4, 3).reshape(27 * chans, 256),
        *pooled_whole,
    )
    if shared:
        piece = lax.dynamic_slice_in_dim(line, after[0], 336, axis=1)
        weights = (line, lax.ppermute(piece, "rep", [(0, 1), (1, 0)]))
    elif chans % 16:
        weights = line.reshape(planes, 27, chans, 256).transpose(1, 0, 2, 3)
        weights = (weights.reshape(1, 27 * 128, 256),)
    else:
        weights = (line,)
    swaps = ()
    if not ride:
        swaps = call(
            edge_stage,
            (bf16((16, 256)), bf16((16, 256))),
            [blocks],
            (marks, *near),
            0,
            16,
            scalars=1,
        )
        near_pairs = [(p, p + 1) for p in range(0, planes - 1, 2)]
        far_pairs = [(p, p + 1) for p in range(1, planes - 1, 2)]
        near_swap = lax.ppermute(swaps[0], "z", near_pairs + [(j, i) for i, j in near_pairs])
        far_swap = lax.ppermute(swaps[1], "z", far_pairs + [(j, i) for i, j in far_pairs])
        swaps = (near_swap, far_swap)
    deep_whole = (exchange(deep, ALL).reshape(n * chans, voxels),)

    riders = near if ride else ()
    deeper = call(
        functools.partial(deeper_stage, len(riders)),
        bf16((n, chans, 128)),
        [blocks],
        (
            marks,
            deeper_kernel.transpose(0, 1, 2, 4, 3).reshape(27 * chans, n * chans),
            *riders,
            *deep_whole,
        ),
        2 * 27 * chans * n * chans * voxels,
        16,
        scalars=1,
    )
    deeper_near = exchange(deeper, ALL)

    partials = call(
        functools.partial(decode_stage, ride),
        (bf16((128, 256)),) * GROUP,
        [
            pltpu.VMEM((10, 10, 24, 128), jnp.float32),
            pltpu.VMEM((640, 1152), jnp.bfloat16),
            pltpu.VMEM((8, 128, 128), jnp.float32),
            blocks,
            pltpu.VMEM((GROUP, 128, 256), jnp.bfloat16),
        ],
        (marks, deeper_near, rise_part, *swaps, *near, *weights),
        2 * 512 * 3456 * 256,
        24,
        scalars=1,
    )
    partials = by_xor(partials, "r")
    out = call(
        final_stage,
        bf16((1024, 128)),
        [pltpu.VMEM((1024, 128), jnp.float32)],
        (*partials, final_kernel.reshape(8, 256, 128)),
        2 * 128 * 256 * 1024,
        16,
    )
    return out.reshape(4, 16, 16, 128)


def solution(mesh):
    reps, n = mesh.devices.shape
    grid = jax.sharding.Mesh(mesh.devices.reshape(reps, n // GROUP, GROUP), ("rep",) + ALL)
    return jax.shard_map(
        body,
        mesh=grid,
        in_specs=(
            P(("rep",) + ALL, None, None, None),
            P(),
            P(),
            P(None, None, None, None, ALL),
            P(None, None, None, None, ALL),
            P(),
            P(None, None, None, ALL, None),
            P(),
        ),
        out_specs=P(("rep",) + ALL, None, None, None),
        check_vma=False,
    )
```

```python
import functools

import jax
import jax.numpy as jnp
import numpy as np
from jax import lax
from jax.experimental import pallas as pl
from jax.experimental.pallas import tpu as pltpu
from jax.sharding import PartitionSpec as P

GROUP = 4
MIB = 1024 * 1024


def call(kernel, outs, scratch, args, flops, vmem_mib, scalars=0, unread=0):
    spaces = [pltpu.SMEM] * scalars + [pltpu.VMEM] * (len(args) - scalars - unread)
    spaces += [pl.ANY] * unread
    return pl.pallas_call(
        kernel,
        out_shape=outs,
        in_specs=[pl.BlockSpec(memory_space=space) for space in spaces],
        out_specs=jax.tree.map(lambda _: pl.BlockSpec(memory_space=pltpu.VMEM), outs),
        scratch_shapes=scratch,
        compiler_params=pltpu.CompilerParams(vmem_limit_bytes=vmem_mib * MIB),
        cost_estimate=pl.CostEstimate(
            flops=flops,
            bytes_accessed=sum(a.size * a.dtype.itemsize for a in args[: len(args) - unread]),
            transcendentals=0,
        ),
    )(*args)


def dot(left, right, dims=((1,), (0,))):
    return lax.dot_general(left, right, (dims, ((), ())), preferred_element_type=jnp.float32)


def round_once(values):
    return values.astype(jnp.bfloat16).astype(jnp.float32)


def fill_patches(framed, patches, slices):
    for b in range(3):
        for c in range(3):
            tap = framed[:, b : b + 8, 7 + c : 15 + c, :].reshape(slices * 64, 128)
            col = (b * 3 + c) * 128
            patches[:, col : col + 128] = tap.astype(jnp.bfloat16)


def shift_slice(shifted, s, values):
    row = lax.broadcasted_iota(jnp.int32, (256, 128), 0) & 15
    here = values.reshape(256, 128).astype(jnp.float32)
    before = jnp.where(row == 0, 0.0, pltpu.roll(here, 1, 0))
    after = jnp.where(row == 15, 0.0, pltpu.roll(here, 255, 0))
    shifted[s, 0] = jnp.zeros((16, 384), jnp.bfloat16)
    shifted[s, 17] = jnp.zeros((16, 384), jnp.bfloat16)
    for c, tap in enumerate((before, here, after)):
        tap = tap.astype(jnp.bfloat16).reshape(16, 16, 128)
        shifted[s, 1:17, :, 128 * c : 128 * c + 128] = tap


def depth_pair(shifted, slices, weights, steps):
    left = jnp.concatenate(
        [shifted[s, b : b + 16].reshape(256, 384) for s in slices for b in range(3)], axis=1
    )
    none = jnp.zeros((1152, 128), jnp.bfloat16)
    right = [
        jnp.concatenate(
            [weights[j] if j < 3 else none, weights[j - 1] if j > 0 else none], axis=1
        )
        for j in steps
    ]
    return dot(left, jnp.concatenate(right, axis=0))


def depth_one(shifted, s, weights):
    left = jnp.concatenate([shifted[s, b : b + 16].reshape(256, 384) for b in range(3)], axis=1)
    return dot(left, weights)


def front_stage(odd, rep, volume, decode, off_chip, on_chip, *refs):
    done = refs[-1]
    pairs = [
        (volume.at[pl.ds(odd[0], 3)], off_chip),
        (volume.at[pl.ds(1 - odd[0], 3)], on_chip),
    ]
    if len(refs) == 2:
        block = refs[0]
        at = pl.multiple_of(528 * rep[0], 16)
        pairs += [
            (decode.at[pl.ds(at, 336)], block.at[pl.ds(0, 336)]),
            (decode.at[pl.ds(336, 192)], block.at[pl.ds(336, 192)]),
        ]
    copies = [
        pltpu.make_async_copy(source, target, done.at[i]) for i, (source, target) in enumerate(pairs)
    ]
    for copy in copies:
        copy.start()
    for copy in copies:
        copy.wait()


def pick_stage(line, _, out, done):
    copy = pltpu.make_async_copy(line.at[:, pl.ds(0, out.shape[1])], out, done)
    copy.start()
    copy.wait()


def own_stage(volume, weights, out, shifted):
    for s in range(4):
        shift_slice(shifted, s, volume[s])
    out[0, :, :128] = jnp.zeros((256, 128), jnp.float32)
    out[0, :, 128:] = depth_one(shifted, 0, weights[2])
    out[1] = depth_pair(shifted, (0, 1, 2), weights, (1, 2, 3))
    out[2] = depth_pair(shifted, (1, 2, 3), weights, (0, 1, 2))
    out[3, :, :128] = depth_one(shifted, 3, weights[0])
    out[3, :, 128:] = jnp.zeros((256, 128), jnp.float32)


def stem_stage(marks, off_chip, on_chip, own, weights, second, order, _, *refs):
    pooled_out, skip_outs = refs[0], refs[1 : 1 + GROUP]
    shifted, halves, framed, patches, quarters, blocks = refs[1 + GROUP :]
    for s in range(3):
        even = marks[4] == 0
        shift_slice(shifted, s, jnp.where(even, off_chip[s], on_chip[s]))
        shift_slice(shifted, 3 + s, jnp.where(even, on_chip[s], off_chip[s]))
    framed[...] = jnp.zeros(framed.shape, jnp.float32)
    for m in range(4):
        if m == 0:
            first = own[0] + depth_pair(shifted, (0, 1, 2), weights, (0, 1, 2))
        elif m == 3:
            first = own[3] + depth_pair(shifted, (3, 4, 5), weights, (1, 2, 3))
        elif m == 1:
            near = own[1, :, :128] + depth_one(shifted, 2, weights[0])
            first = jnp.concatenate([near, own[1, :, 128:]], axis=1)
        else:
            far = own[2, :, 128:] + depth_one(shifted, 3, weights[2])
            first = jnp.concatenate([own[2, :, :128], far], axis=1)
        first = round_once(jnp.maximum(first, 0.0))
        pair = (first[:, :128] + first[:, 128:]).reshape(8, 32, 128)
        halves[...] = (pair[:, :16] + pair[:, 16:]).reshape(128, 128)
        pooled = halves[pl.ds(0, 64, stride=2), :] + halves[pl.ds(1, 64, stride=2), :]
        pooled = round_once(pooled * 0.125)
        if m == 0:
            pooled = jnp.where(marks[5] == 0, 0.0, pooled)
        if m == 3:
            pooled = jnp.where(marks[6] == 0, 0.0, pooled)
        framed[m, 1:9, 8:16, :] = pooled.reshape(8, 8, 128)
    fill_patches(framed, patches, 4)
    skip = dot(patches[0:128], second[0])
    skip += dot(patches[64:192], second[1])
    skip += dot(patches[128:256], second[2])
    skip = jnp.maximum(skip, 0.0).astype(jnp.bfloat16)
    wide = skip.astype(jnp.float32)
    pair = (wide[:64] + wide[64:]).reshape(4, 16, 256)
    pair = (pair[:, :8] + pair[:, 8:]).reshape(32, 256)
    for k in range(2):
        quarters[k] = pair[:, 128 * k : 128 * k + 128]
    pooled = jnp.concatenate(
        [
            quarters[k, pl.ds(0, 16, stride=2), :] + quarters[k, pl.ds(1, 16, stride=2), :]
            for k in range(2)
        ],
        axis=1,
    )
    pooled = (pooled * 0.125).astype(jnp.bfloat16)
    for p in range(pooled_out.shape[0]):
        pooled_out[p] = pooled
    sorted_skip = dot(skip, order[...])
    for r in range(GROUP):
        near, far = sorted_skip[:64, 64 * r : 64 * r + 64], sorted_skip[64:, 64 * r : 64 * r + 64]
        block = jnp.concatenate([near, far], axis=1)
        block = jnp.concatenate([block[:32], block[32:]], axis=1).astype(jnp.bfloat16)
        blocks[r, 0:32, :] = block
        first, last = sorted_skip[16 * r : 16 * r + 16], sorted_skip[64 + 16 * r : 80 + 16 * r]
        blocks[r, 32:48, :] = jnp.where(marks[0] == 0, first, last).astype(jnp.bfloat16)
    for k in range(GROUP):
        skip_outs[k][...] = blocks[marks[0] ^ k]


def edge_slice(block, far):
    lower = lax.broadcasted_iota(jnp.int32, (16, 128), 1) < 64
    sides = []
    for k in range(2):
        half = block[:, 128 * k : 128 * k + 128].astype(jnp.float32)
        top, bottom = half[:16], half[16:]
        if far:
            top = pltpu.roll(top, 64, 1)
        else:
            bottom = pltpu.roll(bottom, 64, 1)
        sides.append(jnp.where(lower, top, bottom))
    return jnp.concatenate(sides, axis=1)


def spread_taps(weights, values, dims, chans, voxels):
    lane = lax.broadcasted_iota(jnp.int32, (chans, voxels), 1)

    def moved(term, tap, step, place, last):
        if tap == 1:
            return term
        keep = place > 0 if tap == 0 else place < last
        return jnp.where(keep, pltpu.roll(term, ((1 - tap) * step) % voxels, 1), 0.0)

    total = None
    for a in range(3):
        products = dot(weights[a * 9 * chans : (a + 1) * 9 * chans, :], values, dims)
        plane = None
        for b in range(3):
            line = None
            for c in range(3):
                at = (b * 3 + c) * chans
                term = moved(products[at : at + chans], c, 1, lane & 3, 3)
                line = term if line is None else line + term
            line = moved(line, b, 4, (lane >> 2) & 3, 3)
            plane = line if plane is None else plane + line
        plane = moved(plane, a, 16, lane >> 4, voxels // 16 - 1)
        total = plane if total is None else total + plane
    return jnp.maximum(total, 0.0)


def by_rank(marks, near, blocks):
    for k in range(GROUP):
        blocks[marks[0] ^ k] = near[k][near[k].shape[0] - 48 :, :]


def by_depth(marks, near, parts, step):
    for k in range(GROUP):
        parts[marks[0] ^ k] = near[k][0 : parts.shape[1], :]
    return jnp.concatenate(
        [
            parts[r, at : at + step, :]
            for at in range(0, parts.shape[1], step)
            for r in range(GROUP)
        ],
        axis=0,
    )


def relay_stage(marks, *refs):
    line, refs = refs[:GROUP], refs[GROUP:]
    step = line[0].shape[0]
    skips, outs = refs[:GROUP], refs[GROUP:]
    for j in range(GROUP):
        for k in range(GROUP):
            outs[j][pl.ds(pl.multiple_of((marks[3] ^ k) * step, 16), step), :] = line[k][...]
        outs[j][GROUP * step :, :] = skips[j][...]


def edge_stage(marks, *refs):
    near, (near_swap, far_swap, blocks) = refs[:GROUP], refs[GROUP:]
    by_rank(marks, near, blocks)
    first = edge_slice(blocks[0, 0:32, :], False)
    last = edge_slice(blocks[GROUP - 1, 0:32, :], True)
    even = marks[2] == 0
    near_swap[...] = jnp.where(even, last, first).astype(jnp.bfloat16)
    far_swap[...] = jnp.where(even, first, last).astype(jnp.bfloat16)


def deep_stage(marks, weights, *refs):
    near, out, parts = refs[:-2], refs[-2], refs[-1]
    _, chans, voxels = out.shape
    values = near[0][...] if len(near) == 1 else by_depth(marks, near, parts, 16)
    deep = spread_taps(weights, values, ((1,), (1,)), chans, voxels).astype(jnp.bfloat16)
    for dest in range(out.shape[0]):
        out[dest] = deep


def deeper_stage(near_count, marks, weights, *refs):
    near, (deep, out, blocks) = refs[:near_count], refs[near_count:]
    n, chans, _ = out.shape
    voxels = deep.shape[1]
    deeper = spread_taps(weights, deep[...], ((1,), (0,)), chans, voxels)
    lane = lax.broadcasted_iota(jnp.int32, (chans, 128), 1)
    planes = n // GROUP
    ride = len(near) == GROUP
    if ride:
        by_rank(marks, near, blocks)
        edges = [blocks[r, 32:48, :].astype(jnp.float32) for r in (0, GROUP - 1)]
        riders = [
            [
                jnp.concatenate(
                    [
                        pltpu.roll(edge[:, at // 128 * 128 : at // 128 * 128 + 128], (96 - at) % 128, 1)
                        for at in (64 * r, 64 * r + 32)
                    ],
                    axis=0,
                )
                for r in range(GROUP)
            ]
            for edge in edges
        ]
    for p in range(planes):
        part = pltpu.roll(deeper, (16 - 64 * p) % voxels, 1)[:, :128]
        if p == 0:
            part = jnp.where(lane < 16, 0.0, part)
        if p == planes - 1:
            part = jnp.where(lane >= 80, 0.0, part)
        for r in range(GROUP):
            whole = part
            if ride:
                rider = jnp.where(marks[3] < p, riders[1][r], riders[0][r])
                whole = jnp.where(lane < 96, part, rider)
            out[GROUP * p + r] = whole.astype(jnp.bfloat16)


def rise_stage(marks, chans, rise, out):
    lane = lax.broadcasted_iota(jnp.int32, (256, 64), 1)
    row = lax.broadcasted_iota(jnp.int32, (256, 64), 0)
    source = (marks[0] + GROUP * (lane // chans)) * chans + lane % chans
    mine = jnp.where(row == source, 1.0, 0.0).astype(jnp.bfloat16)
    for pair in range(4):
        both = [dot(rise[2 * pair + k], mine) for k in range(2)]
        both = jnp.concatenate(both, axis=1).astype(jnp.bfloat16)
        out[:, 128 * pair : 128 * pair + 128] = both


def decode_stage(ride, marks, deeper, rise, *refs):
    swaps = () if ride else refs[:2]
    near, refs = refs[len(swaps) : len(swaps) + GROUP], refs[len(swaps) + GROUP :]
    decode, outs = refs[: -5 - GROUP], refs[-5 - GROUP : -5]
    framed, patches, risen, blocks, parts = refs[-5:]
    by_rank(marks, near, blocks)
    n, chans, _ = deeper.shape
    plane, planes = marks[3], n // GROUP
    upper = lax.broadcasted_iota(jnp.int32, (64, 128), 1) >= 64

    def edge(low):
        if not ride:
            even = marks[2] == 0
            sides = [swap[...].astype(jnp.float32) for swap in swaps]
            side = jnp.where(even, sides[low], sides[not low])
            parts = []
            for k in range(2):
                half = side[:, 128 * k : 128 * k + 128]
                parts += [pltpu.roll(half, 64, 1), half]
            return jnp.concatenate(parts, axis=0)
        other = jnp.maximum(plane - 1, 0) if low else jnp.minimum(plane + 1, planes - 1)
        lane = lax.broadcasted_iota(jnp.int32, (16, 128), 1)
        parts = []
        for r in range(GROUP):
            block = deeper[GROUP * other + r].astype(jnp.float32)
            parts.append(jnp.where(lane < 96, pltpu.roll(block[:16], 96, 1), block[16:]))
        return jnp.where(other == plane, 0.0, jnp.concatenate(parts, axis=0))

    framed[...] = jnp.zeros(framed.shape, jnp.float32)
    spread = round_once(dot(deeper[...].reshape(n * chans, 128).astype(jnp.float32).T.astype(jnp.bfloat16), rise[...]))
    for pair in range(4):
        both = spread[:, 128 * pair : 128 * pair + 128]
        risen[2 * pair] = both
        risen[2 * pair + 1] = pltpu.roll(both, 64, 1)
    for s in range(10):
        d, a = (s + 1) // 2, (s + 1) % 2
        for h in range(4):
            for b in range(2):
                for c in range(2):
                    framed[s, 1 + 2 * h + b, pl.ds(8 + c, 4, stride=2), :] = risen[
                        4 * a + 2 * b + c, 16 * d + 4 * h : 16 * d + 4 * h + 4, :
                    ]
        if s == 0 or s == 9:
            skip = edge(s == 0)
        else:
            both = blocks[(s - 1) // 2, 0:32, :].astype(jnp.float32)
            skip = jnp.concatenate([both[:, :128], both[:, 128:]], axis=0)
            if (s - 1) % 2 == 0:
                skip = pltpu.roll(skip, 64, 1)
        joined = framed[s, 1:9, 8:16, :].reshape(64, 128)
        framed[s, 1:9, 8:16, :] = jnp.where(upper, skip, joined).reshape(8, 8, 128)
    fill_patches(framed, patches, 10)
    def rows_at(rep, z, row):
        if rep == 0 and row >= 528:
            return decode[1][z, row - 528 : row - 512, :]
        if rep == 1 and row < 336:
            return decode[1][z, row : row + 16, :]
        if rep == 1 and row >= 528:
            row -= 528
        return decode[0][z, row : row + 16, :]

    def multiply(rep):
        count = decode[0].shape[0]
        step = 128 // count
        partial = None
        for a in range(3):
            right = [
                rows_at(rep, z, row)
                for tap in range(9 * a, 9 * a + 9)
                for z in range(count)
                for row in range(tap * step, (tap + 1) * step, 16)
            ]
            term = dot(patches[64 * a : 64 * a + 512], jnp.concatenate(right, axis=0))
            partial = term if partial is None else partial + term
        parts[...] = partial.astype(jnp.bfloat16).reshape(GROUP, 128, 256)

    if len(decode) == 1:
        multiply(None)
    else:
        pl.when(marks[1] == 0)(lambda: multiply(0))
        pl.when(marks[1] == 1)(lambda: multiply(1))
    for k in range(GROUP):
        outs[k][...] = parts[marks[0] ^ k]


def final_stage(*refs):
    partials, (weights, out, spaced) = refs[:GROUP], refs[GROUP:]
    decoded = partials[0][...].astype(jnp.float32)
    for partial in partials[1:]:
        decoded += partial[...].astype(jnp.float32)
    decoded = jnp.maximum(decoded, 0.0).astype(jnp.bfloat16)
    for a in range(2):
        for b in range(2):
            for c in range(2):
                values = dot(decoded, weights[4 * a + 2 * b + c])
                for d in range(2):
                    for h in range(8):
                        at = ((2 * d + a) * 16 + 2 * h + b) * 16 + c
                        spaced[pl.ds(at, 8, stride=2), :] = values[64 * d + 8 * h : 64 * d + 8 * h + 8]
    out[...] = spaced[...].astype(jnp.bfloat16)


ALL = ("z", "r")


def exchange(payload, axis):
    return lax.all_to_all(payload, axis, split_axis=0, concat_axis=0, tiled=True)


def by_xor(blocks, axis):
    swaps = [[(r, r ^ k) for r in range(GROUP)] for k in range(GROUP)]
    return [blocks[0]] + [lax.ppermute(blocks[k], axis, swaps[k]) for k in range(1, GROUP)]


def body(
    volume,
    first_kernel,
    second_kernel,
    deep_kernel,
    deeper_kernel,
    rise_kernel,
    decode_kernel,
    final_kernel,
):
    n = lax.axis_size(ALL)
    place = lax.axis_index(ALL)
    planes = n // GROUP
    rank = lax.axis_index("r")
    chans = deep_kernel.shape[4]
    voxels = 16 * n
    bf16 = functools.partial(jax.ShapeDtypeStruct, dtype=jnp.bfloat16)

    rep, plane = lax.axis_index("rep"), lax.axis_index("z")
    marks = jnp.stack([rank, rep, plane % 2, plane, place % 2, place, n - 1 - place])
    marks = marks.astype(jnp.int32)
    decode_block = decode_kernel.reshape(27 * chans, 256)
    shared = lax.axis_size("rep") == 2 and chans == 32
    ride = chans == 32
    paired = planes == GROUP
    halo = bf16((3, 16, 16, 128))
    in_spaces = [pltpu.SMEM, pltpu.SMEM, pl.ANY, pl.ANY]
    off_chip, on_chip, *share = pl.pallas_call(
        front_stage,
        out_shape=(halo, halo) + (bf16((528, 256)),) * shared,
        in_specs=[pl.BlockSpec(memory_space=space) for space in in_spaces],
        out_specs=(pl.BlockSpec(memory_space=pltpu.VMEM),) * (2 + shared),
        scratch_shapes=[pltpu.SemaphoreType.DMA((4,))],
        compiler_params=pltpu.CompilerParams(vmem_limit_bytes=60 * MIB),
        cost_estimate=pl.CostEstimate(flops=0, bytes_accessed=10**6, transcendentals=0),
    )(
        (place % 2).astype(jnp.int32).reshape(1),
        rep.astype(jnp.int32).reshape(1),
        volume,
        decode_block,
    )
    pairs = [(i, i + 1) for i in range(1, n - 1, 2)]
    off_chip = lax.ppermute(off_chip, ALL, pairs + [(j, i) for i, j in pairs])
    on_chip = lax.ppermute(on_chip, ALL, [(i, i ^ 1) for i in range(n)])
    if shared:
        decode_block = share[0]
    line = lax.all_gather(decode_block, "z", axis=0)

    pairs = [(i, i + 1) for i in range(1, n - 1, 2)]
    taps = first_kernel.reshape(3, 1152, 128)
    own = call(
        own_stage,
        jax.ShapeDtypeStruct((4, 256, 256), jnp.float32),
        [pltpu.VMEM((4, 18, 16, 384), jnp.bfloat16)],
        (volume, taps),
        2 * 1024 * 2304 * 256,
        24,
    )
    lane = np.arange(256)
    source = (lane // 64 + GROUP * (lane % 64 // chans)) * chans + lane % chans
    order = jnp.asarray(np.arange(256)[:, None] == source[None, :], jnp.bfloat16)
    rise_part = call(
        lambda marks_ref, *refs: rise_stage(marks_ref, chans, *refs),
        bf16((n * chans, 512)),
        [],
        (marks, rise_kernel.reshape(8, n * chans, 256)),
        2 * 8 * n * chans * 256 * 64,
        16,
        scalars=1,
    )
    pooled_two, *skips = call(
        stem_stage,
        (bf16((1 if paired else n, 16, 256)),) + (bf16((48, 256)),) * GROUP,
        [
            pltpu.VMEM((6, 18, 16, 384), jnp.bfloat16),
            pltpu.VMEM((128, 128), jnp.float32),
            pltpu.VMEM((4, 10, 24, 128), jnp.float32),
            pltpu.VMEM((256, 1152), jnp.bfloat16),
            pltpu.VMEM((2, 32, 128), jnp.float32),
            pltpu.VMEM((GROUP, 48, 256), jnp.bfloat16),
        ],
        (marks, off_chip, on_chip, own, taps, second_kernel.reshape(3, 1152, 256), order, rise_part),
        2 * 1024 * 2304 * 256,
        24,
        scalars=1,
        unread=1,
    )
    if paired:
        line_blocks = by_xor([pooled_two.reshape(16, 256)] * GROUP, "z")
        relays = call(
            relay_stage,
            (bf16((112, 256)),) * GROUP,
            [],
            (marks, *line_blocks, *skips),
            0,
            16,
            scalars=1,
        )
        near = by_xor(relays, "r")
        pooled_whole = near
    else:
        pooled_whole = (exchange(pooled_two, ALL).reshape(voxels, 256),)
        near = by_xor(skips, "r")
    blocks = pltpu.VMEM((GROUP, 48, 256), jnp.bfloat16)

    deep = call(
        deep_stage,
        bf16((n, chans, voxels)),
        [pltpu.VMEM((GROUP, 64, 256), jnp.bfloat16)],
        (
            marks,
            deep_kernel.transpose(0, 1, 2, 4, 3).reshape(27 * chans, 256),
            *pooled_whole,
        ),
        2 * 27 * chans * 256 * voxels,
        16,
        scalars=1,
    )
    if shared:
        piece = call(
            pick_stage,
            bf16((planes, 336, 256)),
            [pltpu.SemaphoreType.DMA],
            (line, deep),
            0,
            16,
            unread=2,
        )
        weights = (line, lax.ppermute(piece, "rep", [(0, 1), (1, 0)]))
    elif chans % 16:
        weights = line.reshape(planes, 27, chans, 256).transpose(1, 0, 2, 3)
        weights = (weights.reshape(1, 27 * 128, 256),)
    else:
        weights = (line,)
    swaps = ()
    if not ride:
        swaps = call(
            edge_stage,
            (bf16((16, 256)), bf16((16, 256))),
            [blocks],
            (marks, *near),
            0,
            16,
            scalars=1,
        )
        near_pairs = [(p, p + 1) for p in range(0, planes - 1, 2)]
        far_pairs = [(p, p + 1) for p in range(1, planes - 1, 2)]
        near_swap = lax.ppermute(swaps[0], "z", near_pairs + [(j, i) for i, j in near_pairs])
        far_swap = lax.ppermute(swaps[1], "z", far_pairs + [(j, i) for i, j in far_pairs])
        swaps = (near_swap, far_swap)
    deep_whole = (exchange(deep, ALL).reshape(n * chans, voxels),)

    riders = near if ride else ()
    deeper = call(
        functools.partial(deeper_stage, len(riders)),
        bf16((n, chans, 128)),
        [blocks],
        (
            marks,
            deeper_kernel.transpose(0, 1, 2, 4, 3).reshape(27 * chans, n * chans),
            *riders,
            *deep_whole,
        ),
        2 * 27 * chans * n * chans * voxels,
        16,
        scalars=1,
    )
    deeper_near = exchange(deeper, ALL)

    partials = call(
        functools.partial(decode_stage, ride),
        (bf16((128, 256)),) * GROUP,
        [
            pltpu.VMEM((10, 10, 24, 128), jnp.float32),
            pltpu.VMEM((640, 1152), jnp.bfloat16),
            pltpu.VMEM((8, 128, 128), jnp.float32),
            blocks,
            pltpu.VMEM((GROUP, 128, 256), jnp.bfloat16),
        ],
        (marks, deeper_near, rise_part, *swaps, *near, *weights),
        2 * 512 * 3456 * 256,
        24,
        scalars=1,
    )
    partials = by_xor(partials, "r")
    out = call(
        final_stage,
        bf16((1024, 128)),
        [pltpu.VMEM((1024, 128), jnp.float32)],
        (*partials, final_kernel.reshape(8, 256, 128)),
        2 * 128 * 256 * 1024,
        16,
    )
    return out.reshape(4, 16, 16, 128)


def solution(mesh):
    reps, n = mesh.devices.shape
    grid = jax.sharding.Mesh(mesh.devices.reshape(reps, n // GROUP, GROUP), ("rep",) + ALL)
    return jax.shard_map(
        body,
        mesh=grid,
        in_specs=(
            P(("rep",) + ALL, None, None, None),
            P(),
            P(),
            P(None, None, None, None, ALL),
            P(None, None, None, None, ALL),
            P(),
            P(None, None, None, ALL, None),
            P(),
        ),
        out_specs=P(("rep",) + ALL, None, None, None),
        check_vma=False,
    )
```

```python
import functools

import jax
import jax.numpy as jnp
import numpy as np
from jax import lax
from jax.experimental import pallas as pl
from jax.experimental.pallas import tpu as pltpu
from jax.sharding import PartitionSpec as P

GROUP = 4
MIB = 1024 * 1024


def call(kernel, outs, scratch, args, flops, vmem_mib, scalars=0, unread=0):
    spaces = [pltpu.SMEM] * scalars + [pltpu.VMEM] * (len(args) - scalars - unread)
    spaces += [pl.ANY] * unread
    return pl.pallas_call(
        kernel,
        out_shape=outs,
        in_specs=[pl.BlockSpec(memory_space=space) for space in spaces],
        out_specs=jax.tree.map(lambda _: pl.BlockSpec(memory_space=pltpu.VMEM), outs),
        scratch_shapes=scratch,
        compiler_params=pltpu.CompilerParams(vmem_limit_bytes=vmem_mib * MIB),
        cost_estimate=pl.CostEstimate(
            flops=flops,
            bytes_accessed=sum(a.size * a.dtype.itemsize for a in args[: len(args) - unread]),
            transcendentals=0,
        ),
    )(*args)


def dot(left, right, dims=((1,), (0,))):
    return lax.dot_general(left, right, (dims, ((), ())), preferred_element_type=jnp.float32)


def round_once(values):
    return values.astype(jnp.bfloat16).astype(jnp.float32)


def fill_patches(framed, patches, slices):
    for b in range(3):
        for c in range(3):
            tap = framed[:, b : b + 8, 7 + c : 15 + c, :].reshape(slices * 64, 128)
            col = (b * 3 + c) * 128
            patches[:, col : col + 128] = tap.astype(jnp.bfloat16)


def shift_slice(shifted, s, values):
    row = lax.broadcasted_iota(jnp.int32, (256, 128), 0) & 15
    here = values.reshape(256, 128).astype(jnp.float32)
    before = jnp.where(row == 0, 0.0, pltpu.roll(here, 1, 0))
    after = jnp.where(row == 15, 0.0, pltpu.roll(here, 255, 0))
    shifted[s, 0] = jnp.zeros((16, 384), jnp.bfloat16)
    shifted[s, 17] = jnp.zeros((16, 384), jnp.bfloat16)
    for c, tap in enumerate((before, here, after)):
        tap = tap.astype(jnp.bfloat16).reshape(16, 16, 128)
        shifted[s, 1:17, :, 128 * c : 128 * c + 128] = tap


def depth_pair(shifted, slices, weights, steps):
    left = jnp.concatenate(
        [shifted[s, b : b + 16].reshape(256, 384) for s in slices for b in range(3)], axis=1
    )
    none = jnp.zeros((1152, 128), jnp.bfloat16)
    right = [
        jnp.concatenate(
            [weights[j] if j < 3 else none, weights[j - 1] if j > 0 else none], axis=1
        )
        for j in steps
    ]
    return dot(left, jnp.concatenate(right, axis=0))


def depth_one(shifted, s, weights):
    left = jnp.concatenate([shifted[s, b : b + 16].reshape(256, 384) for b in range(3)], axis=1)
    return dot(left, weights)


def front_stage(odd, rep, volume, decode, off_chip, on_chip, *refs):
    done = refs[-1]
    pairs = [
        (volume.at[pl.ds(odd[0], 3)], off_chip),
        (volume.at[pl.ds(1 - odd[0], 3)], on_chip),
    ]
    if len(refs) == 2:
        block = refs[0]
        at = pl.multiple_of(528 * rep[0], 16)
        pairs += [
            (decode.at[pl.ds(at, 336)], block.at[pl.ds(0, 336)]),
            (decode.at[pl.ds(336, 192)], block.at[pl.ds(336, 192)]),
        ]
    copies = [
        pltpu.make_async_copy(source, target, done.at[i]) for i, (source, target) in enumerate(pairs)
    ]
    for copy in copies:
        copy.start()
    for copy in copies:
        copy.wait()


def own_stage(volume, weights, out, shifted):
    for s in range(4):
        shift_slice(shifted, s, volume[s])
    out[0, :, :128] = jnp.zeros((256, 128), jnp.float32)
    out[0, :, 128:] = depth_one(shifted, 0, weights[2])
    out[1] = depth_pair(shifted, (0, 1, 2), weights, (1, 2, 3))
    out[2] = depth_pair(shifted, (1, 2, 3), weights, (0, 1, 2))
    out[3, :, :128] = depth_one(shifted, 3, weights[0])
    out[3, :, 128:] = jnp.zeros((256, 128), jnp.float32)


def stem_stage(marks, off_chip, on_chip, own, weights, second, order, _, *refs):
    pooled_out, skip_outs = refs[0], refs[1 : 1 + GROUP]
    shifted, halves, framed, patches, quarters, blocks = refs[1 + GROUP :]
    for s in range(3):
        even = marks[4] == 0
        shift_slice(shifted, s, jnp.where(even, off_chip[s], on_chip[s]))
        shift_slice(shifted, 3 + s, jnp.where(even, on_chip[s], off_chip[s]))
    framed[...] = jnp.zeros(framed.shape, jnp.float32)
    for m in range(4):
        if m == 0:
            first = own[0] + depth_pair(shifted, (0, 1, 2), weights, (0, 1, 2))
        elif m == 3:
            first = own[3] + depth_pair(shifted, (3, 4, 5), weights, (1, 2, 3))
        elif m == 1:
            near = own[1, :, :128] + depth_one(shifted, 2, weights[0])
            first = jnp.concatenate([near, own[1, :, 128:]], axis=1)
        else:
            far = own[2, :, 128:] + depth_one(shifted, 3, weights[2])
            first = jnp.concatenate([own[2, :, :128], far], axis=1)
        first = round_once(jnp.maximum(first, 0.0))
        pair = (first[:, :128] + first[:, 128:]).reshape(8, 32, 128)
        halves[...] = (pair[:, :16] + pair[:, 16:]).reshape(128, 128)
        pooled = halves[pl.ds(0, 64, stride=2), :] + halves[pl.ds(1, 64, stride=2), :]
        pooled = round_once(pooled * 0.125)
        if m == 0:
            pooled = jnp.where(marks[5] == 0, 0.0, pooled)
        if m == 3:
            pooled = jnp.where(marks[6] == 0, 0.0, pooled)
        framed[m, 1:9, 8:16, :] = pooled.reshape(8, 8, 128)
    fill_patches(framed, patches, 4)
    skip = dot(patches[0:128], second[0])
    skip += dot(patches[64:192], second[1])
    skip += dot(patches[128:256], second[2])
    skip = jnp.maximum(skip, 0.0).astype(jnp.bfloat16)
    wide = skip.astype(jnp.float32)
    pair = (wide[:64] + wide[64:]).reshape(4, 16, 256)
    pair = (pair[:, :8] + pair[:, 8:]).reshape(32, 256)
    for k in range(2):
        quarters[k] = pair[:, 128 * k : 128 * k + 128]
    pooled = jnp.concatenate(
        [
            quarters[k, pl.ds(0, 16, stride=2), :] + quarters[k, pl.ds(1, 16, stride=2), :]
            for k in range(2)
        ],
        axis=1,
    )
    pooled = (pooled * 0.125).astype(jnp.bfloat16)
    for p in range(pooled_out.shape[0]):
        pooled_out[p] = pooled
    sorted_skip = dot(skip, order[...])
    for r in range(GROUP):
        near, far = sorted_skip[:64, 64 * r : 64 * r + 64], sorted_skip[64:, 64 * r : 64 * r + 64]
        block = jnp.concatenate([near, far], axis=1)
        block = jnp.concatenate([block[:32], block[32:]], axis=1).astype(jnp.bfloat16)
        blocks[r, 0:32, :] = block
        first, last = sorted_skip[16 * r : 16 * r + 16], sorted_skip[64 + 16 * r : 80 + 16 * r]
        blocks[r, 32:48, :] = jnp.where(marks[0] == 0, first, last).astype(jnp.bfloat16)
    for k in range(GROUP):
        skip_outs[k][...] = blocks[marks[0] ^ k]


def edge_slice(block, far):
    lower = lax.broadcasted_iota(jnp.int32, (16, 128), 1) < 64
    sides = []
    for k in range(2):
        half = block[:, 128 * k : 128 * k + 128].astype(jnp.float32)
        top, bottom = half[:16], half[16:]
        if far:
            top = pltpu.roll(top, 64, 1)
        else:
            bottom = pltpu.roll(bottom, 64, 1)
        sides.append(jnp.where(lower, top, bottom))
    return jnp.concatenate(sides, axis=1)


def spread_taps(weights, values, dims, chans, voxels):
    lane = lax.broadcasted_iota(jnp.int32, (chans, voxels), 1)

    def moved(term, tap, step, place, last):
        if tap == 1:
            return term
        keep = place > 0 if tap == 0 else place < last
        return jnp.where(keep, pltpu.roll(term, ((1 - tap) * step) % voxels, 1), 0.0)

    total = None
    for a in range(3):
        products = dot(weights[a * 9 * chans : (a + 1) * 9 * chans, :], values, dims)
        plane = None
        for b in range(3):
            line = None
            for c in range(3):
                at = (b * 3 + c) * chans
                term = moved(products[at : at + chans], c, 1, lane & 3, 3)
                line = term if line is None else line + term
            line = moved(line, b, 4, (lane >> 2) & 3, 3)
            plane = line if plane is None else plane + line
        plane = moved(plane, a, 16, lane >> 4, voxels // 16 - 1)
        total = plane if total is None else total + plane
    return jnp.maximum(total, 0.0)


def by_rank(marks, near, blocks):
    for k in range(GROUP):
        blocks[marks[0] ^ k] = near[k][near[k].shape[0] - 48 :, :]


def by_depth(marks, near, parts, step):
    for k in range(GROUP):
        parts[marks[0] ^ k] = near[k][0 : parts.shape[1], :]
    return jnp.concatenate(
        [
            parts[r, at : at + step, :]
            for at in range(0, parts.shape[1], step)
            for r in range(GROUP)
        ],
        axis=0,
    )


def relay_stage(marks, *refs):
    line, refs = refs[:GROUP], refs[GROUP:]
    step = line[0].shape[0]
    skips, outs = refs[:GROUP], refs[GROUP:]
    for j in range(GROUP):
        for k in range(GROUP):
            outs[j][pl.ds(pl.multiple_of((marks[3] ^ k) * step, 16), step), :] = line[k][...]
        outs[j][GROUP * step :, :] = skips[j][...]


def edge_stage(marks, *refs):
    near, (near_swap, far_swap, blocks) = refs[:GROUP], refs[GROUP:]
    by_rank(marks, near, blocks)
    first = edge_slice(blocks[0, 0:32, :], False)
    last = edge_slice(blocks[GROUP - 1, 0:32, :], True)
    even = marks[2] == 0
    near_swap[...] = jnp.where(even, last, first).astype(jnp.bfloat16)
    far_swap[...] = jnp.where(even, first, last).astype(jnp.bfloat16)


def deep_stage(marks, weights, *refs):
    near, out, parts = refs[:-2], refs[-2], refs[-1]
    _, chans, voxels = out.shape
    values = near[0][...] if len(near) == 1 else by_depth(marks, near, parts, 16)
    deep = spread_taps(weights, values, ((1,), (1,)), chans, voxels).astype(jnp.bfloat16)
    for dest in range(out.shape[0]):
        out[dest] = deep


def deeper_stage(near_count, marks, weights, *refs):
    near, (deep, out, blocks) = refs[:near_count], refs[near_count:]
    n, chans, _ = out.shape
    voxels = deep.shape[1]
    deeper = spread_taps(weights, deep[...], ((1,), (0,)), chans, voxels)
    lane = lax.broadcasted_iota(jnp.int32, (chans, 128), 1)
    planes = n // GROUP
    ride = len(near) == GROUP
    if ride:
        by_rank(marks, near, blocks)
        edges = [blocks[r, 32:48, :].astype(jnp.float32) for r in (0, GROUP - 1)]
        riders = [
            [
                jnp.concatenate(
                    [
                        pltpu.roll(edge[:, at // 128 * 128 : at // 128 * 128 + 128], (96 - at) % 128, 1)
                        for at in (64 * r, 64 * r + 32)
                    ],
                    axis=0,
                )
                for r in range(GROUP)
            ]
            for edge in edges
        ]
    for p in range(planes):
        part = pltpu.roll(deeper, (16 - 64 * p) % voxels, 1)[:, :128]
        if p == 0:
            part = jnp.where(lane < 16, 0.0, part)
        if p == planes - 1:
            part = jnp.where(lane >= 80, 0.0, part)
        for r in range(GROUP):
            whole = part
            if ride:
                rider = jnp.where(marks[3] < p, riders[1][r], riders[0][r])
                whole = jnp.where(lane < 96, part, rider)
            out[GROUP * p + r] = whole.astype(jnp.bfloat16)


def rise_stage(marks, chans, rise, out):
    lane = lax.broadcasted_iota(jnp.int32, (256, 64), 1)
    row = lax.broadcasted_iota(jnp.int32, (256, 64), 0)
    source = (marks[0] + GROUP * (lane // chans)) * chans + lane % chans
    mine = jnp.where(row == source, 1.0, 0.0).astype(jnp.bfloat16)
    for pair in range(4):
        both = [dot(rise[2 * pair + k], mine) for k in range(2)]
        both = jnp.concatenate(both, axis=1).astype(jnp.bfloat16)
        out[:, 128 * pair : 128 * pair + 128] = both


def decode_stage(ride, marks, deeper, rise, *refs):
    swaps = () if ride else refs[:2]
    near, refs = refs[len(swaps) : len(swaps) + GROUP], refs[len(swaps) + GROUP :]
    decode, outs = refs[: -5 - GROUP], refs[-5 - GROUP : -5]
    framed, patches, risen, blocks, parts = refs[-5:]
    by_rank(marks, near, blocks)
    n, chans, _ = deeper.shape
    plane, planes = marks[3], n // GROUP
    upper = lax.broadcasted_iota(jnp.int32, (64, 128), 1) >= 64

    def edge(low):
        if not ride:
            even = marks[2] == 0
            sides = [swap[...].astype(jnp.float32) for swap in swaps]
            side = jnp.where(even, sides[low], sides[not low])
            parts = []
            for k in range(2):
                half = side[:, 128 * k : 128 * k + 128]
                parts += [pltpu.roll(half, 64, 1), half]
            return jnp.concatenate(parts, axis=0)
        other = jnp.maximum(plane - 1, 0) if low else jnp.minimum(plane + 1, planes - 1)
        lane = lax.broadcasted_iota(jnp.int32, (16, 128), 1)
        parts = []
        for r in range(GROUP):
            block = deeper[GROUP * other + r].astype(jnp.float32)
            parts.append(jnp.where(lane < 96, pltpu.roll(block[:16], 96, 1), block[16:]))
        return jnp.where(other == plane, 0.0, jnp.concatenate(parts, axis=0))

    framed[...] = jnp.zeros(framed.shape, jnp.float32)
    spread = round_once(dot(deeper[...].reshape(n * chans, 128).astype(jnp.float32).T.astype(jnp.bfloat16), rise[...]))
    for pair in range(4):
        both = spread[:, 128 * pair : 128 * pair + 128]
        risen[2 * pair] = both
        risen[2 * pair + 1] = pltpu.roll(both, 64, 1)
    for s in range(10):
        d, a = (s + 1) // 2, (s + 1) % 2
        for h in range(4):
            for b in range(2):
                for c in range(2):
                    framed[s, 1 + 2 * h + b, pl.ds(8 + c, 4, stride=2), :] = risen[
                        4 * a + 2 * b + c, 16 * d + 4 * h : 16 * d + 4 * h + 4, :
                    ]
        if s == 0 or s == 9:
            skip = edge(s == 0)
        else:
            both = blocks[(s - 1) // 2, 0:32, :].astype(jnp.float32)
            skip = jnp.concatenate([both[:, :128], both[:, 128:]], axis=0)
            if (s - 1) % 2 == 0:
                skip = pltpu.roll(skip, 64, 1)
        joined = framed[s, 1:9, 8:16, :].reshape(64, 128)
        framed[s, 1:9, 8:16, :] = jnp.where(upper, skip, joined).reshape(8, 8, 128)
    fill_patches(framed, patches, 10)
    def rows_at(rep, z, row):
        if rep == 0 and row >= 528:
            return decode[1][z, row - 528 : row - 512, :]
        if rep == 1 and row < 336:
            return decode[1][z, row : row + 16, :]
        if rep == 1 and row >= 528:
            row -= 528
        return decode[0][z, row : row + 16, :]

    def multiply(rep):
        count = decode[0].shape[0]
        step = 128 // count
        partial = None
        for a in range(3):
            right = [
                rows_at(rep, z, row)
                for tap in range(9 * a, 9 * a + 9)
                for z in range(count)
                for row in range(tap * step, (tap + 1) * step, 16)
            ]
            term = dot(patches[64 * a : 64 * a + 512], jnp.concatenate(right, axis=0))
            partial = term if partial is None else partial + term
        parts[...] = partial.astype(jnp.bfloat16).reshape(GROUP, 128, 256)

    if len(decode) == 1:
        multiply(None)
    else:
        pl.when(marks[1] == 0)(lambda: multiply(0))
        pl.when(marks[1] == 1)(lambda: multiply(1))
    for k in range(GROUP):
        outs[k][...] = parts[marks[0] ^ k]


def final_stage(*refs):
    partials, (weights, out, spaced) = refs[:GROUP], refs[GROUP:]
    decoded = partials[0][...].astype(jnp.float32)
    for partial in partials[1:]:
        decoded += partial[...].astype(jnp.float32)
    decoded = jnp.maximum(decoded, 0.0).astype(jnp.bfloat16)
    for a in range(2):
        for b in range(2):
            for c in range(2):
                values = dot(decoded, weights[4 * a + 2 * b + c])
                for d in range(2):
                    for h in range(8):
                        at = ((2 * d + a) * 16 + 2 * h + b) * 16 + c
                        spaced[pl.ds(at, 8, stride=2), :] = values[64 * d + 8 * h : 64 * d + 8 * h + 8]
    out[...] = spaced[...].astype(jnp.bfloat16)


ALL = ("z", "r")


def exchange(payload, axis):
    return lax.all_to_all(payload, axis, split_axis=0, concat_axis=0, tiled=True)


def by_xor(blocks, axis):
    swaps = [[(r, r ^ k) for r in range(GROUP)] for k in range(GROUP)]
    return [blocks[0]] + [lax.ppermute(blocks[k], axis, swaps[k]) for k in range(1, GROUP)]


def body(
    volume,
    first_kernel,
    second_kernel,
    deep_kernel,
    deeper_kernel,
    rise_kernel,
    decode_kernel,
    final_kernel,
):
    n = lax.axis_size(ALL)
    place = lax.axis_index(ALL)
    planes = n // GROUP
    rank = lax.axis_index("r")
    chans = deep_kernel.shape[4]
    voxels = 16 * n
    bf16 = functools.partial(jax.ShapeDtypeStruct, dtype=jnp.bfloat16)

    rep, plane = lax.axis_index("rep"), lax.axis_index("z")
    marks = jnp.stack([rank, rep, plane % 2, plane, place % 2, place, n - 1 - place])
    marks = marks.astype(jnp.int32)
    decode_block = decode_kernel.reshape(27 * chans, 256)
    shared = lax.axis_size("rep") == 2 and chans == 32
    ride = chans == 32
    paired = planes == GROUP
    halo = bf16((3, 16, 16, 128))
    in_spaces = [pltpu.SMEM, pltpu.SMEM, pl.ANY, pl.ANY]
    off_chip, on_chip, *share = pl.pallas_call(
        front_stage,
        out_shape=(halo, halo) + (bf16((528, 256)),) * shared,
        in_specs=[pl.BlockSpec(memory_space=space) for space in in_spaces],
        out_specs=(pl.BlockSpec(memory_space=pltpu.VMEM),) * (2 + shared),
        scratch_shapes=[pltpu.SemaphoreType.DMA((4,))],
        compiler_params=pltpu.CompilerParams(vmem_limit_bytes=60 * MIB),
        cost_estimate=pl.CostEstimate(flops=0, bytes_accessed=10**6, transcendentals=0),
    )(
        (place % 2).astype(jnp.int32).reshape(1),
        rep.astype(jnp.int32).reshape(1),
        volume,
        decode_block,
    )
    pairs = [(i, i + 1) for i in range(1, n - 1, 2)]
    off_chip = lax.ppermute(off_chip, ALL, pairs + [(j, i) for i, j in pairs])
    on_chip = lax.ppermute(on_chip, ALL, [(i, i ^ 1) for i in range(n)])
    if shared:
        decode_block = share[0]
    line = lax.all_gather(decode_block, "z", axis=0)

    pairs = [(i, i + 1) for i in range(1, n - 1, 2)]
    taps = first_kernel.reshape(3, 1152, 128)
    own = call(
        own_stage,
        jax.ShapeDtypeStruct((4, 256, 256), jnp.float32),
        [pltpu.VMEM((4, 18, 16, 384), jnp.bfloat16)],
        (volume, taps),
        2 * 1024 * 2304 * 256,
        24,
    )
    lane = np.arange(256)
    source = (lane // 64 + GROUP * (lane % 64 // chans)) * chans + lane % chans
    order = jnp.asarray(np.arange(256)[:, None] == source[None, :], jnp.bfloat16)
    rise_part = call(
        lambda marks_ref, *refs: rise_stage(marks_ref, chans, *refs),
        bf16((n * chans, 512)),
        [],
        (marks, rise_kernel.reshape(8, n * chans, 256)),
        2 * 8 * n * chans * 256 * 64,
        16,
        scalars=1,
    )
    pooled_two, *skips = call(
        stem_stage,
        (bf16((1 if paired else n, 16, 256)),) + (bf16((48, 256)),) * GROUP,
        [
            pltpu.VMEM((6, 18, 16, 384), jnp.bfloat16),
            pltpu.VMEM((128, 128), jnp.float32),
            pltpu.VMEM((4, 10, 24, 128), jnp.float32),
            pltpu.VMEM((256, 1152), jnp.bfloat16),
            pltpu.VMEM((2, 32, 128), jnp.float32),
            pltpu.VMEM((GROUP, 48, 256), jnp.bfloat16),
        ],
        (marks, off_chip, on_chip, own, taps, second_kernel.reshape(3, 1152, 256), order, rise_part),
        2 * 1024 * 2304 * 256,
        24,
        scalars=1,
        unread=1,
    )
    if paired:
        line_blocks = by_xor([pooled_two.reshape(16, 256)] * GROUP, "z")
        relays = call(
            relay_stage,
            (bf16((112, 256)),) * GROUP,
            [],
            (marks, *line_blocks, *skips),
            0,
            16,
            scalars=1,
        )
        near = by_xor(relays, "r")
        pooled_whole = near
    else:
        pooled_whole = (exchange(pooled_two, ALL).reshape(voxels, 256),)
        near = by_xor(skips, "r")
    blocks = pltpu.VMEM((GROUP, 48, 256), jnp.bfloat16)

    deep = call(
        deep_stage,
        bf16((n, chans, voxels)),
        [pltpu.VMEM((GROUP, 64, 256), jnp.bfloat16)],
        (
            marks,
            deep_kernel.transpose(0, 1, 2, 4, 3).reshape(27 * chans, 256),
            *pooled_whole,
        ),
        2 * 27 * chans * 256 * voxels,
        16,
        scalars=1,
    )
    if shared:
        weights = (line, lax.ppermute(line[:, :336], "rep", [(0, 1), (1, 0)]))
    elif chans % 16:
        weights = line.reshape(planes, 27, chans, 256).transpose(1, 0, 2, 3)
        weights = (weights.reshape(1, 27 * 128, 256),)
    else:
        weights = (line,)
    swaps = ()
    if not ride:
        swaps = call(
            edge_stage,
            (bf16((16, 256)), bf16((16, 256))),
            [blocks],
            (marks, *near),
            0,
            16,
            scalars=1,
        )
        near_pairs = [(p, p + 1) for p in range(0, planes - 1, 2)]
        far_pairs = [(p, p + 1) for p in range(1, planes - 1, 2)]
        near_swap = lax.ppermute(swaps[0], "z", near_pairs + [(j, i) for i, j in near_pairs])
        far_swap = lax.ppermute(swaps[1], "z", far_pairs + [(j, i) for i, j in far_pairs])
        swaps = (near_swap, far_swap)
    deep_whole = (exchange(deep, ALL).reshape(n * chans, voxels),)

    riders = near if ride else ()
    deeper = call(
        functools.partial(deeper_stage, len(riders)),
        bf16((n, chans, 128)),
        [blocks],
        (
            marks,
            deeper_kernel.transpose(0, 1, 2, 4, 3).reshape(27 * chans, n * chans),
            *riders,
            *deep_whole,
        ),
        2 * 27 * chans * n * chans * voxels,
        16,
        scalars=1,
    )
    deeper_near = exchange(deeper, ALL)

    partials = call(
        functools.partial(decode_stage, ride),
        (bf16((128, 256)),) * GROUP,
        [
            pltpu.VMEM((10, 10, 24, 128), jnp.float32),
            pltpu.VMEM((640, 1152), jnp.bfloat16),
            pltpu.VMEM((8, 128, 128), jnp.float32),
            blocks,
            pltpu.VMEM((GROUP, 128, 256), jnp.bfloat16),
        ],
        (marks, deeper_near, rise_part, *swaps, *near, *weights),
        2 * 512 * 3456 * 256,
        24,
        scalars=1,
    )
    partials = by_xor(partials, "r")
    out = call(
        final_stage,
        bf16((1024, 128)),
        [pltpu.VMEM((1024, 128), jnp.float32)],
        (*partials, final_kernel.reshape(8, 256, 128)),
        2 * 128 * 256 * 1024,
        16,
    )
    return out.reshape(4, 16, 16, 128)


def solution(mesh):
    reps, n = mesh.devices.shape
    grid = jax.sharding.Mesh(mesh.devices.reshape(reps, n // GROUP, GROUP), ("rep",) + ALL)
    return jax.shard_map(
        body,
        mesh=grid,
        in_specs=(
            P(("rep",) + ALL, None, None, None),
            P(),
            P(),
            P(None, None, None, None, ALL),
            P(None, None, None, None, ALL),
            P(),
            P(None, None, None, ALL, None),
            P(),
        ),
        out_specs=P(("rep",) + ALL, None, None, None),
        check_vma=False,
    )
```

```python
import functools

import jax
import jax.numpy as jnp
import numpy as np
from jax import lax
from jax.experimental import pallas as pl
from jax.experimental.pallas import tpu as pltpu
from jax.sharding import PartitionSpec as P

GROUP = 4
MIB = 1024 * 1024


def call(kernel, outs, scratch, args, flops, vmem_mib, scalars=0, unread=0):
    spaces = [pltpu.SMEM] * scalars + [pltpu.VMEM] * (len(args) - scalars - unread)
    spaces += [pl.ANY] * unread
    return pl.pallas_call(
        kernel,
        out_shape=outs,
        in_specs=[pl.BlockSpec(memory_space=space) for space in spaces],
        out_specs=jax.tree.map(lambda _: pl.BlockSpec(memory_space=pltpu.VMEM), outs),
        scratch_shapes=scratch,
        compiler_params=pltpu.CompilerParams(vmem_limit_bytes=vmem_mib * MIB),
        cost_estimate=pl.CostEstimate(
            flops=flops,
            bytes_accessed=sum(a.size * a.dtype.itemsize for a in args[: len(args) - unread]),
            transcendentals=0,
        ),
    )(*args)


def dot(left, right, dims=((1,), (0,))):
    return lax.dot_general(left, right, (dims, ((), ())), preferred_element_type=jnp.float32)


def round_once(values):
    return values.astype(jnp.bfloat16).astype(jnp.float32)


def fill_patches(framed, patches, slices):
    for b in range(3):
        for c in range(3):
            tap = framed[:, b : b + 8, 7 + c : 15 + c, :].reshape(slices * 64, 128)
            col = (b * 3 + c) * 128
            patches[:, col : col + 128] = tap.astype(jnp.bfloat16)


def shift_slice(shifted, s, values):
    row = lax.broadcasted_iota(jnp.int32, (256, 128), 0) & 15
    here = values.reshape(256, 128).astype(jnp.float32)
    before = jnp.where(row == 0, 0.0, pltpu.roll(here, 1, 0))
    after = jnp.where(row == 15, 0.0, pltpu.roll(here, 255, 0))
    shifted[s, 0] = jnp.zeros((16, 384), jnp.bfloat16)
    shifted[s, 17] = jnp.zeros((16, 384), jnp.bfloat16)
    for c, tap in enumerate((before, here, after)):
        tap = tap.astype(jnp.bfloat16).reshape(16, 16, 128)
        shifted[s, 1:17, :, 128 * c : 128 * c + 128] = tap


def depth_pair(shifted, slices, weights, steps):
    left = jnp.concatenate(
        [shifted[s, b : b + 16].reshape(256, 384) for s in slices for b in range(3)], axis=1
    )
    none = jnp.zeros((1152, 128), jnp.bfloat16)
    right = [
        jnp.concatenate(
            [weights[j] if j < 3 else none, weights[j - 1] if j > 0 else none], axis=1
        )
        for j in steps
    ]
    return dot(left, jnp.concatenate(right, axis=0))


def depth_one(shifted, s, weights):
    left = jnp.concatenate([shifted[s, b : b + 16].reshape(256, 384) for b in range(3)], axis=1)
    return dot(left, weights)


def front_stage(odd, rep, volume, decode, off_chip, on_chip, *refs):
    done = refs[-1]
    pairs = [
        (volume.at[pl.ds(odd[0], 3)], off_chip),
        (volume.at[pl.ds(1 - odd[0], 3)], on_chip),
    ]
    if len(refs) == 2:
        block = refs[0]
        at = pl.multiple_of(528 * rep[0], 16)
        pairs += [
            (decode.at[pl.ds(at, 336)], block.at[pl.ds(0, 336)]),
            (decode.at[pl.ds(336, 192)], block.at[pl.ds(336, 192)]),
        ]
    copies = [
        pltpu.make_async_copy(source, target, done.at[i]) for i, (source, target) in enumerate(pairs)
    ]
    for copy in copies:
        copy.start()
    for copy in copies:
        copy.wait()


def own_stage(volume, weights, out, shifted):
    for s in range(4):
        shift_slice(shifted, s, volume[s])
    out[0, :, :128] = jnp.zeros((256, 128), jnp.float32)
    out[0, :, 128:] = depth_one(shifted, 0, weights[2])
    out[1] = depth_pair(shifted, (0, 1, 2), weights, (1, 2, 3))
    out[2] = depth_pair(shifted, (1, 2, 3), weights, (0, 1, 2))
    out[3, :, :128] = depth_one(shifted, 3, weights[0])
    out[3, :, 128:] = jnp.zeros((256, 128), jnp.float32)


def stem_stage(marks, off_chip, on_chip, own, weights, second, order, _, *refs):
    pooled_out, skip_outs = refs[0], refs[1 : 1 + GROUP]
    shifted, halves, framed, patches, quarters, blocks = refs[1 + GROUP :]
    for s in range(3):
        even = marks[4] == 0
        shift_slice(shifted, s, jnp.where(even, off_chip[s], on_chip[s]))
        shift_slice(shifted, 3 + s, jnp.where(even, on_chip[s], off_chip[s]))
    framed[...] = jnp.zeros(framed.shape, jnp.float32)
    for m in range(4):
        if m == 0:
            first = own[0] + depth_pair(shifted, (0, 1, 2), weights, (0, 1, 2))
        elif m == 3:
            first = own[3] + depth_pair(shifted, (3, 4, 5), weights, (1, 2, 3))
        elif m == 1:
            near = own[1, :, :128] + depth_one(shifted, 2, weights[0])
            first = jnp.concatenate([near, own[1, :, 128:]], axis=1)
        else:
            far = own[2, :, 128:] + depth_one(shifted, 3, weights[2])
            first = jnp.concatenate([own[2, :, :128], far], axis=1)
        first = round_once(jnp.maximum(first, 0.0))
        pair = (first[:, :128] + first[:, 128:]).reshape(8, 32, 128)
        halves[...] = (pair[:, :16] + pair[:, 16:]).reshape(128, 128)
        pooled = halves[pl.ds(0, 64, stride=2), :] + halves[pl.ds(1, 64, stride=2), :]
        pooled = round_once(pooled * 0.125)
        if m == 0:
            pooled = jnp.where(marks[5] == 0, 0.0, pooled)
        if m == 3:
            pooled = jnp.where(marks[6] == 0, 0.0, pooled)
        framed[m, 1:9, 8:16, :] = pooled.reshape(8, 8, 128)
    fill_patches(framed, patches, 4)
    skip = dot(patches[0:128], second[0])
    skip += dot(patches[64:192], second[1])
    skip += dot(patches[128:256], second[2])
    skip = jnp.maximum(skip, 0.0).astype(jnp.bfloat16)
    wide = skip.astype(jnp.float32)
    pair = (wide[:64] + wide[64:]).reshape(4, 16, 256)
    pair = (pair[:, :8] + pair[:, 8:]).reshape(32, 256)
    for k in range(2):
        quarters[k] = pair[:, 128 * k : 128 * k + 128]
    pooled = jnp.concatenate(
        [
            quarters[k, pl.ds(0, 16, stride=2), :] + quarters[k, pl.ds(1, 16, stride=2), :]
            for k in range(2)
        ],
        axis=1,
    )
    pooled = (pooled * 0.125).astype(jnp.bfloat16)
    for p in range(pooled_out.shape[0]):
        pooled_out[p] = pooled
    sorted_skip = dot(skip, order[...])
    for r in range(GROUP):
        near, far = sorted_skip[:64, 64 * r : 64 * r + 64], sorted_skip[64:, 64 * r : 64 * r + 64]
        block = jnp.concatenate([near, far], axis=1)
        block = jnp.concatenate([block[:32], block[32:]], axis=1).astype(jnp.bfloat16)
        blocks[r, 0:32, :] = block
        first, last = sorted_skip[16 * r : 16 * r + 16], sorted_skip[64 + 16 * r : 80 + 16 * r]
        blocks[r, 32:48, :] = jnp.where(marks[0] == 0, first, last).astype(jnp.bfloat16)
    for k in range(GROUP):
        skip_outs[k][...] = blocks[marks[0] ^ k]


def edge_slice(block, far):
    lower = lax.broadcasted_iota(jnp.int32, (16, 128), 1) < 64
    sides = []
    for k in range(2):
        half = block[:, 128 * k : 128 * k + 128].astype(jnp.float32)
        top, bottom = half[:16], half[16:]
        if far:
            top = pltpu.roll(top, 64, 1)
        else:
            bottom = pltpu.roll(bottom, 64, 1)
        sides.append(jnp.where(lower, top, bottom))
    return jnp.concatenate(sides, axis=1)


def spread_taps(weights, values, dims, chans, voxels):
    lane = lax.broadcasted_iota(jnp.int32, (chans, voxels), 1)

    def moved(term, tap, step, place, last):
        if tap == 1:
            return term
        keep = place > 0 if tap == 0 else place < last
        return jnp.where(keep, pltpu.roll(term, ((1 - tap) * step) % voxels, 1), 0.0)

    total = None
    for a in range(3):
        products = dot(weights[a * 9 * chans : (a + 1) * 9 * chans, :], values, dims)
        plane = None
        for b in range(3):
            line = None
            for c in range(3):
                at = (b * 3 + c) * chans
                term = moved(products[at : at + chans], c, 1, lane & 3, 3)
                line = term if line is None else line + term
            line = moved(line, b, 4, (lane >> 2) & 3, 3)
            plane = line if plane is None else plane + line
        plane = moved(plane, a, 16, lane >> 4, voxels // 16 - 1)
        total = plane if total is None else total + plane
    return jnp.maximum(total, 0.0)


def by_rank(marks, near, blocks):
    for k in range(GROUP):
        blocks[marks[0] ^ k] = near[k][near[k].shape[0] - 48 :, :]


def by_depth(marks, near, parts, step):
    for k in range(GROUP):
        parts[marks[0] ^ k] = near[k][0 : parts.shape[1], :]
    return jnp.concatenate(
        [
            parts[r, at : at + step, :]
            for at in range(0, parts.shape[1], step)
            for r in range(GROUP)
        ],
        axis=0,
    )


def relay_stage(marks, *refs):
    line, refs = refs[:GROUP], refs[GROUP:]
    step = line[0].shape[0]
    skips, outs = refs[:GROUP], refs[GROUP:]
    for j in range(GROUP):
        for k in range(GROUP):
            outs[j][pl.ds(pl.multiple_of((marks[3] ^ k) * step, 16), step), :] = line[k][...]
        outs[j][GROUP * step :, :] = skips[j][...]


def edge_stage(marks, *refs):
    near, (near_swap, far_swap, blocks) = refs[:GROUP], refs[GROUP:]
    by_rank(marks, near, blocks)
    first = edge_slice(blocks[0, 0:32, :], False)
    last = edge_slice(blocks[GROUP - 1, 0:32, :], True)
    even = marks[2] == 0
    near_swap[...] = jnp.where(even, last, first).astype(jnp.bfloat16)
    far_swap[...] = jnp.where(even, first, last).astype(jnp.bfloat16)


def deep_stage(marks, weights, *refs):
    near, out, parts = refs[:-2], refs[-2], refs[-1]
    _, chans, voxels = out.shape
    values = near[0][...] if len(near) == 1 else by_depth(marks, near, parts, 16)
    deep = spread_taps(weights, values, ((1,), (1,)), chans, voxels).astype(jnp.bfloat16)
    for dest in range(out.shape[0]):
        out[dest] = deep


def rider_stage(marks, *refs):
    near, (out, blocks) = refs[:GROUP], refs[GROUP:]
    by_rank(marks, near, blocks)
    edges = [blocks[r, 32:48, :].astype(jnp.float32) for r in (0, GROUP - 1)]
    riders = [
        [
            jnp.concatenate(
                [
                    pltpu.roll(edge[:, at // 128 * 128 : at // 128 * 128 + 128], (96 - at) % 128, 1)
                    for at in (64 * r, 64 * r + 32)
                ],
                axis=0,
            )
            for r in range(GROUP)
        ]
        for edge in edges
    ]
    for e in range(2):
        for r in range(GROUP):
            out[e, r] = riders[e][r]


def deeper_stage(near_count, marks, weights, *refs):
    near, (deep, out, blocks) = refs[:near_count], refs[near_count:]
    n, chans, _ = out.shape
    voxels = deep.shape[1]
    deeper = spread_taps(weights, deep[...], ((1,), (0,)), chans, voxels)
    lane = lax.broadcasted_iota(jnp.int32, (chans, 128), 1)
    planes = n // GROUP
    ride = len(near) == 1
    if ride:
        riders = near[0]
    for p in range(planes):
        part = pltpu.roll(deeper, (16 - 64 * p) % voxels, 1)[:, :128]
        if p == 0:
            part = jnp.where(lane < 16, 0.0, part)
        if p == planes - 1:
            part = jnp.where(lane >= 80, 0.0, part)
        for r in range(GROUP):
            whole = part
            if ride:
                rider = jnp.where(marks[3] < p, riders[1, r], riders[0, r])
                whole = jnp.where(lane < 96, part, rider)
            out[GROUP * p + r] = whole.astype(jnp.bfloat16)


def rise_stage(marks, chans, rise, out):
    lane = lax.broadcasted_iota(jnp.int32, (256, 64), 1)
    row = lax.broadcasted_iota(jnp.int32, (256, 64), 0)
    source = (marks[0] + GROUP * (lane // chans)) * chans + lane % chans
    mine = jnp.where(row == source, 1.0, 0.0).astype(jnp.bfloat16)
    for pair in range(4):
        both = [dot(rise[2 * pair + k], mine) for k in range(2)]
        both = jnp.concatenate(both, axis=1).astype(jnp.bfloat16)
        out[:, 128 * pair : 128 * pair + 128] = both


def decode_stage(ride, marks, deeper, rise, *refs):
    swaps = () if ride else refs[:2]
    near, refs = refs[len(swaps) : len(swaps) + GROUP], refs[len(swaps) + GROUP :]
    decode, outs = refs[: -5 - GROUP], refs[-5 - GROUP : -5]
    framed, patches, risen, blocks, parts = refs[-5:]
    by_rank(marks, near, blocks)
    n, chans, _ = deeper.shape
    plane, planes = marks[3], n // GROUP
    upper = lax.broadcasted_iota(jnp.int32, (64, 128), 1) >= 64

    def edge(low):
        if not ride:
            even = marks[2] == 0
            sides = [swap[...].astype(jnp.float32) for swap in swaps]
            side = jnp.where(even, sides[low], sides[not low])
            parts = []
            for k in range(2):
                half = side[:, 128 * k : 128 * k + 128]
                parts += [pltpu.roll(half, 64, 1), half]
            return jnp.concatenate(parts, axis=0)
        other = jnp.maximum(plane - 1, 0) if low else jnp.minimum(plane + 1, planes - 1)
        lane = lax.broadcasted_iota(jnp.int32, (16, 128), 1)
        parts = []
        for r in range(GROUP):
            block = deeper[GROUP * other + r].astype(jnp.float32)
            parts.append(jnp.where(lane < 96, pltpu.roll(block[:16], 96, 1), block[16:]))
        return jnp.where(other == plane, 0.0, jnp.concatenate(parts, axis=0))

    framed[...] = jnp.zeros(framed.shape, jnp.float32)
    spread = round_once(dot(deeper[...].reshape(n * chans, 128).astype(jnp.float32).T.astype(jnp.bfloat16), rise[...]))
    for pair in range(4):
        both = spread[:, 128 * pair : 128 * pair + 128]
        risen[2 * pair] = both
        risen[2 * pair + 1] = pltpu.roll(both, 64, 1)
    for s in range(10):
        d, a = (s + 1) // 2, (s + 1) % 2
        for h in range(4):
            for b in range(2):
                for c in range(2):
                    framed[s, 1 + 2 * h + b, pl.ds(8 + c, 4, stride=2), :] = risen[
                        4 * a + 2 * b + c, 16 * d + 4 * h : 16 * d + 4 * h + 4, :
                    ]
        if s == 0 or s == 9:
            skip = edge(s == 0)
        else:
            both = blocks[(s - 1) // 2, 0:32, :].astype(jnp.float32)
            skip = jnp.concatenate([both[:, :128], both[:, 128:]], axis=0)
            if (s - 1) % 2 == 0:
                skip = pltpu.roll(skip, 64, 1)
        joined = framed[s, 1:9, 8:16, :].reshape(64, 128)
        framed[s, 1:9, 8:16, :] = jnp.where(upper, skip, joined).reshape(8, 8, 128)
    fill_patches(framed, patches, 10)
    def rows_at(rep, z, row):
        if rep == 0 and row >= 528:
            return decode[1][z, row - 528 : row - 512, :]
        if rep == 1 and row < 336:
            return decode[1][z, row : row + 16, :]
        if rep == 1 and row >= 528:
            row -= 528
        return decode[0][z, row : row + 16, :]

    def multiply(rep):
        count = decode[0].shape[0]
        step = 128 // count
        partial = None
        for a in range(3):
            right = [
                rows_at(rep, z, row)
                for tap in range(9 * a, 9 * a + 9)
                for z in range(count)
                for row in range(tap * step, (tap + 1) * step, 16)
            ]
            term = dot(patches[64 * a : 64 * a + 512], jnp.concatenate(right, axis=0))
            partial = term if partial is None else partial + term
        parts[...] = partial.astype(jnp.bfloat16).reshape(GROUP, 128, 256)

    if len(decode) == 1:
        multiply(None)
    else:
        pl.when(marks[1] == 0)(lambda: multiply(0))
        pl.when(marks[1] == 1)(lambda: multiply(1))
    for k in range(GROUP):
        outs[k][...] = parts[marks[0] ^ k]


def final_stage(*refs):
    partials, (weights, out, spaced) = refs[:GROUP], refs[GROUP:]
    decoded = partials[0][...].astype(jnp.float32)
    for partial in partials[1:]:
        decoded += partial[...].astype(jnp.float32)
    decoded = jnp.maximum(decoded, 0.0).astype(jnp.bfloat16)
    for a in range(2):
        for b in range(2):
            for c in range(2):
                values = dot(decoded, weights[4 * a + 2 * b + c])
                for d in range(2):
                    for h in range(8):
                        at = ((2 * d + a) * 16 + 2 * h + b) * 16 + c
                        spaced[pl.ds(at, 8, stride=2), :] = values[64 * d + 8 * h : 64 * d + 8 * h + 8]
    out[...] = spaced[...].astype(jnp.bfloat16)


ALL = ("z", "r")


def exchange(payload, axis):
    return lax.all_to_all(payload, axis, split_axis=0, concat_axis=0, tiled=True)


def by_xor(blocks, axis):
    swaps = [[(r, r ^ k) for r in range(GROUP)] for k in range(GROUP)]
    return [blocks[0]] + [lax.ppermute(blocks[k], axis, swaps[k]) for k in range(1, GROUP)]


def body(
    volume,
    first_kernel,
    second_kernel,
    deep_kernel,
    deeper_kernel,
    rise_kernel,
    decode_kernel,
    final_kernel,
):
    n = lax.axis_size(ALL)
    place = lax.axis_index(ALL)
    planes = n // GROUP
    rank = lax.axis_index("r")
    chans = deep_kernel.shape[4]
    voxels = 16 * n
    bf16 = functools.partial(jax.ShapeDtypeStruct, dtype=jnp.bfloat16)

    rep, plane = lax.axis_index("rep"), lax.axis_index("z")
    marks = jnp.stack([rank, rep, plane % 2, plane, place % 2, place, n - 1 - place])
    marks = marks.astype(jnp.int32)
    decode_block = decode_kernel.reshape(27 * chans, 256)
    shared = lax.axis_size("rep") == 2 and chans == 32
    ride = chans == 32
    paired = planes == GROUP
    halo = bf16((3, 16, 16, 128))
    in_spaces = [pltpu.SMEM, pltpu.SMEM, pl.ANY, pl.ANY]
    off_chip, on_chip, *share = pl.pallas_call(
        front_stage,
        out_shape=(halo, halo) + (bf16((528, 256)),) * shared,
        in_specs=[pl.BlockSpec(memory_space=space) for space in in_spaces],
        out_specs=(pl.BlockSpec(memory_space=pltpu.VMEM),) * (2 + shared),
        scratch_shapes=[pltpu.SemaphoreType.DMA((4,))],
        compiler_params=pltpu.CompilerParams(vmem_limit_bytes=60 * MIB),
        cost_estimate=pl.CostEstimate(flops=0, bytes_accessed=10**6, transcendentals=0),
    )(
        (place % 2).astype(jnp.int32).reshape(1),
        rep.astype(jnp.int32).reshape(1),
        volume,
        decode_block,
    )
    pairs = [(i, i + 1) for i in range(1, n - 1, 2)]
    off_chip = lax.ppermute(off_chip, ALL, pairs + [(j, i) for i, j in pairs])
    on_chip = lax.ppermute(on_chip, ALL, [(i, i ^ 1) for i in range(n)])
    if shared:
        decode_block = share[0]
    line = lax.all_gather(decode_block, "z", axis=0)

    pairs = [(i, i + 1) for i in range(1, n - 1, 2)]
    taps = first_kernel.reshape(3, 1152, 128)
    own = call(
        own_stage,
        jax.ShapeDtypeStruct((4, 256, 256), jnp.float32),
        [pltpu.VMEM((4, 18, 16, 384), jnp.bfloat16)],
        (volume, taps),
        2 * 1024 * 2304 * 256,
        24,
    )
    lane = np.arange(256)
    source = (lane // 64 + GROUP * (lane % 64 // chans)) * chans + lane % chans
    order = jnp.asarray(np.arange(256)[:, None] == source[None, :], jnp.bfloat16)
    rise_part = call(
        lambda marks_ref, *refs: rise_stage(marks_ref, chans, *refs),
        bf16((n * chans, 512)),
        [],
        (marks, rise_kernel.reshape(8, n * chans, 256)),
        2 * 8 * n * chans * 256 * 64,
        16,
        scalars=1,
    )
    pooled_two, *skips = call(
        stem_stage,
        (bf16((1 if paired else n, 16, 256)),) + (bf16((48, 256)),) * GROUP,
        [
            pltpu.VMEM((6, 18, 16, 384), jnp.bfloat16),
            pltpu.VMEM((128, 128), jnp.float32),
            pltpu.VMEM((4, 10, 24, 128), jnp.float32),
            pltpu.VMEM((256, 1152), jnp.bfloat16),
            pltpu.VMEM((2, 32, 128), jnp.float32),
            pltpu.VMEM((GROUP, 48, 256), jnp.bfloat16),
        ],
        (marks, off_chip, on_chip, own, taps, second_kernel.reshape(3, 1152, 256), order, rise_part),
        2 * 1024 * 2304 * 256,
        24,
        scalars=1,
        unread=1,
    )
    if paired:
        line_blocks = by_xor([pooled_two.reshape(16, 256)] * GROUP, "z")
        relays = call(
            relay_stage,
            (bf16((112, 256)),) * GROUP,
            [],
            (marks, *line_blocks, *skips),
            0,
            16,
            scalars=1,
        )
        near = by_xor(relays, "r")
        pooled_whole = near
    else:
        pooled_whole = (exchange(pooled_two, ALL).reshape(voxels, 256),)
        near = by_xor(skips, "r")
    blocks = pltpu.VMEM((GROUP, 48, 256), jnp.bfloat16)

    deep = call(
        deep_stage,
        bf16((n, chans, voxels)),
        [pltpu.VMEM((GROUP, 64, 256), jnp.bfloat16)],
        (
            marks,
            deep_kernel.transpose(0, 1, 2, 4, 3).reshape(27 * chans, 256),
            *pooled_whole,
        ),
        2 * 27 * chans * 256 * voxels,
        16,
        scalars=1,
    )
    if shared:
        weights = (line, lax.ppermute(line[:, :336], "rep", [(0, 1), (1, 0)]))
    elif chans % 16:
        weights = line.reshape(planes, 27, chans, 256).transpose(1, 0, 2, 3)
        weights = (weights.reshape(1, 27 * 128, 256),)
    else:
        weights = (line,)
    swaps = ()
    if not ride:
        swaps = call(
            edge_stage,
            (bf16((16, 256)), bf16((16, 256))),
            [blocks],
            (marks, *near),
            0,
            16,
            scalars=1,
        )
        near_pairs = [(p, p + 1) for p in range(0, planes - 1, 2)]
        far_pairs = [(p, p + 1) for p in range(1, planes - 1, 2)]
        near_swap = lax.ppermute(swaps[0], "z", near_pairs + [(j, i) for i, j in near_pairs])
        far_swap = lax.ppermute(swaps[1], "z", far_pairs + [(j, i) for i, j in far_pairs])
        swaps = (near_swap, far_swap)
    deep_whole = (exchange(deep, ALL).reshape(n * chans, voxels),)

    riders = ()
    if ride:
        shape = jax.ShapeDtypeStruct((2, GROUP, 32, 128), jnp.float32)
        riders = (call(rider_stage, shape, [blocks], (marks, *near), 0, 16, scalars=1),)
    deeper = call(
        functools.partial(deeper_stage, len(riders)),
        bf16((n, chans, 128)),
        [blocks],
        (
            marks,
            deeper_kernel.transpose(0, 1, 2, 4, 3).reshape(27 * chans, n * chans),
            *riders,
            *deep_whole,
        ),
        2 * 27 * chans * n * chans * voxels,
        16,
        scalars=1,
    )
    deeper_near = exchange(deeper, ALL)

    partials = call(
        functools.partial(decode_stage, ride),
        (bf16((128, 256)),) * GROUP,
        [
            pltpu.VMEM((10, 10, 24, 128), jnp.float32),
            pltpu.VMEM((640, 1152), jnp.bfloat16),
            pltpu.VMEM((8, 128, 128), jnp.float32),
            blocks,
            pltpu.VMEM((GROUP, 128, 256), jnp.bfloat16),
        ],
        (marks, deeper_near, rise_part, *swaps, *near, *weights),
        2 * 512 * 3456 * 256,
        24,
        scalars=1,
    )
    partials = by_xor(partials, "r")
    out = call(
        final_stage,
        bf16((1024, 128)),
        [pltpu.VMEM((1024, 128), jnp.float32)],
        (*partials, final_kernel.reshape(8, 256, 128)),
        2 * 128 * 256 * 1024,
        16,
    )
    return out.reshape(4, 16, 16, 128)


def solution(mesh):
    reps, n = mesh.devices.shape
    grid = jax.sharding.Mesh(mesh.devices.reshape(reps, n // GROUP, GROUP), ("rep",) + ALL)
    return jax.shard_map(
        body,
        mesh=grid,
        in_specs=(
            P(("rep",) + ALL, None, None, None),
            P(),
            P(),
            P(None, None, None, None, ALL),
            P(None, None, None, None, ALL),
            P(),
            P(None, None, None, ALL, None),
            P(),
        ),
        out_specs=P(("rep",) + ALL, None, None, None),
        check_vma=False,
    )
```
